128 devices in a mesh: dp: 64 (over y_hi, x, z, core), tensor: 2 (over y_lo).
Axes of the slice: x: 4, y: 4 (y_hi: 2, y_lo: 2; y = y_hi * 2 + y_lo), z: 4, core: 2. Of those that a mesh axis runs over, the one named last changes fastest.
Arguments:
- inputs: bfloat16 [2, 16384, 1536], P(None, ('dp', 'tensor')), may hold values from -24 to 24
- out_grad: bfloat16 [2, 16384, 1536], P(None, ('dp', 'tensor')), may hold values from -24 to 24
- lengths: int32 [2, 64], P(None, 'dp'), may hold values from 64 to 256, as said below
- query_weight: bfloat16 [1536, 1536], P('dp', 'tensor'), may hold values from -0.21875 to 0.21875
- key_matrix: bfloat16 [1536, 768], P('dp', 'tensor'), may hold values from -0.15625 to 0.15625
- value_matrix: bfloat16 [1536, 768], P('dp', 'tensor'), may hold values from -0.15625 to 0.15625
- output_weight: bfloat16 [1536, 1536], P('tensor', 'dp'), may hold values from -0.625 to 0.625
- gate_weight: bfloat16 [1536, 4096], P('dp', 'tensor'), may hold values from -0.15625 to 0.15625
- up_weight: bfloat16 [1536, 4096], P('dp', 'tensor'), may hold values from -0.15625 to 0.15625
- down_weight: bfloat16 [4096, 1536], P('tensor', 'dp'), may hold values from -0.09375 to 0.09375
- attn_gain: bfloat16 [1536], P('dp'), may hold values from 0.5 to 1.5
- mlp_gain: bfloat16 [1536], P('dp'), may hold values from 0.5 to 1.5
Outputs:
- outputs: bfloat16 [2, 16384, 1536], P(None, ('dp', 'tensor'))
- input_grad: float32 [2, 16384, 1536], P(None, ('dp', 'tensor'))
- query_grad: float32 [1536, 1536], P('dp', 'tensor')
- key_grad: float32 [1536, 768], P('dp', 'tensor')
- value_grad: float32 [1536, 768], P('dp', 'tensor')
- output_grad: float32 [1536, 1536], P('tensor', 'dp')
- gate_grad: float32 [1536, 4096], P('dp', 'tensor')
- up_grad: float32 [1536, 4096], P('dp', 'tensor')
- down_grad: float32 [4096, 1536], P('tensor', 'dp')
- attn_gain_grad: float32 [1536], P('dp')
- mlp_gain_grad: float32 [1536], P('dp')
The draws below stay inside these ranges and needn't reach their ends.
Inputs may be any that keep to these rules, and one draw needn't show every extreme that they name: `lengths`: in every group one micro-batch, drawn from the seed, has length 256.
All inputs are finite; a program needn't handle non-finite values.
Results may differ from the reference program's by a relative error of at most 0.015.
Values may be sent and summed in bfloat16 or wider, within the bound.
A program may use at most 320 MiB of HBM per device.

```python
import math
import jax
import jax.numpy as jnp
from jax import lax

MODEL_WIDTH = 1536
QUERY_HEADS = 16
KEY_VALUE_HEADS = 8
HEAD_SIZE = 96
FF = 4096
SEQ = 256
MB = 2
GROUPS = 64
TOKENS = 16384


def draw_lengths(key, part):
    key = jax.random.fold_in(key, 7)
    first_key, second_key = jax.random.split(key)
    drawn = jax.random.randint(first_key, (MB, GROUPS), SEQ // 4, SEQ + 1)
    chosen = jax.random.randint(second_key, (GROUPS,), 0, MB)
    picked = jnp.arange(MB)[:, None] == chosen[None, :]
    return jnp.where(picked, SEQ, drawn).astype(jnp.int32)


def spiked(values, own_key, source, target, shards_of, factor):
    owner, partner = [(jnp.arange(values.shape[position]) // (values.shape[position] // shards_of)).reshape([-1 if axis == position else 1 for axis in range(values.ndim)]) for position in (source, target)]
    chosen = jax.random.permutation(own_key, shards_of)[partner]
    strong = (owner == chosen) | (owner == (partner + shards_of // 2) % shards_of)
    return jnp.where(strong, factor * values, values)


def levels(rng, dims, shards, least, largest):
    level = 1.0
    for position, parts in shards:
        steps = jax.random.uniform(jax.random.fold_in(jax.random.fold_in(rng, 6), position), (parts,), jnp.float32, least / len(shards), largest / len(shards))
        level = level * jnp.repeat(jnp.exp(steps), dims[position] // parts).reshape((-1,) + (1,) * (len(dims) - 1 - position))
    return level


def noise(key, dims, scale, most, cuts=(), kind=jnp.bfloat16):
    entries = scale * jax.random.normal(key, dims, jnp.float32)
    if cuts:
        entries = entries * levels(key, dims, cuts, -0.22, 0.18)
    return jnp.clip(entries, -most, most).astype(kind)


def bell_draw_with(key, extent, scale, most, pieces, heavy, held_as=jnp.bfloat16):
    entries = scale * jax.random.normal(key, extent, jnp.float32)
    if pieces:
        entries = entries * levels(key, extent, pieces, -0.22, 0.18)
    return jnp.clip(spiked(entries, jax.random.fold_in(key, 3), *heavy), -most, most).astype(held_as)


def setup_inputs(seed: int = 0) -> dict:
    arg_keys = jax.random.split(jax.random.key(seed), 13)
    return {
        "inputs": bell_draw_with(arg_keys[0], (MB, TOKENS, MODEL_WIDTH), 1.0, 24.0, ((1, 128),), (1, 2, 128, 5.5)),
        "out_grad": bell_draw_with(arg_keys[1], (MB, TOKENS, MODEL_WIDTH), 1.0, 24.0, ((1, 128),), (1, 2, 128, 5.5)),
        "lengths": draw_lengths(jax.random.fold_in(arg_keys[12], 71), 0),
        "query_weight": noise(arg_keys[3], (MODEL_WIDTH, QUERY_HEADS * HEAD_SIZE), (MODEL_WIDTH // 2) ** -0.5, 0.21875, ((0, 64), (1, 2))),
        "key_matrix": noise(arg_keys[4], (MODEL_WIDTH, KEY_VALUE_HEADS * HEAD_SIZE), MODEL_WIDTH ** -0.5, 0.15625, ((0, 64), (1, 2))),
        "value_matrix": noise(arg_keys[5], (MODEL_WIDTH, KEY_VALUE_HEADS * HEAD_SIZE), MODEL_WIDTH ** -0.5, 0.15625, ((0, 64), (1, 2))),
        "output_weight": noise(arg_keys[6], (QUERY_HEADS * HEAD_SIZE, MODEL_WIDTH), (QUERY_HEADS * HEAD_SIZE // 16) ** -0.5, 0.625, ((0, 2), (1, 64))),
        "gate_weight": noise(arg_keys[7], (MODEL_WIDTH, FF), MODEL_WIDTH ** -0.5, 0.15625, ((0, 64), (1, 2))),
        "up_weight": noise(arg_keys[8], (MODEL_WIDTH, FF), MODEL_WIDTH ** -0.5, 0.15625, ((0, 64), (1, 2))),
        "down_weight": noise(arg_keys[9], (FF, MODEL_WIDTH), FF ** -0.5, 0.09375, ((0, 2), (1, 64))),
        "attn_gain": jnp.clip(1.0 + 0.1 * jax.random.normal(arg_keys[10], (MODEL_WIDTH,), jnp.float32), 0.5, 1.5).astype(jnp.bfloat16),
        "mlp_gain": jnp.clip(1.0 + 0.1 * jax.random.normal(arg_keys[11], (MODEL_WIDTH,), jnp.float32), 0.5, 1.5).astype(jnp.bfloat16),
    }


epsilon = 1e-05
rope_base = 100000.0
highest = lax.Precision.HIGHEST

@jax.custom_vjp
def precision_lowered(v):
    return lax.optimization_barrier(v.astype(jnp.bfloat16)).astype(jnp.float32)

@jax.custom_vjp
def lowered_backward(v):
    return v

def low_keep(v):
    return (precision_lowered(v), None)

def low_pass(kept, grad):
    return (grad,)

def back_keep(v):
    return (v, None)

def back_low(kept, grad):
    return (precision_lowered(grad),)
precision_lowered.defvjp(low_keep, low_pass)
lowered_backward.defvjp(back_keep, back_low)

def matrix_product(left, right):
    return jnp.dot(left, right, precision=highest)

def normed(values, gain):
    return values * lax.rsqrt(lax.optimization_barrier(jnp.mean(values * values, -1, keepdims=True)) + epsilon) * gain

def rope_tables(element_count, width):
    half_width = width // 2
    inverse = rope_base ** (-(jnp.arange(half_width, dtype=jnp.float32) * 2.0) / width)
    angle = jnp.arange(element_count, dtype=jnp.float32)[:, None] * inverse[None, :]
    cosine_table = jnp.cos(angle)
    sine_table = jnp.sin(angle)
    return (jnp.concatenate([cosine_table, cosine_table], -1), jnp.concatenate([sine_table, sine_table], -1))

def rotary_apply(values, cosine_table, sine_table):
    half_width = values.shape[-1] // 2
    turned = jnp.concatenate([-values[..., half_width:], values[..., :half_width]], -1)
    return values * cosine_table[:, None, :] + turned * sine_table[:, None, :]

def layer(xrow, length, weights):
    w_query, key_projection_weight, value_projection_weight, w_output, w_gate, w_upward, w_down, gain_one, gain_two = weights
    element_count = xrow.shape[0]
    query_groups = QUERY_HEADS // KEY_VALUE_HEADS
    cosine_table, sine_table = rope_tables(element_count, HEAD_SIZE)
    normed_first_input = precision_lowered(normed(xrow, gain_one))
    query_rows_all = precision_lowered(rotary_apply(lowered_backward(matrix_product(normed_first_input, w_query)).reshape(element_count, QUERY_HEADS, HEAD_SIZE), cosine_table, sine_table))
    query_rows_all = query_rows_all.reshape(element_count, KEY_VALUE_HEADS, query_groups, HEAD_SIZE)
    expanded_keys = precision_lowered(rotary_apply(lowered_backward(matrix_product(normed_first_input, key_projection_weight)).reshape(element_count, KEY_VALUE_HEADS, HEAD_SIZE), cosine_table, sine_table))
    expanded_values = precision_lowered(lowered_backward(matrix_product(normed_first_input, value_projection_weight))).reshape(element_count, KEY_VALUE_HEADS, HEAD_SIZE)
    scores = lowered_backward(jnp.einsum('qkgd,skd->kgqs', query_rows_all, expanded_keys, precision=highest) * (1.0 / math.sqrt(HEAD_SIZE)))
    positions = jnp.arange(element_count)
    keep = (positions[None, :] <= positions[:, None]) & (positions[None, :] < length)
    scores = jnp.where(keep, scores, -1e+30)
    row_max = lax.optimization_barrier(jnp.max(scores, -1, keepdims=True))
    exp_terms = jnp.exp(scores - row_max)
    probs = precision_lowered(exp_terms / lax.optimization_barrier(jnp.sum(exp_terms, -1, keepdims=True)))
    mixed = lowered_backward(precision_lowered(jnp.einsum('kgqs,skd->qkgd', probs, expanded_values, precision=highest)))
    mixed = mixed.reshape(element_count, QUERY_HEADS * HEAD_SIZE)
    hidden = xrow + lowered_backward(matrix_product(mixed, w_output))
    second_normed = precision_lowered(normed(hidden, gain_two))
    gate_lin = lowered_backward(matrix_product(second_normed, w_gate))
    up_lin = lowered_backward(matrix_product(second_normed, w_upward))
    active = precision_lowered(gate_lin * jax.nn.sigmoid(gate_lin) * up_lin)
    return hidden + lowered_backward(matrix_product(active, w_down))

def reference(inputs, out_grad, lengths, query_weight, key_matrix, value_matrix, output_weight, gate_weight, up_weight, down_weight, attn_gain, mlp_gain):
    sequences = inputs.astype(jnp.float32).reshape(MB * GROUPS, SEQ, MODEL_WIDTH)
    seq_lengths = lengths.reshape(MB * GROUPS)
    valid_rows = (jnp.arange(SEQ)[None, :] < seq_lengths[:, None]).astype(jnp.float32)
    cotangent = out_grad.astype(jnp.float32).reshape(MB * GROUPS, SEQ, MODEL_WIDTH) * valid_rows[:, :, None]
    weights = tuple((w.astype(jnp.float32) for w in (query_weight, key_matrix, value_matrix, output_weight, gate_weight, up_weight, down_weight, attn_gain, mlp_gain)))

    def forward(seqs, params):

        def one_seq(pair_item):
            return jax.checkpoint(layer)(pair_item[0], pair_item[1], params)
        return lax.map(one_seq, (seqs, seq_lengths))
    result, pullback = jax.vjp(forward, sequences, weights)
    seq_grad, weight_grads = pullback(cotangent)
    return (result.reshape(MB, TOKENS, MODEL_WIDTH).astype(jnp.bfloat16), seq_grad.reshape(MB, TOKENS, MODEL_WIDTH), weight_grads[0], weight_grads[1], weight_grads[2], weight_grads[3], weight_grads[4], weight_grads[5], weight_grads[6], weight_grads[7], weight_grads[8])
```

```python
import math

import jax
import jax.numpy as jnp
from jax import lax
from jax.experimental import pallas as pl
from jax.experimental.pallas import tpu as pltpu
from jax.sharding import Mesh
from jax.sharding import PartitionSpec as P

HEAD = 96
EPS = 1e-05
ROPE_BASE = 100000.0
AXES = ("yh", "x", "z", "core", "yl")
DP = ("yh", "x", "z", "core")
MESH = pl.DeviceIdType.MESH
BF = jnp.bfloat16
F32 = jnp.float32
ORDERS = (("x", "y", "z"), ("y", "z", "x"), ("z", "x", "y"))


def coordinates():
    x, z, yh, yl = (lax.axis_index(a) for a in ("x", "z", "yh", "yl"))
    return {"x": x, "z": z, "y": yh * 2 + yl}


def around(value, by):
    return lax.rem(value + (by + 4), 4)


def peer(at, axis, by):
    moved = around(at[axis], by)
    if axis == "y":
        return {"yh": moved // 2, "yl": lax.rem(moved, 2)}
    return {axis: moved}


def place(at, whole=(), half=None, moved=None):
    out = []
    for axis in ("y", "x", "z"):
        if axis in whole:
            if half is not None and half[0] == axis:
                out.append(pl.ds(2 * half[1], 2))
            else:
                out.append(pl.ds(0, 4))
        else:
            value = at[axis] if moved is None or moved[0] != axis else around(at[axis], moved[1])
            out.append(lax.rem(value, 2) * 2 + value // 2 if axis == "y" else value)
    return tuple(out)


def greet(at):
    barrier = pltpu.get_barrier_semaphore()
    for axis in ("x", "y", "z"):
        for by in (1, -1, 2):
            pl.semaphore_signal(barrier, inc=1, device_id=peer(at, axis, by), device_id_type=MESH)
    pl.semaphore_wait(barrier, 9)


def halved(order):
    return "x" if order[2] == "y" else "y"


def gather_kernel(*refs):
    srcs, outs = refs[:3], refs[3:6]
    local, send, recv, last_send, last_recv = refs[6:]
    at = coordinates()
    greet(at)
    own = []
    for p in range(3):
        copy = pltpu.make_async_copy(srcs[p], outs[p].at[place(at)], local.at[p])
        copy.start()
        own.append(copy)
    started = {}
    for stage in range(2):
        for p, order in enumerate(ORDERS):
            if stage:
                own[p].wait()
                for copy in started[p, stage - 1]:
                    copy.wait()
            group = outs[p].at[place(at, order[:stage])]
            started[p, stage] = []
            for d, by in enumerate((1, -1, 2)):
                copy = pltpu.make_async_remote_copy(
                    src_ref=group if stage else srcs[p],
                    dst_ref=group,
                    send_sem=send.at[p, stage, d],
                    recv_sem=recv.at[p, stage, d],
                    device_id=peer(at, order[stage], by),
                    device_id_type=MESH,
                )
                copy.start()
                started[p, stage].append(copy)
    final = {}
    for p, order in enumerate(ORDERS):
        for copy in started[p, 1]:
            copy.wait()
        for turn in range(2):
            for d, by in enumerate((1, -1)):
                h = turn if by == 1 else 1 - turn
                block = outs[p].at[place(at, order[:2], (halved(order), h))]
                copy = pltpu.make_async_remote_copy(
                    src_ref=block,
                    dst_ref=block,
                    send_sem=last_send.at[p, d, h],
                    recv_sem=last_recv.at[p, d, h],
                    device_id=peer(at, order[2], by),
                    device_id_type=MESH,
                )
                copy.start()
                final[p, d, h] = copy
    for p, order in enumerate(ORDERS):
        for d, by in enumerate((1, -1)):
            final[p, d, d].wait_recv()
            block = outs[p].at[
                place(at, order[:2], (halved(order), d), (order[2], -by))
            ]
            copy = pltpu.make_async_remote_copy(
                src_ref=block,
                dst_ref=block,
                send_sem=last_send.at[p, d, 2],
                recv_sem=last_recv.at[p, d, 2],
                device_id=peer(at, order[2], by),
                device_id_type=MESH,
            )
            copy.start()
            final[p, d, 2] = copy
    for p in range(3):
        for d in range(2):
            final[p, d, 0].wait_send()
            final[p, d, 1].wait_send()
            final[p, d, 1 - d].wait_recv()
            final[p, d, 2].wait()


def gathered(pieces, collective_id, name):
    anywhere = pl.BlockSpec(memory_space=pl.ANY)
    size = sum(p.size for p in pieces) * 128
    return pl.pallas_call(
        gather_kernel,
        out_shape=[jax.ShapeDtypeStruct((4, 4, 4) + p.shape, p.dtype) for p in pieces],
        in_specs=[anywhere] * 3,
        out_specs=[anywhere] * 3,
        scratch_shapes=[
            pltpu.SemaphoreType.DMA((3,)),
            pltpu.SemaphoreType.DMA((3, 2, 3)),
            pltpu.SemaphoreType.DMA((3, 2, 3)),
            pltpu.SemaphoreType.DMA((3, 2, 3)),
            pltpu.SemaphoreType.DMA((3, 2, 3)),
        ],
        compiler_params=pltpu.CompilerParams(collective_id=collective_id, has_side_effects=True),
        cost_estimate=pl.CostEstimate(flops=0, bytes_accessed=2 * size, transcendentals=0),
        name=name,
    )(*pieces)


def reduce_kernel(widths, *refs):
    parts = len(widths)
    ins = refs[: 6 * parts]
    outs = refs[6 * parts : 6 * parts + 3]
    data, far, near, second, third = (refs[6 * parts + 3 + 3 * k : 6 * parts + 6 + 3 * k] for k in range(5))
    load, first_send, first_recv, send, recv = refs[6 * parts + 18 :]
    at = coordinates()
    loads = []
    for p in range(3):
        for yl in range(2):
            column = 0
            for k, width in enumerate(widths):
                copy = pltpu.make_async_copy(
                    ins[(p * 2 + yl) * parts + k],
                    data[p].at[pl.ds(2 * yl, 2), :, :, :, pl.ds(column, width)],
                    load.at[p, yl, k],
                )
                copy.start()
                loads.append(copy)
                column += width
    greet(at)
    for copy in loads:
        copy.wait()

    def sent(src, dst, s, r, axis, by):
        copy = pltpu.make_async_remote_copy(
            src_ref=src, dst_ref=dst, send_sem=s, recv_sem=r, device_id=peer(at, axis, by), device_id_type=MESH
        )
        copy.start()
        return copy

    opposite, neighbour = {}, {}
    for p, order in enumerate(ORDERS):
        axis = order[2]
        for d, by in enumerate((1, -1)):
            block = data[p].at[place(at, order[:2], (halved(order), d), (axis, 2))]
            opposite[p, d] = sent(block, far[p].at[d], first_send.at[p, d, 0], first_recv.at[p, d, 0], axis, by)
        for d, by in enumerate((1, -1)):
            h = 1 - d
            block = data[p].at[place(at, order[:2], (halved(order), h), (axis, by))]
            neighbour[p, d, 1] = sent(
                block, near[p].at[d, pl.ds(2 * h, 2)], first_send.at[p, d, 1], first_recv.at[p, d, 1], axis, by
            )
    for p, order in enumerate(ORDERS):
        axis = order[2]
        for d, by in enumerate((1, -1)):
            opposite[p, d].wait_recv()
            where = place(at, order[:2], (halved(order), d), (axis, by))
            block = data[p].at[where]

            @pl.loop(0, 8)
            def _(i, p=p, d=d, block=block):
                a, b = i // 4, lax.rem(i, 4)
                total = block[a, b].astype(F32) + far[p][d, a, b].astype(F32)
                block[a, b] = total.astype(BF)

            neighbour[p, d, 0] = sent(
                block, near[p].at[d, pl.ds(2 * d, 2)], first_send.at[p, d, 2], first_recv.at[p, d, 2], axis, by
            )
    later = {}
    for p, order in enumerate(ORDERS):
        for d in range(2):
            for h in range(2):
                neighbour[p, d, h].wait_recv()
        block = data[p].at[place(at, order[:2])]

        @pl.loop(0, 16)
        def _(i, p=p, block=block):
            a, b = i // 4, lax.rem(i, 4)
            total = block[a, b].astype(F32) + near[p][0, a, b].astype(F32) + near[p][1, a, b].astype(F32)
            block[a, b] = total.astype(BF)

        for d, by in enumerate((1, -1, 2)):
            later[p, 0, d] = sent(
                data[p].at[place(at, order[:1], None, (order[1], by))],
                second[p].at[d],
                send.at[p, 0, d],
                recv.at[p, 0, d],
                order[1],
                by,
            )
    for p, order in enumerate(ORDERS):
        for d in range(3):
            later[p, 0, d].wait_recv()
        block = data[p].at[place(at, order[:1])]

        @pl.loop(0, 4)
        def _(i, p=p, block=block):
            total = block[i].astype(F32)
            for d in range(3):
                total = total + second[p][d, i].astype(F32)
            block[i] = total.astype(BF)

        for d, by in enumerate((1, -1, 2)):
            later[p, 1, d] = sent(
                data[p].at[place(at, (), None, (order[0], by))],
                third[p].at[d],
                send.at[p, 1, d],
                recv.at[p, 1, d],
                order[0],
                by,
            )
    for p, order in enumerate(ORDERS):
        for d in range(3):
            later[p, 1, d].wait_recv()
        total = data[p][place(at)].astype(F32)
        for d in range(3):
            total = total + third[p][d].astype(F32)
        outs[p][...] = total
    for copy in (*opposite.values(), *neighbour.values(), *later.values()):
        copy.wait_send()


def reduced(pieces, widths, collective_id, name):
    anywhere = pl.BlockSpec(memory_space=pl.ANY)
    whole = sum(widths)
    flat = [array for piece in pieces for half in piece for array in half]

    def per_piece(*shape):
        return [pltpu.VMEM(shape + (48, whole), BF) for _ in range(3)]

    return pl.pallas_call(
        lambda *refs: reduce_kernel(widths, *refs),
        out_shape=[jax.ShapeDtypeStruct((48, whole), F32)] * 3,
        in_specs=[anywhere] * len(flat),
        out_specs=[pl.BlockSpec(memory_space=pltpu.VMEM)] * 3,
        scratch_shapes=[
            *per_piece(4, 4, 4),
            *per_piece(2, 2, 4),
            *per_piece(2, 4, 4),
            *per_piece(3, 4),
            *per_piece(3),
            pltpu.SemaphoreType.DMA((3, 2, len(widths))),
            pltpu.SemaphoreType.DMA((3, 2, 3)),
            pltpu.SemaphoreType.DMA((3, 2, 3)),
            pltpu.SemaphoreType.DMA((3, 2, 3)),
            pltpu.SemaphoreType.DMA((3, 2, 3)),
        ],
        compiler_params=pltpu.CompilerParams(
            collective_id=collective_id, has_side_effects=True, vmem_limit_bytes=60 * 1024 * 1024
        ),
        name=name,
    )(*flat)


def rope_tables(count):
    half = HEAD // 2
    inverse = ROPE_BASE ** (-(jnp.arange(half, dtype=F32) * 2.0) / HEAD)
    angle = jnp.arange(count, dtype=F32)[:, None] * inverse[None, :]
    cosine, sine = jnp.cos(angle), jnp.sin(angle)
    return jnp.concatenate([cosine, cosine], -1), jnp.concatenate([sine, sine], -1)


def rotary(values, cosine, sine):
    half = HEAD // 2
    turned = jnp.concatenate([-values[..., half:], values[..., :half]], -1)
    return values * cosine + turned * sine


def rotary_back(grads, cosine, sine):
    half = HEAD // 2
    shifted = grads * sine
    turned = jnp.concatenate([shifted[..., half:], -shifted[..., :half]], -1)
    return grads * cosine + turned


def normalize(values):
    inverse = lax.rsqrt(jnp.mean(values * values, -1, keepdims=True) + EPS)
    return values * inverse, inverse


def norm_back(grad, unit, inverse, gain):
    scaled = grad * gain
    return inverse * (scaled - unit * jnp.mean(scaled * unit, -1, keepdims=True))


def dot(spec, left, right, kind=F32):
    return jnp.einsum(spec, left, right, preferred_element_type=kind)


def body(
    inputs,
    out_grad,
    lengths,
    query_weight,
    key_matrix,
    value_matrix,
    output_weight,
    gate_weight,
    up_weight,
    down_weight,
    attn_gain,
    mlp_gain,
):
    rows, width = inputs.shape[1:]
    slots = 2 * rows
    core = lax.axis_index("core")
    yl = lax.axis_index("yl")

    def halves(weight):
        return weight.reshape(weight.shape[0], 2, -1)

    blocks = [
        halves(query_weight),
        halves(key_matrix),
        halves(value_matrix),
        halves(output_weight.T),
        halves(gate_weight),
        halves(up_weight),
        halves(down_weight.T),
    ]
    sizes = [b.shape[2] for b in blocks]
    packed = jnp.moveaxis(jnp.concatenate(blocks, -1), 1, 0)
    packed = lax.all_to_all(packed, "core", 0, 0, tiled=True).reshape(48, -1)
    gains = lax.all_gather(jnp.stack([attn_gain, mlp_gain], 1), DP, axis=0, tiled=True).astype(F32)
    gain_one, gain_two = gains[:, 0], gains[:, 1]
    third = sizes[0]
    attn_pieces = [packed[:, k * third : (k + 1) * third] for k in range(3)]
    wide = sizes[4]
    mlp_pieces = [packed[:, 3 * third + k * wide : 3 * third + (k + 1) * wide] for k in range(3)]

    both = jnp.stack([inputs, out_grad], 1)
    both = lax.all_to_all(both, "yl", 0, 2, tiled=True)
    both = lax.all_gather(both, "core", axis=0, tiled=True)
    length = lax.all_gather(lax.dynamic_index_in_dim(lengths, yl, 0), "core", axis=0, tiled=True)[:, 0]
    in_rows = both[:, 0].astype(F32)
    valid = (jnp.arange(slots)[None, :] < length[:, None]).astype(F32)
    grad_out = both[:, 1].astype(F32) * valid[:, :, None]

    attn_full = gathered(attn_pieces, 1, "gather_attn")
    mlp_full = gathered([lax.optimization_barrier((p, attn_full[0]))[0] for p in mlp_pieces], 2, "gather_mlp")
    full_query, full_kv, full_output = (w.reshape(2, width, -1) for w in attn_full)
    full_gate, full_up, full_down = (w.reshape(2, width, -1) for w in mlp_full)

    cosine, sine = rope_tables(slots)
    cosine, sine = cosine[:, None, :], sine[:, None, :]
    scale = 1.0 / math.sqrt(HEAD)

    unit_one, inverse_one = normalize(in_rows)
    normed_one = (unit_one * gain_one).astype(BF).reshape(2 * slots, width)
    normed_pair = jnp.broadcast_to(normed_one, (2,) + normed_one.shape)
    query = dot("ytm,ymc->ytc", normed_pair, full_query)
    query = rotary(query.reshape(2, 2, slots, -1, HEAD), cosine, sine).astype(BF)
    kv = dot("ytm,ymc->ytc", normed_pair, full_kv)
    key = rotary(kv[..., : sizes[1]].reshape(2, 2, slots, -1, HEAD), cosine, sine).astype(BF)
    value = kv[..., sizes[1] :].reshape(2, 2, slots, -1, HEAD).astype(BF)
    heads_kv = key.shape[3]
    query = query.reshape(2, 2, slots, heads_kv, -1, HEAD)
    positions = jnp.arange(slots)
    keep = (positions[None, None, :] <= positions[None, :, None]) & (
        positions[None, None, :] < length[:, None, None]
    )
    keep = keep[None, :, None, None]
    scores = dot("yntkgd,ynskd->ynkgts", query, key) * scale
    scores = jnp.where(keep, scores, -1e30)
    row_max = jnp.max(scores, -1, keepdims=True)
    terms = jnp.exp(scores - row_max)
    probs = terms / jnp.sum(terms, -1, keepdims=True)
    probs_low = probs.astype(BF)
    mixed = dot("ynkgts,ynskd->yntkgd", probs_low, value).astype(BF).reshape(2, 2 * slots, -1)
    attn_part = dot("ytc,ymc->tm", mixed, full_output).astype(BF)
    attn_out = lax.psum(attn_part, "core").astype(F32).reshape(2, slots, width)
    hidden = in_rows + attn_out
    unit_two, inverse_two = normalize(hidden)
    normed_two = (unit_two * gain_two).astype(BF).reshape(2 * slots, width)

    normed_pair_two = jnp.broadcast_to(normed_two, (2,) + normed_two.shape)
    gate = dot("ytm,ymc->ytc", normed_pair_two, full_gate)
    up = dot("ytm,ymc->ytc", normed_pair_two, full_up)
    sigma = jax.nn.sigmoid(gate)
    active = (gate * sigma * up).astype(BF)
    mlp_part = dot("ytc,ymc->tm", active, full_down).astype(BF).reshape(2, slots, width)
    mlp_out = lax.psum_scatter(mlp_part, "core", scatter_dimension=0, tiled=True)[0].astype(F32)
    own_hidden = lax.dynamic_index_in_dim(hidden, core, 0, False)
    result = (own_hidden + mlp_out).astype(BF).reshape(2, rows, width)
    result = lax.all_to_all(result, "yl", 0, 0, tiled=True)

    cotangent = grad_out.astype(BF).reshape(2 * slots, width)
    cotangent_pair = jnp.broadcast_to(cotangent, (2,) + cotangent.shape)
    down_part = dot("ytm,ytc->ymc", cotangent_pair, active, BF)
    grad_active = dot("ytm,ymc->ytc", cotangent_pair, full_down)
    grad_gate = (grad_active * up * sigma * (1.0 + gate * (1.0 - sigma))).astype(BF)
    grad_up = (grad_active * gate * sigma).astype(BF)
    gate_part = dot("ytm,ytc->ymc", normed_pair_two, grad_gate, BF)
    up_part = dot("ytm,ytc->ymc", normed_pair_two, grad_up, BF)
    grad_two = dot("ytc,ymc->tm", grad_gate, full_gate) + dot("ytc,ymc->tm", grad_up, full_up)
    grad_two = lax.psum(grad_two.astype(BF), "core").astype(F32).reshape(2, slots, width)
    gain_two_part = jnp.sum(grad_two * unit_two, (0, 1))
    grad_hidden = grad_out + norm_back(grad_two, unit_two, inverse_two, gain_two)

    branch = grad_hidden.astype(BF).reshape(2 * slots, width)
    branch_pair = jnp.broadcast_to(branch, (2,) + branch.shape)
    output_part = dot("ytm,ytc->ymc", branch_pair, mixed, BF)
    grad_mixed = dot("ytm,ymc->ytc", branch_pair, full_output).astype(BF)
    grad_mixed = grad_mixed.reshape(2, 2, slots, heads_kv, -1, HEAD)
    grad_probs = dot("yntkgd,ynskd->ynkgts", grad_mixed, value)
    grad_scores = (probs * (grad_probs - jnp.sum(grad_probs * probs, -1, keepdims=True))).astype(BF)
    grad_query = dot("ynkgts,ynskd->yntkgd", grad_scores, key) * scale
    grad_key = dot("ynkgts,yntkgd->ynskd", grad_scores, query) * scale
    grad_value = dot("ynkgts,yntkgd->ynskd", probs_low, grad_mixed)
    query_back = rotary_back(grad_query.reshape(2, 2, slots, -1, HEAD), cosine, sine).astype(BF)
    query_back = query_back.reshape(2, 2 * slots, -1)
    key_back = rotary_back(grad_key, cosine, sine).astype(BF).reshape(2, 2 * slots, -1)
    kv_back = jnp.concatenate([key_back, grad_value.astype(BF).reshape(2, 2 * slots, -1)], -1)
    query_part = dot("ytm,ytc->ymc", normed_pair, query_back, BF)
    kv_part = dot("ytm,ytc->ymc", normed_pair, kv_back, BF)
    grad_one = dot("ytc,ymc->tm", query_back, full_query) + dot("ytc,ymc->tm", kv_back, full_kv)
    grad_one = lax.psum_scatter(
        grad_one.astype(BF).reshape(2, slots, width), "core", scatter_dimension=0, tiled=True
    )[0].astype(F32)
    own_unit = lax.dynamic_index_in_dim(unit_one, core, 0, False)
    own_inverse = lax.dynamic_index_in_dim(inverse_one, core, 0, False)
    own_grad_hidden = lax.dynamic_index_in_dim(grad_hidden, core, 0, False)
    own_grad_two = lax.dynamic_index_in_dim(grad_two, core, 0, False)
    own_unit_two = lax.dynamic_index_in_dim(unit_two, core, 0, False)
    gain_one_part = jnp.sum(grad_one * own_unit, 0)
    gain_two_part = jnp.sum(own_grad_two * own_unit_two, 0)
    in_grad = own_grad_hidden + norm_back(grad_one, own_unit, own_inverse, gain_one)
    in_grad = lax.all_to_all(in_grad.reshape(2, rows, width), "yl", 0, 0, tiled=True)

    def blocked(part):
        parts = part.reshape(2, 2, 4, 4, 48, -1)
        return parts[0], parts[1]

    pieces = []
    for wide_part, thin_part in ((gate_part, query_part), (up_part, kv_part), (down_part, output_part)):
        wide_parts, thin_parts = blocked(wide_part), blocked(thin_part)
        pieces.append([[wide_parts[0], thin_parts[0]], [wide_parts[1], thin_parts[1]]])
    sums = reduced(pieces, (wide, third), 3, "reduce_grads")
    mine = jnp.concatenate(
        [sums[0][:, wide:], sums[1][:, wide:], sums[2][:, wide:], sums[0][:, :wide], sums[1][:, :wide], sums[2][:, :wide]],
        -1,
    )
    mine = lax.all_to_all(mine.reshape(2, 24, -1), "core", 0, 0, tiled=True)
    shards, start = [], 0
    for size in sizes:
        shards.append(jnp.concatenate([mine[0, :, start : start + size], mine[1, :, start : start + size]], -1))
        start += size
    gain_sums = lax.psum_scatter(
        lax.psum(jnp.stack([gain_one_part, gain_two_part], 1), "yl"), DP, scatter_dimension=0, tiled=True
    )
    return (
        result,
        in_grad,
        shards[0],
        shards[1],
        shards[2],
        shards[3].T,
        shards[4],
        shards[5],
        shards[6].T,
        gain_sums[:, 0],
        gain_sums[:, 1],
    )


def solution(mesh):
    fine = Mesh(mesh.devices.reshape(2, 4, 4, 2, 2), AXES)
    rows = P(None, AXES, None)
    into, out = P(DP, "yl"), P("yl", DP)
    return jax.shard_map(
        body,
        mesh=fine,
        in_specs=(rows, rows, P(None, DP), into, into, into, out, into, into, out, P(DP), P(DP)),
        out_specs=(rows, rows, into, into, into, out, into, into, out, P(DP), P(DP)),
        check_vma=False,
    )
```

```python
import math

import jax
import jax.numpy as jnp
import numpy as np
from jax import lax
from jax.experimental import pallas as pl
from jax.experimental.pallas import tpu as pltpu
from jax.sharding import Mesh
from jax.sharding import PartitionSpec as P

HEAD = 96
EPS = 1e-05
ROPE_BASE = 100000.0
AXES = ("yh", "x", "z", "core", "yl")
DP = ("yh", "x", "z", "core")
MESH = pl.DeviceIdType.MESH
BF = jnp.bfloat16
F32 = jnp.float32
ORDERS = (("x", "y", "z"), ("y", "z", "x"), ("z", "x", "y"))
SEQ = 256
ROWS = 512
STEP = 128
VMEM_LIMIT = 62 * 1024 * 1024


def coordinates():
    x, z, yh, yl = (lax.axis_index(a) for a in ("x", "z", "yh", "yl"))
    return {"x": x, "z": z, "y": yh * 2 + yl}


def around(value, by):
    return lax.rem(value + (by + 4), 4)


def peer(at, axis, by):
    moved = around(at[axis], by)
    if axis == "y":
        return {"yh": moved // 2, "yl": lax.rem(moved, 2)}
    return {axis: moved}


def sibling():
    return {"core": 1 - lax.axis_index("core")}


def partner():
    return {"yl": 1 - lax.axis_index("yl")}


def place(at, whole=(), half=None, moved=None):
    out = []
    for axis in ("y", "x", "z"):
        if axis in whole:
            if half is not None and half[0] == axis:
                out.append(pl.ds(2 * half[1], 2))
            else:
                out.append(pl.ds(0, 4))
        else:
            value = at[axis] if moved is None or moved[0] != axis else around(at[axis], moved[1])
            out.append(lax.rem(value, 2) * 2 + value // 2 if axis == "y" else value)
    return tuple(out)


def greet(at):
    barrier = pltpu.get_barrier_semaphore()
    for axis in ("x", "y", "z"):
        for by in (1, -1, 2):
            pl.semaphore_signal(barrier, inc=1, device_id=peer(at, axis, by), device_id_type=MESH)
    pl.semaphore_signal(barrier, inc=1, device_id=sibling(), device_id_type=MESH)
    pl.semaphore_wait(barrier, 10)


def pair_greet():
    barrier = pltpu.get_barrier_semaphore()
    pl.semaphore_signal(barrier, inc=1, device_id=sibling(), device_id_type=MESH)
    pl.semaphore_wait(barrier, 1)


def sent(src, dst, send, recv, device):
    copy = pltpu.make_async_remote_copy(
        src_ref=src, dst_ref=dst, send_sem=send, recv_sem=recv, device_id=device, device_id_type=MESH
    )
    copy.start()
    return copy


def moved(src, dst, sem):
    copy = pltpu.make_async_copy(src, dst, sem)
    copy.start()
    return copy


def halved(order):
    return "x" if order[2] == "y" else "y"


class Gather:
    semaphores = (
        pltpu.SemaphoreType.DMA((3,)),
        pltpu.SemaphoreType.DMA((3, 2, 3)),
        pltpu.SemaphoreType.DMA((3, 2, 3)),
        pltpu.SemaphoreType.DMA((3, 2, 3)),
        pltpu.SemaphoreType.DMA((3, 2, 3)),
    )

    def __init__(self, at, srcs, outs, semaphores):
        self.at, self.srcs, self.outs = at, srcs, outs
        self.local, self.send, self.recv, self.last_send, self.last_recv = semaphores
        self.own, self.started, self.final = [], {}, {}

    def stage(self, stage):
        at = self.at
        for p, order in enumerate(ORDERS):
            if stage:
                self.own[p].wait()
                for copy in self.started[p, 0]:
                    copy.wait()
            else:
                self.own.append(moved(self.srcs[p], self.outs[p].at[place(at)], self.local.at[p]))
            group = self.outs[p].at[place(at, order[:stage])]
            self.started[p, stage] = [
                sent(
                    group if stage else self.srcs[p],
                    group,
                    self.send.at[p, stage, d],
                    self.recv.at[p, stage, d],
                    peer(at, order[stage], by),
                )
                for d, by in enumerate((1, -1, 2))
            ]

    def spread(self):
        at = self.at
        for p, order in enumerate(ORDERS):
            for copy in self.started[p, 1]:
                copy.wait()
            for t in range(2):
                for d, by in enumerate((1, -1)):
                    h = t if by == 1 else 1 - t
                    block = self.outs[p].at[place(at, order[:2], (halved(order), h))]
                    self.final[p, d, h] = sent(
                        block, block, self.last_send.at[p, d, h], self.last_recv.at[p, d, h], peer(at, order[2], by)
                    )

    def forward(self):
        at = self.at
        for p, order in enumerate(ORDERS):
            for d, by in enumerate((1, -1)):
                self.final[p, d, d].wait_recv()
                block = self.outs[p].at[place(at, order[:2], (halved(order), d), (order[2], -by))]
                self.final[p, d, 2] = sent(
                    block, block, self.last_send.at[p, d, 2], self.last_recv.at[p, d, 2], peer(at, order[2], by)
                )

    def finish(self):
        for p in range(3):
            for d in range(2):
                self.final[p, d, 0].wait_send()
                self.final[p, d, 1].wait_send()
                self.final[p, d, 1 - d].wait_recv()
                self.final[p, d, 2].wait()


class Reduce:
    semaphores = (
        pltpu.SemaphoreType.DMA((3, 3)),
        pltpu.SemaphoreType.DMA((3, 2, 3)),
        pltpu.SemaphoreType.DMA((3, 2, 3)),
        pltpu.SemaphoreType.DMA((3, 2, 3)),
        pltpu.SemaphoreType.DMA((3, 2, 3)),
        pltpu.SemaphoreType.DMA((3, 2)),
        pltpu.SemaphoreType.DMA((3, 2)),
    )

    @staticmethod
    def buffers(columns):
        def per_piece(*shape):
            return [pltpu.VMEM(shape + (48, columns), BF) for _ in range(3)]

        return [
            *per_piece(2, 2, 4),
            *per_piece(4, 4),
            *per_piece(2, 2, 4),
            *per_piece(2, 4, 4),
            *per_piece(3, 4),
            *per_piece(3),
            *[pltpu.VMEM((48, columns), F32) for _ in range(3)],
        ]

    def __init__(self, at, data, buffers, semaphores):
        self.at, self.data = at, data
        self.side, self.kept, self.far, self.near, self.second, self.third, self.sums = (
            buffers[3 * k : 3 * k + 3] for k in range(7)
        )
        self.load, self.first_send, self.first_recv, self.send, self.recv, self.end_send, self.end_recv = semaphores
        self.loads, self.copies = {}, {}

    def start(self):
        at, s, r = self.at, self.first_send, self.first_recv
        for p, order in enumerate(ORDERS):
            axis = order[2]
            for d, by in enumerate((1, -1)):
                block = self.data[p].at[place(at, order[:2], (halved(order), d), (axis, 2))]
                self.copies[p, d, 0] = sent(block, self.far[p].at[d], s.at[p, d, 0], r.at[p, d, 0], peer(at, axis, by))
            for d, by in enumerate((1, -1)):
                h = 1 - d
                block = self.data[p].at[place(at, order[:2], (halved(order), h), (axis, by))]
                self.copies[p, d, 1] = sent(
                    block, self.near[p].at[d, pl.ds(2 * h, 2)], s.at[p, d, 1], r.at[p, d, 1], peer(at, axis, by)
                )
                block = self.data[p].at[place(at, order[:2], (halved(order), d), (axis, by))]
                self.loads[p, d] = moved(block, self.side[p].at[d], self.load.at[p, d])
            self.loads[p, 2] = moved(self.data[p].at[place(at, order[:2])], self.kept[p], self.load.at[p, 2])

    def relay(self):
        for p, order in enumerate(ORDERS):
            for d, by in enumerate((1, -1)):
                self.loads[p, d].wait()
                self.copies[p, d, 0].wait_recv()
                side, far = self.side[p], self.far[p]

                @pl.loop(0, 8)
                def _(i, d=d, side=side, far=far):
                    a, b = i // 4, lax.rem(i, 4)
                    side[d, a, b] = (side[d, a, b].astype(F32) + far[d, a, b].astype(F32)).astype(BF)

                self.copies[p, d, 2] = sent(
                    side.at[d],
                    self.near[p].at[d, pl.ds(2 * d, 2)],
                    self.first_send.at[p, d, 2],
                    self.first_recv.at[p, d, 2],
                    peer(self.at, order[2], by),
                )

    def inner(self, p, by):
        order = ORDERS[p]
        left = [a for a in ("y", "x", "z") if a != order[2]]
        value = around(self.at[order[1]], by)
        if order[1] == "y":
            value = lax.rem(value, 2) * 2 + value // 2
        return value, left[0] == order[1]

    def spread(self):
        for p, order in enumerate(ORDERS):
            self.loads[p, 2].wait()
            for d in range(2):
                self.copies[p, d, 1].wait_recv()
                self.copies[p, d, 2].wait_recv()
            kept, near = self.kept[p], self.near[p]

            @pl.loop(0, 16)
            def _(i, kept=kept, near=near):
                a, b = i // 4, lax.rem(i, 4)
                total = kept[a, b].astype(F32) + near[0, a, b].astype(F32) + near[1, a, b].astype(F32)
                kept[a, b] = total.astype(BF)

            for d, by in enumerate((1, -1, 2)):
                value, first = self.inner(p, by)
                block = kept.at[value] if first else kept.at[:, value]
                self.copies[p, "b", d] = sent(
                    block, self.second[p].at[d], self.send.at[p, 0, d], self.recv.at[p, 0, d], peer(self.at, order[1], by)
                )

    def narrow(self):
        for p, order in enumerate(ORDERS):
            for d in range(3):
                self.copies[p, "b", d].wait_recv()
            kept, second = self.kept[p], self.second[p]
            value, first = self.inner(p, 0)

            @pl.loop(0, 4)
            def _(i, kept=kept, second=second, value=value, first=first):
                where = (value, i) if first else (i, value)
                total = kept[where].astype(F32)
                for d in range(3):
                    total = total + second[d, i].astype(F32)
                kept[where] = total.astype(BF)

            for d, by in enumerate((1, -1, 2)):
                index = around(self.at[order[0]], by)
                if order[0] == "y":
                    index = lax.rem(index, 2) * 2 + index // 2
                block = kept.at[(value, index) if first else (index, value)]
                self.copies[p, "c", d] = sent(
                    block, self.third[p].at[d], self.send.at[p, 1, d], self.recv.at[p, 1, d], peer(self.at, order[0], by)
                )

    def finish(self, outs):
        core = lax.axis_index("core")
        ends = []
        for p, order in enumerate(ORDERS):
            for d in range(3):
                self.copies[p, "c", d].wait_recv()
            value, first = self.inner(p, 0)
            index = self.at[order[0]]
            if order[0] == "y":
                index = lax.rem(index, 2) * 2 + index // 2
            total = self.kept[p][(value, index) if first else (index, value)].astype(F32)
            for d in range(3):
                total = total + self.third[p][d].astype(F32)
            self.sums[p][...] = total
            theirs = self.sums[p].at[pl.ds(pl.multiple_of(24 * (1 - core), 8), 24)]
            mine = self.sums[p].at[pl.ds(pl.multiple_of(24 * core, 8), 24)]
            ends.append(sent(theirs, outs[p].at[core], self.end_send.at[p, 0], self.end_recv.at[p, 0], sibling()))
            ends.append(moved(mine, outs[p].at[core], self.end_send.at[p, 1]))
        for key, copy in self.copies.items():
            copy.wait_send()
        for copy in ends:
            copy.wait()


def nn(left, right):
    return lax.dot_general(left, right, (((1,), (0,)), ((), ())), preferred_element_type=F32)


def nt(left, right):
    return lax.dot_general(left, right, (((1,), (1,)), ((), ())), preferred_element_type=F32)


def tn(left, right):
    return lax.dot_general(left, right, (((0,), (0,)), ((), ())), preferred_element_type=F32)


def inverse_rms(values):
    return lax.rsqrt(jnp.mean(values * values, -1, keepdims=True) + EPS)


def swap(values, first):
    width = values.shape[-1]
    return jnp.where(first, pltpu.roll(values, width - HEAD // 2, 1), pltpu.roll(values, HEAD // 2, 1))


def first_half(shape):
    return lax.rem(lax.broadcasted_iota(jnp.int32, shape, 1), HEAD) < HEAD // 2


def rows_at(start, size):
    return pl.ds(pl.multiple_of(start, size), size)


ANY = pl.BlockSpec(memory_space=pl.ANY)
VMEM = pl.BlockSpec(memory_space=pltpu.VMEM)


def shaped(shape, kind=BF):
    return jax.ShapeDtypeStruct(shape, kind)


def call(kernel, operands, in_specs, results, out_specs, scratch, name, collective_id, **more):
    return pl.pallas_call(
        kernel,
        out_shape=results,
        in_specs=in_specs,
        out_specs=out_specs,
        scratch_shapes=scratch,
        compiler_params=pltpu.CompilerParams(
            collective_id=collective_id, has_side_effects=True, vmem_limit_bytes=VMEM_LIMIT
        ),
        name=name,
        **more,
    )(*operands)


def forward_kernel(third, wide, *refs):
    shard, xin, gin, tables = refs[:4]
    full_mlp, x_out, cot_out, cott_out, n1t_out, q_out, kv_out, probs_out, mixed_out, hidden_out, n2_out, n2t_out, valid_out = (
        refs[4:7],
        *refs[7:19],
    )
    attn_out = refs[19:22]
    (
        got_shard, packed, xs, gs, normed, q, kv, probs, mixed, hidden, normed_two, part, arrived, turned, valid,
    ) = refs[22:37]
    full_attn = refs[37:40]
    attn_sems, mlp_sems = refs[40:45], refs[45:50]
    pair_send, pair_recv, row_send, row_recv, out_sem = refs[50:]
    at = coordinates()
    core, yl = lax.axis_index("core"), lax.axis_index("yl")
    own_x = moved(xin.at[yl], xs.at[core, yl], out_sem.at[0])
    own_g = moved(gin.at[yl], gs.at[core, yl], out_sem.at[1])
    greet(at)
    swap_shard = sent(shard.at[1 - core], got_shard, pair_send.at[0], pair_recv.at[0], sibling())

    rows = {}
    for k, (src, dst) in enumerate(((xin, xs), (gin, gs))):
        rows[k, 0] = sent(src.at[1 - yl], dst.at[core, yl], row_send.at[k, 0], row_recv.at[k, 0], partner())
        rows[k, 1] = sent(src.at[yl], dst.at[core, yl], row_send.at[k, 1], row_recv.at[k, 1], sibling())

    swap_shard.wait()
    low, high = shard[core], got_shard[...]
    first, last = jnp.where(core == 0, low, high), jnp.where(core == 0, high, low)
    packed[...] = jnp.concatenate([first[:24], last[:24]], 0).astype(BF)
    for c, rows_of in enumerate((first, last)):
        valid[c] = jnp.where(yl == 0, rows_of[24:32, :SEQ], rows_of[24:32, SEQ : 2 * SEQ])

    def pieces(start, size):
        return [packed.at[:, pl.ds(start + k * size, size)] for k in range(3)]

    attn = Gather(at, pieces(0, third), full_attn, attn_sems)
    mlp_gather = Gather(at, pieces(3 * third, wide), full_mlp, mlp_sems)
    attn.stage(0)
    mlp_gather.stage(0)
    attn.stage(1)
    attn.spread()
    for k, dst in enumerate((xs, gs)):
        rows[k, 0].wait_recv()
        rows[k, 2] = sent(dst.at[core, 1 - yl], dst.at[core, 1 - yl], row_send.at[k, 2], row_recv.at[k, 2], sibling())
    attn.forward()
    mlp_gather.stage(1)
    own_x.wait()
    own_g.wait()
    for k in range(2):
        rows[k, 0].wait_send()
        rows[k, 1].wait()
        rows[k, 2].wait()
    outs = [moved(xs, x_out, out_sem.at[0])]

    @pl.loop(0, ROWS // STEP)
    def _(i):
        block = rows_at(i * STEP, STEP)
        values = xs[i // 2, lax.rem(i, 2)].astype(F32)
        normed[block] = (values * inverse_rms(values)).astype(BF)

    turned[0] = normed[...].T
    outs.append(moved(turned.at[0], n1t_out, out_sem.at[1]))
    outs.append(moved(valid, valid_out, out_sem.at[2]))
    attn.finish()
    outs.extend(moved(full_attn[p], attn_out[p], out_sem.at[12 + p]) for p in range(3))
    wq, wkv, wo = full_attn

    def weight(ref, y):
        return ref[pl.ds(2 * y, 2)].reshape(-1, third)

    @pl.loop(0, 2)
    def _(y):
        @pl.loop(0, ROWS // SEQ)
        def _(n):
            block = rows_at(n * SEQ, SEQ)
            left = normed[block]
            first = first_half((SEQ, third))
            for k, (w, result) in enumerate(((wq, q), (wkv, kv))):
                lin = nn(left, weight(w, y))
                result[y, block] = (lin * tables[2 * k] + swap(lin, first) * tables[2 * k + 1]).astype(BF)

    outs.append(moved(q, q_out, out_sem.at[3]))
    outs.append(moved(kv, kv_out, out_sem.at[4]))
    scale = 1.0 / math.sqrt(HEAD)

    @pl.loop(0, 4)
    def _(i):
        y, n = i // 2, lax.rem(i, 2)
        block = rows_at(n * SEQ, SEQ)
        t = lax.broadcasted_iota(jnp.int32, (SEQ, SEQ), 0)
        s = lax.broadcasted_iota(jnp.int32, (SEQ, SEQ), 1)
        keep = (s <= t) & (valid[n, 0:1, :] > 0.5)
        queries, keys = q[y, block], kv[y, block]
        results = []
        for h in range(4):
            g = h // 2
            scores = nt(queries[:, h * HEAD : (h + 1) * HEAD], keys[:, g * HEAD : (g + 1) * HEAD]) * scale
            scores = jnp.where(keep, scores, -1e30)
            terms = jnp.exp(scores - jnp.max(scores, -1, keepdims=True))
            low = (terms / jnp.sum(terms, -1, keepdims=True)).astype(BF)
            probs[i, h] = low
            results.append(nn(low, keys[:, (2 + g) * HEAD : (3 + g) * HEAD]))
        mixed[y, block] = jnp.concatenate(results, -1).astype(BF)

    outs.append(moved(probs, probs_out, out_sem.at[5]))
    outs.append(moved(mixed, mixed_out, out_sem.at[6]))
    mlp_gather.spread()
    copies = []
    for i in range(ROWS // STEP):
        block = pl.ds(i * STEP, STEP)
        part[block] = (nt(mixed[0, block], weight(wo, 0)) + nt(mixed[1, block], weight(wo, 1))).astype(BF)
        copies.append(sent(part.at[block], arrived.at[block], pair_send.at[1 + i], pair_recv.at[1 + i], sibling()))
    for i in range(ROWS // STEP):
        block = pl.ds(i * STEP, STEP)
        copies[i].wait()
        values = xs[i // 2, i % 2].astype(F32) + (part[block].astype(F32) + arrived[block].astype(F32))
        hidden[block] = values
        normed_two[block] = (values * inverse_rms(values)).astype(BF)
    outs.append(moved(hidden, hidden_out, out_sem.at[7]))
    outs.append(moved(normed_two, n2_out, out_sem.at[8]))
    mlp_gather.forward()
    turned[1] = normed_two[...].T
    outs.append(moved(turned.at[1], n2t_out, out_sem.at[9]))

    for c in range(2):
        for half in range(2):
            block = pl.ds((2 * c + half) * STEP, STEP)
            mask = valid[c][:, half * STEP : (half + 1) * STEP].T[:, 0:1]
            part[block] = (gs[c, half].astype(F32) * mask).astype(BF)
    turned[2] = part[...].T
    outs.append(moved(part, cot_out, out_sem.at[10]))
    outs.append(moved(turned.at[2], cott_out, out_sem.at[11]))
    mlp_gather.finish()
    for copy in outs:
        copy.wait()


def forward(shard, xin, gin, tables, third, wide):
    width = xin.shape[2]
    rows = (ROWS, width)
    heads = (2, ROWS, third)
    square = (4, 4, SEQ, SEQ)
    return call(
        lambda *refs: forward_kernel(third, wide, *refs),
        (shard, xin, gin, tables),
        [VMEM, ANY, ANY, VMEM],
        [shaped((4, 4, 4, 48, wide))] * 3
        + [
            shaped((2, 2, 128, width)),
            shaped(rows),
            shaped(rows[::-1]),
            shaped(rows[::-1]),
            shaped(heads),
            shaped(heads),
            shaped(square),
            shaped(heads),
            shaped(rows, F32),
            shaped(rows),
            shaped(rows[::-1]),
            shaped((2, 8, SEQ), F32),
        ]
        + [shaped((4, 4, 4, 48, third))] * 3,
        [ANY] * 18,
        [
            pltpu.VMEM(shard.shape[1:], F32),
            pltpu.VMEM((48, shard.shape[2]), BF),
            pltpu.VMEM((2, 2, 128, width), BF),
            pltpu.VMEM((2, 2, 128, width), BF),
            pltpu.VMEM(rows, BF),
            pltpu.VMEM(heads, BF),
            pltpu.VMEM(heads, BF),
            pltpu.VMEM(square, BF),
            pltpu.VMEM(heads, BF),
            pltpu.VMEM(rows, F32),
            pltpu.VMEM(rows, BF),
            pltpu.VMEM(rows, BF),
            pltpu.VMEM(rows, BF),
            pltpu.VMEM((3,) + rows[::-1], BF),
            pltpu.VMEM((2, 8, SEQ), F32),
            *[pltpu.VMEM((4, 4, 4, 48, third), BF) for _ in range(3)],
            *Gather.semaphores,
            *Gather.semaphores,
            pltpu.SemaphoreType.DMA((5,)),
            pltpu.SemaphoreType.DMA((5,)),
            pltpu.SemaphoreType.DMA((2, 3)),
            pltpu.SemaphoreType.DMA((2, 3)),
            pltpu.SemaphoreType.DMA((15,)),
        ],
        "gather_attn_forward",
        1,
    )


def mlp_kernel(
    n2, cot, hidden, n2t, cott, wg, wu, wd, dg, du, dd, result, branch, grad_hidden,
    out_acc, grad_acc, out_part, out_in, grad_part, grad_in, send, recv
):
    step = pl.program_id(0)
    core = lax.axis_index("core")

    @pl.when(step == 0)
    def _():
        pair_greet()
        out_acc[...] = jnp.zeros_like(out_acc)
        grad_acc[...] = jnp.zeros_like(grad_acc)

    gate_w, up_w, down_w = wg[0], wu[0], wd[0]
    gate = nn(n2[...], gate_w)
    up = nn(n2[...], up_w)
    sigma = jax.nn.sigmoid(gate)
    silu = gate * sigma
    active = (silu * up).astype(BF)
    grad_active = nn(cot[...], down_w)
    grad_gate = (grad_active * up * (sigma + silu * (1.0 - sigma))).astype(BF)
    grad_up = (grad_active * silu).astype(BF)
    dd[0] = nn(cott[...], active).astype(BF)
    dg[0] = nn(n2t[...], grad_gate).astype(BF)
    du[0] = nn(n2t[...], grad_up).astype(BF)
    out_acc[...] += nt(active, down_w)
    grad_acc[...] += nt(grad_gate, gate_w) + nt(grad_up, up_w)

    @pl.when(step == pl.num_programs(0) - 1)
    def _():
        own = rows_at(core * SEQ, SEQ)
        other = rows_at((1 - core) * SEQ, SEQ)
        grad_part[...] = grad_acc[...].astype(BF)
        copies = [sent(grad_part, grad_in, send.at[0], recv.at[0], sibling())]
        out_part[...] = out_acc[other].astype(BF)
        copies.append(sent(out_part, out_in, send.at[1], recv.at[1], sibling()))
        copies[0].wait()

        @pl.loop(0, ROWS // STEP)
        def _(i):
            rows = rows_at(i * STEP, STEP)
            grad = grad_part[rows].astype(F32) + grad_in[rows].astype(F32)
            values = hidden[rows]
            inverse = inverse_rms(values)
            unit = values * inverse
            back = inverse * (grad - unit * jnp.mean(grad * unit, -1, keepdims=True))
            grad_acc[rows] = cot[rows].astype(F32) + back
            branch[rows] = grad_acc[rows].astype(BF)

        grad_hidden[...] = grad_acc[own]
        copies[1].wait()
        result[...] = (hidden[own] + (out_acc[own] + out_in[...].astype(F32))).astype(BF)


def mlp(n2, cot, hidden, n2t, cott, wg, wu, wd):
    rows, width = n2.shape
    chunk = 256
    per = wg.shape[2] // chunk
    block = pl.BlockSpec((1, width, chunk), lambda i: (i // per, 0, lax.rem(i, per)))
    return call(
        mlp_kernel,
        (n2, cot, hidden, n2t, cott, wg, wu, wd),
        [VMEM] * 5 + [block] * 3,
        [shaped(wg.shape)] * 3 + [shaped((SEQ, width)), shaped((rows, width)), shaped((SEQ, width), F32)],
        [block] * 3 + [VMEM] * 3,
        [
            pltpu.VMEM((rows, width), F32),
            pltpu.VMEM((rows, width), F32),
            pltpu.VMEM((SEQ, width), BF),
            pltpu.VMEM((SEQ, width), BF),
            pltpu.VMEM((rows, width), BF),
            pltpu.VMEM((rows, width), BF),
            pltpu.SemaphoreType.DMA((2,)),
            pltpu.SemaphoreType.DMA((2,)),
        ],
        "mlp",
        2,
        grid=(2 * per,),
    )


def backward_kernel(*refs):
    xall, grad_hidden_in, branch_in, n1t_in, q_in, kv_in, probs_in, mixed_in, wq_in, wkv_in, wo_in, tables = refs[:12]
    data, result = refs[12:15], refs[15]
    mlp_outs, result_out, dq_out, dkv_out, do_out, in_grad_out = refs[16:19], *refs[19:24]
    (
        xs, gh, branch, branch_t, normed_t, q, kv, probs, mixed, wq, wkv, wo,
        grad_mixed, dq, dkv, part, keep_part, arrived, in_grad, stage,
    ) = refs[24:44]
    buffers = refs[44:65]
    reduce_sems = refs[65:72]
    load, put, send, recv = refs[72:]
    at = coordinates()
    core, yl = lax.axis_index("core"), lax.axis_index("yl")
    loads = [
        moved(src, dst, load.at[k])
        for k, (src, dst) in enumerate(
            (
                (branch_in, branch),
                (wo_in, wo),
                (mixed_in, mixed),
                (q_in, q),
                (kv_in, kv),
                (probs_in, probs),
                (wq_in, wq),
                (wkv_in, wkv),
                (n1t_in, normed_t),
                (grad_hidden_in, gh),
                (xall.at[core], xs),
            )
        )
    ]
    greet(at)
    mlp_sum = Reduce(at, data, buffers, reduce_sems)
    mlp_sum.start()
    halves = [
        moved(result.at[yl], result_out.at[yl], put.at[0]),
        sent(result.at[1 - yl], result_out.at[yl], send.at[0], recv.at[0], partner()),
    ]
    for k in range(3):
        loads[k].wait()
    branch_t[...] = branch[...].T
    third = wq.shape[2]
    outs = {}

    def put_out(k, y, value):
        slot = (2 * k + y) % 2
        if (k, y) != (0, 0) and (k, y) != (0, 1):
            outs.pop(slot).wait()
        stage[slot] = value.astype(BF)
        outs[slot] = moved(stage.at[slot], (do_out, dq_out, dkv_out)[k].at[y], put.at[1 + slot])

    for y in range(2):
        grad_mixed[y] = nn(branch[...], wo[y]).astype(BF)
        put_out(0, y, nn(branch_t[...], mixed[y]))
    for k in range(3, 6):
        loads[k].wait()
    scale = 1.0 / math.sqrt(HEAD)

    @pl.loop(0, 4)
    def _(i):
        y, n = i // 2, lax.rem(i, 2)
        rows = rows_at(n * SEQ, SEQ)
        queries, keys, grads = q[y, rows], kv[y, rows], grad_mixed[y, rows]
        grad_q, grad_k, grad_v = [], [None, None], [None, None]
        for h in range(4):
            g = h // 2
            key = keys[:, g * HEAD : (g + 1) * HEAD]
            value = keys[:, (2 + g) * HEAD : (3 + g) * HEAD]
            query = queries[:, h * HEAD : (h + 1) * HEAD]
            grad = grads[:, h * HEAD : (h + 1) * HEAD]
            low = probs[i, h]
            prob = low.astype(F32)
            grad_probs = nt(grad, value)
            grad_scores = (prob * (grad_probs - jnp.sum(grad_probs * prob, -1, keepdims=True))).astype(BF)
            grad_q.append(nn(grad_scores, key) * scale)
            back_k = tn(grad_scores, query) * scale
            back_v = tn(low, grad)
            grad_k[g] = back_k if grad_k[g] is None else grad_k[g] + back_k
            grad_v[g] = back_v if grad_v[g] is None else grad_v[g] + back_v
        first = first_half((SEQ, 4 * HEAD))
        for k, (pieces, target) in enumerate(((grad_q, dq), (grad_k + grad_v, dkv))):
            values = jnp.concatenate(pieces, -1)
            target[y, rows] = (values * tables[2 * k] - swap(values, first) * tables[2 * k + 1]).astype(BF)

    for k in range(6, 11):
        loads[k].wait()

    def back(start):
        rows = rows_at(start, SEQ)
        return (nt(dq[0, rows], wq[0]) + nt(dq[1, rows], wq[1])) + (nt(dkv[0, rows], wkv[0]) + nt(dkv[1, rows], wkv[1]))

    part[...] = back((1 - core) * SEQ).astype(BF)
    pair = sent(part, arrived, send.at[1], recv.at[1], sibling())
    mlp_sum.relay()
    keep_part[...] = back(core * SEQ)
    pair.wait()

    @pl.loop(0, SEQ // STEP)
    def _(i):
        rows = rows_at(i * STEP, STEP)
        grad = keep_part[rows] + arrived[rows].astype(F32)
        values = xs[i].astype(F32)
        inverse = inverse_rms(values)
        unit = values * inverse
        change = inverse * (grad - unit * jnp.mean(grad * unit, -1, keepdims=True))
        in_grad[i] = gh[rows] + change

    halves.append(moved(in_grad.at[yl], in_grad_out.at[yl], put.at[3]))
    halves.append(sent(in_grad.at[1 - yl], in_grad_out.at[yl], send.at[2], recv.at[2], partner()))
    for k, source in ((1, dq), (2, dkv)):
        for y in range(2):
            put_out(k, y, nn(normed_t[...], source[y]))
    mlp_sum.spread()
    mlp_sum.narrow()
    mlp_sum.finish(mlp_outs)
    for copy in (*halves, *outs.values()):
        copy.wait()


def backward(x, grad_hidden, branch, n1t, q, kv, probs, mixed, wq, wkv, wo, tables, data, result):
    rows, width = branch.shape
    third, wide = wq.shape[2], data[0].shape[-1]
    heads = (2, rows, third)
    weights = (2, width, third)
    half = (2, 128, width)
    return call(
        backward_kernel,
        (x, grad_hidden, branch, n1t, q, kv, probs, mixed, wq, wkv, wo, tables, *data, result),
        [ANY] * 11 + [VMEM] + [ANY] * 4,
        [shaped((2, 24, wide), F32)] * 3 + [shaped(half)] + [shaped(weights)] * 3 + [shaped(half, F32)],
        [ANY] * 8,
        [
            pltpu.VMEM(half, BF),
            pltpu.VMEM((SEQ, width), F32),
            pltpu.VMEM((rows, width), BF),
            pltpu.VMEM((width, rows), BF),
            pltpu.VMEM((width, rows), BF),
            pltpu.VMEM(heads, BF),
            pltpu.VMEM(heads, BF),
            pltpu.VMEM((4, 4, SEQ, SEQ), BF),
            pltpu.VMEM(heads, BF),
            pltpu.VMEM(weights, BF),
            pltpu.VMEM(weights, BF),
            pltpu.VMEM(weights, BF),
            pltpu.VMEM(heads, BF),
            pltpu.VMEM(heads, BF),
            pltpu.VMEM(heads, BF),
            pltpu.VMEM((SEQ, width), BF),
            pltpu.VMEM((SEQ, width), F32),
            pltpu.VMEM((SEQ, width), BF),
            pltpu.VMEM(half, F32),
            pltpu.VMEM(weights, BF),
            *Reduce.buffers(wide),
            *Reduce.semaphores,
            pltpu.SemaphoreType.DMA((11,)),
            pltpu.SemaphoreType.DMA((4,)),
            pltpu.SemaphoreType.DMA((3,)),
            pltpu.SemaphoreType.DMA((3,)),
        ],
        "reduce_mlp_attn_backward",
        3,
    )


def last_kernel(*refs):
    data, outs = refs[:3], refs[3:6]
    at = coordinates()
    greet(at)
    total = Reduce(at, data, refs[6:27], refs[27:])
    total.start()
    total.relay()
    total.spread()
    total.narrow()
    total.finish(outs)


def last_sums(data):
    columns = data[0].shape[-1]
    return call(
        last_kernel,
        data,
        [ANY] * 3,
        [shaped((2, 24, columns), F32)] * 3,
        [ANY] * 3,
        [*Reduce.buffers(columns), *Reduce.semaphores],
        "reduce_attn",
        4,
    )


def tables_for(count, heads, plain):
    half = HEAD // 2
    inverse = np.float32(ROPE_BASE) ** (-(np.arange(half, dtype=np.float32) * np.float32(2.0)) / np.float32(HEAD))
    angle = np.arange(count, dtype=np.float32)[:, None] * inverse.astype(np.float32)[None, :]
    cosine, sine = np.cos(angle), np.sin(angle)
    cosine = np.tile(np.concatenate([cosine, cosine], -1), (1, heads))
    sine = np.tile(np.concatenate([-sine, sine], -1), (1, heads))
    cosine = np.concatenate([cosine, np.ones((count, plain), np.float32)], -1)
    sine = np.concatenate([sine, np.zeros((count, plain), np.float32)], -1)
    return np.stack([cosine, sine]).astype(np.float32)


def body(
    inputs,
    out_grad,
    lengths,
    query_weight,
    key_matrix,
    value_matrix,
    output_weight,
    gate_weight,
    up_weight,
    down_weight,
    attn_gain,
    mlp_gain,
):
    width = inputs.shape[2]
    gain_one = attn_gain.astype(F32)[:, None]
    gain_two = mlp_gain.astype(F32)[:, None]

    def halves(weight):
        return weight.reshape(weight.shape[0], 2, -1)

    query32, key32, value32, gate32, up32 = (
        w.astype(F32) for w in (query_weight, key_matrix, value_matrix, gate_weight, up_weight)
    )
    blocks = [
        halves(query32 * gain_one),
        halves(key32 * gain_one),
        halves(value32 * gain_one),
        halves(output_weight.astype(F32).T),
        halves(gate32 * gain_two),
        halves(up32 * gain_two),
        halves(down_weight.astype(F32).T),
    ]
    sizes = [b.shape[2] for b in blocks]
    third, wide = sizes[0], sizes[4]
    shard = jnp.moveaxis(jnp.concatenate(blocks, -1), 1, 0)
    valid = (jnp.arange(SEQ)[None, :] < lengths).astype(F32).reshape(1, 1, 2 * SEQ)
    valid = jnp.broadcast_to(valid, (2, 8, 2 * SEQ))
    valid = jnp.pad(valid, ((0, 0), (0, 0), (0, shard.shape[2] - 2 * SEQ)))
    shard = jnp.concatenate([shard, valid], 1)
    tables = jnp.asarray(np.concatenate([tables_for(SEQ, 4, 0), tables_for(SEQ, 2, 2 * HEAD)]))

    wg, wu, wd, x, cot, cott, n1t, q, kv, probs, mixed, hidden, n2, n2t, _, wq, wkv, wo = forward(
        shard, inputs, out_grad, tables, third, wide
    )

    def joined(w):
        return w.reshape(2, width, -1)

    def blocked(w):
        return w.reshape(4, 4, 4, 48, -1)

    dg, du, dd, result, branch, grad_hidden = mlp(n2, cot, hidden, n2t, cott, joined(wg), joined(wu), joined(wd))
    *mlp_sums, result, dq, dkv, do, in_grad = backward(
        x,
        grad_hidden,
        branch,
        n1t,
        q,
        kv,
        probs,
        mixed,
        joined(wq),
        joined(wkv),
        joined(wo),
        tables,
        [blocked(w) for w in (dg, du, dd)],
        result.reshape(2, 128, width),
    )
    attn_sums = last_sums([blocked(w) for w in (dq, dkv, do)])

    def whole(part):
        return jnp.moveaxis(part, 0, 1).reshape(24, -1)

    key_size = sizes[1]
    dquery, doutput = whole(attn_sums[0]), whole(attn_sums[2])
    dkey, dvalue = whole(attn_sums[1][..., :key_size]), whole(attn_sums[1][..., key_size:])
    dgate, dup, ddown = (whole(part) for part in mlp_sums)
    gain_grads = jnp.stack(
        [
            sum(jnp.sum(w * g, -1) for w, g in ((query32, dquery), (key32, dkey), (value32, dvalue))),
            sum(jnp.sum(w * g, -1) for w, g in ((gate32, dgate), (up32, dup))),
        ]
    )
    gain_grads = lax.psum(gain_grads, "yl")
    return (
        result,
        in_grad,
        dquery * gain_one,
        dkey * gain_one,
        dvalue * gain_one,
        doutput.T,
        dgate * gain_two,
        dup * gain_two,
        ddown.T,
        gain_grads[0],
        gain_grads[1],
    )


def solution(mesh):
    fine = Mesh(mesh.devices.reshape(2, 4, 4, 2, 2), AXES)
    rows = P(None, AXES, None)
    into, out = P(DP, "yl"), P("yl", DP)
    return jax.shard_map(
        body,
        mesh=fine,
        in_specs=(rows, rows, P(None, DP), into, into, into, out, into, into, out, P(DP), P(DP)),
        out_specs=(rows, rows, into, into, into, out, into, into, out, P(DP), P(DP)),
        check_vma=False,
    )
```

```python
import math

import jax
import jax.numpy as jnp
import numpy as np
from jax import lax
from jax.experimental import pallas as pl
from jax.experimental.pallas import tpu as pltpu
from jax.sharding import Mesh
from jax.sharding import PartitionSpec as P

HEAD = 96
EPS = 1e-05
ROPE_BASE = 100000.0
AXES = ("yh", "x", "z", "core", "yl")
DP = ("yh", "x", "z", "core")
MESH = pl.DeviceIdType.MESH
BF = jnp.bfloat16
F32 = jnp.float32
ORDERS = (("x", "y", "z"), ("y", "z", "x"), ("z", "x", "y"))
SEQ = 256
ROWS = 512
STEP = 128
CHUNK = 256
VMEM_LIMIT = 62 * 1024 * 1024


def coordinates():
    x, z, yh, yl = (lax.axis_index(a) for a in ("x", "z", "yh", "yl"))
    return {"x": x, "z": z, "y": yh * 2 + yl}


def around(value, by):
    return lax.rem(value + (by + 4), 4)


def peer(at, axis, by):
    moved = around(at[axis], by)
    if axis == "y":
        return {"yh": moved // 2, "yl": lax.rem(moved, 2)}
    return {axis: moved}


def sibling():
    return {"core": 1 - lax.axis_index("core")}


def partner():
    return {"yl": 1 - lax.axis_index("yl")}


def place(at, whole=(), half=None, moved=None):
    out = []
    for axis in ("y", "x", "z"):
        if axis in whole:
            if half is not None and half[0] == axis:
                out.append(pl.ds(2 * half[1], 2))
            else:
                out.append(pl.ds(0, 4))
        else:
            value = at[axis] if moved is None or moved[0] != axis else around(at[axis], moved[1])
            out.append(lax.rem(value, 2) * 2 + value // 2 if axis == "y" else value)
    return tuple(out)


def greet(at):
    barrier = pltpu.get_barrier_semaphore()
    for axis in ("x", "y", "z"):
        for by in (1, -1, 2):
            pl.semaphore_signal(barrier, inc=1, device_id=peer(at, axis, by), device_id_type=MESH)
    pl.semaphore_signal(barrier, inc=1, device_id=sibling(), device_id_type=MESH)
    pl.semaphore_wait(barrier, 10)


def pair_greet():
    barrier = pltpu.get_barrier_semaphore()
    pl.semaphore_signal(barrier, inc=1, device_id=sibling(), device_id_type=MESH)
    pl.semaphore_wait(barrier, 1)


def sent(src, dst, send, recv, device):
    copy = pltpu.make_async_remote_copy(
        src_ref=src, dst_ref=dst, send_sem=send, recv_sem=recv, device_id=device, device_id_type=MESH
    )
    copy.start()
    return copy


def moved(src, dst, sem):
    copy = pltpu.make_async_copy(src, dst, sem)
    copy.start()
    return copy


def halved(order):
    return "x" if order[2] == "y" else "y"


class Gather:
    semaphores = (
        pltpu.SemaphoreType.DMA((3,)),
        pltpu.SemaphoreType.DMA((3, 2, 3)),
        pltpu.SemaphoreType.DMA((3, 2, 3)),
        pltpu.SemaphoreType.DMA((3, 2, 3)),
        pltpu.SemaphoreType.DMA((3, 2, 3)),
    )

    def __init__(self, at, srcs, outs, semaphores):
        self.at, self.srcs, self.outs = at, srcs, outs
        self.local, self.send, self.recv, self.last_send, self.last_recv = semaphores
        self.own, self.started, self.final = [], {}, {}

    def stage(self, stage):
        at = self.at
        for p, order in enumerate(ORDERS):
            if stage:
                self.own[p].wait()
                for copy in self.started[p, 0]:
                    copy.wait()
            else:
                self.own.append(moved(self.srcs[p], self.outs[p].at[place(at)], self.local.at[p]))
            group = self.outs[p].at[place(at, order[:stage])]
            self.started[p, stage] = [
                sent(
                    group if stage else self.srcs[p],
                    group,
                    self.send.at[p, stage, d],
                    self.recv.at[p, stage, d],
                    peer(at, order[stage], by),
                )
                for d, by in enumerate((1, -1, 2))
            ]

    def spread(self):
        at = self.at
        for p, order in enumerate(ORDERS):
            for copy in self.started[p, 1]:
                copy.wait()
            for t in range(2):
                for d, by in enumerate((1, -1)):
                    h = t if by == 1 else 1 - t
                    block = self.outs[p].at[place(at, order[:2], (halved(order), h))]
                    self.final[p, d, h] = sent(
                        block, block, self.last_send.at[p, d, h], self.last_recv.at[p, d, h], peer(at, order[2], by)
                    )

    def forward(self):
        at = self.at
        for p, order in enumerate(ORDERS):
            for d, by in enumerate((1, -1)):
                self.final[p, d, d].wait_recv()
                block = self.outs[p].at[place(at, order[:2], (halved(order), d), (order[2], -by))]
                self.final[p, d, 2] = sent(
                    block, block, self.last_send.at[p, d, 2], self.last_recv.at[p, d, 2], peer(at, order[2], by)
                )

    def finish(self):
        for p in range(3):
            for d in range(2):
                self.final[p, d, 0].wait_send()
                self.final[p, d, 1].wait_send()
                self.final[p, d, 1 - d].wait_recv()
                self.final[p, d, 2].wait()


class Reduce:
    semaphores = (
        pltpu.SemaphoreType.DMA((3, 3)),
        pltpu.SemaphoreType.DMA((3, 2, 3)),
        pltpu.SemaphoreType.DMA((3, 2, 3)),
        pltpu.SemaphoreType.DMA((3, 2, 3)),
        pltpu.SemaphoreType.DMA((3, 2, 3)),
        pltpu.SemaphoreType.DMA((3, 2)),
        pltpu.SemaphoreType.DMA((3, 2)),
    )

    @staticmethod
    def buffers(columns):
        def per_piece(*shape):
            return [pltpu.VMEM(shape + (48, columns), BF) for _ in range(3)]

        return [
            *per_piece(2, 2, 4),
            *per_piece(4, 4),
            *per_piece(2, 2, 4),
            *per_piece(2, 4, 4),
            *per_piece(3, 4),
            *per_piece(3),
            *[pltpu.VMEM((48, columns), F32) for _ in range(3)],
        ]

    def __init__(self, at, data, buffers, semaphores):
        self.at, self.data = at, data
        self.side, self.kept, self.far, self.near, self.second, self.third, self.sums = (
            buffers[3 * k : 3 * k + 3] for k in range(7)
        )
        self.load, self.first_send, self.first_recv, self.send, self.recv, self.end_send, self.end_recv = semaphores
        self.loads, self.copies = {}, {}

    def start(self):
        at, s, r = self.at, self.first_send, self.first_recv
        for p, order in enumerate(ORDERS):
            axis = order[2]
            for d, by in enumerate((1, -1)):
                block = self.data[p].at[place(at, order[:2], (halved(order), d), (axis, 2))]
                self.copies[p, d, 0] = sent(block, self.far[p].at[d], s.at[p, d, 0], r.at[p, d, 0], peer(at, axis, by))
            for d, by in enumerate((1, -1)):
                h = 1 - d
                block = self.data[p].at[place(at, order[:2], (halved(order), h), (axis, by))]
                self.copies[p, d, 1] = sent(
                    block, self.near[p].at[d, pl.ds(2 * h, 2)], s.at[p, d, 1], r.at[p, d, 1], peer(at, axis, by)
                )
                block = self.data[p].at[place(at, order[:2], (halved(order), d), (axis, by))]
                self.loads[p, d] = moved(block, self.side[p].at[d], self.load.at[p, d])
            self.loads[p, 2] = moved(self.data[p].at[place(at, order[:2])], self.kept[p], self.load.at[p, 2])

    def relay(self):
        for p, order in enumerate(ORDERS):
            for d, by in enumerate((1, -1)):
                self.loads[p, d].wait()
                self.copies[p, d, 0].wait_recv()
                side, far = self.side[p], self.far[p]

                @pl.loop(0, 8)
                def _(i, d=d, side=side, far=far):
                    a, b = i // 4, lax.rem(i, 4)
                    side[d, a, b] = (side[d, a, b].astype(F32) + far[d, a, b].astype(F32)).astype(BF)

                self.copies[p, d, 2] = sent(
                    side.at[d],
                    self.near[p].at[d, pl.ds(2 * d, 2)],
                    self.first_send.at[p, d, 2],
                    self.first_recv.at[p, d, 2],
                    peer(self.at, order[2], by),
                )

    def inner(self, p, by):
        order = ORDERS[p]
        left = [a for a in ("y", "x", "z") if a != order[2]]
        value = around(self.at[order[1]], by)
        if order[1] == "y":
            value = lax.rem(value, 2) * 2 + value // 2
        return value, left[0] == order[1]

    def spread(self):
        for p, order in enumerate(ORDERS):
            self.loads[p, 2].wait()
            for d in range(2):
                self.copies[p, d, 1].wait_recv()
                self.copies[p, d, 2].wait_recv()
            kept, near = self.kept[p], self.near[p]

            @pl.loop(0, 16)
            def _(i, kept=kept, near=near):
                a, b = i // 4, lax.rem(i, 4)
                total = kept[a, b].astype(F32) + near[0, a, b].astype(F32) + near[1, a, b].astype(F32)
                kept[a, b] = total.astype(BF)

            for d, by in enumerate((1, -1, 2)):
                value, first = self.inner(p, by)
                block = kept.at[value] if first else kept.at[:, value]
                self.copies[p, "b", d] = sent(
                    block, self.second[p].at[d], self.send.at[p, 0, d], self.recv.at[p, 0, d], peer(self.at, order[1], by)
                )

    def narrow(self):
        for p, order in enumerate(ORDERS):
            for d in range(3):
                self.copies[p, "b", d].wait_recv()
            kept, second = self.kept[p], self.second[p]
            value, first = self.inner(p, 0)

            @pl.loop(0, 4)
            def _(i, kept=kept, second=second, value=value, first=first):
                where = (value, i) if first else (i, value)
                total = kept[where].astype(F32)
                for d in range(3):
                    total = total + second[d, i].astype(F32)
                kept[where] = total.astype(BF)

            for d, by in enumerate((1, -1, 2)):
                index = around(self.at[order[0]], by)
                if order[0] == "y":
                    index = lax.rem(index, 2) * 2 + index // 2
                block = kept.at[(value, index) if first else (index, value)]
                self.copies[p, "c", d] = sent(
                    block, self.third[p].at[d], self.send.at[p, 1, d], self.recv.at[p, 1, d], peer(self.at, order[0], by)
                )

    def finish(self, outs):
        core = lax.axis_index("core")
        ends = []
        for p, order in enumerate(ORDERS):
            for d in range(3):
                self.copies[p, "c", d].wait_recv()
            value, first = self.inner(p, 0)
            index = self.at[order[0]]
            if order[0] == "y":
                index = lax.rem(index, 2) * 2 + index // 2
            total = self.kept[p][(value, index) if first else (index, value)].astype(F32)
            for d in range(3):
                total = total + self.third[p][d].astype(F32)
            self.sums[p][...] = total
            theirs = self.sums[p].at[pl.ds(pl.multiple_of(24 * (1 - core), 8), 24)]
            mine = self.sums[p].at[pl.ds(pl.multiple_of(24 * core, 8), 24)]
            ends.append(sent(theirs, outs[p].at[core], self.end_send.at[p, 0], self.end_recv.at[p, 0], sibling()))
            ends.append(moved(mine, outs[p].at[core], self.end_send.at[p, 1]))
        for key, copy in self.copies.items():
            copy.wait_send()
        for copy in ends:
            copy.wait()


def nn(left, right):
    return lax.dot_general(left, right, (((1,), (0,)), ((), ())), preferred_element_type=F32)


def nt(left, right):
    return lax.dot_general(left, right, (((1,), (1,)), ((), ())), preferred_element_type=F32)


def tn(left, right):
    return lax.dot_general(left, right, (((0,), (0,)), ((), ())), preferred_element_type=F32)


def inverse_rms(values):
    return lax.rsqrt(jnp.mean(values * values, -1, keepdims=True) + EPS)


def swap(values, first):
    width = values.shape[-1]
    return jnp.where(first, pltpu.roll(values, width - HEAD // 2, 1), pltpu.roll(values, HEAD // 2, 1))


def first_half(shape):
    return lax.rem(lax.broadcasted_iota(jnp.int32, shape, 1), HEAD) < HEAD // 2


def rows_at(start, size):
    return pl.ds(pl.multiple_of(start, size), size)


ANY = pl.BlockSpec(memory_space=pl.ANY)
VMEM = pl.BlockSpec(memory_space=pltpu.VMEM)


def shaped(shape, kind=BF):
    return jax.ShapeDtypeStruct(shape, kind)


def call(kernel, operands, in_specs, results, out_specs, scratch, name, collective_id, **more):
    return pl.pallas_call(
        kernel,
        out_shape=results,
        in_specs=in_specs,
        out_specs=out_specs,
        scratch_shapes=scratch,
        compiler_params=pltpu.CompilerParams(
            collective_id=collective_id, has_side_effects=True, vmem_limit_bytes=VMEM_LIMIT
        ),
        name=name,
        **more,
    )(*operands)


def mlp_step(n2, cot, n2t, cott, gate_w, up_w, down_w, out_acc, grad_acc):
    gate = nn(n2[...], gate_w)
    up = nn(n2[...], up_w)
    sigma = jax.nn.sigmoid(gate)
    silu = gate * sigma
    active = (silu * up).astype(BF)
    grad_active = nn(cot[...], down_w)
    grad_gate = (grad_active * up * (sigma + silu * (1.0 - sigma))).astype(BF)
    grad_up = (grad_active * silu).astype(BF)
    out_acc[...] += nt(active, down_w)
    grad_acc[...] += nt(grad_gate, gate_w) + nt(grad_up, up_w)
    return (
        nn(n2t[...], grad_gate).astype(BF),
        nn(n2t[...], grad_up).astype(BF),
        nn(cott[...], active).astype(BF),
    )


def mlp_chunk(step, acts, weights, accs, staging, outs, sems, waits):
    y, sub = step // 2, step % 2
    columns = pl.ds(sub * CHUNK, CHUNK)
    values = mlp_step(*acts, *(w[pl.ds(2 * y, 2), :, :, :, columns].reshape(-1, CHUNK) for w in weights), *accs)
    slot = step % 2
    for p in range(3):
        if (p, slot) in waits:
            waits[p, slot].wait()
        staging[slot, p] = values[p]
        waits[p, slot] = moved(staging.at[slot, p], outs[p].at[y, :, columns], sems.at[p, slot])


def forward_kernel(third, wide, *refs):
    shard, xin, gin, tables = refs[:4]
    full_two = refs[4:7]
    (
        x_out, cot_out, cott_out, n1t_out, q_out, kv_out, probs_out, mixed_out, hidden_out, n2_out, n2t_out,
        out_acc_out, grad_acc_out,
    ) = refs[7:20]
    attn_out, grads_out = refs[20:23], refs[23:26]
    (
        got_shard, packed, xs, gs, normed, q, kv, probs, mixed, hidden, normed_two, part, arrived, turned, valid,
        out_acc, grad_acc, staging,
    ) = refs[26:44]
    full_attn, weights = refs[44:47], refs[47:50]
    attn_sems, one_sems, two_sems = refs[50:55], refs[55:60], refs[60:65]
    pair_send, pair_recv, row_send, row_recv, out_sem, put_sem = refs[65:]
    at = coordinates()
    core, yl = lax.axis_index("core"), lax.axis_index("yl")
    own_x = moved(xin.at[yl], xs.at[core, yl], out_sem.at[0])
    own_g = moved(gin.at[yl], gs.at[core, yl], out_sem.at[1])
    greet(at)
    swap_shard = sent(shard.at[1 - core], got_shard, pair_send.at[0], pair_recv.at[0], sibling())

    rows = {}
    for k, (src, dst) in enumerate(((xin, xs), (gin, gs))):
        rows[k, 0] = sent(src.at[1 - yl], dst.at[core, yl], row_send.at[k, 0], row_recv.at[k, 0], partner())
        rows[k, 1] = sent(src.at[yl], dst.at[core, yl], row_send.at[k, 1], row_recv.at[k, 1], sibling())

    swap_shard.wait()
    low, high = shard[core], got_shard[...]
    first, last = jnp.where(core == 0, low, high), jnp.where(core == 0, high, low)
    packed[...] = jnp.concatenate([first[:24], last[:24]], 0).astype(BF)
    for c, rows_of in enumerate((first, last)):
        valid[c] = jnp.where(yl == 0, rows_of[24:32, :SEQ], rows_of[24:32, SEQ : 2 * SEQ])

    def pieces(start, size, step):
        return [packed.at[:, pl.ds(start + k * step, size)] for k in range(3)]

    half = wide // 2
    attn = Gather(at, pieces(0, third, third), full_attn, attn_sems)
    one = Gather(at, pieces(3 * third, half, wide), weights, one_sems)
    two = Gather(at, pieces(3 * third + half, half, wide), full_two, two_sems)
    attn.stage(0)
    one.stage(0)
    two.stage(0)
    attn.stage(1)
    one.stage(1)
    attn.spread()
    for k, dst in enumerate((xs, gs)):
        rows[k, 0].wait_recv()
        rows[k, 2] = sent(dst.at[core, 1 - yl], dst.at[core, 1 - yl], row_send.at[k, 2], row_recv.at[k, 2], sibling())
    attn.forward()
    one.spread()
    own_x.wait()
    own_g.wait()
    for k in range(2):
        rows[k, 0].wait_send()
        rows[k, 1].wait()
        rows[k, 2].wait()
    outs = [moved(xs, x_out, out_sem.at[0])]

    @pl.loop(0, ROWS // STEP)
    def _(i):
        block = rows_at(i * STEP, STEP)
        values = xs[i // 2, lax.rem(i, 2)].astype(F32)
        normed[block] = (values * inverse_rms(values)).astype(BF)

    turned[0] = normed[...].T
    outs.append(moved(turned.at[0], n1t_out, out_sem.at[1]))

    cot = arrived
    for c in range(2):
        for h in range(2):
            block = pl.ds((2 * c + h) * STEP, STEP)
            mask = valid[c][:, h * STEP : (h + 1) * STEP].T[:, 0:1]
            gs[c, h] = (gs[c, h].astype(F32) * mask).astype(BF)
    out_acc[...] = jnp.zeros_like(out_acc)
    grad_acc[...] = jnp.zeros_like(grad_acc)
    attn.finish()
    two.stage(1)
    outs.extend(moved(full_attn[p], attn_out[p], out_sem.at[12 + p]) for p in range(3))
    wq, wkv, wo = full_attn

    def weight(ref, y):
        return ref[pl.ds(2 * y, 2)].reshape(-1, third)

    @pl.loop(0, 2)
    def _(y):
        @pl.loop(0, ROWS // SEQ)
        def _(n):
            block = rows_at(n * SEQ, SEQ)
            left = normed[block]
            is_first = first_half((SEQ, third))
            for k, (w, result) in enumerate(((wq, q), (wkv, kv))):
                lin = nn(left, weight(w, y))
                result[y, block] = (lin * tables[2 * k] + swap(lin, is_first) * tables[2 * k + 1]).astype(BF)

    outs.append(moved(q, q_out, out_sem.at[3]))
    outs.append(moved(kv, kv_out, out_sem.at[4]))
    one.forward()
    scale = 1.0 / math.sqrt(HEAD)

    @pl.loop(0, 4)
    def _(i):
        y, n = i // 2, lax.rem(i, 2)
        block = rows_at(n * SEQ, SEQ)
        t = lax.broadcasted_iota(jnp.int32, (SEQ, SEQ), 0)
        s = lax.broadcasted_iota(jnp.int32, (SEQ, SEQ), 1)
        keep = (s <= t) & (valid[n, 0:1, :] > 0.5)
        queries, keys = q[y, block], kv[y, block]
        results = []
        for h in range(4):
            g = h // 2
            scores = nt(queries[:, h * HEAD : (h + 1) * HEAD], keys[:, g * HEAD : (g + 1) * HEAD]) * scale
            scores = jnp.where(keep, scores, -1e30)
            terms = jnp.exp(scores - jnp.max(scores, -1, keepdims=True))
            low = (terms / jnp.sum(terms, -1, keepdims=True)).astype(BF)
            probs[i, h] = low
            results.append(nn(low, keys[:, (2 + g) * HEAD : (3 + g) * HEAD]))
        mixed[y, block] = jnp.concatenate(results, -1).astype(BF)

    outs.append(moved(probs, probs_out, out_sem.at[5]))
    outs.append(moved(mixed, mixed_out, out_sem.at[6]))
    copies = []
    for i in range(ROWS // STEP):
        block = pl.ds(i * STEP, STEP)
        part[block] = (nt(mixed[0, block], weight(wo, 0)) + nt(mixed[1, block], weight(wo, 1))).astype(BF)
        copies.append(sent(part.at[block], arrived.at[block], pair_send.at[1 + i], pair_recv.at[1 + i], sibling()))
    two.spread()
    for i in range(ROWS // STEP):
        block = pl.ds(i * STEP, STEP)
        copies[i].wait()
        values = xs[i // 2, i % 2].astype(F32) + (part[block].astype(F32) + arrived[block].astype(F32))
        hidden[block] = values
        normed_two[block] = (values * inverse_rms(values)).astype(BF)
    outs.append(moved(hidden, hidden_out, out_sem.at[7]))
    outs.append(moved(normed_two, n2_out, out_sem.at[8]))
    turned[1] = normed_two[...].T
    outs.append(moved(turned.at[1], n2t_out, out_sem.at[9]))
    for i in range(ROWS // STEP):
        cot[pl.ds(i * STEP, STEP)] = gs[i // 2, i % 2]
    turned[2] = cot[...].T
    outs.append(moved(cot, cot_out, out_sem.at[10]))
    outs.append(moved(turned.at[2], cott_out, out_sem.at[11]))
    one.finish()
    acts, accs, waits = (normed_two, cot, turned.at[1], turned.at[2]), (out_acc, grad_acc), {}
    for step in range(4):
        mlp_chunk(step, acts, weights, accs, staging, grads_out, put_sem, waits)
        if step == 1:
            two.forward()
    outs.append(moved(out_acc, out_acc_out, out_sem.at[2]))
    outs.append(moved(grad_acc, grad_acc_out, out_sem.at[15]))
    two.finish()
    for copy in (*outs, *waits.values()):
        copy.wait()


def forward(shard, xin, gin, tables, third, wide):
    width = xin.shape[2]
    rows = (ROWS, width)
    heads = (2, ROWS, third)
    square = (4, 4, SEQ, SEQ)
    half = wide // 2
    return call(
        lambda *refs: forward_kernel(third, wide, *refs),
        (shard, xin, gin, tables),
        [VMEM, ANY, ANY, VMEM],
        [shaped((4, 4, 4, 48, half))] * 3
        + [
            shaped((2, 2, 128, width)),
            shaped(rows),
            shaped(rows[::-1]),
            shaped(rows[::-1]),
            shaped(heads),
            shaped(heads),
            shaped(square),
            shaped(heads),
            shaped(rows, F32),
            shaped(rows),
            shaped(rows[::-1]),
            shaped(rows, F32),
            shaped(rows, F32),
        ]
        + [shaped((4, 4, 4, 48, third))] * 3
        + [shaped((2, width, half))] * 3,
        [ANY] * 22,
        [
            pltpu.VMEM(shard.shape[1:], F32),
            pltpu.VMEM((48, shard.shape[2]), BF),
            pltpu.VMEM((2, 2, 128, width), BF),
            pltpu.VMEM((2, 2, 128, width), BF),
            pltpu.VMEM(rows, BF),
            pltpu.VMEM(heads, BF),
            pltpu.VMEM(heads, BF),
            pltpu.VMEM(square, BF),
            pltpu.VMEM(heads, BF),
            pltpu.VMEM(rows, F32),
            pltpu.VMEM(rows, BF),
            pltpu.VMEM(rows, BF),
            pltpu.VMEM(rows, BF),
            pltpu.VMEM((3,) + rows[::-1], BF),
            pltpu.VMEM((2, 8, SEQ), F32),
            pltpu.VMEM(rows, F32),
            pltpu.VMEM(rows, F32),
            pltpu.VMEM((2, 3, width, CHUNK), BF),
            *[pltpu.VMEM((4, 4, 4, 48, third), BF) for _ in range(3)],
            *[pltpu.VMEM((4, 4, 4, 48, half), BF) for _ in range(3)],
            *Gather.semaphores,
            *Gather.semaphores,
            *Gather.semaphores,
            pltpu.SemaphoreType.DMA((5,)),
            pltpu.SemaphoreType.DMA((5,)),
            pltpu.SemaphoreType.DMA((2, 3)),
            pltpu.SemaphoreType.DMA((2, 3)),
            pltpu.SemaphoreType.DMA((16,)),
            pltpu.SemaphoreType.DMA((3, 2)),
        ],
        "gather_attn_forward_mlp",
        1,
    )


def middle_kernel(*refs):
    n2_in, cot_in, hidden_in, n2t_in, cott_in, out_acc_in, grad_acc_in = refs[:7]
    weights_in, data = refs[7:10], refs[10:13]
    sums_out, grads_out = refs[13:16], refs[16:19]
    result_out, branch_out, grad_hidden_out = refs[19:22]
    (
        n2, cot, hidden, n2t, cott, out_acc, grad_acc, staging, out_part, out_in, grad_part, grad_in, result, branch,
    ) = refs[22:36]
    weights, buffers = refs[36:39], refs[39:60]
    reduce_sems = refs[60:67]
    load, put, put_sem, send, recv = refs[67:]
    core = lax.axis_index("core")
    at = coordinates()
    loads = [
        moved(src, dst, load.at[k])
        for k, (src, dst) in enumerate(
            (
                (n2_in, n2),
                (weights_in[0], weights[0]),
                (weights_in[1], weights[1]),
                (cot_in, cot),
                (weights_in[2], weights[2]),
                (n2t_in, n2t),
                (cott_in, cott),
                (out_acc_in, out_acc),
                (grad_acc_in, grad_acc),
                (hidden_in, hidden),
            )
        )
    ]
    greet(at)
    total = Reduce(at, data, buffers, reduce_sems)
    total.start()
    for k in range(9):
        loads[k].wait()
    acts, accs, waits = (n2, cot, n2t, cott), (out_acc, grad_acc), {}
    for step in range(4):
        mlp_chunk(step, acts, weights, accs, staging, grads_out, put_sem, waits)
        if step == 2:
            total.relay()
    own = rows_at(core * SEQ, SEQ)
    other = rows_at((1 - core) * SEQ, SEQ)
    grad_part[...] = grad_acc[...].astype(BF)
    copies = [sent(grad_part, grad_in, send.at[0], recv.at[0], sibling())]
    out_part[...] = out_acc[other].astype(BF)
    copies.append(sent(out_part, out_in, send.at[1], recv.at[1], sibling()))
    loads[9].wait()
    total.spread()
    copies[0].wait()

    @pl.loop(0, ROWS // STEP)
    def _(i):
        rows = rows_at(i * STEP, STEP)
        grad = grad_part[rows].astype(F32) + grad_in[rows].astype(F32)
        values = hidden[rows]
        inverse = inverse_rms(values)
        unit = values * inverse
        back = inverse * (grad - unit * jnp.mean(grad * unit, -1, keepdims=True))
        grad_acc[rows] = cot[rows].astype(F32) + back
        branch[rows] = grad_acc[rows].astype(BF)

    outs = [moved(branch, branch_out, put.at[0]), moved(grad_acc.at[own], grad_hidden_out, put.at[1])]
    copies[1].wait()
    result[...] = (hidden[own] + (out_acc[own] + out_in[...].astype(F32))).astype(BF)
    outs.append(moved(result, result_out, put.at[2]))
    total.narrow()
    total.finish(sums_out)
    for copy in (*outs, *waits.values()):
        copy.wait()


def middle(n2, cot, hidden, n2t, cott, out_acc, grad_acc, weights, data):
    rows, width = n2.shape
    half = weights[0].shape[-1]
    return call(
        middle_kernel,
        (n2, cot, hidden, n2t, cott, out_acc, grad_acc, *weights, *data),
        [ANY] * 13,
        [shaped((2, 24, half), F32)] * 3
        + [shaped((2, width, half))] * 3
        + [shaped((SEQ, width)), shaped((rows, width)), shaped((SEQ, width), F32)],
        [ANY] * 9,
        [
            pltpu.VMEM((rows, width), BF),
            pltpu.VMEM((rows, width), BF),
            pltpu.VMEM((rows, width), F32),
            pltpu.VMEM((width, rows), BF),
            pltpu.VMEM((width, rows), BF),
            pltpu.VMEM((rows, width), F32),
            pltpu.VMEM((rows, width), F32),
            pltpu.VMEM((2, 3, width, CHUNK), BF),
            pltpu.VMEM((SEQ, width), BF),
            pltpu.VMEM((SEQ, width), BF),
            pltpu.VMEM((rows, width), BF),
            pltpu.VMEM((rows, width), BF),
            pltpu.VMEM((SEQ, width), BF),
            pltpu.VMEM((rows, width), BF),
            *[pltpu.VMEM((4, 4, 4, 48, half), BF) for _ in range(3)],
            *Reduce.buffers(half),
            *Reduce.semaphores,
            pltpu.SemaphoreType.DMA((10,)),
            pltpu.SemaphoreType.DMA((3,)),
            pltpu.SemaphoreType.DMA((3, 2)),
            pltpu.SemaphoreType.DMA((2,)),
            pltpu.SemaphoreType.DMA((2,)),
        ],
        "mlp_reduce",
        2,
    )


def backward_kernel(*refs):
    xall, grad_hidden_in, branch_in, n1t_in, q_in, kv_in, probs_in, mixed_in, wq_in, wkv_in, wo_in, tables = refs[:12]
    data, result = refs[12:15], refs[15]
    mlp_outs, attn_outs, attn_grads, result_out, in_grad_out = refs[16:19], refs[19:22], refs[22:25], *refs[25:27]
    (
        xs, gh, branch, branch_t, normed_t, q, kv, probs, mixed, wq, wkv, wo,
        grad_mixed, dq, dkv, part, keep_part, arrived, in_grad, stage,
    ) = refs[27:47]
    mlp_buffers, attn_buffers = refs[47:68], refs[68:89]
    mlp_sems, attn_sems = refs[89:96], refs[96:103]
    load, put, send, recv = refs[103:]
    at = coordinates()
    core, yl = lax.axis_index("core"), lax.axis_index("yl")
    loads = [
        moved(src, dst, load.at[k])
        for k, (src, dst) in enumerate(
            (
                (branch_in, branch),
                (wo_in, wo),
                (mixed_in, mixed),
                (q_in, q),
                (kv_in, kv),
                (probs_in, probs),
                (wq_in, wq),
                (wkv_in, wkv),
                (n1t_in, normed_t),
                (grad_hidden_in, gh),
                (xall.at[core], xs),
            )
        )
    ]
    greet(at)
    mlp_sum = Reduce(at, data, mlp_buffers, mlp_sems)
    attn_sum = Reduce(at, attn_grads, attn_buffers, attn_sems)
    mlp_sum.start()
    halves = [
        moved(result.at[yl], result_out.at[yl], put.at[0]),
        sent(result.at[1 - yl], result_out.at[yl], send.at[0], recv.at[0], partner()),
    ]
    for k in range(3):
        loads[k].wait()
    branch_t[...] = branch[...].T
    third = wq.shape[2]
    outs = {}

    def put_out(k, y, value):
        slot = (2 * k + y) % 2
        if (k, y) != (0, 0) and (k, y) != (0, 1):
            outs.pop(slot).wait()
        stage[slot] = value.astype(BF).reshape(stage.shape[1:])
        target = (attn_grads[2], attn_grads[0], attn_grads[1])[k]
        outs[slot] = moved(stage.at[slot], target.at[pl.ds(2 * y, 2)], put.at[1 + slot])

    for y in range(2):
        grad_mixed[y] = nn(branch[...], wo[y]).astype(BF)
        put_out(0, y, nn(branch_t[...], mixed[y]))
    for k in range(3, 6):
        loads[k].wait()
    scale = 1.0 / math.sqrt(HEAD)

    @pl.loop(0, 4)
    def _(i):
        y, n = i // 2, lax.rem(i, 2)
        rows = rows_at(n * SEQ, SEQ)
        queries, keys, grads = q[y, rows], kv[y, rows], grad_mixed[y, rows]
        grad_q, grad_k, grad_v = [], [None, None], [None, None]
        for h in range(4):
            g = h // 2
            key = keys[:, g * HEAD : (g + 1) * HEAD]
            value = keys[:, (2 + g) * HEAD : (3 + g) * HEAD]
            query = queries[:, h * HEAD : (h + 1) * HEAD]
            grad = grads[:, h * HEAD : (h + 1) * HEAD]
            low = probs[i, h]
            prob = low.astype(F32)
            grad_probs = nt(grad, value)
            grad_scores = (prob * (grad_probs - jnp.sum(grad_probs * prob, -1, keepdims=True))).astype(BF)
            grad_q.append(nn(grad_scores, key) * scale)
            back_k = tn(grad_scores, query) * scale
            back_v = tn(low, grad)
            grad_k[g] = back_k if grad_k[g] is None else grad_k[g] + back_k
            grad_v[g] = back_v if grad_v[g] is None else grad_v[g] + back_v
        first = first_half((SEQ, 4 * HEAD))
        for k, (pieces, target) in enumerate(((grad_q, dq), (grad_k + grad_v, dkv))):
            values = jnp.concatenate(pieces, -1)
            target[y, rows] = (values * tables[2 * k] - swap(values, first) * tables[2 * k + 1]).astype(BF)

    mlp_sum.relay()
    for k in range(6, 11):
        loads[k].wait()
    for k, source in ((1, dq), (2, dkv)):
        for y in range(2):
            put_out(k, y, nn(normed_t[...], source[y]))

    def back(start):
        rows = rows_at(start, SEQ)
        return (nt(dq[0, rows], wq[0]) + nt(dq[1, rows], wq[1])) + (nt(dkv[0, rows], wkv[0]) + nt(dkv[1, rows], wkv[1]))

    part[...] = back((1 - core) * SEQ).astype(BF)
    pair = sent(part, arrived, send.at[1], recv.at[1], sibling())
    for copy in outs.values():
        copy.wait()
    attn_sum.start()
    mlp_sum.spread()
    keep_part[...] = back(core * SEQ)
    pair.wait()

    @pl.loop(0, SEQ // STEP)
    def _(i):
        rows = rows_at(i * STEP, STEP)
        grad = keep_part[rows] + arrived[rows].astype(F32)
        values = xs[i].astype(F32)
        inverse = inverse_rms(values)
        unit = values * inverse
        change = inverse * (grad - unit * jnp.mean(grad * unit, -1, keepdims=True))
        in_grad[i] = gh[rows] + change

    halves.append(moved(in_grad.at[yl], in_grad_out.at[yl], put.at[3]))
    halves.append(sent(in_grad.at[1 - yl], in_grad_out.at[yl], send.at[2], recv.at[2], partner()))
    attn_sum.relay()
    mlp_sum.narrow()
    attn_sum.spread()
    mlp_sum.finish(mlp_outs)
    attn_sum.narrow()
    attn_sum.finish(attn_outs)
    for copy in halves:
        copy.wait()


def backward(x, grad_hidden, branch, n1t, q, kv, probs, mixed, wq, wkv, wo, tables, data, result):
    rows, width = branch.shape
    third, wide = wq.shape[2], data[0].shape[-1]
    heads = (2, rows, third)
    weights = (2, width, third)
    half = (2, 128, width)
    return call(
        backward_kernel,
        (x, grad_hidden, branch, n1t, q, kv, probs, mixed, wq, wkv, wo, tables, *data, result),
        [ANY] * 11 + [VMEM] + [ANY] * 4,
        [shaped((2, 24, wide), F32)] * 3
        + [shaped((2, 24, third), F32)] * 3
        + [shaped((4, 4, 4, 48, third))] * 3
        + [shaped(half), shaped(half, F32)],
        [ANY] * 11,
        [
            pltpu.VMEM(half, BF),
            pltpu.VMEM((SEQ, width), F32),
            pltpu.VMEM((rows, width), BF),
            pltpu.VMEM((width, rows), BF),
            pltpu.VMEM((width, rows), BF),
            pltpu.VMEM(heads, BF),
            pltpu.VMEM(heads, BF),
            pltpu.VMEM((4, 4, SEQ, SEQ), BF),
            pltpu.VMEM(heads, BF),
            pltpu.VMEM(weights, BF),
            pltpu.VMEM(weights, BF),
            pltpu.VMEM(weights, BF),
            pltpu.VMEM(heads, BF),
            pltpu.VMEM(heads, BF),
            pltpu.VMEM(heads, BF),
            pltpu.VMEM((SEQ, width), BF),
            pltpu.VMEM((SEQ, width), F32),
            pltpu.VMEM((SEQ, width), BF),
            pltpu.VMEM(half, F32),
            pltpu.VMEM((2, 2, 4, 4, 48, third), BF),
            *Reduce.buffers(wide),
            *Reduce.buffers(third),
            *Reduce.semaphores,
            *Reduce.semaphores,
            pltpu.SemaphoreType.DMA((11,)),
            pltpu.SemaphoreType.DMA((4,)),
            pltpu.SemaphoreType.DMA((3,)),
            pltpu.SemaphoreType.DMA((3,)),
        ],
        "attn_backward_reduce",
        3,
    )


def tables_for(count, heads, plain):
    half = HEAD // 2
    inverse = np.float32(ROPE_BASE) ** (-(np.arange(half, dtype=np.float32) * np.float32(2.0)) / np.float32(HEAD))
    angle = np.arange(count, dtype=np.float32)[:, None] * inverse.astype(np.float32)[None, :]
    cosine, sine = np.cos(angle), np.sin(angle)
    cosine = np.tile(np.concatenate([cosine, cosine], -1), (1, heads))
    sine = np.tile(np.concatenate([-sine, sine], -1), (1, heads))
    cosine = np.concatenate([cosine, np.ones((count, plain), np.float32)], -1)
    sine = np.concatenate([sine, np.zeros((count, plain), np.float32)], -1)
    return np.stack([cosine, sine]).astype(np.float32)


def body(
    inputs,
    out_grad,
    lengths,
    query_weight,
    key_matrix,
    value_matrix,
    output_weight,
    gate_weight,
    up_weight,
    down_weight,
    attn_gain,
    mlp_gain,
):
    width = inputs.shape[2]
    gain_one = attn_gain.astype(F32)[:, None]
    gain_two = mlp_gain.astype(F32)[:, None]

    def halves(weight):
        return weight.reshape(weight.shape[0], 2, -1)

    query32, key32, value32, gate32, up32 = (
        w.astype(F32) for w in (query_weight, key_matrix, value_matrix, gate_weight, up_weight)
    )
    blocks = [
        halves(query32 * gain_one),
        halves(key32 * gain_one),
        halves(value32 * gain_one),
        halves(output_weight.astype(F32).T),
        halves(gate32 * gain_two),
        halves(up32 * gain_two),
        halves(down_weight.astype(F32).T),
    ]
    sizes = [b.shape[2] for b in blocks]
    third, wide = sizes[0], sizes[4]
    shard = jnp.moveaxis(jnp.concatenate(blocks, -1), 1, 0)
    valid = (jnp.arange(SEQ)[None, :] < lengths).astype(F32).reshape(1, 1, 2 * SEQ)
    valid = jnp.broadcast_to(valid, (2, 8, 2 * SEQ))
    valid = jnp.pad(valid, ((0, 0), (0, 0), (0, shard.shape[2] - 2 * SEQ)))
    shard = jnp.concatenate([shard, valid], 1)
    tables = jnp.asarray(np.concatenate([tables_for(SEQ, 4, 0), tables_for(SEQ, 2, 2 * HEAD)]))

    *two, x, cot, cott, n1t, q, kv, probs, mixed, hidden, n2, n2t, out_acc, grad_acc, wq, wkv, wo, dg, du, dd = forward(
        shard, inputs, out_grad, tables, third, wide
    )

    def joined(w):
        return w.reshape(2, width, -1)

    def blocked(w):
        return w.reshape(4, 4, 4, 48, -1)

    *one_sums, dg, du, dd, result, branch, grad_hidden = middle(
        n2, cot, hidden, n2t, cott, out_acc, grad_acc, two, [blocked(w) for w in (dg, du, dd)]
    )
    *sums, _, _, _, result, in_grad = backward(
        x,
        grad_hidden,
        branch,
        n1t,
        q,
        kv,
        probs,
        mixed,
        joined(wq),
        joined(wkv),
        joined(wo),
        tables,
        [blocked(w) for w in (dg, du, dd)],
        result.reshape(2, 128, width),
    )
    mlp_sums = [jnp.concatenate(parts, -1) for parts in zip(one_sums, sums[:3])]
    attn_sums = sums[3:]

    def whole(part):
        return jnp.moveaxis(part, 0, 1).reshape(24, -1)

    key_size = sizes[1]
    dquery, doutput = whole(attn_sums[0]), whole(attn_sums[2])
    dkey, dvalue = whole(attn_sums[1][..., :key_size]), whole(attn_sums[1][..., key_size:])
    dgate, dup, ddown = (whole(part) for part in mlp_sums)
    gain_grads = jnp.stack(
        [
            sum(jnp.sum(w * g, -1) for w, g in ((query32, dquery), (key32, dkey), (value32, dvalue))),
            sum(jnp.sum(w * g, -1) for w, g in ((gate32, dgate), (up32, dup))),
        ]
    )
    gain_grads = lax.psum(gain_grads, "yl")
    return (
        result,
        in_grad,
        dquery * gain_one,
        dkey * gain_one,
        dvalue * gain_one,
        doutput.T,
        dgate * gain_two,
        dup * gain_two,
        ddown.T,
        gain_grads[0],
        gain_grads[1],
    )


def solution(mesh):
    fine = Mesh(mesh.devices.reshape(2, 4, 4, 2, 2), AXES)
    rows = P(None, AXES, None)
    into, out = P(DP, "yl"), P("yl", DP)
    return jax.shard_map(
        body,
        mesh=fine,
        in_specs=(rows, rows, P(None, DP), into, into, into, out, into, into, out, P(DP), P(DP)),
        out_specs=(rows, rows, into, into, into, out, into, into, out, P(DP), P(DP)),
        check_vma=False,
    )
```

```python
import math

import jax
import jax.numpy as jnp
import numpy as np
from jax import lax
from jax.experimental import pallas as pl
from jax.experimental.pallas import tpu as pltpu
from jax.sharding import Mesh
from jax.sharding import PartitionSpec as P

HEAD = 96
EPS = 1e-05
ROPE_BASE = 100000.0
AXES = ("yh", "x", "z", "core", "yl")
DP = ("yh", "x", "z", "core")
MESH = pl.DeviceIdType.MESH
BF = jnp.bfloat16
F32 = jnp.float32
EVEN = (("x", "y", "z"), ("y", "z", "x"), ("z", "x", "y"))
SPARE_Y = (("x", "z", "y"), ("y", "x", "z"), ("y", "z", "x"))
SPARE_Y_TOO = (("y", "x", "z"), ("y", "z", "x"), ("z", "x", "y"))
SEQ = 256
ROWS = 512
STEP = 128
CHUNK = 256
VMEM_LIMIT = 62 * 1024 * 1024


def coordinates():
    x, z, yh, yl = (lax.axis_index(a) for a in ("x", "z", "yh", "yl"))
    return {"x": x, "z": z, "y": yh * 2 + yl}


def around(value, by):
    return lax.rem(value + (by + 4), 4)


def peer(at, axis, by):
    moved = around(at[axis], by)
    if axis == "y":
        return {"yh": moved // 2, "yl": lax.rem(moved, 2)}
    return {axis: moved}


def sibling():
    return {"core": 1 - lax.axis_index("core")}


def partner():
    return {"yl": 1 - lax.axis_index("yl")}


def place(at, whole=(), half=None, moved=None):
    out = []
    for axis in ("y", "x", "z"):
        if axis in whole:
            if half is not None and half[0] == axis:
                out.append(pl.ds(2 * half[1], 2))
            else:
                out.append(pl.ds(0, 4))
        else:
            value = at[axis] if moved is None or moved[0] != axis else around(at[axis], moved[1])
            out.append(lax.rem(value, 2) * 2 + value // 2 if axis == "y" else value)
    return tuple(out)


def greet(at):
    barrier = pltpu.get_barrier_semaphore()
    for axis in ("x", "y", "z"):
        for by in (1, -1, 2):
            pl.semaphore_signal(barrier, inc=1, device_id=peer(at, axis, by), device_id_type=MESH)
    pl.semaphore_signal(barrier, inc=1, device_id=sibling(), device_id_type=MESH)
    pl.semaphore_wait(barrier, 10)


def pair_greet():
    barrier = pltpu.get_barrier_semaphore()
    pl.semaphore_signal(barrier, inc=1, device_id=sibling(), device_id_type=MESH)
    pl.semaphore_wait(barrier, 1)


def sent(src, dst, send, recv, device):
    copy = pltpu.make_async_remote_copy(
        src_ref=src, dst_ref=dst, send_sem=send, recv_sem=recv, device_id=device, device_id_type=MESH
    )
    copy.start()
    return copy


def moved(src, dst, sem):
    copy = pltpu.make_async_copy(src, dst, sem)
    copy.start()
    return copy


def halved(order):
    return "x" if order[2] == "y" else "y"


class Gather:
    semaphores = (
        pltpu.SemaphoreType.DMA((3,)),
        pltpu.SemaphoreType.DMA((3, 2, 3)),
        pltpu.SemaphoreType.DMA((3, 2, 3)),
        pltpu.SemaphoreType.DMA((3, 2, 2, 3)),
        pltpu.SemaphoreType.DMA((3, 2, 2, 3)),
    )

    def __init__(self, at, srcs, outs, semaphores, orders):
        self.at, self.srcs, self.outs, self.orders = at, srcs, outs, orders
        self.local, self.send, self.recv, self.ring_send, self.ring_recv = semaphores
        self.own, self.direct, self.ring = [], {}, {}

    def arrive(self, p, stage):
        for copy in self.direct.get((p, stage), ()):
            copy.wait_recv()
        if (p, stage, 0, 0) in self.ring:
            for d in range(2):
                self.ring[p, stage, d, 1 - d].wait_recv()
                self.ring[p, stage, d, 2].wait_recv()

    def to_all(self, stage):
        at = self.at
        for p, order in enumerate(self.orders):
            if stage:
                self.own[p].wait()
                self.arrive(p, 0)
            else:
                self.own.append(moved(self.srcs[p], self.outs[p].at[place(at)], self.local.at[p]))
            group = self.outs[p].at[place(at, order[:stage])]
            self.direct[p, stage] = [
                sent(
                    group if stage else self.srcs[p],
                    group,
                    self.send.at[p, stage, d],
                    self.recv.at[p, stage, d],
                    peer(at, order[stage], by),
                )
                for d, by in enumerate((1, -1, 2))
            ]

    def pass_on(self, p, stage, d, k, block):
        self.ring[p, stage, d, k] = sent(
            block,
            block,
            self.ring_send.at[p, stage - 1, d, k],
            self.ring_recv.at[p, stage - 1, d, k],
            peer(self.at, self.orders[p][stage], 1 - 2 * d),
        )

    def spread(self, stage):
        for p, order in enumerate(self.orders):
            if stage == 1:
                self.own[p].wait()
            self.arrive(p, stage - 1)
            for t in range(2):
                for d in range(2):
                    h = t if d == 0 else 1 - t
                    self.pass_on(
                        p, stage, d, h, self.outs[p].at[place(self.at, order[:stage], (order[0], h))]
                    )

    def forward(self, stage):
        for p, order in enumerate(self.orders):
            for d, by in enumerate((1, -1)):
                self.ring[p, stage, d, d].wait_recv()
                where = place(self.at, order[:stage], (order[0], d), (order[stage], -by))
                self.pass_on(p, stage, d, 2, self.outs[p].at[where])

    def finish(self):
        for p in range(3):
            self.arrive(p, 2)
        for copies in self.direct.values():
            for copy in copies:
                copy.wait_send()
        for copy in self.ring.values():
            copy.wait_send()


class Reduce:
    semaphores = (
        pltpu.SemaphoreType.DMA((3, 3)),
        pltpu.SemaphoreType.DMA((3, 2, 3)),
        pltpu.SemaphoreType.DMA((3, 2, 3)),
        pltpu.SemaphoreType.DMA((3, 2, 3)),
        pltpu.SemaphoreType.DMA((3, 2, 3)),
        pltpu.SemaphoreType.DMA((3, 2)),
        pltpu.SemaphoreType.DMA((3, 2)),
    )

    @staticmethod
    def buffers(columns):
        def per_piece(*shape):
            return [pltpu.VMEM(shape + (48, columns), BF) for _ in range(3)]

        return [
            *per_piece(2, 2, 4),
            *per_piece(4, 4),
            *per_piece(2, 2, 4),
            *per_piece(2, 4, 4),
            *per_piece(3, 4),
            *per_piece(3),
            *[pltpu.VMEM((48, columns), F32) for _ in range(3)],
        ]

    def __init__(self, at, data, buffers, semaphores, orders):
        self.at, self.data, self.orders = at, data, orders
        self.side, self.kept, self.far, self.near, self.second, self.third, self.sums = (
            buffers[3 * k : 3 * k + 3] for k in range(7)
        )
        self.load, self.first_send, self.first_recv, self.send, self.recv, self.end_send, self.end_recv = semaphores
        self.loads, self.copies = {}, {}

    def start(self):
        at, s, r = self.at, self.first_send, self.first_recv
        for p, order in enumerate(self.orders):
            axis = order[2]
            for d, by in enumerate((1, -1)):
                block = self.data[p].at[place(at, order[:2], (halved(order), d), (axis, 2))]
                self.copies[p, d, 0] = sent(block, self.far[p].at[d], s.at[p, d, 0], r.at[p, d, 0], peer(at, axis, by))
            for d, by in enumerate((1, -1)):
                h = 1 - d
                block = self.data[p].at[place(at, order[:2], (halved(order), h), (axis, by))]
                self.copies[p, d, 1] = sent(
                    block, self.near[p].at[d, pl.ds(2 * h, 2)], s.at[p, d, 1], r.at[p, d, 1], peer(at, axis, by)
                )
                block = self.data[p].at[place(at, order[:2], (halved(order), d), (axis, by))]
                self.loads[p, d] = moved(block, self.side[p].at[d], self.load.at[p, d])
            self.loads[p, 2] = moved(self.data[p].at[place(at, order[:2])], self.kept[p], self.load.at[p, 2])

    def relay(self):
        for p, order in enumerate(self.orders):
            for d, by in enumerate((1, -1)):
                self.loads[p, d].wait()
                self.copies[p, d, 0].wait_recv()
                side, far = self.side[p], self.far[p]

                @pl.loop(0, 8)
                def _(i, d=d, side=side, far=far):
                    a, b = i // 4, lax.rem(i, 4)
                    side[d, a, b] = (side[d, a, b].astype(F32) + far[d, a, b].astype(F32)).astype(BF)

                self.copies[p, d, 2] = sent(
                    side.at[d],
                    self.near[p].at[d, pl.ds(2 * d, 2)],
                    self.first_send.at[p, d, 2],
                    self.first_recv.at[p, d, 2],
                    peer(self.at, order[2], by),
                )

    def inner(self, p, by):
        order = self.orders[p]
        left = [a for a in ("y", "x", "z") if a != order[2]]
        value = around(self.at[order[1]], by)
        if order[1] == "y":
            value = lax.rem(value, 2) * 2 + value // 2
        return value, left[0] == order[1]

    def spread(self):
        for p, order in enumerate(self.orders):
            self.loads[p, 2].wait()
            for d in range(2):
                self.copies[p, d, 1].wait_recv()
                self.copies[p, d, 2].wait_recv()
            kept, near = self.kept[p], self.near[p]

            @pl.loop(0, 16)
            def _(i, kept=kept, near=near):
                a, b = i // 4, lax.rem(i, 4)
                total = kept[a, b].astype(F32) + near[0, a, b].astype(F32) + near[1, a, b].astype(F32)
                kept[a, b] = total.astype(BF)

            for d, by in enumerate((1, -1, 2)):
                value, first = self.inner(p, by)
                block = kept.at[value] if first else kept.at[:, value]
                self.copies[p, "b", d] = sent(
                    block, self.second[p].at[d], self.send.at[p, 0, d], self.recv.at[p, 0, d], peer(self.at, order[1], by)
                )

    def narrow(self):
        for p, order in enumerate(self.orders):
            for d in range(3):
                self.copies[p, "b", d].wait_recv()
            kept, second = self.kept[p], self.second[p]
            value, first = self.inner(p, 0)

            @pl.loop(0, 4)
            def _(i, kept=kept, second=second, value=value, first=first):
                where = (value, i) if first else (i, value)
                total = kept[where].astype(F32)
                for d in range(3):
                    total = total + second[d, i].astype(F32)
                kept[where] = total.astype(BF)

            for d, by in enumerate((1, -1, 2)):
                index = around(self.at[order[0]], by)
                if order[0] == "y":
                    index = lax.rem(index, 2) * 2 + index // 2
                block = kept.at[(value, index) if first else (index, value)]
                self.copies[p, "c", d] = sent(
                    block, self.third[p].at[d], self.send.at[p, 1, d], self.recv.at[p, 1, d], peer(self.at, order[0], by)
                )

    def finish(self, outs):
        core = lax.axis_index("core")
        ends = []
        for p, order in enumerate(self.orders):
            for d in range(3):
                self.copies[p, "c", d].wait_recv()
            value, first = self.inner(p, 0)
            index = self.at[order[0]]
            if order[0] == "y":
                index = lax.rem(index, 2) * 2 + index // 2
            total = self.kept[p][(value, index) if first else (index, value)].astype(F32)
            for d in range(3):
                total = total + self.third[p][d].astype(F32)
            self.sums[p][...] = total
            theirs = self.sums[p].at[pl.ds(pl.multiple_of(24 * (1 - core), 8), 24)]
            mine = self.sums[p].at[pl.ds(pl.multiple_of(24 * core, 8), 24)]
            ends.append(sent(theirs, outs[p].at[core], self.end_send.at[p, 0], self.end_recv.at[p, 0], sibling()))
            ends.append(moved(mine, outs[p].at[core], self.end_send.at[p, 1]))
        for key, copy in self.copies.items():
            copy.wait_send()
        for copy in ends:
            copy.wait()


def nn(left, right):
    return lax.dot_general(left, right, (((1,), (0,)), ((), ())), preferred_element_type=F32)


def nt(left, right):
    return lax.dot_general(left, right, (((1,), (1,)), ((), ())), preferred_element_type=F32)


def tn(left, right):
    return lax.dot_general(left, right, (((0,), (0,)), ((), ())), preferred_element_type=F32)


def inverse_rms(values):
    return lax.rsqrt(jnp.mean(values * values, -1, keepdims=True) + EPS)


def swap(values, first):
    width = values.shape[-1]
    return jnp.where(first, pltpu.roll(values, width - HEAD // 2, 1), pltpu.roll(values, HEAD // 2, 1))


def first_half(shape):
    return lax.rem(lax.broadcasted_iota(jnp.int32, shape, 1), HEAD) < HEAD // 2


def rows_at(start, size):
    return pl.ds(pl.multiple_of(start, size), size)


ANY = pl.BlockSpec(memory_space=pl.ANY)
VMEM = pl.BlockSpec(memory_space=pltpu.VMEM)


def shaped(shape, kind=BF):
    return jax.ShapeDtypeStruct(shape, kind)


def call(kernel, operands, in_specs, results, out_specs, scratch, name, collective_id, **more):
    return pl.pallas_call(
        kernel,
        out_shape=results,
        in_specs=in_specs,
        out_specs=out_specs,
        scratch_shapes=scratch,
        compiler_params=pltpu.CompilerParams(
            collective_id=collective_id, has_side_effects=True, vmem_limit_bytes=VMEM_LIMIT
        ),
        name=name,
        **more,
    )(*operands)


def mlp_step(n2, cot, n2t, cott, gate_w, up_w, down_w, out_acc, grad_acc):
    gate = nn(n2[...], gate_w)
    up = nn(n2[...], up_w)
    sigma = jax.nn.sigmoid(gate)
    silu = gate * sigma
    active = (silu * up).astype(BF)
    grad_active = nn(cot[...], down_w)
    grad_gate = (grad_active * up * (sigma + silu * (1.0 - sigma))).astype(BF)
    grad_up = (grad_active * silu).astype(BF)
    out_acc[...] += nt(active, down_w)
    grad_acc[...] += nt(grad_gate, gate_w) + nt(grad_up, up_w)
    return (
        nn(n2t[...], grad_gate).astype(BF),
        nn(n2t[...], grad_up).astype(BF),
        nn(cott[...], active).astype(BF),
    )


def mlp_chunk(step, acts, weights, accs, staging, outs, sems, waits):
    y, sub = step // 2, step % 2
    columns = pl.ds(sub * CHUNK, CHUNK)
    values = mlp_step(*acts, *(w[pl.ds(2 * y, 2), :, :, :, columns].reshape(-1, CHUNK) for w in weights), *accs)
    slot = step % 2
    for p in range(3):
        if (p, slot) in waits:
            waits[p, slot].wait()
        staging[slot, p] = values[p]
        waits[p, slot] = moved(staging.at[slot, p], outs[p].at[y, :, columns], sems.at[p, slot])


def forward_kernel(third, wide, *refs):
    own_weights, gains, lengths, xin, gin, tables = refs[:7], *refs[7:12]
    refs = refs[8:]
    full_two = refs[4:7]
    (
        x_out, cot_out, cott_out, n1t_out, q_out, kv_out, probs_out, mixed_out, hidden_out, n2_out, n2t_out,
        out_acc_out, grad_acc_out,
    ) = refs[7:20]
    attn_out, grads_out = refs[20:23], refs[23:26]
    (
        shard, got_shard, packed, xs, gs, normed, q, kv, probs, mixed, hidden, normed_two, part, arrived, turned, valid,
        out_acc, grad_acc, staging,
    ) = refs[26:45]
    full_attn, weights = refs[45:48], refs[48:51]
    attn_sems, one_sems, two_sems = refs[51:56], refs[56:61], refs[61:66]
    pair_send, pair_recv, row_send, row_recv, out_sem, put_sem = refs[66:]
    at = coordinates()
    core, yl = lax.axis_index("core"), lax.axis_index("yl")
    own_x = moved(xin.at[yl], xs.at[core, yl], out_sem.at[0])
    own_g = moved(gin.at[yl], gs.at[core, yl], out_sem.at[1])

    column = 0
    query, key, value, output, *mlp_weights = (ref[...].astype(F32) for ref in own_weights)
    gain_one, gain_two = gains[:, 0:1].astype(F32), gains[:, 1:2].astype(F32)
    small = key.shape[1] // 2
    for c in range(2):
        thin = slice(c * small, (c + 1) * small)
        parts = [
            query[:, c * third : (c + 1) * third] * gain_one,
            jnp.concatenate([key[:, thin] * gain_one, value[:, thin] * gain_one], -1),
            output[:, c * third : (c + 1) * third],
            *(
                w[:, c * wide : (c + 1) * wide] * g
                for w, g in zip(mlp_weights, (gain_two, gain_two, jnp.ones_like(gain_two)))
            ),
        ]
        column = 0
        for part_value in parts:
            shard[c, :24, column : column + part_value.shape[1]] = part_value
            column += part_value.shape[1]
        lane = lax.broadcasted_iota(jnp.int32, (8, 2 * SEQ), 1)
        ends = jnp.where(lane < SEQ, lengths[0, 0], lengths[1, 0] + SEQ)
        shard[c, 24:, : 2 * SEQ] = jnp.where(lane < ends, 1.0, 0.0)
    greet(at)
    swap_shard = sent(shard.at[1 - core], got_shard, pair_send.at[0], pair_recv.at[0], sibling())

    rows = {}
    for k, (src, dst) in enumerate(((xin, xs), (gin, gs))):
        rows[k, 0] = sent(src.at[1 - yl], dst.at[core, yl], row_send.at[k, 0], row_recv.at[k, 0], partner())
        rows[k, 1] = sent(src.at[yl], dst.at[core, yl], row_send.at[k, 1], row_recv.at[k, 1], sibling())

    swap_shard.wait()
    low, high = shard[core], got_shard[...]
    first, last = jnp.where(core == 0, low, high), jnp.where(core == 0, high, low)
    packed[...] = jnp.concatenate([first[:24], last[:24]], 0).astype(BF)
    for c, rows_of in enumerate((first, last)):
        valid[c] = jnp.where(yl == 0, rows_of[24:32, :SEQ], rows_of[24:32, SEQ : 2 * SEQ])

    def pieces(start, size, step):
        return [packed.at[:, pl.ds(start + k * step, size)] for k in range(3)]

    half = wide // 2
    attn = Gather(at, pieces(0, third, third), full_attn, attn_sems, EVEN)
    one = Gather(at, pieces(3 * third, half, wide), weights, one_sems, SPARE_Y)
    two = Gather(at, pieces(3 * third + half, half, wide), full_two, two_sems, SPARE_Y_TOO)
    attn.to_all(0)
    one.to_all(0)
    two.to_all(0)
    attn.to_all(1)
    one.spread(1)
    attn.spread(2)
    one.forward(1)
    for k, dst in enumerate((xs, gs)):
        rows[k, 0].wait_recv()
        rows[k, 2] = sent(dst.at[core, 1 - yl], dst.at[core, 1 - yl], row_send.at[k, 2], row_recv.at[k, 2], sibling())
    attn.forward(2)
    one.spread(2)
    two.spread(1)
    own_x.wait()
    own_g.wait()
    for k in range(2):
        rows[k, 0].wait_send()
        rows[k, 1].wait()
        rows[k, 2].wait()
    outs = [moved(xs, x_out, out_sem.at[0])]

    @pl.loop(0, ROWS // STEP)
    def _(i):
        block = rows_at(i * STEP, STEP)
        values = xs[i // 2, lax.rem(i, 2)].astype(F32)
        normed[block] = (values * inverse_rms(values)).astype(BF)

    turned[0] = normed[...].T
    outs.append(moved(turned.at[0], n1t_out, out_sem.at[1]))

    cot = arrived
    for c in range(2):
        for h in range(2):
            block = pl.ds((2 * c + h) * STEP, STEP)
            mask = valid[c][:, h * STEP : (h + 1) * STEP].T[:, 0:1]
            gs[c, h] = (gs[c, h].astype(F32) * mask).astype(BF)
    out_acc[...] = jnp.zeros_like(out_acc)
    grad_acc[...] = jnp.zeros_like(grad_acc)
    attn.finish()
    two.forward(1)
    outs.extend(moved(full_attn[p], attn_out[p], out_sem.at[12 + p]) for p in range(3))
    wq, wkv, wo = full_attn

    def weight(ref, y):
        return ref[pl.ds(2 * y, 2)].reshape(-1, third)

    @pl.loop(0, 2)
    def _(y):
        @pl.loop(0, ROWS // SEQ)
        def _(n):
            block = rows_at(n * SEQ, SEQ)
            left = normed[block]
            is_first = first_half((SEQ, third))
            for k, (w, result) in enumerate(((wq, q), (wkv, kv))):
                lin = nn(left, weight(w, y))
                result[y, block] = (lin * tables[2 * k] + swap(lin, is_first) * tables[2 * k + 1]).astype(BF)

    outs.append(moved(q, q_out, out_sem.at[3]))
    outs.append(moved(kv, kv_out, out_sem.at[4]))
    one.forward(2)
    scale = 1.0 / math.sqrt(HEAD)

    @pl.loop(0, 4)
    def _(i):
        y, n = i // 2, lax.rem(i, 2)
        block = rows_at(n * SEQ, SEQ)
        t = lax.broadcasted_iota(jnp.int32, (SEQ, SEQ), 0)
        s = lax.broadcasted_iota(jnp.int32, (SEQ, SEQ), 1)
        keep = (s <= t) & (valid[n, 0:1, :] > 0.5)
        queries, keys = q[y, block], kv[y, block]
        results = []
        for h in range(4):
            g = h // 2
            scores = nt(queries[:, h * HEAD : (h + 1) * HEAD], keys[:, g * HEAD : (g + 1) * HEAD]) * scale
            scores = jnp.where(keep, scores, -1e30)
            terms = jnp.exp(scores - jnp.max(scores, -1, keepdims=True))
            low = (terms / jnp.sum(terms, -1, keepdims=True)).astype(BF)
            probs[i, h] = low
            results.append(nn(low, keys[:, (2 + g) * HEAD : (3 + g) * HEAD]))
        mixed[y, block] = jnp.concatenate(results, -1).astype(BF)

    outs.append(moved(probs, probs_out, out_sem.at[5]))
    outs.append(moved(mixed, mixed_out, out_sem.at[6]))
    copies = []
    for i in range(ROWS // STEP):
        block = pl.ds(i * STEP, STEP)
        part[block] = (nt(mixed[0, block], weight(wo, 0)) + nt(mixed[1, block], weight(wo, 1))).astype(BF)
        copies.append(sent(part.at[block], arrived.at[block], pair_send.at[1 + i], pair_recv.at[1 + i], sibling()))
    two.spread(2)
    for i in range(ROWS // STEP):
        block = pl.ds(i * STEP, STEP)
        copies[i].wait()
        values = xs[i // 2, i % 2].astype(F32) + (part[block].astype(F32) + arrived[block].astype(F32))
        hidden[block] = values
        normed_two[block] = (values * inverse_rms(values)).astype(BF)
    outs.append(moved(hidden, hidden_out, out_sem.at[7]))
    outs.append(moved(normed_two, n2_out, out_sem.at[8]))
    turned[1] = normed_two[...].T
    outs.append(moved(turned.at[1], n2t_out, out_sem.at[9]))
    for i in range(ROWS // STEP):
        cot[pl.ds(i * STEP, STEP)] = gs[i // 2, i % 2]
    turned[2] = cot[...].T
    outs.append(moved(cot, cot_out, out_sem.at[10]))
    outs.append(moved(turned.at[2], cott_out, out_sem.at[11]))
    one.finish()
    acts, accs, waits = (normed_two, cot, turned.at[1], turned.at[2]), (out_acc, grad_acc), {}
    for step in range(4):
        mlp_chunk(step, acts, weights, accs, staging, grads_out, put_sem, waits)
        if step == 1:
            two.forward(2)
    outs.append(moved(out_acc, out_acc_out, out_sem.at[2]))
    outs.append(moved(grad_acc, grad_acc_out, out_sem.at[15]))
    two.finish()
    for copy in (*outs, *waits.values()):
        copy.wait()


def forward(own_weights, gains, lengths, xin, gin, tables, third, wide):
    width = xin.shape[2]
    rows = (ROWS, width)
    heads = (2, ROWS, third)
    square = (4, 4, SEQ, SEQ)
    half = wide // 2
    return call(
        lambda *refs: forward_kernel(third, wide, *refs),
        (*own_weights, gains, lengths, xin, gin, tables),
        [VMEM] * 8 + [pl.BlockSpec(memory_space=pltpu.SMEM), ANY, ANY, VMEM],
        [shaped((4, 4, 4, 48, half))] * 3
        + [
            shaped((2, 2, 128, width)),
            shaped(rows),
            shaped(rows[::-1]),
            shaped(rows[::-1]),
            shaped(heads),
            shaped(heads),
            shaped(square),
            shaped(heads),
            shaped(rows, F32),
            shaped(rows),
            shaped(rows[::-1]),
            shaped(rows, F32),
            shaped(rows, F32),
        ]
        + [shaped((4, 4, 4, 48, third))] * 3
        + [shaped((2, width, half))] * 3,
        [ANY] * 22,
        [
            pltpu.VMEM((2, 32, 3 * third + 3 * wide), F32),
            pltpu.VMEM((32, 3 * third + 3 * wide), F32),
            pltpu.VMEM((48, 3 * third + 3 * wide), BF),
            pltpu.VMEM((2, 2, 128, width), BF),
            pltpu.VMEM((2, 2, 128, width), BF),
            pltpu.VMEM(rows, BF),
            pltpu.VMEM(heads, BF),
            pltpu.VMEM(heads, BF),
            pltpu.VMEM(square, BF),
            pltpu.VMEM(heads, BF),
            pltpu.VMEM(rows, F32),
            pltpu.VMEM(rows, BF),
            pltpu.VMEM(rows, BF),
            pltpu.VMEM(rows, BF),
            pltpu.VMEM((3,) + rows[::-1], BF),
            pltpu.VMEM((2, 8, SEQ), F32),
            pltpu.VMEM(rows, F32),
            pltpu.VMEM(rows, F32),
            pltpu.VMEM((2, 3, width, CHUNK), BF),
            *[pltpu.VMEM((4, 4, 4, 48, third), BF) for _ in range(3)],
            *[pltpu.VMEM((4, 4, 4, 48, half), BF) for _ in range(3)],
            *Gather.semaphores,
            *Gather.semaphores,
            *Gather.semaphores,
            pltpu.SemaphoreType.DMA((5,)),
            pltpu.SemaphoreType.DMA((5,)),
            pltpu.SemaphoreType.DMA((2, 3)),
            pltpu.SemaphoreType.DMA((2, 3)),
            pltpu.SemaphoreType.DMA((16,)),
            pltpu.SemaphoreType.DMA((3, 2)),
        ],
        "gather_attn_forward_mlp",
        1,
    )


def middle_kernel(*refs):
    n2_in, cot_in, hidden_in, n2t_in, cott_in, out_acc_in, grad_acc_in = refs[:7]
    weights_in, data = refs[7:10], refs[10:13]
    sums_out, grads_out = refs[13:16], refs[16:19]
    result_out, branch_out, grad_hidden_out = refs[19:22]
    (
        n2, cot, hidden, n2t, cott, out_acc, grad_acc, staging, out_part, out_in, grad_part, grad_in, result, branch,
    ) = refs[22:36]
    weights, buffers = refs[36:39], refs[39:60]
    reduce_sems = refs[60:67]
    load, put, put_sem, send, recv = refs[67:]
    core = lax.axis_index("core")
    at = coordinates()
    loads = [
        moved(src, dst, load.at[k])
        for k, (src, dst) in enumerate(
            (
                (n2_in, n2),
                (weights_in[0], weights[0]),
                (weights_in[1], weights[1]),
                (cot_in, cot),
                (weights_in[2], weights[2]),
                (n2t_in, n2t),
                (cott_in, cott),
                (out_acc_in, out_acc),
                (grad_acc_in, grad_acc),
                (hidden_in, hidden),
            )
        )
    ]
    greet(at)
    total = Reduce(at, data, buffers, reduce_sems, EVEN)
    total.start()
    for k in range(9):
        loads[k].wait()
    acts, accs, waits = (n2, cot, n2t, cott), (out_acc, grad_acc), {}
    for step in range(4):
        mlp_chunk(step, acts, weights, accs, staging, grads_out, put_sem, waits)
        if step == 2:
            total.relay()
    own = rows_at(core * SEQ, SEQ)
    other = rows_at((1 - core) * SEQ, SEQ)
    grad_part[...] = grad_acc[...].astype(BF)
    copies = [sent(grad_part, grad_in, send.at[0], recv.at[0], sibling())]
    out_part[...] = out_acc[other].astype(BF)
    copies.append(sent(out_part, out_in, send.at[1], recv.at[1], sibling()))
    loads[9].wait()
    total.spread()
    copies[0].wait()

    @pl.loop(0, ROWS // STEP)
    def _(i):
        rows = rows_at(i * STEP, STEP)
        grad = grad_part[rows].astype(F32) + grad_in[rows].astype(F32)
        values = hidden[rows]
        inverse = inverse_rms(values)
        unit = values * inverse
        back = inverse * (grad - unit * jnp.mean(grad * unit, -1, keepdims=True))
        grad_acc[rows] = cot[rows].astype(F32) + back
        branch[rows] = grad_acc[rows].astype(BF)

    outs = [moved(branch, branch_out, put.at[0]), moved(grad_acc.at[own], grad_hidden_out, put.at[1])]
    copies[1].wait()
    result[...] = (hidden[own] + (out_acc[own] + out_in[...].astype(F32))).astype(BF)
    outs.append(moved(result, result_out, put.at[2]))
    total.narrow()
    total.finish(sums_out)
    for copy in (*outs, *waits.values()):
        copy.wait()


def middle(n2, cot, hidden, n2t, cott, out_acc, grad_acc, weights, data):
    rows, width = n2.shape
    half = weights[0].shape[-1]
    return call(
        middle_kernel,
        (n2, cot, hidden, n2t, cott, out_acc, grad_acc, *weights, *data),
        [ANY] * 13,
        [shaped((2, 24, half), F32)] * 3
        + [shaped((2, width, half))] * 3
        + [shaped((SEQ, width)), shaped((rows, width)), shaped((SEQ, width), F32)],
        [ANY] * 9,
        [
            pltpu.VMEM((rows, width), BF),
            pltpu.VMEM((rows, width), BF),
            pltpu.VMEM((rows, width), F32),
            pltpu.VMEM((width, rows), BF),
            pltpu.VMEM((width, rows), BF),
            pltpu.VMEM((rows, width), F32),
            pltpu.VMEM((rows, width), F32),
            pltpu.VMEM((2, 3, width, CHUNK), BF),
            pltpu.VMEM((SEQ, width), BF),
            pltpu.VMEM((SEQ, width), BF),
            pltpu.VMEM((rows, width), BF),
            pltpu.VMEM((rows, width), BF),
            pltpu.VMEM((SEQ, width), BF),
            pltpu.VMEM((rows, width), BF),
            *[pltpu.VMEM((4, 4, 4, 48, half), BF) for _ in range(3)],
            *Reduce.buffers(half),
            *Reduce.semaphores,
            pltpu.SemaphoreType.DMA((10,)),
            pltpu.SemaphoreType.DMA((3,)),
            pltpu.SemaphoreType.DMA((3, 2)),
            pltpu.SemaphoreType.DMA((2,)),
            pltpu.SemaphoreType.DMA((2,)),
        ],
        "mlp_reduce",
        2,
    )


def backward_kernel(*refs):
    xall, grad_hidden_in, branch_in, n1t_in, q_in, kv_in, probs_in, mixed_in, wq_in, wkv_in, wo_in, tables = refs[:12]
    data, result = refs[12:15], refs[15]
    mlp_outs, attn_outs, attn_grads = refs[16:19], refs[19:22], refs[22:25]
    result_out, in_grad_out, from_partner = refs[25:28]
    (
        xs, gh, branch, branch_t, normed_t, q, kv, probs, mixed, wq, wkv, wo,
        grad_mixed, dq, dkv, part, keep_part, arrived, in_grad, for_partner, stage,
    ) = refs[28:49]
    mlp_buffers, attn_buffers = refs[49:70], refs[70:91]
    mlp_sems, attn_sems = refs[91:98], refs[98:105]
    load, put, send, recv = refs[105:]
    at = coordinates()
    core, yl = lax.axis_index("core"), lax.axis_index("yl")
    loads = [
        moved(src, dst, load.at[k])
        for k, (src, dst) in enumerate(
            (
                (branch_in, branch),
                (wo_in, wo),
                (mixed_in, mixed),
                (q_in, q),
                (kv_in, kv),
                (probs_in, probs),
                (wq_in, wq),
                (wkv_in, wkv),
                (n1t_in, normed_t),
                (grad_hidden_in, gh),
                (xall.at[core], xs),
            )
        )
    ]
    greet(at)
    mlp_sum = Reduce(at, data, mlp_buffers, mlp_sems, SPARE_Y_TOO)
    attn_sum = Reduce(at, attn_grads, attn_buffers, attn_sems, SPARE_Y)
    mlp_sum.start()
    halves = [
        moved(result.at[yl], result_out.at[yl], put.at[0]),
        sent(result.at[1 - yl], result_out.at[yl], send.at[0], recv.at[0], partner()),
    ]
    for k in range(3):
        loads[k].wait()
    branch_t[...] = branch[...].T
    third = wq.shape[2]
    outs = {}

    def put_out(k, y, value):
        slot = (2 * k + y) % 2
        if (k, y) != (0, 0) and (k, y) != (0, 1):
            outs.pop(slot).wait()
        stage[slot] = value.astype(BF).reshape(stage.shape[1:])
        target = (attn_grads[2], attn_grads[0], attn_grads[1])[k]
        outs[slot] = moved(stage.at[slot], target.at[pl.ds(2 * y, 2)], put.at[1 + slot])

    for y in range(2):
        grad_mixed[y] = nn(branch[...], wo[y]).astype(BF)
        put_out(0, y, nn(branch_t[...], mixed[y]))
    for k in range(3, 6):
        loads[k].wait()
    scale = 1.0 / math.sqrt(HEAD)

    @pl.loop(0, 4)
    def _(i):
        y, n = i // 2, lax.rem(i, 2)
        rows = rows_at(n * SEQ, SEQ)
        queries, keys, grads = q[y, rows], kv[y, rows], grad_mixed[y, rows]
        grad_q, grad_k, grad_v = [], [None, None], [None, None]
        for h in range(4):
            g = h // 2
            key = keys[:, g * HEAD : (g + 1) * HEAD]
            value = keys[:, (2 + g) * HEAD : (3 + g) * HEAD]
            query = queries[:, h * HEAD : (h + 1) * HEAD]
            grad = grads[:, h * HEAD : (h + 1) * HEAD]
            low = probs[i, h]
            prob = low.astype(F32)
            grad_probs = nt(grad, value)
            grad_scores = (prob * (grad_probs - jnp.sum(grad_probs * prob, -1, keepdims=True))).astype(BF)
            grad_q.append(nn(grad_scores, key) * scale)
            back_k = tn(grad_scores, query) * scale
            back_v = tn(low, grad)
            grad_k[g] = back_k if grad_k[g] is None else grad_k[g] + back_k
            grad_v[g] = back_v if grad_v[g] is None else grad_v[g] + back_v
        first = first_half((SEQ, 4 * HEAD))
        for k, (pieces, target) in enumerate(((grad_q, dq), (grad_k + grad_v, dkv))):
            values = jnp.concatenate(pieces, -1)
            target[y, rows] = (values * tables[2 * k] - swap(values, first) * tables[2 * k + 1]).astype(BF)

    mlp_sum.relay()
    for k in range(6, 11):
        loads[k].wait()
    for k, source in ((1, dq), (2, dkv)):
        for y in range(2):
            put_out(k, y, nn(normed_t[...], source[y]))

    def back(start):
        rows = rows_at(start, SEQ)
        return (nt(dq[0, rows], wq[0]) + nt(dq[1, rows], wq[1])) + (nt(dkv[0, rows], wkv[0]) + nt(dkv[1, rows], wkv[1]))

    part[...] = back((1 - core) * SEQ).astype(BF)
    pair = sent(part, arrived, send.at[1], recv.at[1], sibling())
    for copy in outs.values():
        copy.wait()
    attn_sum.start()
    mlp_sum.spread()
    keep_part[...] = back(core * SEQ)
    pair.wait()

    @pl.loop(0, SEQ // STEP)
    def _(i):
        rows = rows_at(i * STEP, STEP)
        grad = keep_part[rows] + arrived[rows].astype(F32)
        values = xs[i].astype(F32)
        inverse = inverse_rms(values)
        unit = values * inverse
        change = inverse * (grad - unit * jnp.mean(grad * unit, -1, keepdims=True))
        in_grad[i] = gh[rows] + change

    for_partner[...] = in_grad[1 - yl].astype(BF)
    halves.append(moved(in_grad.at[yl], in_grad_out, put.at[3]))
    halves.append(sent(for_partner, from_partner, send.at[2], recv.at[2], partner()))
    attn_sum.relay()
    mlp_sum.narrow()
    attn_sum.spread()
    mlp_sum.finish(mlp_outs)
    attn_sum.narrow()
    attn_sum.finish(attn_outs)
    for copy in halves:
        copy.wait()


def backward(x, grad_hidden, branch, n1t, q, kv, probs, mixed, wq, wkv, wo, tables, data, result):
    rows, width = branch.shape
    third, wide = wq.shape[2], data[0].shape[-1]
    heads = (2, rows, third)
    weights = (2, width, third)
    half = (2, 128, width)
    return call(
        backward_kernel,
        (x, grad_hidden, branch, n1t, q, kv, probs, mixed, wq, wkv, wo, tables, *data, result),
        [ANY] * 11 + [VMEM] + [ANY] * 4,
        [shaped((2, 24, wide), F32)] * 3
        + [shaped((2, 24, third), F32)] * 3
        + [shaped((4, 4, 4, 48, third))] * 3
        + [shaped(half), shaped(half[1:], F32), shaped(half[1:])],
        [ANY] * 12,
        [
            pltpu.VMEM(half, BF),
            pltpu.VMEM((SEQ, width), F32),
            pltpu.VMEM((rows, width), BF),
            pltpu.VMEM((width, rows), BF),
            pltpu.VMEM((width, rows), BF),
            pltpu.VMEM(heads, BF),
            pltpu.VMEM(heads, BF),
            pltpu.VMEM((4, 4, SEQ, SEQ), BF),
            pltpu.VMEM(heads, BF),
            pltpu.VMEM(weights, BF),
            pltpu.VMEM(weights, BF),
            pltpu.VMEM(weights, BF),
            pltpu.VMEM(heads, BF),
            pltpu.VMEM(heads, BF),
            pltpu.VMEM(heads, BF),
            pltpu.VMEM((SEQ, width), BF),
            pltpu.VMEM((SEQ, width), F32),
            pltpu.VMEM((SEQ, width), BF),
            pltpu.VMEM(half, F32),
            pltpu.VMEM(half[1:], BF),
            pltpu.VMEM((2, 2, 4, 4, 48, third), BF),
            *Reduce.buffers(wide),
            *Reduce.buffers(third),
            *Reduce.semaphores,
            *Reduce.semaphores,
            pltpu.SemaphoreType.DMA((11,)),
            pltpu.SemaphoreType.DMA((4,)),
            pltpu.SemaphoreType.DMA((3,)),
            pltpu.SemaphoreType.DMA((3,)),
        ],
        "attn_backward_reduce",
        3,
    )


def tables_for(count, heads, plain):
    half = HEAD // 2
    inverse = np.float32(ROPE_BASE) ** (-(np.arange(half, dtype=np.float32) * np.float32(2.0)) / np.float32(HEAD))
    angle = np.arange(count, dtype=np.float32)[:, None] * inverse.astype(np.float32)[None, :]
    cosine, sine = np.cos(angle), np.sin(angle)
    cosine = np.tile(np.concatenate([cosine, cosine], -1), (1, heads))
    sine = np.tile(np.concatenate([-sine, sine], -1), (1, heads))
    cosine = np.concatenate([cosine, np.ones((count, plain), np.float32)], -1)
    sine = np.concatenate([sine, np.zeros((count, plain), np.float32)], -1)
    return np.stack([cosine, sine]).astype(np.float32)


def body(
    inputs,
    out_grad,
    lengths,
    query_weight,
    key_matrix,
    value_matrix,
    output_weight,
    gate_weight,
    up_weight,
    down_weight,
    attn_gain,
    mlp_gain,
):
    width = inputs.shape[2]
    gain_one = attn_gain.astype(F32)[:, None]
    gain_two = mlp_gain.astype(F32)[:, None]

    own_weights = (
        query_weight,
        key_matrix,
        value_matrix,
        output_weight.T,
        gate_weight,
        up_weight,
        down_weight.T,
    )
    query32, key32, value32, gate32, up32 = (
        w.astype(F32) for w in (query_weight, key_matrix, value_matrix, gate_weight, up_weight)
    )
    third, wide = query_weight.shape[1] // 2, gate_weight.shape[1] // 2
    tables = jnp.asarray(np.concatenate([tables_for(SEQ, 4, 0), tables_for(SEQ, 2, 2 * HEAD)]))

    *two, x, cot, cott, n1t, q, kv, probs, mixed, hidden, n2, n2t, out_acc, grad_acc, wq, wkv, wo, dg, du, dd = forward(
        own_weights, jnp.stack([attn_gain, mlp_gain], 1), lengths, inputs, out_grad, tables, third, wide
    )

    def joined(w):
        return w.reshape(2, width, -1)

    def blocked(w):
        return w.reshape(4, 4, 4, 48, -1)

    *one_sums, dg, du, dd, result, branch, grad_hidden = middle(
        n2, cot, hidden, n2t, cott, out_acc, grad_acc, two, [blocked(w) for w in (dg, du, dd)]
    )
    *sums, _, _, _, result, in_grad, in_grad_theirs = backward(
        x,
        grad_hidden,
        branch,
        n1t,
        q,
        kv,
        probs,
        mixed,
        joined(wq),
        joined(wkv),
        joined(wo),
        tables,
        [blocked(w) for w in (dg, du, dd)],
        result.reshape(2, 128, width),
    )
    mine = jnp.arange(2)[:, None, None] == lax.axis_index("yl")
    in_grad = jnp.where(mine, in_grad[None], in_grad_theirs[None].astype(F32))
    mlp_sums = [jnp.concatenate(parts, -1) for parts in zip(one_sums, sums[:3])]
    attn_sums = sums[3:]

    def whole(part):
        return jnp.moveaxis(part, 0, 1).reshape(24, -1)

    key_size = key_matrix.shape[1] // 2
    dquery, doutput = whole(attn_sums[0]), whole(attn_sums[2])
    dkey, dvalue = whole(attn_sums[1][..., :key_size]), whole(attn_sums[1][..., key_size:])
    dgate, dup, ddown = (whole(part) for part in mlp_sums)
    gain_grads = jnp.stack(
        [
            sum(jnp.sum(w * g, -1) for w, g in ((query32, dquery), (key32, dkey), (value32, dvalue))),
            sum(jnp.sum(w * g, -1) for w, g in ((gate32, dgate), (up32, dup))),
        ]
    )
    gain_grads = lax.psum(gain_grads, "yl")
    return (
        result,
        in_grad,
        dquery * gain_one,
        dkey * gain_one,
        dvalue * gain_one,
        doutput.T,
        dgate * gain_two,
        dup * gain_two,
        ddown.T,
        gain_grads[0],
        gain_grads[1],
    )


def solution(mesh):
    fine = Mesh(mesh.devices.reshape(2, 4, 4, 2, 2), AXES)
    rows = P(None, AXES, None)
    into, out = P(DP, "yl"), P("yl", DP)
    return jax.shard_map(
        body,
        mesh=fine,
        in_specs=(rows, rows, P(None, DP), into, into, into, out, into, into, out, P(DP), P(DP)),
        out_specs=(rows, rows, into, into, into, out, into, into, out, P(DP), P(DP)),
        check_vma=False,
    )
```

```python
import math

import jax
import jax.numpy as jnp
import numpy as np
from jax import lax
from jax.experimental import pallas as pl
from jax.experimental.pallas import tpu as pltpu
from jax.sharding import Mesh
from jax.sharding import PartitionSpec as P

HEAD = 96
EPS = 1e-05
ROPE_BASE = 100000.0
AXES = ("yh", "x", "z", "core", "yl")
DP = ("yh", "x", "z", "core")
MESH = pl.DeviceIdType.MESH
BF = jnp.bfloat16
F32 = jnp.float32
EVEN = (("x", "y", "z"), ("y", "z", "x"), ("z", "x", "y"))
SPARE_X = (("y", "z", "x"), ("x", "y", "z"), ("x", "z", "y"))
PLANE_Z = (("w", "x", "z"), ("w", "z", "x"), ("w", "x", "z"))
PLANE_X = (("w", "z", "x"), ("w", "x", "z"), ("w", "z", "x"))
SEQ = 256
ROWS = 512
STEP = 128
CHUNK = 256
VMEM_LIMIT = 62 * 1024 * 1024


def coordinates():
    x, z, yh, yl = (lax.axis_index(a) for a in ("x", "z", "yh", "yl"))
    return {"x": x, "z": z, "y": yh * 2 + yl, "w": yh}


def extent(axis):
    return 2 if axis == "w" else 4


def around(at, axis, by):
    return lax.rem(at[axis] + (by + 4), extent(axis))


def others(axis):
    return (1,) if axis == "w" else (1, -1, 2)


def peer(at, axis, by):
    value = around(at, axis, by)
    if axis == "y":
        return {"yh": value // 2, "yl": lax.rem(value, 2)}
    return {"yh" if axis == "w" else axis: value}


def sibling():
    return {"core": 1 - lax.axis_index("core")}


def partner():
    return {"yl": 1 - lax.axis_index("yl")}


def slot(at, axis, by=0):
    value = around(at, axis, by)
    return lax.rem(value, 2) * 2 + value // 2 if axis == "y" else value


def dimensions(order):
    return ("w" if "w" in order else "y", "x", "z")


def place(at, order, count, half=None, shifted=None):
    out = []
    for axis in dimensions(order):
        if axis in order[:count]:
            size = extent(axis)
            if half is not None and half[0] == axis:
                out.append(pl.ds(size // 2 * half[1], size // 2))
            else:
                out.append(pl.ds(0, size))
        else:
            out.append(slot(at, axis, shifted[1] if shifted is not None and shifted[0] == axis else 0))
    return tuple(out)


def greet(at):
    barrier = pltpu.get_barrier_semaphore()
    for axis in ("x", "y", "z"):
        for by in (1, -1, 2):
            pl.semaphore_signal(barrier, inc=1, device_id=peer(at, axis, by), device_id_type=MESH)
    pl.semaphore_signal(barrier, inc=1, device_id=sibling(), device_id_type=MESH)
    pl.semaphore_wait(barrier, 10)


def sent(src, dst, send, recv, device):
    copy = pltpu.make_async_remote_copy(
        src_ref=src, dst_ref=dst, send_sem=send, recv_sem=recv, device_id=device, device_id_type=MESH
    )
    copy.start()
    return copy


def moved(src, dst, sem):
    copy = pltpu.make_async_copy(src, dst, sem)
    copy.start()
    return copy


class Gather:
    semaphores = (
        pltpu.SemaphoreType.DMA((3,)),
        pltpu.SemaphoreType.DMA((3, 2, 3)),
        pltpu.SemaphoreType.DMA((3, 2, 3)),
        pltpu.SemaphoreType.DMA((3, 2, 2, 3)),
        pltpu.SemaphoreType.DMA((3, 2, 2, 3)),
    )

    def __init__(self, at, srcs, outs, semaphores, orders):
        self.at, self.srcs, self.outs, self.orders = at, srcs, outs, orders
        self.local, self.send, self.recv, self.ring_send, self.ring_recv = semaphores
        self.own, self.direct, self.ring = [], {}, {}

    def arrive(self, p, stage):
        for copy in self.direct.get((p, stage), ()):
            copy.wait_recv()
        if (p, stage, 0, 0) in self.ring:
            for d in range(2):
                self.ring[p, stage, d, 1 - d].wait_recv()
                self.ring[p, stage, d, 2].wait_recv()

    def to_all(self, stage):
        at = self.at
        for p, order in enumerate(self.orders):
            if stage:
                self.own[p].wait()
                self.arrive(p, 0)
            else:
                self.own.append(moved(self.srcs[p], self.outs[p].at[place(at, order, 0)], self.local.at[p]))
            group = self.outs[p].at[place(at, order, stage)]
            self.direct[p, stage] = [
                sent(
                    group if stage else self.srcs[p],
                    group,
                    self.send.at[p, stage, d],
                    self.recv.at[p, stage, d],
                    peer(at, order[stage], by),
                )
                for d, by in enumerate(others(order[stage]))
            ]

    def pass_on(self, p, stage, d, k, block):
        self.ring[p, stage, d, k] = sent(
            block,
            block,
            self.ring_send.at[p, stage - 1, d, k],
            self.ring_recv.at[p, stage - 1, d, k],
            peer(self.at, self.orders[p][stage], 1 - 2 * d),
        )

    def spread(self, stage):
        for p, order in enumerate(self.orders):
            if stage == 1:
                self.own[p].wait()
            self.arrive(p, stage - 1)
            for t in range(2):
                for d in range(2):
                    h = t if d == 0 else 1 - t
                    self.pass_on(p, stage, d, h, self.outs[p].at[place(self.at, order, stage, (order[0], h))])

    def forward(self, stage):
        for p, order in enumerate(self.orders):
            for d, by in enumerate((1, -1)):
                self.ring[p, stage, d, d].wait_recv()
                where = place(self.at, order, stage, (order[0], d), (order[stage], -by))
                self.pass_on(p, stage, d, 2, self.outs[p].at[where])

    def finish(self):
        for p in range(3):
            self.arrive(p, 2)
        for copies in self.direct.values():
            for copy in copies:
                copy.wait_send()
        for copy in self.ring.values():
            copy.wait_send()


class Reduce:
    semaphores = (
        pltpu.SemaphoreType.DMA((3, 3)),
        pltpu.SemaphoreType.DMA((3, 2, 3)),
        pltpu.SemaphoreType.DMA((3, 2, 3)),
        pltpu.SemaphoreType.DMA((3, 2, 3)),
        pltpu.SemaphoreType.DMA((3, 2, 3)),
        pltpu.SemaphoreType.DMA((3, 2)),
        pltpu.SemaphoreType.DMA((3, 2)),
    )

    @staticmethod
    def buffers(columns, orders):
        def per_piece(*shape):
            return [pltpu.VMEM(shape + (48, columns), BF) for _ in range(3)]

        size = extent(dimensions(orders[0])[0])
        return [
            *per_piece(2, size // 2, 4),
            *per_piece(size, 4),
            *per_piece(2, size // 2, 4),
            *per_piece(2, size, 4),
            *per_piece(3, size),
            *per_piece(3),
            *[pltpu.VMEM((48, columns), F32) for _ in range(3)],
        ]

    def __init__(self, at, data, buffers, semaphores, orders):
        self.at, self.data, self.orders = at, data, orders
        self.side, self.kept, self.far, self.near, self.second, self.third, self.sums = (
            buffers[3 * k : 3 * k + 3] for k in range(7)
        )
        self.load, self.first_send, self.first_recv, self.send, self.recv, self.end_send, self.end_recv = semaphores
        self.loads, self.copies = {}, {}

    def left(self, p):
        order = self.orders[p]
        return [axis for axis in dimensions(order) if axis != order[2]]

    def inside(self, p, first, second=None):
        whole = slice(None) if second is None else second
        return (first, whole) if self.left(p)[0] == self.orders[p][1] else (whole, first)

    def start(self):
        at, s, r = self.at, self.first_send, self.first_recv
        for p, order in enumerate(self.orders):
            axis, cut = order[2], self.left(p)[0]
            size = extent(cut) // 2
            for d, by in enumerate((1, -1)):
                block = self.data[p].at[place(at, order, 2, (cut, d), (axis, 2))]
                self.copies[p, d, 0] = sent(block, self.far[p].at[d], s.at[p, d, 0], r.at[p, d, 0], peer(at, axis, by))
            for d, by in enumerate((1, -1)):
                h = 1 - d
                block = self.data[p].at[place(at, order, 2, (cut, h), (axis, by))]
                self.copies[p, d, 1] = sent(
                    block, self.near[p].at[d, pl.ds(size * h, size)], s.at[p, d, 1], r.at[p, d, 1], peer(at, axis, by)
                )
                block = self.data[p].at[place(at, order, 2, (cut, d), (axis, by))]
                self.loads[p, d] = moved(block, self.side[p].at[d], self.load.at[p, d])
            self.loads[p, 2] = moved(self.data[p].at[place(at, order, 2)], self.kept[p], self.load.at[p, 2])

    def relay(self):
        for p, order in enumerate(self.orders):
            size = extent(self.left(p)[0]) // 2
            for d, by in enumerate((1, -1)):
                self.loads[p, d].wait()
                self.copies[p, d, 0].wait_recv()
                side, far = self.side[p], self.far[p]

                @pl.loop(0, 4 * size)
                def _(i, d=d, side=side, far=far):
                    a, b = i // 4, lax.rem(i, 4)
                    side[d, a, b] = (side[d, a, b].astype(F32) + far[d, a, b].astype(F32)).astype(BF)

                self.copies[p, d, 2] = sent(
                    side.at[d],
                    self.near[p].at[d, pl.ds(size * d, size)],
                    self.first_send.at[p, d, 2],
                    self.first_recv.at[p, d, 2],
                    peer(self.at, order[2], by),
                )

    def spread(self):
        at = self.at
        for p, order in enumerate(self.orders):
            self.loads[p, 2].wait()
            for d in range(2):
                self.copies[p, d, 1].wait_recv()
                self.copies[p, d, 2].wait_recv()
            kept, near = self.kept[p], self.near[p]

            @pl.loop(0, 4 * extent(self.left(p)[0]))
            def _(i, kept=kept, near=near):
                a, b = i // 4, lax.rem(i, 4)
                total = kept[a, b].astype(F32) + near[0, a, b].astype(F32) + near[1, a, b].astype(F32)
                kept[a, b] = total.astype(BF)

            for d, by in enumerate(others(order[1])):
                block = kept.at[self.inside(p, slot(at, order[1], by))]
                self.copies[p, "b", d] = sent(
                    block, self.second[p].at[d], self.send.at[p, 0, d], self.recv.at[p, 0, d], peer(at, order[1], by)
                )

    def narrow(self):
        at = self.at
        for p, order in enumerate(self.orders):
            for d in range(len(others(order[1]))):
                self.copies[p, "b", d].wait_recv()
            kept, second, mine = self.kept[p], self.second[p], slot(at, order[1])

            @pl.loop(0, extent(order[0]))
            def _(i, p=p, kept=kept, second=second, mine=mine):
                total = kept[self.inside(p, mine, i)].astype(F32)
                for d in range(3):
                    total = total + second[d, i].astype(F32)
                kept[self.inside(p, mine, i)] = total.astype(BF)

            for d, by in enumerate(others(order[0])):
                block = kept.at[self.inside(p, mine, slot(at, order[0], by))]
                self.copies[p, "c", d] = sent(
                    block, self.third[p].at[d], self.send.at[p, 1, d], self.recv.at[p, 1, d], peer(at, order[0], by)
                )

    def finish(self, outs):
        at, core, ends = self.at, lax.axis_index("core"), []
        for p, order in enumerate(self.orders):
            total = self.kept[p][self.inside(p, slot(at, order[1]), slot(at, order[0]))].astype(F32)
            for d in range(len(others(order[0]))):
                self.copies[p, "c", d].wait_recv()
                total = total + self.third[p][d].astype(F32)
            self.sums[p][...] = total
            theirs = self.sums[p].at[pl.ds(pl.multiple_of(24 * (1 - core), 8), 24)]
            mine = self.sums[p].at[pl.ds(pl.multiple_of(24 * core, 8), 24)]
            ends.append(sent(theirs, outs[p].at[core], self.end_send.at[p, 0], self.end_recv.at[p, 0], sibling()))
            ends.append(moved(mine, outs[p].at[core], self.end_send.at[p, 1]))
        for copy in self.copies.values():
            copy.wait_send()
        for copy in ends:
            copy.wait()


def nn(left, right):
    return lax.dot_general(left, right, (((1,), (0,)), ((), ())), preferred_element_type=F32)


def nt(left, right):
    return lax.dot_general(left, right, (((1,), (1,)), ((), ())), preferred_element_type=F32)


def tn(left, right):
    return lax.dot_general(left, right, (((0,), (0,)), ((), ())), preferred_element_type=F32)


def inverse_rms(values):
    return lax.rsqrt(jnp.mean(values * values, -1, keepdims=True) + EPS)


def swap(values, first):
    width = values.shape[-1]
    return jnp.where(first, pltpu.roll(values, width - HEAD // 2, 1), pltpu.roll(values, HEAD // 2, 1))


def first_half(shape):
    return lax.rem(lax.broadcasted_iota(jnp.int32, shape, 1), HEAD) < HEAD // 2


def rows_at(start, size):
    return pl.ds(pl.multiple_of(start, size), size)


ANY = pl.BlockSpec(memory_space=pl.ANY)
VMEM = pl.BlockSpec(memory_space=pltpu.VMEM)


def shaped(shape, kind=BF):
    return jax.ShapeDtypeStruct(shape, kind)


def call(kernel, operands, in_specs, results, out_specs, scratch, name, collective_id, **more):
    return pl.pallas_call(
        kernel,
        out_shape=results,
        in_specs=in_specs,
        out_specs=out_specs,
        scratch_shapes=scratch,
        compiler_params=pltpu.CompilerParams(
            collective_id=collective_id, has_side_effects=True, vmem_limit_bytes=VMEM_LIMIT
        ),
        name=name,
        **more,
    )(*operands)


def hidden_units(m, sub, n2, cot, weights, acts):
    rows = rows_at(m * ROWS, ROWS)
    columns = pl.ds(sub * CHUNK, CHUNK)
    gate_w, up_w, down_w = (w[..., columns].reshape(-1, CHUNK) for w in weights)
    gate = nn(n2[rows], gate_w)
    up = nn(n2[rows], up_w)
    sigma = jax.nn.sigmoid(gate)
    silu = gate * sigma
    grad_active = nn(cot[m].reshape(ROWS, -1), down_w)
    acts[0][rows, columns] = (silu * up).astype(BF)
    acts[1][rows, columns] = (grad_active * up * (sigma + silu * (1.0 - sigma))).astype(BF)
    acts[2][rows, columns] = (grad_active * silu).astype(BF)


def unit_gradients(n2t, cott, acts, staging, outs, sems):
    waits = {}
    for k, (left, right, target) in enumerate(((n2t, acts[1], 0), (n2t, acts[2], 1), (cott, acts[0], 2))):
        for sub in range(2):
            columns = pl.ds(sub * CHUNK, CHUNK)
            place_in = (2 * k + sub) % 4
            if place_in in waits:
                waits[place_in].wait()
            staging[place_in] = nn(left[...], right[:, columns]).astype(BF)
            waits[place_in] = moved(staging.at[place_in], outs[target].at[:, columns], sems.at[place_in])
    return list(waits.values())


def forward_kernel(third, wide, *refs):
    own_weights, gains, lengths, xin, gin, tables = refs[:7], *refs[7:12]
    full_two, full_one = refs[12:15], refs[15:18]
    (
        x_out, n1t_out, q_out, kv_out, probs_out, mixed_out, hidden_out, n2_out, n2t_out, cot_out, cott_out,
    ) = refs[18:29]
    attn_out, grads_out, acts_out = refs[29:32], refs[32:35], refs[35:38]
    (
        shard, got_shard, packed, xs, gs, normed, q, kv, probs, mixed, hidden, n2, n2t, cott, part, arrived, n1t,
        valid, staging,
    ) = refs[38:57]
    full_attn, weights, acts = refs[57:60], refs[60:63], refs[63:66]
    attn_sems, one_sems, two_sems = refs[66:71], refs[71:76], refs[76:81]
    pair_send, pair_recv, row_send, row_recv, far_send, far_recv, own_sem, out_sem, put_sem = refs[81:]
    at = coordinates()
    core, yl = lax.axis_index("core"), lax.axis_index("yl")
    own_x = moved(xin.at[yl], xs.at[core, yl], own_sem.at[0])
    own_g = moved(gin, gs.at[:, core, yl], own_sem.at[1])

    query, key, value, output, *mlp_weights = (ref[...].astype(F32) for ref in own_weights)
    gain_one, gain_two = gains[:, 0:1].astype(F32), gains[:, 1:2].astype(F32)
    small = key.shape[1] // 2
    for c in range(2):
        thin = slice(c * small, (c + 1) * small)
        parts = [
            query[:, c * third : (c + 1) * third] * gain_one,
            jnp.concatenate([key[:, thin] * gain_one, value[:, thin] * gain_one], -1),
            output[:, c * third : (c + 1) * third],
            *(
                w[:, c * wide : (c + 1) * wide] * g
                for w, g in zip(mlp_weights, (gain_two, gain_two, jnp.ones_like(gain_two)))
            ),
        ]
        column = 0
        for part_value in parts:
            shard[c, :24, column : column + part_value.shape[1]] = part_value
            column += part_value.shape[1]
        lane = lax.broadcasted_iota(jnp.int32, (8, 2 * SEQ), 1)
        ends = jnp.where(lane < SEQ, lengths[0, 0], lengths[1, 0] + SEQ)
        shard[c, 24:, : 2 * SEQ] = jnp.where(lane < ends, 1.0, 0.0)
    greet(at)
    swap_shard = sent(shard.at[1 - core], got_shard, pair_send.at[0], pair_recv.at[0], sibling())

    rows = {}

    def exchange(k):
        ours, theirs, dst = (
            (xin.at[yl], xin.at[1 - yl], xs.at[core, yl]),
            (gin, gin, gs.at[:, core, yl]),
        )[k]
        rows[k, 0] = sent(theirs, dst, row_send.at[k, 0], row_recv.at[k, 0], partner())
        rows[k, 1] = sent(ours, dst, row_send.at[k, 1], row_recv.at[k, 1], sibling())

    def share(k):
        block = (xs.at[core, 1 - yl], gs.at[:, core, 1 - yl])[k]
        rows[k, 0].wait_recv()
        rows[k, 2] = sent(block, block, row_send.at[k, 2], row_recv.at[k, 2], sibling())

    def settle(k):
        (own_x, own_g)[k].wait()
        rows[k, 0].wait_send()
        rows[k, 1].wait()
        rows[k, 2].wait()

    swap_shard.wait()
    low, high = shard[core], got_shard[...]
    first, last = jnp.where(core == 0, low, high), jnp.where(core == 0, high, low)
    packed[...] = jnp.concatenate([first[:24], last[:24]], 0).astype(BF)
    for c, rows_of in enumerate((first, last)):
        for m in range(2):
            valid[m, c] = rows_of[24:32, m * SEQ : (m + 1) * SEQ]

    def pieces(start, size, step):
        return [packed.at[:, pl.ds(start + k * step, size)] for k in range(3)]

    half = wide // 2
    attn = Gather(at, pieces(0, third, third), full_attn, attn_sems, EVEN)
    one = Gather(at, pieces(3 * third, half, wide), weights, one_sems, PLANE_Z)
    two = Gather(at, pieces(3 * third + half, half, wide), full_two, two_sems, PLANE_X)
    attn.to_all(0)
    one.to_all(0)
    two.to_all(0)
    attn.to_all(1)
    one.spread(1)
    exchange(0)
    attn.spread(2)
    one.forward(1)
    two.spread(1)
    attn.forward(2)
    two.forward(1)
    one.spread(2)
    exchange(1)
    share(0)
    settle(0)
    outs = [moved(xs, x_out, out_sem.at[0])]

    @pl.loop(0, ROWS // STEP)
    def _(i):
        block = rows_at(i * STEP, STEP)
        values = xs[i // 2, lax.rem(i, 2)].astype(F32)
        normed[block] = (values * inverse_rms(values)).astype(BF)

    n1t[...] = normed[...].T
    outs.append(moved(n1t, n1t_out, out_sem.at[1]))
    attn.finish()
    outs.extend(moved(full_attn[p], attn_out[p], out_sem.at[2 + p]) for p in range(3))
    wq, wkv, wo = full_attn

    def weight(ref, y):
        return ref[pl.ds(2 * y, 2)].reshape(-1, third)

    @pl.loop(0, 2)
    def _(y):
        @pl.loop(0, ROWS // SEQ)
        def _(n):
            block = rows_at(n * SEQ, SEQ)
            left = normed[block]
            is_first = first_half((SEQ, third))
            for k, (w, result) in enumerate(((wq, q), (wkv, kv))):
                lin = nn(left, weight(w, y))
                result[y, block] = (lin * tables[2 * k] + swap(lin, is_first) * tables[2 * k + 1]).astype(BF)

    outs.append(moved(q, q_out, out_sem.at[5]))
    outs.append(moved(kv, kv_out, out_sem.at[6]))
    one.forward(2)
    scale = 1.0 / math.sqrt(HEAD)

    @pl.loop(0, 4)
    def _(i):
        y, n = i // 2, lax.rem(i, 2)
        block = rows_at(n * SEQ, SEQ)
        t = lax.broadcasted_iota(jnp.int32, (SEQ, SEQ), 0)
        s = lax.broadcasted_iota(jnp.int32, (SEQ, SEQ), 1)
        keep = (s <= t) & (valid[yl, n, 0:1, :] > 0.5)
        queries, keys = q[y, block], kv[y, block]
        results = []
        for h in range(4):
            g = h // 2
            scores = nt(queries[:, h * HEAD : (h + 1) * HEAD], keys[:, g * HEAD : (g + 1) * HEAD]) * scale
            scores = jnp.where(keep, scores, -1e30)
            terms = jnp.exp(scores - jnp.max(scores, -1, keepdims=True))
            low_probs = (terms / jnp.sum(terms, -1, keepdims=True)).astype(BF)
            probs[i, h] = low_probs
            results.append(nn(low_probs, keys[:, (2 + g) * HEAD : (3 + g) * HEAD]))
        mixed[y, block] = jnp.concatenate(results, -1).astype(BF)

    outs.append(moved(probs, probs_out, out_sem.at[7]))
    outs.append(moved(mixed, mixed_out, out_sem.at[8]))
    two.spread(2)

    copies = []
    for i in range(ROWS // STEP):
        block = rows_at(lax.rem(2 * (1 - core) + i, 4) * STEP, STEP)
        part[block] = (nt(mixed[0, block], weight(wo, 0)) + nt(mixed[1, block], weight(wo, 1))).astype(BF)
        copies.append(sent(part.at[block], arrived.at[block], pair_send.at[1 + i], pair_recv.at[1 + i], sibling()))
    second_rows = {}
    mine, theirs = yl * ROWS, (1 - yl) * ROWS
    for i in range(ROWS // STEP):
        copies[(i + 2) % 4 if i < 2 else i - 2].wait_send()
        copies[i].wait_recv()
        number = lax.rem(2 * core + i, 4)
        block = rows_at(number * STEP, STEP)
        values = xs[number // 2, lax.rem(number, 2)].astype(F32) + (
            part[block].astype(F32) + arrived[block].astype(F32)
        )
        hidden[block] = values
        target = rows_at(mine + number * STEP, STEP)
        n2[target] = (values * inverse_rms(values)).astype(BF)
        if i < 2:
            second_rows[0, i] = sent(n2.at[target], n2.at[target], far_send.at[0, i], far_recv.at[0, i], partner())
    outs.append(moved(hidden.at[rows_at(core * SEQ, SEQ)], hidden_out, out_sem.at[9]))
    share(1)
    settle(1)

    for m in range(2):
        for c in range(2):
            for h in range(2):
                mask = valid[m, c][:, h * STEP : (h + 1) * STEP].T[:, 0:1]
                gs[m, c, h] = (gs[m, c, h].astype(F32) * mask).astype(BF)
    outs.append(moved(gs, cot_out, out_sem.at[10]))

    one.finish()
    outs.extend(moved(weights[p], full_one[p], out_sem.at[11 + p]) for p in range(3))
    for i in range(2):
        second_rows[0, i].wait_recv()
        block = rows_at(theirs + (2 * core + i) * STEP, STEP)
        second_rows[1, i] = sent(n2.at[block], n2.at[block], far_send.at[1, i], far_recv.at[1, i], sibling())
    for sub in range(2):
        hidden_units(yl, sub, n2, gs, weights, acts)
    for m in range(2):
        for c in range(2):
            for h in range(2):
                cott[:, pl.ds(m * ROWS + (2 * c + h) * STEP, STEP)] = gs[m, c, h].T
    outs.append(moved(cott, cott_out, out_sem.at[14]))
    two.forward(2)
    for i in range(2):
        second_rows[0, i].wait_send()
        second_rows[1, i].wait()
    for sub in range(2):
        hidden_units(1 - yl, sub, n2, gs, weights, acts)
    outs.extend(moved(acts[p], acts_out[p], out_sem.at[15 + p]) for p in range(3))
    outs.append(moved(n2, n2_out, out_sem.at[18]))
    for i in range(2 * ROWS // STEP):
        n2t[:, pl.ds(i * STEP, STEP)] = n2[pl.ds(i * STEP, STEP)].T
    outs.append(moved(n2t, n2t_out, out_sem.at[19]))
    outs.extend(unit_gradients(n2t, cott, acts, staging, grads_out, put_sem))
    two.finish()
    for copy in outs:
        copy.wait()


def forward(own_weights, gains, lengths, xin, gin, tables, third, wide):
    width = xin.shape[2]
    rows = (ROWS, width)
    both = (2 * ROWS, width)
    heads = (2, ROWS, third)
    square = (4, 4, SEQ, SEQ)
    half = wide // 2
    piece = (2, 4, 4, 48, half)
    return call(
        lambda *refs: forward_kernel(third, wide, *refs),
        (*own_weights, gains, lengths, xin, gin, tables),
        [VMEM] * 8 + [pl.BlockSpec(memory_space=pltpu.SMEM), ANY, ANY, VMEM],
        [shaped(piece)] * 6
        + [
            shaped((2, 2, 128, width)),
            shaped(rows[::-1]),
            shaped(heads),
            shaped(heads),
            shaped(square),
            shaped(heads),
            shaped((SEQ, width), F32),
            shaped(both),
            shaped(both[::-1]),
            shaped((2, 2, 2, 128, width)),
            shaped(both[::-1]),
        ]
        + [shaped((4, 4, 4, 48, third))] * 3
        + [shaped((width, half))] * 3
        + [shaped((2 * ROWS, half))] * 3,
        [ANY] * 26,
        [
            pltpu.VMEM((2, 32, 3 * third + 3 * wide), F32),
            pltpu.VMEM((32, 3 * third + 3 * wide), F32),
            pltpu.VMEM((48, 3 * third + 3 * wide), BF),
            pltpu.VMEM((2, 2, 128, width), BF),
            pltpu.VMEM((2, 2, 2, 128, width), BF),
            pltpu.VMEM(rows, BF),
            pltpu.VMEM(heads, BF),
            pltpu.VMEM(heads, BF),
            pltpu.VMEM(square, BF),
            pltpu.VMEM(heads, BF),
            pltpu.VMEM(rows, F32),
            pltpu.VMEM(both, BF),
            pltpu.VMEM(both[::-1], BF),
            pltpu.VMEM(both[::-1], BF),
            pltpu.VMEM(rows, BF),
            pltpu.VMEM(rows, BF),
            pltpu.VMEM(rows[::-1], BF),
            pltpu.VMEM((2, 2, 8, SEQ), F32),
            pltpu.VMEM((4, width, CHUNK), BF),
            *[pltpu.VMEM((4, 4, 4, 48, third), BF) for _ in range(3)],
            *[pltpu.VMEM(piece, BF) for _ in range(3)],
            *[pltpu.VMEM((2 * ROWS, half), BF) for _ in range(3)],
            *Gather.semaphores,
            *Gather.semaphores,
            *Gather.semaphores,
            pltpu.SemaphoreType.DMA((5,)),
            pltpu.SemaphoreType.DMA((5,)),
            pltpu.SemaphoreType.DMA((2, 3)),
            pltpu.SemaphoreType.DMA((2, 3)),
            pltpu.SemaphoreType.DMA((2, 2)),
            pltpu.SemaphoreType.DMA((2, 2)),
            pltpu.SemaphoreType.DMA((2,)),
            pltpu.SemaphoreType.DMA((20,)),
            pltpu.SemaphoreType.DMA((4,)),
        ],
        "gather_attn_forward_mlp",
        1,
    )


def middle_kernel(*refs):
    n2_in, cot_in, hidden_in, n2t_in, cott_in = refs[:5]
    one_in, two_in, acts_in, data = refs[5:8], refs[8:11], refs[11:14], refs[14:17]
    sums_out, grads_out = refs[17:20], refs[20:23]
    result_out, branch_out, grad_hidden_out = refs[23:26]
    n2, cot, hidden, n2t, cott, staging, to_pair, from_pair, to_far, from_far, keep, result, branch, gh = refs[26:40]
    one, two, acts_one, acts_two = refs[40:43], refs[43:46], refs[46:49], refs[49:52]
    buffers, reduce_sems = refs[52:73], refs[73:80]
    load, put, put_sem, pair_send, pair_recv, far_send, far_recv = refs[80:]
    core, yl = lax.axis_index("core"), lax.axis_index("yl")
    at = coordinates()
    order = (
        (n2_in, n2),
        (two_in[0], two[0]),
        (two_in[1], two[1]),
        (cot_in, cot),
        (two_in[2], two[2]),
        *zip(acts_in[1:], acts_one[1:]),
        *zip(one_in[:2], one[:2]),
        (acts_in[0], acts_one[0]),
        (one_in[2], one[2]),
        (n2t_in, n2t),
        (cott_in, cott),
        (hidden_in, hidden),
    )
    loads = [moved(src, dst, load.at[k]) for k, (src, dst) in enumerate(order)]
    greet(at)
    total = Reduce(at, data, buffers, reduce_sems, PLANE_Z)
    total.start()
    for k in range(5):
        loads[k].wait()
    for sub in range(2):
        hidden_units(1 - yl, sub, n2, cot, two, acts_two)
    for k in range(5, 11):
        loads[k].wait()

    def weight(ref):
        return ref[...].reshape(n2.shape[1], -1)

    def grad_rows(m, c):
        rows = rows_at(m * ROWS + c * SEQ, SEQ)
        return (nt(acts_one[1][rows], weight(one[0])) + nt(acts_one[2][rows], weight(one[1]))) + (
            nt(acts_two[1][rows], weight(two[0])) + nt(acts_two[2][rows], weight(two[1]))
        )

    def out_rows(m, c):
        rows = rows_at(m * ROWS + c * SEQ, SEQ)
        return nt(acts_one[0][rows], weight(one[2])) + nt(acts_two[0][rows], weight(two[2]))

    pair, far = {}, {}

    def to_sibling(k, value):
        to_pair[k] = value.astype(BF)
        pair[k] = sent(to_pair.at[k], from_pair.at[k], pair_send.at[k], pair_recv.at[k], sibling())

    def to_partner(k, value):
        pair[k].wait_recv()
        to_far[k] = (value + from_pair[k].astype(F32)).astype(BF)
        far[k] = sent(to_far.at[k], from_far.at[k], far_send.at[k], far_recv.at[k], partner())

    to_sibling(0, grad_rows(1 - yl, 1 - core))
    to_partner(0, grad_rows(1 - yl, core))
    to_sibling(1, out_rows(1 - yl, 1 - core))
    total.relay()
    to_partner(1, out_rows(1 - yl, core))
    for sub in range(2):
        hidden_units(yl, sub, n2, cot, two, acts_two)
    to_sibling(2, grad_rows(yl, 1 - core))
    keep[...] = grad_rows(yl, core)
    for k in range(11, 14):
        loads[k].wait()
    pair[2].wait_recv()
    far[0].wait_recv()

    @pl.loop(0, SEQ // STEP)
    def _(i):
        rows = rows_at(i * STEP, STEP)
        grad = keep[rows] + (from_pair[2, rows].astype(F32) + from_far[0, rows].astype(F32))
        values = hidden[rows]
        inverse = inverse_rms(values)
        unit = values * inverse
        back = inverse * (grad - unit * jnp.mean(grad * unit, -1, keepdims=True))
        gh[rows] = cot[yl, core, i].astype(F32) + back
        branch[rows] = gh[rows].astype(BF)

    own = rows_at(core * SEQ, SEQ)
    shared = sent(branch, branch_out.at[own], pair_send.at[4], pair_recv.at[4], sibling())
    outs = [moved(branch, branch_out.at[own], put.at[0]), moved(gh, grad_hidden_out, put.at[1])]
    to_sibling(3, out_rows(yl, 1 - core))
    keep[...] = out_rows(yl, core)
    total.spread()
    pair[3].wait_recv()
    far[1].wait_recv()

    @pl.loop(0, SEQ // STEP)
    def _(i):
        rows = rows_at(i * STEP, STEP)
        change = keep[rows] + (from_pair[3, rows].astype(F32) + from_far[1, rows].astype(F32))
        result[rows] = (hidden[rows] + change).astype(BF)

    outs.append(moved(result, result_out, put.at[2]))
    outs.extend(unit_gradients(n2t, cott, acts_two, staging, grads_out, put_sem))
    total.narrow()
    total.finish(sums_out)
    shared.wait()
    for copy in (*pair.values(), *far.values()):
        copy.wait_send()
    for copy in outs:
        copy.wait()


def middle(n2, cot, hidden, n2t, cott, one, two, acts, data):
    rows, width = n2.shape
    half = one[0].shape[-1]
    block = (SEQ, width)
    return call(
        middle_kernel,
        (n2, cot, hidden, n2t, cott, *one, *two, *acts, *data),
        [ANY] * 17,
        [shaped((2, 24, half), F32)] * 3
        + [shaped((width, half))] * 3
        + [shaped(block), shaped((ROWS, width)), shaped(block, F32)],
        [ANY] * 9,
        [
            pltpu.VMEM((rows, width), BF),
            pltpu.VMEM(cot.shape, BF),
            pltpu.VMEM(block, F32),
            pltpu.VMEM((width, rows), BF),
            pltpu.VMEM((width, rows), BF),
            pltpu.VMEM((4, width, CHUNK), BF),
            pltpu.VMEM((4,) + block, BF),
            pltpu.VMEM((4,) + block, BF),
            pltpu.VMEM((2,) + block, BF),
            pltpu.VMEM((2,) + block, BF),
            pltpu.VMEM(block, F32),
            pltpu.VMEM(block, BF),
            pltpu.VMEM(block, BF),
            pltpu.VMEM(block, F32),
            *[pltpu.VMEM(one[0].shape, BF) for _ in range(6)],
            *[pltpu.VMEM((rows, half), BF) for _ in range(6)],
            *Reduce.buffers(half, PLANE_Z),
            *Reduce.semaphores,
            pltpu.SemaphoreType.DMA((14,)),
            pltpu.SemaphoreType.DMA((3,)),
            pltpu.SemaphoreType.DMA((4,)),
            pltpu.SemaphoreType.DMA((5,)),
            pltpu.SemaphoreType.DMA((5,)),
            pltpu.SemaphoreType.DMA((2,)),
            pltpu.SemaphoreType.DMA((2,)),
        ],
        "mlp_reduce",
        2,
    )


def backward_kernel(*refs):
    xall, grad_hidden_in, branch_in, n1t_in, q_in, kv_in, probs_in, mixed_in, wq_in, wkv_in, wo_in, tables = refs[:12]
    data, result = refs[12:15], refs[15]
    mlp_outs, attn_outs, attn_grads = refs[16:19], refs[19:22], refs[22:25]
    result_out, in_grad_out, from_partner = refs[25:28]
    (
        xs, gh, branch, branch_t, normed_t, q, kv, probs, mixed, wq, wkv, wo,
        grad_mixed, dq, dkv, part, keep_part, arrived, in_grad, for_partner, stage,
    ) = refs[28:49]
    mlp_buffers, attn_buffers = refs[49:70], refs[70:91]
    mlp_sems, attn_sems = refs[91:98], refs[98:105]
    load, put, send, recv = refs[105:]
    at = coordinates()
    core, yl = lax.axis_index("core"), lax.axis_index("yl")
    loads = [
        moved(src, dst, load.at[k])
        for k, (src, dst) in enumerate(
            (
                (branch_in, branch),
                (wo_in, wo),
                (mixed_in, mixed),
                (q_in, q),
                (kv_in, kv),
                (probs_in, probs),
                (wq_in, wq),
                (wkv_in, wkv),
                (n1t_in, normed_t),
                (grad_hidden_in, gh),
                (xall.at[core], xs),
            )
        )
    ]
    greet(at)
    mlp_sum = Reduce(at, data, mlp_buffers, mlp_sems, PLANE_X)
    attn_sum = Reduce(at, attn_grads, attn_buffers, attn_sems, SPARE_X)
    mlp_sum.start()
    halves = [
        moved(result.at[yl], result_out.at[yl], put.at[0]),
        sent(result.at[1 - yl], result_out.at[yl], send.at[0], recv.at[0], partner()),
    ]
    for k in range(3):
        loads[k].wait()
    branch_t[...] = branch[...].T
    third = wq.shape[2]
    outs = {}

    def put_out(k, y, value):
        slot = (2 * k + y) % 2
        if (k, y) != (0, 0) and (k, y) != (0, 1):
            outs.pop(slot).wait()
        stage[slot] = value.astype(BF).reshape(stage.shape[1:])
        target = (attn_grads[2], attn_grads[0], attn_grads[1])[k]
        outs[slot] = moved(stage.at[slot], target.at[pl.ds(2 * y, 2)], put.at[1 + slot])

    for y in range(2):
        grad_mixed[y] = nn(branch[...], wo[y]).astype(BF)
        put_out(0, y, nn(branch_t[...], mixed[y]))
    for k in range(3, 6):
        loads[k].wait()
    scale = 1.0 / math.sqrt(HEAD)

    @pl.loop(0, 4)
    def _(i):
        y, n = i // 2, lax.rem(i, 2)
        rows = rows_at(n * SEQ, SEQ)
        queries, keys, grads = q[y, rows], kv[y, rows], grad_mixed[y, rows]
        grad_q, grad_k, grad_v = [], [None, None], [None, None]
        for h in range(4):
            g = h // 2
            key = keys[:, g * HEAD : (g + 1) * HEAD]
            value = keys[:, (2 + g) * HEAD : (3 + g) * HEAD]
            query = queries[:, h * HEAD : (h + 1) * HEAD]
            grad = grads[:, h * HEAD : (h + 1) * HEAD]
            low = probs[i, h]
            prob = low.astype(F32)
            grad_probs = nt(grad, value)
            grad_scores = (prob * (grad_probs - jnp.sum(grad_probs * prob, -1, keepdims=True))).astype(BF)
            grad_q.append(nn(grad_scores, key) * scale)
            back_k = tn(grad_scores, query) * scale
            back_v = tn(low, grad)
            grad_k[g] = back_k if grad_k[g] is None else grad_k[g] + back_k
            grad_v[g] = back_v if grad_v[g] is None else grad_v[g] + back_v
        first = first_half((SEQ, 4 * HEAD))
        for k, (pieces, target) in enumerate(((grad_q, dq), (grad_k + grad_v, dkv))):
            values = jnp.concatenate(pieces, -1)
            target[y, rows] = (values * tables[2 * k] - swap(values, first) * tables[2 * k + 1]).astype(BF)

    mlp_sum.relay()
    for k in range(6, 11):
        loads[k].wait()
    for k, source in ((1, dq), (2, dkv)):
        for y in range(2):
            put_out(k, y, nn(normed_t[...], source[y]))

    def back(start):
        rows = rows_at(start, SEQ)
        return (nt(dq[0, rows], wq[0]) + nt(dq[1, rows], wq[1])) + (nt(dkv[0, rows], wkv[0]) + nt(dkv[1, rows], wkv[1]))

    part[...] = back((1 - core) * SEQ).astype(BF)
    pair = sent(part, arrived, send.at[1], recv.at[1], sibling())
    for copy in outs.values():
        copy.wait()
    attn_sum.start()
    mlp_sum.spread()
    keep_part[...] = back(core * SEQ)
    pair.wait()

    @pl.loop(0, SEQ // STEP)
    def _(i):
        rows = rows_at(i * STEP, STEP)
        grad = keep_part[rows] + arrived[rows].astype(F32)
        values = xs[i].astype(F32)
        inverse = inverse_rms(values)
        unit = values * inverse
        change = inverse * (grad - unit * jnp.mean(grad * unit, -1, keepdims=True))
        in_grad[i] = gh[rows] + change

    for_partner[...] = in_grad[1 - yl].astype(BF)
    halves.append(moved(in_grad.at[yl], in_grad_out, put.at[3]))
    halves.append(sent(for_partner, from_partner, send.at[2], recv.at[2], partner()))
    attn_sum.relay()
    mlp_sum.narrow()
    attn_sum.spread()
    mlp_sum.finish(mlp_outs)
    attn_sum.narrow()
    attn_sum.finish(attn_outs)
    for copy in halves:
        copy.wait()


def backward(x, grad_hidden, branch, n1t, q, kv, probs, mixed, wq, wkv, wo, tables, data, result):
    rows, width = branch.shape
    third, wide = wq.shape[2], data[0].shape[-1]
    heads = (2, rows, third)
    weights = (2, width, third)
    half = (2, 128, width)
    return call(
        backward_kernel,
        (x, grad_hidden, branch, n1t, q, kv, probs, mixed, wq, wkv, wo, tables, *data, result),
        [ANY] * 11 + [VMEM] + [ANY] * 4,
        [shaped((2, 24, wide), F32)] * 3
        + [shaped((2, 24, third), F32)] * 3
        + [shaped((4, 4, 4, 48, third))] * 3
        + [shaped(half), shaped(half[1:], F32), shaped(half[1:])],
        [ANY] * 12,
        [
            pltpu.VMEM(half, BF),
            pltpu.VMEM((SEQ, width), F32),
            pltpu.VMEM((rows, width), BF),
            pltpu.VMEM((width, rows), BF),
            pltpu.VMEM((width, rows), BF),
            pltpu.VMEM(heads, BF),
            pltpu.VMEM(heads, BF),
            pltpu.VMEM((4, 4, SEQ, SEQ), BF),
            pltpu.VMEM(heads, BF),
            pltpu.VMEM(weights, BF),
            pltpu.VMEM(weights, BF),
            pltpu.VMEM(weights, BF),
            pltpu.VMEM(heads, BF),
            pltpu.VMEM(heads, BF),
            pltpu.VMEM(heads, BF),
            pltpu.VMEM((SEQ, width), BF),
            pltpu.VMEM((SEQ, width), F32),
            pltpu.VMEM((SEQ, width), BF),
            pltpu.VMEM(half, F32),
            pltpu.VMEM(half[1:], BF),
            pltpu.VMEM((2, 2, 4, 4, 48, third), BF),
            *Reduce.buffers(wide, PLANE_X),
            *Reduce.buffers(third, SPARE_X),
            *Reduce.semaphores,
            *Reduce.semaphores,
            pltpu.SemaphoreType.DMA((11,)),
            pltpu.SemaphoreType.DMA((4,)),
            pltpu.SemaphoreType.DMA((3,)),
            pltpu.SemaphoreType.DMA((3,)),
        ],
        "attn_backward_reduce",
        3,
    )


def tables_for(count, heads, plain):
    half = HEAD // 2
    inverse = np.float32(ROPE_BASE) ** (-(np.arange(half, dtype=np.float32) * np.float32(2.0)) / np.float32(HEAD))
    angle = np.arange(count, dtype=np.float32)[:, None] * inverse.astype(np.float32)[None, :]
    cosine, sine = np.cos(angle), np.sin(angle)
    cosine = np.tile(np.concatenate([cosine, cosine], -1), (1, heads))
    sine = np.tile(np.concatenate([-sine, sine], -1), (1, heads))
    cosine = np.concatenate([cosine, np.ones((count, plain), np.float32)], -1)
    sine = np.concatenate([sine, np.zeros((count, plain), np.float32)], -1)
    return np.stack([cosine, sine]).astype(np.float32)


def body(
    inputs,
    out_grad,
    lengths,
    query_weight,
    key_matrix,
    value_matrix,
    output_weight,
    gate_weight,
    up_weight,
    down_weight,
    attn_gain,
    mlp_gain,
):
    width = inputs.shape[2]
    gain_one = attn_gain.astype(F32)[:, None]
    gain_two = mlp_gain.astype(F32)[:, None]

    own_weights = (
        query_weight,
        key_matrix,
        value_matrix,
        output_weight.T,
        gate_weight,
        up_weight,
        down_weight.T,
    )
    query32, key32, value32, gate32, up32 = (
        w.astype(F32) for w in (query_weight, key_matrix, value_matrix, gate_weight, up_weight)
    )
    third, wide = query_weight.shape[1] // 2, gate_weight.shape[1] // 2
    tables = jnp.asarray(np.concatenate([tables_for(SEQ, 4, 0), tables_for(SEQ, 2, 2 * HEAD)]))

    results = forward(
        own_weights, jnp.stack([attn_gain, mlp_gain], 1), lengths, inputs, out_grad, tables, third, wide
    )
    two, one = results[:3], results[3:6]
    x, n1t, q, kv, probs, mixed, hidden, n2, n2t, cot, cott = results[6:17]
    (wq, wkv, wo), grads, acts = results[17:20], results[20:23], results[23:26]

    def joined(w):
        return w.reshape(2, width, -1)

    def blocked(w):
        return w.reshape(2, 4, 4, 48, -1)

    *one_sums, dg, du, dd, result, branch, grad_hidden = middle(
        n2, cot, hidden, n2t, cott, one, two, acts, [blocked(w) for w in grads]
    )
    *sums, _, _, _, result, in_grad, in_grad_theirs = backward(
        x,
        grad_hidden,
        branch,
        n1t,
        q,
        kv,
        probs,
        mixed,
        joined(wq),
        joined(wkv),
        joined(wo),
        tables,
        [blocked(w) for w in (dg, du, dd)],
        result.reshape(2, 128, width),
    )
    mine = jnp.arange(2)[:, None, None] == lax.axis_index("yl")
    in_grad = jnp.where(mine, in_grad[None], in_grad_theirs[None].astype(F32))
    mlp_sums = [jnp.concatenate(parts, -1) for parts in zip(one_sums, sums[:3])]
    attn_sums = sums[3:]

    def whole(part):
        return jnp.moveaxis(part, 0, 1).reshape(24, -1)

    key_size = key_matrix.shape[1] // 2
    dquery, doutput = whole(attn_sums[0]), whole(attn_sums[2])
    dkey, dvalue = whole(attn_sums[1][..., :key_size]), whole(attn_sums[1][..., key_size:])
    dgate, dup, ddown = (whole(part) for part in mlp_sums)
    gain_grads = jnp.stack(
        [
            sum(jnp.sum(w * g, -1) for w, g in ((query32, dquery), (key32, dkey), (value32, dvalue))),
            sum(jnp.sum(w * g, -1) for w, g in ((gate32, dgate), (up32, dup))),
        ]
    )
    gain_grads = lax.psum(gain_grads, "yl")
    return (
        result,
        in_grad,
        dquery * gain_one,
        dkey * gain_one,
        dvalue * gain_one,
        doutput.T,
        dgate * gain_two,
        dup * gain_two,
        ddown.T,
        gain_grads[0],
        gain_grads[1],
    )


def solution(mesh):
    fine = Mesh(mesh.devices.reshape(2, 4, 4, 2, 2), AXES)
    rows = P(None, AXES, None)
    into, out = P(DP, "yl"), P("yl", DP)
    return jax.shard_map(
        body,
        mesh=fine,
        in_specs=(rows, rows, P(None, DP), into, into, into, out, into, into, out, P(DP), P(DP)),
        out_specs=(rows, rows, into, into, into, out, into, into, out, P(DP), P(DP)),
        check_vma=False,
    )
```

```python
import math

import jax
import jax.numpy as jnp
import numpy as np
from jax import lax
from jax.experimental import pallas as pl
from jax.experimental.pallas import tpu as pltpu
from jax.sharding import Mesh
from jax.sharding import PartitionSpec as P

HEAD = 96
EPS = 1e-05
ROPE_BASE = 100000.0
AXES = ("yh", "x", "z", "core", "yl")
DP = ("yh", "x", "z", "core")
MESH = pl.DeviceIdType.MESH
BF = jnp.bfloat16
F32 = jnp.float32
EVEN = (("x", "y", "z"), ("y", "z", "x"), ("z", "x", "y"))
SPARE_Y = (("x", "z", "y"), ("y", "x", "z"), ("y", "z", "x"))
PLANE_Z = (("w", "x", "z"), ("w", "z", "x"), ("w", "x", "z"))
PLANE_X = (("w", "z", "x"), ("w", "x", "z"), ("w", "z", "x"))
SEQ = 256
ROWS = 512
STEP = 128
CHUNK = 256
VMEM_LIMIT = 62 * 1024 * 1024


def coordinates():
    x, z, yh, yl = (lax.axis_index(a) for a in ("x", "z", "yh", "yl"))
    return {"x": x, "z": z, "y": yh * 2 + yl, "w": yh}


def extent(axis):
    return 2 if axis == "w" else 4


def around(at, axis, by):
    return lax.rem(at[axis] + (by + 4), extent(axis))


def others(axis):
    return (1,) if axis == "w" else (1, -1, 2)


def peer(at, axis, by):
    value = around(at, axis, by)
    if axis == "y":
        return {"yh": value // 2, "yl": lax.rem(value, 2)}
    return {"yh" if axis == "w" else axis: value}


def sibling():
    return {"core": 1 - lax.axis_index("core")}


def partner():
    return {"yl": 1 - lax.axis_index("yl")}


def slot(at, axis, by=0):
    value = around(at, axis, by)
    return lax.rem(value, 2) * 2 + value // 2 if axis == "y" else value


def dimensions(order):
    return ("w" if "w" in order else "y", "x", "z")


def place(at, order, count, half=None, shifted=None):
    out = []
    for axis in dimensions(order):
        if axis in order[:count]:
            size = extent(axis)
            if half is not None and half[0] == axis:
                out.append(pl.ds(size // 2 * half[1], size // 2))
            else:
                out.append(pl.ds(0, size))
        else:
            out.append(slot(at, axis, shifted[1] if shifted is not None and shifted[0] == axis else 0))
    return tuple(out)


def greet(at):
    barrier = pltpu.get_barrier_semaphore()
    for axis in ("x", "y", "z"):
        for by in (1, -1, 2):
            pl.semaphore_signal(barrier, inc=1, device_id=peer(at, axis, by), device_id_type=MESH)
    pl.semaphore_signal(barrier, inc=1, device_id=sibling(), device_id_type=MESH)
    pl.semaphore_wait(barrier, 10)


def sent(src, dst, send, recv, device):
    copy = pltpu.make_async_remote_copy(
        src_ref=src, dst_ref=dst, send_sem=send, recv_sem=recv, device_id=device, device_id_type=MESH
    )
    copy.start()
    return copy


def moved(src, dst, sem):
    copy = pltpu.make_async_copy(src, dst, sem)
    copy.start()
    return copy


class Gather:
    semaphores = (
        pltpu.SemaphoreType.DMA((3,)),
        pltpu.SemaphoreType.DMA((3, 2, 3)),
        pltpu.SemaphoreType.DMA((3, 2, 3)),
        pltpu.SemaphoreType.DMA((3, 2, 2, 3)),
        pltpu.SemaphoreType.DMA((3, 2, 2, 3)),
    )

    def __init__(self, at, srcs, outs, semaphores, orders):
        self.at, self.srcs, self.outs, self.orders = at, srcs, outs, orders
        self.local, self.send, self.recv, self.ring_send, self.ring_recv = semaphores
        self.own, self.direct, self.ring = [], {}, {}

    def arrive(self, p, stage):
        for copy in self.direct.get((p, stage), ()):
            copy.wait_recv()
        if (p, stage, 0, 0) in self.ring:
            for d in range(2):
                self.ring[p, stage, d, 1 - d].wait_recv()
                self.ring[p, stage, d, 2].wait_recv()

    def to_all(self, stage):
        at = self.at
        for p, order in enumerate(self.orders):
            if stage:
                self.own[p].wait()
                self.arrive(p, 0)
            else:
                self.own.append(moved(self.srcs[p], self.outs[p].at[place(at, order, 0)], self.local.at[p]))
            group = self.outs[p].at[place(at, order, stage)]
            self.direct[p, stage] = [
                sent(
                    group if stage else self.srcs[p],
                    group,
                    self.send.at[p, stage, d],
                    self.recv.at[p, stage, d],
                    peer(at, order[stage], by),
                )
                for d, by in enumerate(others(order[stage]))
            ]

    def pass_on(self, p, stage, d, k, block):
        self.ring[p, stage, d, k] = sent(
            block,
            block,
            self.ring_send.at[p, stage - 1, d, k],
            self.ring_recv.at[p, stage - 1, d, k],
            peer(self.at, self.orders[p][stage], 1 - 2 * d),
        )

    def spread(self, stage, *pieces):
        for p in pieces or range(3):
            order = self.orders[p]
            if stage == 1:
                self.own[p].wait()
            self.arrive(p, stage - 1)
            for t in range(2):
                for d in range(2):
                    h = t if d == 0 else 1 - t
                    self.pass_on(p, stage, d, h, self.outs[p].at[place(self.at, order, stage, (order[0], h))])

    def forward(self, stage):
        for p, order in enumerate(self.orders):
            for d, by in enumerate((1, -1)):
                self.ring[p, stage, d, d].wait_recv()
                where = place(self.at, order, stage, (order[0], d), (order[stage], -by))
                self.pass_on(p, stage, d, 2, self.outs[p].at[where])

    def finish(self):
        for copies in self.direct.values():
            for copy in copies:
                copy.wait_send()
        for copy in self.ring.values():
            copy.wait_send()


class Reduce:
    semaphores = (
        pltpu.SemaphoreType.DMA((3, 3)),
        pltpu.SemaphoreType.DMA((3, 2, 3)),
        pltpu.SemaphoreType.DMA((3, 2, 3)),
        pltpu.SemaphoreType.DMA((3, 2, 3)),
        pltpu.SemaphoreType.DMA((3, 2, 3)),
        pltpu.SemaphoreType.DMA((3, 2)),
        pltpu.SemaphoreType.DMA((3, 2)),
    )

    @staticmethod
    def buffers(columns, orders):
        def per_piece(*shape):
            return [pltpu.VMEM(shape + (48, columns), BF) for _ in range(3)]

        size = extent(dimensions(orders[0])[0])
        return [
            *per_piece(2, size // 2, 4),
            *per_piece(size, 4),
            *per_piece(2, size // 2, 4),
            *per_piece(2, size, 4),
            *per_piece(3, size),
            *per_piece(3),
            *[pltpu.VMEM((48, columns), F32) for _ in range(3)],
        ]

    def __init__(self, at, data, buffers, semaphores, orders):
        self.at, self.data, self.orders = at, data, orders
        self.side, self.kept, self.far, self.near, self.second, self.third, self.sums = (
            buffers[3 * k : 3 * k + 3] for k in range(7)
        )
        self.load, self.first_send, self.first_recv, self.send, self.recv, self.end_send, self.end_recv = semaphores
        self.loads, self.copies = {}, {}

    def left(self, p):
        order = self.orders[p]
        return [axis for axis in dimensions(order) if axis != order[2]]

    def inside(self, p, first, second=None):
        whole = slice(None) if second is None else second
        return (first, whole) if self.left(p)[0] == self.orders[p][1] else (whole, first)

    def start(self, *pieces):
        at, s, r = self.at, self.first_send, self.first_recv
        for p in pieces or range(3):
            order = self.orders[p]
            axis, cut = order[2], self.left(p)[0]
            size = extent(cut) // 2
            for d, by in enumerate((1, -1)):
                block = self.data[p].at[place(at, order, 2, (cut, d), (axis, 2))]
                self.copies[p, d, 0] = sent(block, self.far[p].at[d], s.at[p, d, 0], r.at[p, d, 0], peer(at, axis, by))
            for d, by in enumerate((1, -1)):
                h = 1 - d
                block = self.data[p].at[place(at, order, 2, (cut, h), (axis, by))]
                self.copies[p, d, 1] = sent(
                    block, self.near[p].at[d, pl.ds(size * h, size)], s.at[p, d, 1], r.at[p, d, 1], peer(at, axis, by)
                )
                block = self.data[p].at[place(at, order, 2, (cut, d), (axis, by))]
                self.loads[p, d] = moved(block, self.side[p].at[d], self.load.at[p, d])
            self.loads[p, 2] = moved(self.data[p].at[place(at, order, 2)], self.kept[p], self.load.at[p, 2])

    def relay(self):
        for p, order in enumerate(self.orders):
            size = extent(self.left(p)[0]) // 2
            for d, by in enumerate((1, -1)):
                self.loads[p, d].wait()
                self.copies[p, d, 0].wait_recv()
                side, far = self.side[p], self.far[p]

                @pl.loop(0, 4 * size)
                def _(i, d=d, side=side, far=far):
                    a, b = i // 4, lax.rem(i, 4)
                    side[d, a, b] = (side[d, a, b].astype(F32) + far[d, a, b].astype(F32)).astype(BF)

                self.copies[p, d, 2] = sent(
                    side.at[d],
                    self.near[p].at[d, pl.ds(size * d, size)],
                    self.first_send.at[p, d, 2],
                    self.first_recv.at[p, d, 2],
                    peer(self.at, order[2], by),
                )

    def spread(self):
        at = self.at
        for p, order in enumerate(self.orders):
            self.loads[p, 2].wait()
            for d in range(2):
                self.copies[p, d, 1].wait_recv()
                self.copies[p, d, 2].wait_recv()
            kept, near = self.kept[p], self.near[p]

            @pl.loop(0, 4 * extent(self.left(p)[0]))
            def _(i, kept=kept, near=near):
                a, b = i // 4, lax.rem(i, 4)
                total = kept[a, b].astype(F32) + near[0, a, b].astype(F32) + near[1, a, b].astype(F32)
                kept[a, b] = total.astype(BF)

            for d, by in enumerate(others(order[1])):
                block = kept.at[self.inside(p, slot(at, order[1], by))]
                self.copies[p, "b", d] = sent(
                    block, self.second[p].at[d], self.send.at[p, 0, d], self.recv.at[p, 0, d], peer(at, order[1], by)
                )

    def narrow(self):
        at = self.at
        for p, order in enumerate(self.orders):
            for d in range(len(others(order[1]))):
                self.copies[p, "b", d].wait_recv()
            kept, second, mine = self.kept[p], self.second[p], slot(at, order[1])

            @pl.loop(0, extent(order[0]))
            def _(i, p=p, kept=kept, second=second, mine=mine):
                total = kept[self.inside(p, mine, i)].astype(F32)
                for d in range(3):
                    total = total + second[d, i].astype(F32)
                kept[self.inside(p, mine, i)] = total.astype(BF)

            for d, by in enumerate(others(order[0])):
                block = kept.at[self.inside(p, mine, slot(at, order[0], by))]
                self.copies[p, "c", d] = sent(
                    block, self.third[p].at[d], self.send.at[p, 1, d], self.recv.at[p, 1, d], peer(at, order[0], by)
                )

    def finish(self, outs):
        at, core, ends = self.at, lax.axis_index("core"), []
        for p, order in enumerate(self.orders):
            total = self.kept[p][self.inside(p, slot(at, order[1]), slot(at, order[0]))].astype(F32)
            for d in range(len(others(order[0]))):
                self.copies[p, "c", d].wait_recv()
                total = total + self.third[p][d].astype(F32)
            self.sums[p][...] = total
            theirs = self.sums[p].at[pl.ds(pl.multiple_of(24 * (1 - core), 8), 24)]
            mine = self.sums[p].at[pl.ds(pl.multiple_of(24 * core, 8), 24)]
            ends.append(sent(theirs, outs[p].at[core], self.end_send.at[p, 0], self.end_recv.at[p, 0], sibling()))
            ends.append(moved(mine, outs[p].at[core], self.end_send.at[p, 1]))
        for copy in self.copies.values():
            copy.wait_send()
        for copy in ends:
            copy.wait()


def nn(left, right):
    return lax.dot_general(left, right, (((1,), (0,)), ((), ())), preferred_element_type=F32)


def nt(left, right):
    return lax.dot_general(left, right, (((1,), (1,)), ((), ())), preferred_element_type=F32)


def tn(left, right):
    return lax.dot_general(left, right, (((0,), (0,)), ((), ())), preferred_element_type=F32)


def inverse_rms(values):
    return lax.rsqrt(jnp.mean(values * values, -1, keepdims=True) + EPS)


def swap(values, first):
    width = values.shape[-1]
    return jnp.where(first, pltpu.roll(values, width - HEAD // 2, 1), pltpu.roll(values, HEAD // 2, 1))


def first_half(shape):
    return lax.rem(lax.broadcasted_iota(jnp.int32, shape, 1), HEAD) < HEAD // 2


def rows_at(start, size):
    return pl.ds(pl.multiple_of(start, size), size)


ANY = pl.BlockSpec(memory_space=pl.ANY)
VMEM = pl.BlockSpec(memory_space=pltpu.VMEM)


def shaped(shape, kind=BF):
    return jax.ShapeDtypeStruct(shape, kind)


def call(kernel, operands, in_specs, results, out_specs, scratch, name, collective_id, **more):
    return pl.pallas_call(
        kernel,
        out_shape=results,
        in_specs=in_specs,
        out_specs=out_specs,
        scratch_shapes=scratch,
        compiler_params=pltpu.CompilerParams(
            collective_id=collective_id, has_side_effects=True, vmem_limit_bytes=VMEM_LIMIT
        ),
        name=name,
        **more,
    )(*operands)


def hidden_units(m, sub, n2, cot, weights, acts):
    rows = rows_at(m * ROWS, ROWS)
    columns = pl.ds(sub * CHUNK, CHUNK)
    gate_w, up_w, down_w = (w[..., columns].reshape(-1, CHUNK) for w in weights)
    gate = nn(n2[rows], gate_w)
    up = nn(n2[rows], up_w)
    sigma = 0.5 + 0.5 * jnp.tanh(0.5 * gate)
    silu = gate * sigma
    grad_active = nn(cot[m].reshape(ROWS, -1), down_w)
    acts[0][rows, columns] = (silu * up).astype(BF)
    acts[1][rows, columns] = (grad_active * up * (sigma + silu * (1.0 - sigma))).astype(BF)
    acts[2][rows, columns] = (grad_active * silu).astype(BF)


def unit_gradients(n2t, cott, acts, staging, outs, sems):
    waits = {}
    for k, (left, right, target) in enumerate(((n2t, acts[1], 0), (n2t, acts[2], 1), (cott, acts[0], 2))):
        for sub in range(2):
            columns = pl.ds(sub * CHUNK, CHUNK)
            place_in = (2 * k + sub) % 4
            if place_in in waits:
                waits[place_in].wait()
            staging[place_in] = nn(left[...], right[:, columns]).astype(BF)
            waits[place_in] = moved(staging.at[place_in], outs[target].at[:, columns], sems.at[place_in])
    return list(waits.values())


def forward_kernel(third, wide, *refs):
    own_weights, gains, lengths, xin, gin, tables = refs[:7], *refs[7:12]
    full_two, full_one = refs[12:15], refs[15:18]
    (
        x_out, n1t_out, q_out, kv_out, probs_out, mixed_out, hidden_out, n2_out, n2t_out, cot_out, cott_out,
    ) = refs[18:29]
    attn_out, grads_out, acts_out = refs[29:32], refs[32:35], refs[35:38]
    (
        shard, got_shard, packed, xs, gs, normed, q, kv, probs, mixed, hidden, n2, n2t, cott, part, arrived, n1t,
        valid, staging,
    ) = refs[38:57]
    full_attn, weights, acts = refs[57:60], refs[60:63], refs[63:66]
    attn_sems, one_sems, two_sems = refs[66:71], refs[71:76], refs[76:81]
    pair_send, pair_recv, row_send, row_recv, far_send, far_recv, own_sem, out_sem, put_sem = refs[81:]
    at = coordinates()
    core, yl = lax.axis_index("core"), lax.axis_index("yl")
    own_x = moved(xin.at[yl], xs.at[core, yl], own_sem.at[0])
    own_g = moved(gin, gs.at[:, core, yl], own_sem.at[1])

    query, key, value, output, *mlp_weights = (ref[...].astype(F32) for ref in own_weights)
    gain_one, gain_two = gains[:, 0:1].astype(F32), gains[:, 1:2].astype(F32)
    small = key.shape[1] // 2
    for c in range(2):
        thin = slice(c * small, (c + 1) * small)
        parts = [
            query[:, c * third : (c + 1) * third] * gain_one,
            jnp.concatenate([key[:, thin] * gain_one, value[:, thin] * gain_one], -1),
            output[:, c * third : (c + 1) * third],
            *(
                w[:, c * wide : (c + 1) * wide] * g
                for w, g in zip(mlp_weights, (gain_two, gain_two, jnp.ones_like(gain_two)))
            ),
        ]
        column = 0
        for part_value in parts:
            shard[c, :24, column : column + part_value.shape[1]] = part_value
            column += part_value.shape[1]
        lane = lax.broadcasted_iota(jnp.int32, (8, 2 * SEQ), 1)
        ends = jnp.where(lane < SEQ, lengths[0, 0], lengths[1, 0] + SEQ)
        shard[c, 24:, : 2 * SEQ] = jnp.where(lane < ends, 1.0, 0.0)
    greet(at)
    swap_shard = sent(shard.at[1 - core], got_shard, pair_send.at[0], pair_recv.at[0], sibling())

    rows = {}

    def exchange(k):
        ours, theirs, dst = (
            (xin.at[yl], xin.at[1 - yl], xs.at[core, yl]),
            (gin, gin, gs.at[:, core, yl]),
        )[k]
        rows[k, 0] = sent(theirs, dst, row_send.at[k, 0], row_recv.at[k, 0], partner())
        rows[k, 1] = sent(ours, dst, row_send.at[k, 1], row_recv.at[k, 1], sibling())

    def share(k):
        block = (xs.at[core, 1 - yl], gs.at[:, core, 1 - yl])[k]
        rows[k, 0].wait_recv()
        rows[k, 2] = sent(block, block, row_send.at[k, 2], row_recv.at[k, 2], sibling())

    def settle(k):
        (own_x, own_g)[k].wait()
        rows[k, 0].wait_send()
        rows[k, 1].wait()
        rows[k, 2].wait()

    swap_shard.wait()
    low, high = shard[core], got_shard[...]
    first, last = jnp.where(core == 0, low, high), jnp.where(core == 0, high, low)
    packed[...] = jnp.concatenate([first[:24], last[:24]], 0).astype(BF)
    for c, rows_of in enumerate((first, last)):
        for m in range(2):
            valid[m, c] = rows_of[24:32, m * SEQ : (m + 1) * SEQ]

    def pieces(start, size, step):
        return [packed.at[:, pl.ds(start + k * step, size)] for k in range(3)]

    half = wide // 2
    attn = Gather(at, pieces(0, third, third), full_attn, attn_sems, EVEN)
    one = Gather(at, pieces(3 * third, half, wide), weights, one_sems, PLANE_Z)
    two = Gather(at, pieces(3 * third + half, half, wide), full_two, two_sems, PLANE_X)
    attn.to_all(0)
    one.to_all(0)
    two.to_all(0)
    attn.to_all(1)
    one.spread(1)
    attn.spread(2, 0, 1)
    exchange(0)
    attn.spread(2, 2)
    one.forward(1)
    two.spread(1)
    attn.forward(2)
    two.forward(1)
    one.spread(2)
    share(0)
    settle(0)
    exchange(1)
    outs = [moved(xs, x_out, out_sem.at[0])]

    @pl.loop(0, ROWS // STEP)
    def _(i):
        block = rows_at(i * STEP, STEP)
        values = xs[i // 2, lax.rem(i, 2)].astype(F32)
        normed[block] = (values * inverse_rms(values)).astype(BF)

    for p in range(2):
        attn.arrive(p, 2)
    two.spread(2)
    wq, wkv, wo = full_attn

    def weight(ref, y):
        return ref[pl.ds(2 * y, 2)].reshape(-1, third)

    @pl.loop(0, 2)
    def _(y):
        @pl.loop(0, ROWS // SEQ)
        def _(n):
            block = rows_at(n * SEQ, SEQ)
            left = normed[block]
            is_first = first_half((SEQ, third))
            for k, (w, result) in enumerate(((wq, q), (wkv, kv))):
                lin = nn(left, weight(w, y))
                result[y, block] = (lin * tables[2 * k] + swap(lin, is_first) * tables[2 * k + 1]).astype(BF)

    outs.append(moved(q, q_out, out_sem.at[5]))
    outs.append(moved(kv, kv_out, out_sem.at[6]))
    one.forward(2)
    scale = 1.0 / math.sqrt(HEAD)

    @pl.loop(0, 4)
    def _(i):
        y, n = i // 2, lax.rem(i, 2)
        block = rows_at(n * SEQ, SEQ)
        t = lax.broadcasted_iota(jnp.int32, (SEQ, SEQ), 0)
        s = lax.broadcasted_iota(jnp.int32, (SEQ, SEQ), 1)
        keep = (s <= t) & (valid[yl, n, 0:1, :] > 0.5)
        queries, keys = q[y, block], kv[y, block]
        results = []
        for h in range(4):
            g = h // 2
            scores = nt(queries[:, h * HEAD : (h + 1) * HEAD], keys[:, g * HEAD : (g + 1) * HEAD]) * scale
            scores = jnp.where(keep, scores, -1e30)
            terms = jnp.exp(scores - jnp.max(scores, -1, keepdims=True))
            low_probs = (terms * (1.0 / jnp.sum(terms, -1, keepdims=True))).astype(BF)
            probs[i, h] = low_probs
            results.append(nn(low_probs, keys[:, (2 + g) * HEAD : (3 + g) * HEAD]))
        mixed[y, block] = jnp.concatenate(results, -1).astype(BF)

    outs.append(moved(probs, probs_out, out_sem.at[7]))
    outs.append(moved(mixed, mixed_out, out_sem.at[8]))
    two.forward(2)

    attn.arrive(2, 2)
    copies = []
    for i in range(ROWS // STEP):
        block = rows_at(lax.rem(2 * (1 - core) + i, 4) * STEP, STEP)
        part[block] = (nt(mixed[0, block], weight(wo, 0)) + nt(mixed[1, block], weight(wo, 1))).astype(BF)
        copies.append(sent(part.at[block], arrived.at[block], pair_send.at[1 + i], pair_recv.at[1 + i], sibling()))
    second_rows = {}
    mine, theirs = yl * ROWS, (1 - yl) * ROWS
    for i in range(ROWS // STEP):
        copies[(i + 2) % 4 if i < 2 else i - 2].wait_send()
        copies[i].wait_recv()
        number = lax.rem(2 * core + i, 4)
        block = rows_at(number * STEP, STEP)
        values = xs[number // 2, lax.rem(number, 2)].astype(F32) + (
            part[block].astype(F32) + arrived[block].astype(F32)
        )
        hidden[block] = values
        target = rows_at(mine + number * STEP, STEP)
        n2[target] = (values * inverse_rms(values)).astype(BF)
        if i < 2:
            second_rows[0, i] = sent(n2.at[target], n2.at[target], far_send.at[0, i], far_recv.at[0, i], partner())
    outs.append(moved(hidden.at[rows_at(core * SEQ, SEQ)], hidden_out, out_sem.at[9]))
    attn.finish()
    outs.extend(moved(full_attn[p], attn_out[p], out_sem.at[2 + p]) for p in range(3))
    share(1)
    settle(1)

    for m in range(2):
        for c in range(2):
            for h in range(2):
                mask = valid[m, c][:, h * STEP : (h + 1) * STEP].T[:, 0:1]
                gs[m, c, h] = (gs[m, c, h].astype(F32) * mask).astype(BF)
    outs.append(moved(gs, cot_out, out_sem.at[10]))

    for p in range(3):
        one.arrive(p, 2)
    one.finish()
    outs.extend(moved(weights[p], full_one[p], out_sem.at[11 + p]) for p in range(3))
    for sub in range(2):
        hidden_units(yl, sub, n2, gs, weights, acts)
    for m in range(2):
        for c in range(2):
            for h in range(2):
                cott[:, pl.ds(m * ROWS + (2 * c + h) * STEP, STEP)] = gs[m, c, h].T
    outs.append(moved(cott, cott_out, out_sem.at[14]))
    for i in range(ROWS // STEP):
        block = rows_at(mine + i * STEP, STEP)
        n2t[:, block] = n2[block].T
    n1t[...] = normed[...].T
    outs.append(moved(n1t, n1t_out, out_sem.at[1]))
    for i in range(2):
        second_rows[0, i].wait_recv()
        block = rows_at(theirs + (2 * core + i) * STEP, STEP)
        second_rows[1, i] = sent(n2.at[block], n2.at[block], far_send.at[1, i], far_recv.at[1, i], sibling())
    for i in range(2):
        second_rows[0, i].wait_send()
        second_rows[1, i].wait()
    for sub in range(2):
        hidden_units(1 - yl, sub, n2, gs, weights, acts)
    outs.extend(moved(acts[p], acts_out[p], out_sem.at[15 + p]) for p in range(3))
    outs.append(moved(n2, n2_out, out_sem.at[18]))
    for i in range(ROWS // STEP):
        block = rows_at(theirs + i * STEP, STEP)
        n2t[:, block] = n2[block].T
    outs.append(moved(n2t, n2t_out, out_sem.at[19]))
    outs.extend(unit_gradients(n2t, cott, acts, staging, grads_out, put_sem))
    for p in range(3):
        two.arrive(p, 2)
    two.finish()
    for copy in outs:
        copy.wait()


def forward(own_weights, gains, lengths, xin, gin, tables, third, wide):
    width = xin.shape[2]
    rows = (ROWS, width)
    both = (2 * ROWS, width)
    heads = (2, ROWS, third)
    square = (4, 4, SEQ, SEQ)
    half = wide // 2
    piece = (2, 4, 4, 48, half)
    return call(
        lambda *refs: forward_kernel(third, wide, *refs),
        (*own_weights, gains, lengths, xin, gin, tables),
        [VMEM] * 8 + [pl.BlockSpec(memory_space=pltpu.SMEM), ANY, ANY, VMEM],
        [shaped(piece)] * 6
        + [
            shaped((2, 2, 128, width)),
            shaped(rows[::-1]),
            shaped(heads),
            shaped(heads),
            shaped(square),
            shaped(heads),
            shaped((SEQ, width), F32),
            shaped(both),
            shaped(both[::-1]),
            shaped((2, 2, 2, 128, width)),
            shaped(both[::-1]),
        ]
        + [shaped((4, 4, 4, 48, third))] * 3
        + [shaped((width, half))] * 3
        + [shaped((2 * ROWS, half))] * 3,
        [ANY] * 26,
        [
            pltpu.VMEM((2, 32, 3 * third + 3 * wide), F32),
            pltpu.VMEM((32, 3 * third + 3 * wide), F32),
            pltpu.VMEM((48, 3 * third + 3 * wide), BF),
            pltpu.VMEM((2, 2, 128, width), BF),
            pltpu.VMEM((2, 2, 2, 128, width), BF),
            pltpu.VMEM(rows, BF),
            pltpu.VMEM(heads, BF),
            pltpu.VMEM(heads, BF),
            pltpu.VMEM(square, BF),
            pltpu.VMEM(heads, BF),
            pltpu.VMEM(rows, F32),
            pltpu.VMEM(both, BF),
            pltpu.VMEM(both[::-1], BF),
            pltpu.VMEM(both[::-1], BF),
            pltpu.VMEM(rows, BF),
            pltpu.VMEM(rows, BF),
            pltpu.VMEM(rows[::-1], BF),
            pltpu.VMEM((2, 2, 8, SEQ), F32),
            pltpu.VMEM((4, width, CHUNK), BF),
            *[pltpu.VMEM((4, 4, 4, 48, third), BF) for _ in range(3)],
            *[pltpu.VMEM(piece, BF) for _ in range(3)],
            *[pltpu.VMEM((2 * ROWS, half), BF) for _ in range(3)],
            *Gather.semaphores,
            *Gather.semaphores,
            *Gather.semaphores,
            pltpu.SemaphoreType.DMA((5,)),
            pltpu.SemaphoreType.DMA((5,)),
            pltpu.SemaphoreType.DMA((2, 3)),
            pltpu.SemaphoreType.DMA((2, 3)),
            pltpu.SemaphoreType.DMA((2, 2)),
            pltpu.SemaphoreType.DMA((2, 2)),
            pltpu.SemaphoreType.DMA((2,)),
            pltpu.SemaphoreType.DMA((20,)),
            pltpu.SemaphoreType.DMA((4,)),
        ],
        "gather_attn_forward_mlp",
        1,
    )


def middle_kernel(*refs):
    n2_in, cot_in, hidden_in, n2t_in, cott_in = refs[:5]
    one_in, two_in, acts_in, data = refs[5:8], refs[8:11], refs[11:14], refs[14:17]
    sums_out, grads_out = refs[17:20], refs[20:23]
    kept_out, away_out, branch_out, grad_hidden_out = refs[23:27]
    (
        n2, cot, hidden, n2t, cott, staging, to_pair, from_pair, whole, from_far, keep, halves, to_far, branch, gh,
    ) = refs[27:42]
    one, two, acts_one, acts_two = refs[42:45], refs[45:48], refs[48:51], refs[51:54]
    buffers, reduce_sems = refs[54:75], refs[75:82]
    load, put, put_sem, pair_send, pair_recv, far_send, far_recv = refs[82:]
    core, yl = lax.axis_index("core"), lax.axis_index("yl")
    at = coordinates()
    order = (
        (n2_in, n2),
        (two_in[0], two[0]),
        (two_in[1], two[1]),
        (cot_in, cot),
        (two_in[2], two[2]),
        *zip(acts_in[1:], acts_one[1:]),
        *zip(one_in[:2], one[:2]),
        (acts_in[0], acts_one[0]),
        (one_in[2], one[2]),
        (n2t_in, n2t),
        (cott_in, cott),
        (hidden_in, hidden),
    )
    loads = [moved(src, dst, load.at[k]) for k, (src, dst) in enumerate(order)]
    greet(at)
    total = Reduce(at, data, buffers, reduce_sems, PLANE_Z)
    total.start()
    for k in range(5):
        loads[k].wait()
    for sub in range(2):
        hidden_units(1 - yl, sub, n2, cot, two, acts_two)
    for k in range(5, 11):
        loads[k].wait()

    def weight(ref):
        return ref[...].reshape(n2.shape[1], -1)

    def grad_rows(m, c):
        rows = rows_at(m * ROWS + c * SEQ, SEQ)
        return (nt(acts_one[1][rows], weight(one[0])) + nt(acts_one[2][rows], weight(one[1]))) + (
            nt(acts_two[1][rows], weight(two[0])) + nt(acts_two[2][rows], weight(two[1]))
        )

    def out_rows(m, c):
        rows = rows_at(m * ROWS + c * SEQ, SEQ)
        return nt(acts_one[0][rows], weight(one[2])) + nt(acts_two[0][rows], weight(two[2]))

    pair, far = {}, {}

    def to_sibling(k, value):
        to_pair[k] = value.astype(BF)
        pair[k] = sent(to_pair.at[k], from_pair.at[k], pair_send.at[k], pair_recv.at[k], sibling())

    def to_partner(k, value):
        pair[k].wait_recv()
        whole[...] = (value + from_pair[k].astype(F32)).astype(BF)
        far[k] = sent(whole, from_far, far_send, far_recv, partner())

    to_sibling(0, grad_rows(1 - yl, 1 - core))
    to_partner(0, grad_rows(1 - yl, core))
    total.relay()
    for sub in range(2):
        hidden_units(yl, sub, n2, cot, two, acts_two)
    to_sibling(1, grad_rows(yl, 1 - core))
    keep[...] = grad_rows(yl, core)
    to_sibling(2, out_rows(1 - yl, 1 - core))
    to_sibling(3, out_rows(yl, 1 - core))
    for k in range(11, 14):
        loads[k].wait()
    outs = unit_gradients(n2t, cott, acts_two, staging, grads_out, put_sem)
    total.spread()

    for k, m in ((2, 1 - yl), (3, yl)):
        pair[k].wait_recv()
        value = out_rows(m, core) + from_pair[k].astype(F32)
        if k == 3:
            value = value + hidden[...]
        halves[k - 2] = value.reshape(2, STEP, -1)
        to_far[k - 2] = halves[k - 2, 1 - yl].astype(BF)
        outs.append(moved(halves.at[k - 2, yl], kept_out.at[k - 2], put.at[k]))
        outs.append(moved(to_far.at[k - 2], away_out.at[k - 2], put.at[k + 2]))
    pair[1].wait_recv()
    far[0].wait_recv()

    @pl.loop(0, SEQ // STEP)
    def _(i):
        rows = rows_at(i * STEP, STEP)
        grad = keep[rows] + (from_pair[1, rows].astype(F32) + from_far[rows].astype(F32))
        values = hidden[rows]
        inverse = inverse_rms(values)
        unit = values * inverse
        back = inverse * (grad - unit * jnp.mean(grad * unit, -1, keepdims=True))
        gh[rows] = cot[yl, core, i].astype(F32) + back
        branch[rows] = gh[rows].astype(BF)

    own = rows_at(core * SEQ, SEQ)
    shared = sent(branch, branch_out.at[own], pair_send.at[4], pair_recv.at[4], sibling())
    outs.extend((moved(branch, branch_out.at[own], put.at[0]), moved(gh, grad_hidden_out, put.at[1])))
    total.narrow()
    total.finish(sums_out)
    shared.wait()
    for copy in (*pair.values(), *far.values()):
        copy.wait_send()
    for copy in outs:
        copy.wait()


def middle(n2, cot, hidden, n2t, cott, one, two, acts, data):
    rows, width = n2.shape
    half = one[0].shape[-1]
    block = (SEQ, width)
    return call(
        middle_kernel,
        (n2, cot, hidden, n2t, cott, *one, *two, *acts, *data),
        [ANY] * 17,
        [shaped((2, 24, half), F32)] * 3
        + [shaped((width, half))] * 3
        + [
            shaped((2, STEP, width), F32),
            shaped((2, STEP, width)),
            shaped((ROWS, width)),
            shaped(block, F32),
        ],
        [ANY] * 10,
        [
            pltpu.VMEM((rows, width), BF),
            pltpu.VMEM(cot.shape, BF),
            pltpu.VMEM(block, F32),
            pltpu.VMEM((width, rows), BF),
            pltpu.VMEM((width, rows), BF),
            pltpu.VMEM((4, width, CHUNK), BF),
            pltpu.VMEM((4,) + block, BF),
            pltpu.VMEM((4,) + block, BF),
            pltpu.VMEM(block, BF),
            pltpu.VMEM(block, BF),
            pltpu.VMEM(block, F32),
            pltpu.VMEM((2, 2, STEP, width), F32),
            pltpu.VMEM((2, STEP, width), BF),
            pltpu.VMEM(block, BF),
            pltpu.VMEM(block, F32),
            *[pltpu.VMEM(one[0].shape, BF) for _ in range(6)],
            *[pltpu.VMEM((rows, half), BF) for _ in range(6)],
            *Reduce.buffers(half, PLANE_Z),
            *Reduce.semaphores,
            pltpu.SemaphoreType.DMA((14,)),
            pltpu.SemaphoreType.DMA((6,)),
            pltpu.SemaphoreType.DMA((4,)),
            pltpu.SemaphoreType.DMA((5,)),
            pltpu.SemaphoreType.DMA((5,)),
            pltpu.SemaphoreType.DMA,
            pltpu.SemaphoreType.DMA,
        ],
        "mlp_reduce",
        2,
    )


def backward_kernel(*refs):
    xall, grad_hidden_in, branch_in, n1t_in, q_in, kv_in, probs_in, mixed_in, wq_in, wkv_in, wo_in, tables = refs[:12]
    data, kept_in, away = refs[12:15], refs[15], refs[16]
    mlp_outs, attn_outs, result_out, in_grad_out, from_partner = refs[17:20], refs[20:23], *refs[23:26]
    (
        xs, gh, branch, branch_t, normed_t, q, kv, probs, mixed, wq, wkv, wo,
        grad_mixed, dq, dkv, part, keep_part, arrived, in_grad, for_partner, kept, others_half, result,
    ) = refs[26:49]
    attn_grads = refs[49:52]
    mlp_buffers, attn_buffers = refs[52:73], refs[73:94]
    mlp_sems, attn_sems = refs[94:101], refs[101:108]
    load, put, send, recv = refs[108:]
    at = coordinates()
    core, yl = lax.axis_index("core"), lax.axis_index("yl")
    loads = [
        moved(src, dst, load.at[k])
        for k, (src, dst) in enumerate(
            (
                (branch_in, branch),
                (wo_in, wo),
                (mixed_in, mixed),
                (q_in, q),
                (kv_in, kv),
                (probs_in, probs),
                (n1t_in, normed_t),
                (wq_in, wq),
                (wkv_in, wkv),
                (grad_hidden_in, gh),
                (xall.at[core], xs),
                (kept_in, kept),
            )
        )
    ]
    greet(at)
    mlp_sum = Reduce(at, data, mlp_buffers, mlp_sems, PLANE_X)
    attn_sum = Reduce(at, attn_grads, attn_buffers, attn_sems, SPARE_Y)
    mlp_sum.start()
    finals = [sent(away.at[k], others_half.at[k], send.at[2 + k], recv.at[2 + k], partner()) for k in range(2)]
    for k in range(2):
        loads[k].wait()
    for y in range(2):
        grad_mixed[y] = nn(branch[...], wo[y]).astype(BF)
    for k in range(2, 6):
        loads[k].wait()
    scale = 1.0 / math.sqrt(HEAD)

    @pl.loop(0, 4)
    def _(i):
        y, n = i // 2, lax.rem(i, 2)
        rows = rows_at(n * SEQ, SEQ)
        queries, keys, grads = q[y, rows], kv[y, rows], grad_mixed[y, rows]
        grad_q, grad_k, grad_v = [], [None, None], [None, None]
        for h in range(4):
            g = h // 2
            key = keys[:, g * HEAD : (g + 1) * HEAD]
            value = keys[:, (2 + g) * HEAD : (3 + g) * HEAD]
            query = queries[:, h * HEAD : (h + 1) * HEAD]
            grad = grads[:, h * HEAD : (h + 1) * HEAD]
            low = probs[i, h]
            prob = low.astype(F32)
            grad_probs = nt(grad, value)
            grad_scores = (prob * (grad_probs - jnp.sum(grad_probs * prob, -1, keepdims=True))).astype(BF)
            grad_q.append(nn(grad_scores, key) * scale)
            back_k = tn(grad_scores, query) * scale
            back_v = tn(low, grad)
            grad_k[g] = back_k if grad_k[g] is None else grad_k[g] + back_k
            grad_v[g] = back_v if grad_v[g] is None else grad_v[g] + back_v
        first = first_half((SEQ, 4 * HEAD))
        for k, (pieces, target) in enumerate(((grad_q, dq), (grad_k + grad_v, dkv))):
            values = jnp.concatenate(pieces, -1)
            target[y, rows] = (values * tables[2 * k] - swap(values, first) * tables[2 * k + 1]).astype(BF)

    loads[6].wait()

    def weight_grad(p, left, right):
        for y in range(2):
            target = attn_grads[p].at[pl.ds(2 * y, 2)]
            target[...] = nn(left[...], right[y]).astype(BF).reshape(target.shape)
        attn_sum.start(p)

    weight_grad(0, normed_t, dq)
    weight_grad(1, normed_t, dkv)
    mlp_sum.relay()
    branch_t[...] = branch[...].T
    weight_grad(2, branch_t, mixed)
    for k in range(7, 12):
        loads[k].wait()

    def back(start):
        rows = rows_at(start, SEQ)
        return (nt(dq[0, rows], wq[0]) + nt(dq[1, rows], wq[1])) + (nt(dkv[0, rows], wkv[0]) + nt(dkv[1, rows], wkv[1]))

    part[...] = back((1 - core) * SEQ).astype(BF)
    pair = sent(part, arrived, send.at[0], recv.at[0], sibling())
    attn_sum.relay()
    keep_part[...] = back(core * SEQ)
    mlp_sum.spread()
    pair.wait()

    @pl.loop(0, SEQ // STEP)
    def _(i):
        rows = rows_at(i * STEP, STEP)
        grad = keep_part[rows] + arrived[rows].astype(F32)
        values = xs[i].astype(F32)
        inverse = inverse_rms(values)
        unit = values * inverse
        change = inverse * (grad - unit * jnp.mean(grad * unit, -1, keepdims=True))
        in_grad[i] = gh[rows] + change

    for_partner[...] = in_grad[1 - yl].astype(BF)
    ends = [
        moved(in_grad.at[yl], in_grad_out, put.at[0]),
        sent(for_partner, from_partner, send.at[1], recv.at[1], partner()),
    ]
    mlp_sum.narrow()
    attn_sum.spread()
    for copy in finals:
        copy.wait()
    result[1 - yl] = (kept[0] + others_half[1].astype(F32)).astype(BF)
    result[yl] = (kept[1] + others_half[0].astype(F32)).astype(BF)
    ends.append(moved(result, result_out, put.at[1]))
    mlp_sum.finish(mlp_outs)
    attn_sum.narrow()
    attn_sum.finish(attn_outs)
    for copy in ends:
        copy.wait()


def backward(x, grad_hidden, branch, n1t, q, kv, probs, mixed, wq, wkv, wo, tables, data, kept, away):
    rows, width = branch.shape
    third, wide = wq.shape[2], data[0].shape[-1]
    heads = (2, rows, third)
    weights = (2, width, third)
    half = (2, STEP, width)
    return call(
        backward_kernel,
        (x, grad_hidden, branch, n1t, q, kv, probs, mixed, wq, wkv, wo, tables, *data, kept, away),
        [ANY] * 11 + [VMEM] + [ANY] * 5,
        [shaped((2, 24, wide), F32)] * 3
        + [shaped((2, 24, third), F32)] * 3
        + [shaped(half), shaped(half[1:], F32), shaped(half[1:])],
        [ANY] * 9,
        [
            pltpu.VMEM(half, BF),
            pltpu.VMEM((SEQ, width), F32),
            pltpu.VMEM((rows, width), BF),
            pltpu.VMEM((width, rows), BF),
            pltpu.VMEM((width, rows), BF),
            pltpu.VMEM(heads, BF),
            pltpu.VMEM(heads, BF),
            pltpu.VMEM((4, 4, SEQ, SEQ), BF),
            pltpu.VMEM(heads, BF),
            pltpu.VMEM(weights, BF),
            pltpu.VMEM(weights, BF),
            pltpu.VMEM(weights, BF),
            pltpu.VMEM(heads, BF),
            pltpu.VMEM(heads, BF),
            pltpu.VMEM(heads, BF),
            pltpu.VMEM((SEQ, width), BF),
            pltpu.VMEM((SEQ, width), F32),
            pltpu.VMEM((SEQ, width), BF),
            pltpu.VMEM(half, F32),
            pltpu.VMEM(half[1:], BF),
            pltpu.VMEM(half, F32),
            pltpu.VMEM(half, BF),
            pltpu.VMEM(half, BF),
            *[pltpu.VMEM((4, 4, 4, 48, third), BF) for _ in range(3)],
            *Reduce.buffers(wide, PLANE_X),
            *Reduce.buffers(third, SPARE_Y),
            *Reduce.semaphores,
            *Reduce.semaphores,
            pltpu.SemaphoreType.DMA((12,)),
            pltpu.SemaphoreType.DMA((2,)),
            pltpu.SemaphoreType.DMA((4,)),
            pltpu.SemaphoreType.DMA((4,)),
        ],
        "attn_backward_reduce",
        3,
    )


def tables_for(count, heads, plain):
    half = HEAD // 2
    inverse = np.float32(ROPE_BASE) ** (-(np.arange(half, dtype=np.float32) * np.float32(2.0)) / np.float32(HEAD))
    angle = np.arange(count, dtype=np.float32)[:, None] * inverse.astype(np.float32)[None, :]
    cosine, sine = np.cos(angle), np.sin(angle)
    cosine = np.tile(np.concatenate([cosine, cosine], -1), (1, heads))
    sine = np.tile(np.concatenate([-sine, sine], -1), (1, heads))
    cosine = np.concatenate([cosine, np.ones((count, plain), np.float32)], -1)
    sine = np.concatenate([sine, np.zeros((count, plain), np.float32)], -1)
    return np.stack([cosine, sine]).astype(np.float32)


def body(
    inputs,
    out_grad,
    lengths,
    query_weight,
    key_matrix,
    value_matrix,
    output_weight,
    gate_weight,
    up_weight,
    down_weight,
    attn_gain,
    mlp_gain,
):
    width = inputs.shape[2]
    gain_one = attn_gain.astype(F32)[:, None]
    gain_two = mlp_gain.astype(F32)[:, None]

    own_weights = (
        query_weight,
        key_matrix,
        value_matrix,
        output_weight.T,
        gate_weight,
        up_weight,
        down_weight.T,
    )
    query32, key32, value32, gate32, up32 = (
        w.astype(F32) for w in (query_weight, key_matrix, value_matrix, gate_weight, up_weight)
    )
    third, wide = query_weight.shape[1] // 2, gate_weight.shape[1] // 2
    tables = jnp.asarray(np.concatenate([tables_for(SEQ, 4, 0), tables_for(SEQ, 2, 2 * HEAD)]))

    results = forward(
        own_weights, jnp.stack([attn_gain, mlp_gain], 1), lengths, inputs, out_grad, tables, third, wide
    )
    two, one = results[:3], results[3:6]
    x, n1t, q, kv, probs, mixed, hidden, n2, n2t, cot, cott = results[6:17]
    (wq, wkv, wo), grads, acts = results[17:20], results[20:23], results[23:26]

    def joined(w):
        return w.reshape(2, width, -1)

    def blocked(w):
        return w.reshape(2, 4, 4, 48, -1)

    *one_sums, dg, du, dd, kept, away, branch, grad_hidden = middle(
        n2, cot, hidden, n2t, cott, one, two, acts, [blocked(w) for w in grads]
    )
    *sums, result, in_grad, in_grad_theirs = backward(
        x,
        grad_hidden,
        branch,
        n1t,
        q,
        kv,
        probs,
        mixed,
        joined(wq),
        joined(wkv),
        joined(wo),
        tables,
        [blocked(w) for w in (dg, du, dd)],
        kept,
        away,
    )
    mine = jnp.arange(2)[:, None, None] == lax.axis_index("yl")
    in_grad = jnp.where(mine, in_grad[None], in_grad_theirs[None].astype(F32))
    mlp_sums = [jnp.concatenate(parts, -1) for parts in zip(one_sums, sums[:3])]
    attn_sums = sums[3:]

    def whole(part):
        return jnp.moveaxis(part, 0, 1).reshape(24, -1)

    key_size = key_matrix.shape[1] // 2
    dquery, doutput = whole(attn_sums[0]), whole(attn_sums[2])
    dkey, dvalue = whole(attn_sums[1][..., :key_size]), whole(attn_sums[1][..., key_size:])
    dgate, dup, ddown = (whole(part) for part in mlp_sums)
    gain_grads = jnp.stack(
        [
            sum(jnp.sum(w * g, -1) for w, g in ((query32, dquery), (key32, dkey), (value32, dvalue))),
            sum(jnp.sum(w * g, -1) for w, g in ((gate32, dgate), (up32, dup))),
        ]
    )
    gain_grads = lax.psum(gain_grads, "yl")
    return (
        result,
        in_grad,
        dquery * gain_one,
        dkey * gain_one,
        dvalue * gain_one,
        doutput.T,
        dgate * gain_two,
        dup * gain_two,
        ddown.T,
        gain_grads[0],
        gain_grads[1],
    )


def solution(mesh):
    fine = Mesh(mesh.devices.reshape(2, 4, 4, 2, 2), AXES)
    rows = P(None, AXES, None)
    into, out = P(DP, "yl"), P("yl", DP)
    return jax.shard_map(
        body,
        mesh=fine,
        in_specs=(rows, rows, P(None, DP), into, into, into, out, into, into, out, P(DP), P(DP)),
        out_specs=(rows, rows, into, into, into, out, into, into, out, P(DP), P(DP)),
        check_vma=False,
    )
```

```python
import math

import jax
import jax.numpy as jnp
import numpy as np
from jax import lax
from jax.experimental import pallas as pl
from jax.experimental.pallas import tpu as pltpu
from jax.sharding import Mesh
from jax.sharding import PartitionSpec as P

HEAD = 96
EPS = 1e-05
ROPE_BASE = 100000.0
AXES = ("yh", "x", "z", "core", "yl")
DP = ("yh", "x", "z", "core")
MESH = pl.DeviceIdType.MESH
BF = jnp.bfloat16
F32 = jnp.float32
EVEN = (("x", "y", "z"), ("y", "z", "x"), ("z", "x", "y"))
SPARE_Y = (("x", "z", "y"), ("y", "x", "z"), ("y", "z", "x"))
PLANE_Z = (("w", "x", "z"), ("w", "z", "x"), ("w", "x", "z"))
PLANE_X = (("w", "z", "x"), ("w", "x", "z"), ("w", "z", "x"))
SEQ = 256
ROWS = 512
STEP = 128
CHUNK = 256
VMEM_LIMIT = 62 * 1024 * 1024


def coordinates():
    x, z, yh, yl = (lax.axis_index(a) for a in ("x", "z", "yh", "yl"))
    return {"x": x, "z": z, "y": yh * 2 + yl, "w": yh}


def extent(axis):
    return 2 if axis == "w" else 4


def around(at, axis, by):
    return lax.rem(at[axis] + (by + 4), extent(axis))


def others(axis):
    return (1,) if axis == "w" else (1, -1, 2)


def peer(at, axis, by):
    value = around(at, axis, by)
    if axis == "y":
        return {"yh": value // 2, "yl": lax.rem(value, 2)}
    return {"yh" if axis == "w" else axis: value}


def sibling():
    return {"core": 1 - lax.axis_index("core")}


def partner():
    return {"yl": 1 - lax.axis_index("yl")}


def slot(at, axis, by=0):
    value = around(at, axis, by)
    return lax.rem(value, 2) * 2 + value // 2 if axis == "y" else value


def dimensions(order):
    return ("w" if "w" in order else "y", "x", "z")


def place(at, order, count, half=None, shifted=None):
    out = []
    for axis in dimensions(order):
        if axis in order[:count]:
            size = extent(axis)
            if half is not None and half[0] == axis:
                out.append(pl.ds(size // 2 * half[1], size // 2))
            else:
                out.append(pl.ds(0, size))
        else:
            out.append(slot(at, axis, shifted[1] if shifted is not None and shifted[0] == axis else 0))
    return tuple(out)


def greet(at):
    barrier = pltpu.get_barrier_semaphore()
    for axis in ("x", "y", "z"):
        for by in (1, -1, 2):
            pl.semaphore_signal(barrier, inc=1, device_id=peer(at, axis, by), device_id_type=MESH)
    pl.semaphore_signal(barrier, inc=1, device_id=sibling(), device_id_type=MESH)
    pl.semaphore_wait(barrier, 10)


def sent(src, dst, send, recv, device):
    copy = pltpu.make_async_remote_copy(
        src_ref=src, dst_ref=dst, send_sem=send, recv_sem=recv, device_id=device, device_id_type=MESH
    )
    copy.start()
    return copy


def moved(src, dst, sem):
    copy = pltpu.make_async_copy(src, dst, sem)
    copy.start()
    return copy


class Gather:
    semaphores = (
        pltpu.SemaphoreType.DMA((3,)),
        pltpu.SemaphoreType.DMA((3, 2, 3)),
        pltpu.SemaphoreType.DMA((3, 2, 3)),
        pltpu.SemaphoreType.DMA((3, 2, 2, 3)),
        pltpu.SemaphoreType.DMA((3, 2, 2, 3)),
    )

    def __init__(self, at, srcs, outs, semaphores, orders):
        self.at, self.srcs, self.outs, self.orders = at, srcs, outs, orders
        self.local, self.send, self.recv, self.ring_send, self.ring_recv = semaphores
        self.own, self.direct, self.ring = [], {}, {}

    def arrive(self, p, stage):
        for copy in self.direct.get((p, stage), ()):
            copy.wait_recv()
        if (p, stage, 0, 0) in self.ring:
            for d in range(2):
                self.ring[p, stage, d, 1 - d].wait_recv()
                self.ring[p, stage, d, 2].wait_recv()

    def to_all(self, stage):
        at = self.at
        for p, order in enumerate(self.orders):
            if stage:
                self.own[p].wait()
                self.arrive(p, 0)
            else:
                self.own.append(moved(self.srcs[p], self.outs[p].at[place(at, order, 0)], self.local.at[p]))
            group = self.outs[p].at[place(at, order, stage)]
            self.direct[p, stage] = [
                sent(
                    group if stage else self.srcs[p],
                    group,
                    self.send.at[p, stage, d],
                    self.recv.at[p, stage, d],
                    peer(at, order[stage], by),
                )
                for d, by in enumerate(others(order[stage]))
            ]

    def pass_on(self, p, stage, d, k, block):
        self.ring[p, stage, d, k] = sent(
            block,
            block,
            self.ring_send.at[p, stage - 1, d, k],
            self.ring_recv.at[p, stage - 1, d, k],
            peer(self.at, self.orders[p][stage], 1 - 2 * d),
        )

    def spread(self, stage, *pieces):
        for p in pieces or range(3):
            order = self.orders[p]
            if stage == 1:
                self.own[p].wait()
            self.arrive(p, stage - 1)
            for t in range(2):
                for d in range(2):
                    h = t if d == 0 else 1 - t
                    self.pass_on(p, stage, d, h, self.outs[p].at[place(self.at, order, stage, (order[0], h))])

    def forward(self, stage):
        for p, order in enumerate(self.orders):
            for d, by in enumerate((1, -1)):
                self.ring[p, stage, d, d].wait_recv()
                where = place(self.at, order, stage, (order[0], d), (order[stage], -by))
                self.pass_on(p, stage, d, 2, self.outs[p].at[where])

    def finish(self):
        for copies in self.direct.values():
            for copy in copies:
                copy.wait_send()
        for copy in self.ring.values():
            copy.wait_send()


class Reduce:
    semaphores = (
        pltpu.SemaphoreType.DMA((3, 3)),
        pltpu.SemaphoreType.DMA((3, 2, 3)),
        pltpu.SemaphoreType.DMA((3, 2, 3)),
        pltpu.SemaphoreType.DMA((3, 2, 3)),
        pltpu.SemaphoreType.DMA((3, 2, 3)),
        pltpu.SemaphoreType.DMA((3, 2)),
        pltpu.SemaphoreType.DMA((3, 2)),
    )

    @staticmethod
    def buffers(columns, orders):
        def per_piece(*shape):
            return [pltpu.VMEM(shape + (48, columns), BF) for _ in range(3)]

        size = extent(dimensions(orders[0])[0])
        return [
            *per_piece(2, size // 2, 4),
            *per_piece(size, 4),
            *per_piece(2, size // 2, 4),
            *per_piece(2, size, 4),
            *per_piece(3, size),
            *per_piece(3),
            *[pltpu.VMEM((48, columns), F32) for _ in range(3)],
        ]

    def __init__(self, at, data, buffers, semaphores, orders):
        self.at, self.data, self.orders = at, data, orders
        self.side, self.kept, self.far, self.near, self.second, self.third, self.sums = (
            buffers[3 * k : 3 * k + 3] for k in range(7)
        )
        self.load, self.first_send, self.first_recv, self.send, self.recv, self.end_send, self.end_recv = semaphores
        self.loads, self.copies = {}, {}

    def left(self, p):
        order = self.orders[p]
        return [axis for axis in dimensions(order) if axis != order[2]]

    def inside(self, p, first, second=None):
        whole = slice(None) if second is None else second
        return (first, whole) if self.left(p)[0] == self.orders[p][1] else (whole, first)

    def start(self, *pieces):
        at, s, r = self.at, self.first_send, self.first_recv
        for p in pieces or range(3):
            order = self.orders[p]
            axis, cut = order[2], self.left(p)[0]
            size = extent(cut) // 2
            for d, by in enumerate((1, -1)):
                block = self.data[p].at[place(at, order, 2, (cut, d), (axis, 2))]
                self.copies[p, d, 0] = sent(block, self.far[p].at[d], s.at[p, d, 0], r.at[p, d, 0], peer(at, axis, by))
            for d, by in enumerate((1, -1)):
                h = 1 - d
                block = self.data[p].at[place(at, order, 2, (cut, h), (axis, by))]
                self.copies[p, d, 1] = sent(
                    block, self.near[p].at[d, pl.ds(size * h, size)], s.at[p, d, 1], r.at[p, d, 1], peer(at, axis, by)
                )
                block = self.data[p].at[place(at, order, 2, (cut, d), (axis, by))]
                self.loads[p, d] = moved(block, self.side[p].at[d], self.load.at[p, d])
            self.loads[p, 2] = moved(self.data[p].at[place(at, order, 2)], self.kept[p], self.load.at[p, 2])

    def relay(self):
        for p, order in enumerate(self.orders):
            size = extent(self.left(p)[0]) // 2
            for d, by in enumerate((1, -1)):
                self.loads[p, d].wait()
                self.copies[p, d, 0].wait_recv()
                side, far = self.side[p], self.far[p]

                @pl.loop(0, 4 * size)
                def _(i, d=d, side=side, far=far):
                    a, b = i // 4, lax.rem(i, 4)
                    side[d, a, b] = (side[d, a, b].astype(F32) + far[d, a, b].astype(F32)).astype(BF)

                self.copies[p, d, 2] = sent(
                    side.at[d],
                    self.near[p].at[d, pl.ds(size * d, size)],
                    self.first_send.at[p, d, 2],
                    self.first_recv.at[p, d, 2],
                    peer(self.at, order[2], by),
                )

    def spread(self):
        at = self.at
        for p, order in enumerate(self.orders):
            self.loads[p, 2].wait()
            for d in range(2):
                self.copies[p, d, 1].wait_recv()
                self.copies[p, d, 2].wait_recv()
            kept, near = self.kept[p], self.near[p]

            @pl.loop(0, 4 * extent(self.left(p)[0]))
            def _(i, kept=kept, near=near):
                a, b = i // 4, lax.rem(i, 4)
                total = kept[a, b].astype(F32) + near[0, a, b].astype(F32) + near[1, a, b].astype(F32)
                kept[a, b] = total.astype(BF)

            for d, by in enumerate(others(order[1])):
                block = kept.at[self.inside(p, slot(at, order[1], by))]
                self.copies[p, "b", d] = sent(
                    block, self.second[p].at[d], self.send.at[p, 0, d], self.recv.at[p, 0, d], peer(at, order[1], by)
                )

    def narrow(self):
        at = self.at
        for p, order in enumerate(self.orders):
            for d in range(len(others(order[1]))):
                self.copies[p, "b", d].wait_recv()
            kept, second, mine = self.kept[p], self.second[p], slot(at, order[1])

            @pl.loop(0, extent(order[0]))
            def _(i, p=p, kept=kept, second=second, mine=mine):
                total = kept[self.inside(p, mine, i)].astype(F32)
                for d in range(3):
                    total = total + second[d, i].astype(F32)
                kept[self.inside(p, mine, i)] = total.astype(BF)

            for d, by in enumerate(others(order[0])):
                block = kept.at[self.inside(p, mine, slot(at, order[0], by))]
                self.copies[p, "c", d] = sent(
                    block, self.third[p].at[d], self.send.at[p, 1, d], self.recv.at[p, 1, d], peer(at, order[0], by)
                )

    def finish(self, outs):
        at, core, ends = self.at, lax.axis_index("core"), []
        for p, order in enumerate(self.orders):
            total = self.kept[p][self.inside(p, slot(at, order[1]), slot(at, order[0]))].astype(F32)
            for d in range(len(others(order[0]))):
                self.copies[p, "c", d].wait_recv()
                total = total + self.third[p][d].astype(F32)
            self.sums[p][...] = total
            theirs = self.sums[p].at[pl.ds(pl.multiple_of(24 * (1 - core), 8), 24)]
            mine = self.sums[p].at[pl.ds(pl.multiple_of(24 * core, 8), 24)]
            ends.append(sent(theirs, outs[p].at[core], self.end_send.at[p, 0], self.end_recv.at[p, 0], sibling()))
            ends.append(moved(mine, outs[p].at[core], self.end_send.at[p, 1]))
        for copy in self.copies.values():
            copy.wait_send()
        for copy in ends:
            copy.wait()


def nn(left, right):
    return lax.dot_general(left, right, (((1,), (0,)), ((), ())), preferred_element_type=F32)


def nt(left, right):
    return lax.dot_general(left, right, (((1,), (1,)), ((), ())), preferred_element_type=F32)


def tn(left, right):
    return lax.dot_general(left, right, (((0,), (0,)), ((), ())), preferred_element_type=F32)


def inverse_rms(values):
    return lax.rsqrt(jnp.mean(values * values, -1, keepdims=True) + EPS)


def swap(values, first):
    width = values.shape[-1]
    return jnp.where(first, pltpu.roll(values, width - HEAD // 2, 1), pltpu.roll(values, HEAD // 2, 1))


def first_half(shape):
    return lax.rem(lax.broadcasted_iota(jnp.int32, shape, 1), HEAD) < HEAD // 2


def as_column(row):
    size = row.shape[1]
    square = jnp.broadcast_to(row[...].astype(F32), (size, size))
    diagonal = lax.broadcasted_iota(jnp.int32, (size, size), 0) == lax.broadcasted_iota(jnp.int32, (size, size), 1)
    return jnp.sum(jnp.where(diagonal, square, 0.0), -1, keepdims=True)


def rows_at(start, size):
    return pl.ds(pl.multiple_of(start, size), size)


ANY = pl.BlockSpec(memory_space=pl.ANY)
VMEM = pl.BlockSpec(memory_space=pltpu.VMEM)


def shaped(shape, kind=BF):
    return jax.ShapeDtypeStruct(shape, kind)


def call(kernel, operands, in_specs, results, out_specs, scratch, name, collective_id, **more):
    return pl.pallas_call(
        kernel,
        out_shape=results,
        in_specs=in_specs,
        out_specs=out_specs,
        scratch_shapes=scratch,
        compiler_params=pltpu.CompilerParams(
            collective_id=collective_id, has_side_effects=True, vmem_limit_bytes=VMEM_LIMIT
        ),
        name=name,
        **more,
    )(*operands)


def hidden_units(m, c, count, sub, n2, cot, weights, acts):
    rows = pl.ds(pl.multiple_of(m * ROWS + c * SEQ, SEQ), count * SEQ)
    columns = pl.ds(sub * CHUNK, CHUNK)
    gate_w, up_w, down_w = (w[..., columns].reshape(-1, CHUNK) for w in weights)
    gate = nn(n2[rows], gate_w)
    up = nn(n2[rows], up_w)
    sigma = 0.5 + 0.5 * jnp.tanh(0.5 * gate)
    silu = gate * sigma
    grad_active = nn(cot[m, pl.ds(c, count)].reshape(count * SEQ, -1), down_w)
    acts[0][rows, columns] = (silu * up).astype(BF)
    acts[1][rows, columns] = (grad_active * up * (sigma + silu * (1.0 - sigma))).astype(BF)
    acts[2][rows, columns] = (grad_active * silu).astype(BF)


def unit_gradients(n2t, cott, acts, staging, outs, sems, rows=None, added=False, written=True):
    whole, copies = slice(None) if rows is None else rows, []
    for k, (left, right, target) in enumerate(((n2t, acts[1], 0), (n2t, acts[2], 1), (cott, acts[0], 2))):
        for sub in range(2):
            columns = pl.ds(sub * CHUNK, CHUNK)
            value = nn(left[:, whole], right[whole, columns])
            if added:
                value = value + staging[2 * k + sub].astype(F32)
            staging[2 * k + sub] = value.astype(BF)
            if written:
                copies.append(moved(staging.at[2 * k + sub], outs[target].at[:, columns], sems.at[2 * k + sub]))
    return copies


def forward_kernel(third, wide, *refs):
    own_weights, gains_one, gains_two, lengths, xin, gin, tables = refs[:7], *refs[7:13]
    refs = refs[1:]
    full_two, full_one = refs[12:15], refs[15:18]
    (
        x_out, n1t_out, q_out, kv_out, probs_out, mixed_out, hidden_out, n2_out, n2t_out, cot_out, cott_out,
    ) = refs[18:29]
    attn_out, grads_out, acts_out, shard_out = refs[29:32], refs[32:35], refs[35:38], refs[38]
    refs = refs[1:]
    (
        shard, got_shard, packed, xs, gs, normed, q, kv, probs, mixed, hidden, n2, n2t, cott, part, arrived, n1t,
        valid, staging,
    ) = refs[38:57]
    full_attn, weights, acts = refs[57:60], refs[60:63], refs[63:66]
    attn_sems, one_sems, two_sems = refs[66:71], refs[71:76], refs[76:81]
    pair_send, pair_recv, row_send, row_recv, far_send, far_recv, own_sem, out_sem, put_sem = refs[81:]
    at = coordinates()
    core, yl = lax.axis_index("core"), lax.axis_index("yl")
    own_x = moved(xin.at[yl], xs.at[core, yl], own_sem.at[0])
    own_g = moved(gin, gs.at[:, core, yl], own_sem.at[1])

    query, key, value, output, *mlp_weights = (ref[...].astype(F32) for ref in own_weights)
    gain_one, gain_two = as_column(gains_one), as_column(gains_two)
    small = key.shape[1] // 2
    for c in range(2):
        thin = slice(c * small, (c + 1) * small)
        parts = [
            query[:, c * third : (c + 1) * third] * gain_one,
            jnp.concatenate([key[:, thin] * gain_one, value[:, thin] * gain_one], -1),
            output[:, c * third : (c + 1) * third],
            *(
                w[:, c * wide : (c + 1) * wide] * g
                for w, g in zip(mlp_weights, (gain_two, gain_two, jnp.ones_like(gain_two)))
            ),
        ]
        column = 0
        for part_value in parts:
            shard[c, :24, column : column + part_value.shape[1]] = part_value
            column += part_value.shape[1]
        lane = lax.broadcasted_iota(jnp.int32, (8, 2 * SEQ), 1)
        ends = jnp.where(lane < SEQ, lengths[:, 0:1], lengths[:, 1:2] + SEQ)
        shard[c, 24:, : 2 * SEQ] = jnp.where(lane < ends, 1.0, 0.0)
    greet(at)
    swap_shard = sent(shard.at[1 - core], got_shard, pair_send.at[0], pair_recv.at[0], sibling())

    rows = {}

    def exchange(k):
        ours, theirs, dst = (
            (xin.at[yl], xin.at[1 - yl], xs.at[core, yl]),
            (gin, gin, gs.at[:, core, yl]),
        )[k]
        rows[k, 0] = sent(theirs, dst, row_send.at[k, 0], row_recv.at[k, 0], partner())
        rows[k, 1] = sent(ours, dst, row_send.at[k, 1], row_recv.at[k, 1], sibling())

    def share(k):
        block = (xs.at[core, 1 - yl], gs.at[:, core, 1 - yl])[k]
        rows[k, 0].wait_recv()
        rows[k, 2] = sent(block, block, row_send.at[k, 2], row_recv.at[k, 2], sibling())

    def settle(k):
        (own_x, own_g)[k].wait()
        rows[k, 0].wait_send()
        rows[k, 1].wait()
        rows[k, 2].wait()

    swap_shard.wait()
    low, high = shard[core], got_shard[...]
    first, last = jnp.where(core == 0, low, high), jnp.where(core == 0, high, low)
    packed[...] = jnp.concatenate([first[:24], last[:24]], 0).astype(BF)
    for c, rows_of in enumerate((first, last)):
        for m in range(2):
            valid[m, c] = rows_of[24:32, m * SEQ : (m + 1) * SEQ]

    def pieces(start, size, step):
        return [packed.at[:, pl.ds(start + k * step, size)] for k in range(3)]

    half = wide // 2
    attn = Gather(at, pieces(0, third, third), full_attn, attn_sems, EVEN)
    one = Gather(at, pieces(3 * third, half, wide), weights, one_sems, PLANE_Z)
    two = Gather(at, pieces(3 * third + half, half, wide), full_two, two_sems, PLANE_X)
    attn.to_all(0)
    one.to_all(0)
    two.to_all(0)
    attn.to_all(1)
    one.spread(1)
    attn.spread(2, 0, 1)
    exchange(0)
    attn.spread(2, 2)
    one.forward(1)
    two.spread(1)
    attn.forward(2)
    two.forward(1)
    one.spread(2)
    share(0)
    settle(0)
    exchange(1)
    outs = [moved(xs, x_out, out_sem.at[0]), moved(shard, shard_out, out_sem.at[24])]

    @pl.loop(0, ROWS // STEP)
    def _(i):
        block = rows_at(i * STEP, STEP)
        values = xs[i // 2, lax.rem(i, 2)].astype(F32)
        normed[block] = (values * inverse_rms(values)).astype(BF)

    for p in range(2):
        attn.arrive(p, 2)
    two.spread(2)
    wq, wkv, wo = full_attn

    def weight(ref, y):
        return ref[pl.ds(2 * y, 2)].reshape(-1, third)

    @pl.loop(0, 2)
    def _(y):
        @pl.loop(0, ROWS // SEQ)
        def _(n):
            block = rows_at(n * SEQ, SEQ)
            left = normed[block]
            is_first = first_half((SEQ, third))
            for k, (w, result) in enumerate(((wq, q), (wkv, kv))):
                lin = nn(left, weight(w, y))
                result[y, block] = (lin * tables[2 * k] + swap(lin, is_first) * tables[2 * k + 1]).astype(BF)

    outs.append(moved(q, q_out, out_sem.at[5]))
    outs.append(moved(kv, kv_out, out_sem.at[6]))
    one.forward(2)
    scale = 1.0 / math.sqrt(HEAD)

    @pl.loop(0, 4)
    def _(i):
        y, n = i // 2, lax.rem(i, 2)
        block = rows_at(n * SEQ, SEQ)
        t = lax.broadcasted_iota(jnp.int32, (SEQ, SEQ), 0)
        s = lax.broadcasted_iota(jnp.int32, (SEQ, SEQ), 1)
        keep = (s <= t) & (valid[yl, n, 0:1, :] > 0.5)
        queries, keys = q[y, block], kv[y, block]
        results = []
        for h in range(4):
            g = h // 2
            scores = nt(queries[:, h * HEAD : (h + 1) * HEAD], keys[:, g * HEAD : (g + 1) * HEAD]) * scale
            scores = jnp.where(keep, scores, -1e30)
            terms = jnp.exp(scores - jnp.max(scores, -1, keepdims=True))
            low_probs = (terms * (1.0 / jnp.sum(terms, -1, keepdims=True))).astype(BF)
            probs[i, h] = low_probs
            results.append(nn(low_probs, keys[:, (2 + g) * HEAD : (3 + g) * HEAD]))
        mixed[y, block] = jnp.concatenate(results, -1).astype(BF)

    outs.append(moved(probs, probs_out, out_sem.at[7]))
    outs.append(moved(mixed, mixed_out, out_sem.at[8]))
    two.forward(2)

    attn.arrive(2, 2)
    copies = []
    for i in range(ROWS // STEP):
        block = rows_at(lax.rem(2 * (1 - core) + i, 4) * STEP, STEP)
        part[block] = (nt(mixed[0, block], weight(wo, 0)) + nt(mixed[1, block], weight(wo, 1))).astype(BF)
        copies.append(sent(part.at[block], arrived.at[block], pair_send.at[1 + i], pair_recv.at[1 + i], sibling()))
    second_rows = {}
    mine, theirs = yl * ROWS, (1 - yl) * ROWS
    for i in range(ROWS // STEP):
        copies[(i + 2) % 4 if i < 2 else i - 2].wait_send()
        copies[i].wait_recv()
        number = lax.rem(2 * core + i, 4)
        block = rows_at(number * STEP, STEP)
        values = xs[number // 2, lax.rem(number, 2)].astype(F32) + (
            part[block].astype(F32) + arrived[block].astype(F32)
        )
        hidden[block] = values
        target = rows_at(mine + number * STEP, STEP)
        n2[target] = (values * inverse_rms(values)).astype(BF)
        if i < 2:
            second_rows[0, i] = sent(n2.at[target], n2.at[target], far_send.at[0, i], far_recv.at[0, i], partner())
    outs.append(moved(hidden.at[rows_at(core * SEQ, SEQ)], hidden_out, out_sem.at[9]))
    attn.finish()
    outs.extend(moved(full_attn[p], attn_out[p], out_sem.at[2 + p]) for p in range(3))
    share(1)
    settle(1)

    for m in range(2):
        for c in range(2):
            for h in range(2):
                mask = valid[m, c][:, h * STEP : (h + 1) * STEP].T[:, 0:1]
                gs[m, c, h] = (gs[m, c, h].astype(F32) * mask).astype(BF)
    outs.append(moved(gs, cot_out, out_sem.at[10]))

    for p in range(3):
        one.arrive(p, 2)
    one.finish()
    outs.extend(moved(weights[p], full_one[p], out_sem.at[11 + p]) for p in range(3))
    mine_rows, their_rows = rows_at(mine, ROWS), rows_at(theirs, ROWS)
    for sub in range(2):
        hidden_units(yl, 0, 2, sub, n2, gs, weights, acts)
    outs.extend(moved(acts[p].at[mine_rows], acts_out[p].at[mine_rows], out_sem.at[15 + p]) for p in range(3))
    outs.append(moved(n2.at[mine_rows], n2_out.at[mine_rows], out_sem.at[18]))
    for m in range(2):
        for c in range(2):
            for h in range(2):
                cott[:, pl.ds(m * ROWS + (2 * c + h) * STEP, STEP)] = gs[m, c, h].T
    outs.append(moved(cott, cott_out, out_sem.at[14]))
    for i in range(ROWS // STEP):
        block = rows_at(mine + i * STEP, STEP)
        n2t[:, block] = n2[block].T
    unit_gradients(n2t, cott, acts, staging, grads_out, put_sem, mine_rows, written=False)
    n1t[...] = normed[...].T
    outs.append(moved(n1t, n1t_out, out_sem.at[1]))

    for i in range(2):
        second_rows[0, i].wait_recv()
        block = rows_at(theirs + (2 * core + i) * STEP, STEP)
        second_rows[1, i] = sent(n2.at[block], n2.at[block], far_send.at[1, i], far_recv.at[1, i], sibling())
    for sub in range(2):
        hidden_units(1 - yl, core, 1, sub, n2, gs, weights, acts)
    for i in range(2):
        second_rows[0, i].wait_send()
        second_rows[1, i].wait()
    for sub in range(2):
        hidden_units(1 - yl, 1 - core, 1, sub, n2, gs, weights, acts)
    outs.extend(moved(acts[p].at[their_rows], acts_out[p].at[their_rows], out_sem.at[20 + p]) for p in range(3))
    outs.append(moved(n2.at[their_rows], n2_out.at[their_rows], out_sem.at[23]))
    for i in range(ROWS // STEP):
        block = rows_at(theirs + i * STEP, STEP)
        n2t[:, block] = n2[block].T
    outs.append(moved(n2t, n2t_out, out_sem.at[19]))
    outs.extend(unit_gradients(n2t, cott, acts, staging, grads_out, put_sem, their_rows, added=True))
    for p in range(3):
        two.arrive(p, 2)
    two.finish()
    for copy in outs:
        copy.wait()


def forward(own_weights, gains, lengths, xin, gin, tables, third, wide):
    width = xin.shape[2]
    rows = (ROWS, width)
    both = (2 * ROWS, width)
    heads = (2, ROWS, third)
    square = (4, 4, SEQ, SEQ)
    half = wide // 2
    piece = (2, 4, 4, 48, half)
    return call(
        lambda *refs: forward_kernel(third, wide, *refs),
        (*own_weights, *gains, lengths, xin, gin, tables),
        [VMEM] * 10 + [ANY, ANY, VMEM],
        [shaped(piece)] * 6
        + [
            shaped((2, 2, 128, width)),
            shaped(rows[::-1]),
            shaped(heads),
            shaped(heads),
            shaped(square),
            shaped(heads),
            shaped((SEQ, width), F32),
            shaped(both),
            shaped(both[::-1]),
            shaped((2, 2, 2, 128, width)),
            shaped(both[::-1]),
        ]
        + [shaped((4, 4, 4, 48, third))] * 3
        + [shaped((width, half))] * 3
        + [shaped((2 * ROWS, half))] * 3
        + [shaped((2, 32, 3 * third + 3 * wide), F32)],
        [ANY] * 27,
        [
            pltpu.VMEM((2, 32, 3 * third + 3 * wide), F32),
            pltpu.VMEM((32, 3 * third + 3 * wide), F32),
            pltpu.VMEM((48, 3 * third + 3 * wide), BF),
            pltpu.VMEM((2, 2, 128, width), BF),
            pltpu.VMEM((2, 2, 2, 128, width), BF),
            pltpu.VMEM(rows, BF),
            pltpu.VMEM(heads, BF),
            pltpu.VMEM(heads, BF),
            pltpu.VMEM(square, BF),
            pltpu.VMEM(heads, BF),
            pltpu.VMEM(rows, F32),
            pltpu.VMEM(both, BF),
            pltpu.VMEM(both[::-1], BF),
            pltpu.VMEM(both[::-1], BF),
            pltpu.VMEM(rows, BF),
            pltpu.VMEM(rows, BF),
            pltpu.VMEM(rows[::-1], BF),
            pltpu.VMEM((2, 2, 8, SEQ), F32),
            pltpu.VMEM((6, width, CHUNK), BF),
            *[pltpu.VMEM((4, 4, 4, 48, third), BF) for _ in range(3)],
            *[pltpu.VMEM(piece, BF) for _ in range(3)],
            *[pltpu.VMEM((2 * ROWS, half), BF) for _ in range(3)],
            *Gather.semaphores,
            *Gather.semaphores,
            *Gather.semaphores,
            pltpu.SemaphoreType.DMA((5,)),
            pltpu.SemaphoreType.DMA((5,)),
            pltpu.SemaphoreType.DMA((2, 3)),
            pltpu.SemaphoreType.DMA((2, 3)),
            pltpu.SemaphoreType.DMA((2, 2)),
            pltpu.SemaphoreType.DMA((2, 2)),
            pltpu.SemaphoreType.DMA((2,)),
            pltpu.SemaphoreType.DMA((25,)),
            pltpu.SemaphoreType.DMA((6,)),
        ],
        "gather_attn_forward_mlp",
        1,
    )


def middle_kernel(*refs):
    n2_in, cot_in, hidden_in, n2t_in, cott_in = refs[:5]
    one_in, two_in, acts_in, data = refs[5:8], refs[8:11], refs[11:14], refs[14:17]
    sums_out, grads_out = refs[17:20], refs[20:23]
    kept_out, away_out, branch_out, grad_hidden_out = refs[23:27]
    (
        n2, cot, hidden, n2t, cott, staging, to_pair, from_pair, whole, from_far, keep, halves, to_far, branch, gh,
    ) = refs[27:42]
    one, two, acts_one, acts_two = refs[42:45], refs[45:48], refs[48:51], refs[51:54]
    buffers, reduce_sems = refs[54:75], refs[75:82]
    load, put, put_sem, pair_send, pair_recv, part_send, part_recv, far_send, far_recv = refs[82:]
    core, yl = lax.axis_index("core"), lax.axis_index("yl")
    at = coordinates()
    order = (
        (n2_in, n2),
        (two_in[0], two[0]),
        (two_in[1], two[1]),
        (cot_in, cot),
        (two_in[2], two[2]),
        *zip(acts_in[1:], acts_one[1:]),
        *zip(one_in[:2], one[:2]),
        (acts_in[0], acts_one[0]),
        (one_in[2], one[2]),
        (n2t_in, n2t),
        (cott_in, cott),
        (hidden_in, hidden),
    )
    loads = [moved(src, dst, load.at[k]) for k, (src, dst) in enumerate(order)]
    greet(at)
    total = Reduce(at, data, buffers, reduce_sems, PLANE_Z)
    total.start()
    for k in range(5):
        loads[k].wait()
    for sub in range(2):
        hidden_units(1 - yl, 0, 2, sub, n2, cot, two, acts_two)
    for k in range(5, 11):
        loads[k].wait()

    def weight(ref):
        return ref[...].reshape(n2.shape[1], -1)

    def grad_rows(m, c):
        rows = rows_at(m * ROWS + c * SEQ, SEQ)
        return (nt(acts_one[1][rows], weight(one[0])) + nt(acts_one[2][rows], weight(one[1]))) + (
            nt(acts_two[1][rows], weight(two[0])) + nt(acts_two[2][rows], weight(two[1]))
        )

    def out_rows(m, c):
        rows = rows_at(m * ROWS + c * SEQ, SEQ)
        return nt(acts_one[0][rows], weight(one[2])) + nt(acts_two[0][rows], weight(two[2]))

    pair, far, shared = {}, {}, []

    def to_sibling(k, value):
        to_pair[k] = value.astype(BF)
        pair[k] = sent(to_pair.at[k], from_pair.at[k], pair_send.at[k], pair_recv.at[k], sibling())

    blocks = [pl.ds(i * STEP, STEP) for i in range(2)]
    to_pair[0] = grad_rows(1 - yl, 1 - core).astype(BF)
    for i, rows in enumerate(blocks):
        pair["far", i] = sent(
            to_pair.at[0, rows], from_pair.at[0, rows], part_send.at[0, i], part_recv.at[0, i], sibling()
        )
    keep[...] = grad_rows(1 - yl, core)
    for i, rows in enumerate(blocks):
        pair["far", i].wait_recv()
        whole[rows] = (keep[rows] + from_pair[0, rows].astype(F32)).astype(BF)
        far[i] = sent(whole.at[rows], from_far.at[rows], far_send.at[i], far_recv.at[i], partner())
    total.relay()
    for sub in range(2):
        hidden_units(yl, 0, 2, sub, n2, cot, two, acts_two)
    to_sibling(1, grad_rows(yl, 1 - core))
    keep[...] = grad_rows(yl, core)
    to_sibling(2, out_rows(1 - yl, 1 - core))
    to_sibling(3, out_rows(yl, 1 - core))
    for k in range(11, 14):
        loads[k].wait()
    outs = unit_gradients(n2t, cott, acts_two, staging, grads_out, put_sem)
    total.spread()

    for k, m in ((2, 1 - yl), (3, yl)):
        pair[k].wait_recv()
        value = out_rows(m, core) + from_pair[k].astype(F32)
        if k == 3:
            value = value + hidden[...]
        halves[k - 2] = value.reshape(2, STEP, -1)
        to_far[k - 2] = halves[k - 2, 1 - yl].astype(BF)
        outs.append(moved(halves.at[k - 2, yl], kept_out.at[k - 2], put.at[k]))
        outs.append(moved(to_far.at[k - 2], away_out.at[k - 2], put.at[k + 2]))
    pair[1].wait_recv()

    for i, rows in enumerate(blocks):
        far[i].wait_recv()
        grad = keep[rows] + (from_pair[1, rows].astype(F32) + from_far[rows].astype(F32))
        values = hidden[rows]
        inverse = inverse_rms(values)
        unit = values * inverse
        back = inverse * (grad - unit * jnp.mean(grad * unit, -1, keepdims=True))
        gh[rows] = cot[yl, core, i].astype(F32) + back
        branch[rows] = gh[rows].astype(BF)
        target = rows_at(core * SEQ + i * STEP, STEP)
        shared.append(
            sent(branch.at[rows], branch_out.at[target], part_send.at[1, i], part_recv.at[1, i], sibling())
        )
        outs.append(moved(branch.at[rows], branch_out.at[target], put.at[6 + i]))
    outs.append(moved(gh, grad_hidden_out, put.at[0]))
    total.narrow()
    total.finish(sums_out)
    for copy in shared:
        copy.wait()
    for copy in (*pair.values(), *far.values()):
        copy.wait_send()
    for copy in outs:
        copy.wait()


def middle(n2, cot, hidden, n2t, cott, one, two, acts, data):
    rows, width = n2.shape
    half = one[0].shape[-1]
    block = (SEQ, width)
    return call(
        middle_kernel,
        (n2, cot, hidden, n2t, cott, *one, *two, *acts, *data),
        [ANY] * 17,
        [shaped((2, 24, half), F32)] * 3
        + [shaped((width, half))] * 3
        + [
            shaped((2, STEP, width), F32),
            shaped((2, STEP, width)),
            shaped((ROWS, width)),
            shaped(block, F32),
        ],
        [ANY] * 10,
        [
            pltpu.VMEM((rows, width), BF),
            pltpu.VMEM(cot.shape, BF),
            pltpu.VMEM(block, F32),
            pltpu.VMEM((width, rows), BF),
            pltpu.VMEM((width, rows), BF),
            pltpu.VMEM((6, width, CHUNK), BF),
            pltpu.VMEM((4,) + block, BF),
            pltpu.VMEM((4,) + block, BF),
            pltpu.VMEM(block, BF),
            pltpu.VMEM(block, BF),
            pltpu.VMEM(block, F32),
            pltpu.VMEM((2, 2, STEP, width), F32),
            pltpu.VMEM((2, STEP, width), BF),
            pltpu.VMEM(block, BF),
            pltpu.VMEM(block, F32),
            *[pltpu.VMEM(one[0].shape, BF) for _ in range(6)],
            *[pltpu.VMEM((rows, half), BF) for _ in range(6)],
            *Reduce.buffers(half, PLANE_Z),
            *Reduce.semaphores,
            pltpu.SemaphoreType.DMA((14,)),
            pltpu.SemaphoreType.DMA((8,)),
            pltpu.SemaphoreType.DMA((6,)),
            pltpu.SemaphoreType.DMA((4,)),
            pltpu.SemaphoreType.DMA((4,)),
            pltpu.SemaphoreType.DMA((2, 2)),
            pltpu.SemaphoreType.DMA((2, 2)),
            pltpu.SemaphoreType.DMA((2,)),
            pltpu.SemaphoreType.DMA((2,)),
        ],
        "mlp_reduce",
        2,
    )


def backward_kernel(*refs):
    xall, grad_hidden_in, branch_in, n1t_in, q_in, kv_in, probs_in, mixed_in, wq_in, wkv_in, wo_in, tables = refs[:12]
    data, kept_in, away, shard_in, one_in = refs[12:15], *refs[15:18], refs[18:20]
    refs = refs[3:]
    mlp_outs, attn_outs, result_out, in_grad_out, from_partner = refs[17:20], refs[20:23], *refs[23:26]
    gains_out = refs[26]
    refs = refs[1:]
    (
        xs, gh, branch, branch_t, normed_t, q, kv, probs, mixed, wq, wkv, wo,
        grad_mixed, dq, dkv, part, keep_part, arrived, in_grad, for_partner, kept, others_half, result,
    ) = refs[26:49]
    attn_grads = refs[49:52]
    mlp_buffers, attn_buffers = refs[52:73], refs[73:94]
    mlp_sems, attn_sems = refs[94:101], refs[101:108]
    mlp_ends, attn_ends, shard, one_sums, gain_part, gain_in = refs[108:111], refs[111:114], *refs[114:118]
    load, put, send, recv = refs[118:]
    at = coordinates()
    core, yl = lax.axis_index("core"), lax.axis_index("yl")
    loads = [
        moved(src, dst, load.at[k])
        for k, (src, dst) in enumerate(
            (
                (branch_in, branch),
                (wo_in, wo),
                (mixed_in, mixed),
                (q_in, q),
                (kv_in, kv),
                (probs_in, probs),
                (n1t_in, normed_t),
                (wq_in, wq),
                (wkv_in, wkv),
                (grad_hidden_in, gh),
                (xall.at[core], xs),
                (kept_in, kept),
                (shard_in, shard),
                (one_in[0], one_sums.at[0]),
                (one_in[1], one_sums.at[1]),
            )
        )
    ]
    greet(at)
    mlp_sum = Reduce(at, data, mlp_buffers, mlp_sems, PLANE_X)
    attn_sum = Reduce(at, attn_grads, attn_buffers, attn_sems, SPARE_Y)
    mlp_sum.start()
    finals = [sent(away.at[k], others_half.at[k], send.at[2 + k], recv.at[2 + k], partner()) for k in range(2)]
    for k in range(2):
        loads[k].wait()
    for y in range(2):
        grad_mixed[y] = nn(branch[...], wo[y]).astype(BF)
    for k in range(2, 6):
        loads[k].wait()
    scale = 1.0 / math.sqrt(HEAD)

    @pl.loop(0, 4)
    def _(i):
        y, n = i // 2, lax.rem(i, 2)
        rows = rows_at(n * SEQ, SEQ)
        queries, keys, grads = q[y, rows], kv[y, rows], grad_mixed[y, rows]
        grad_q, grad_k, grad_v = [], [None, None], [None, None]
        for h in range(4):
            g = h // 2
            key = keys[:, g * HEAD : (g + 1) * HEAD]
            value = keys[:, (2 + g) * HEAD : (3 + g) * HEAD]
            query = queries[:, h * HEAD : (h + 1) * HEAD]
            grad = grads[:, h * HEAD : (h + 1) * HEAD]
            low = probs[i, h]
            prob = low.astype(F32)
            grad_probs = nt(grad, value)
            grad_scores = (prob * (grad_probs - jnp.sum(grad_probs * prob, -1, keepdims=True))).astype(BF)
            grad_q.append(nn(grad_scores, key) * scale)
            back_k = tn(grad_scores, query) * scale
            back_v = tn(low, grad)
            grad_k[g] = back_k if grad_k[g] is None else grad_k[g] + back_k
            grad_v[g] = back_v if grad_v[g] is None else grad_v[g] + back_v
        first = first_half((SEQ, 4 * HEAD))
        for k, (pieces, target) in enumerate(((grad_q, dq), (grad_k + grad_v, dkv))):
            values = jnp.concatenate(pieces, -1)
            target[y, rows] = (values * tables[2 * k] - swap(values, first) * tables[2 * k + 1]).astype(BF)

    loads[6].wait()

    def weight_grad(p, left, right):
        for y in range(2):
            target = attn_grads[p].at[pl.ds(2 * y, 2)]
            target[...] = nn(left[...], right[y]).astype(BF).reshape(target.shape)
        attn_sum.start(p)

    weight_grad(0, normed_t, dq)
    weight_grad(1, normed_t, dkv)
    mlp_sum.relay()
    branch_t[...] = branch[...].T
    weight_grad(2, branch_t, mixed)
    for k in range(7, 15):
        loads[k].wait()

    def back(start):
        rows = rows_at(start, SEQ)
        return (nt(dq[0, rows], wq[0]) + nt(dq[1, rows], wq[1])) + (nt(dkv[0, rows], wkv[0]) + nt(dkv[1, rows], wkv[1]))

    part[...] = back((1 - core) * SEQ).astype(BF)
    pair = sent(part, arrived, send.at[0], recv.at[0], sibling())
    attn_sum.relay()
    keep_part[...] = back(core * SEQ)
    mlp_sum.spread()
    pair.wait()

    @pl.loop(0, SEQ // STEP)
    def _(i):
        rows = rows_at(i * STEP, STEP)
        grad = keep_part[rows] + arrived[rows].astype(F32)
        values = xs[i].astype(F32)
        inverse = inverse_rms(values)
        unit = values * inverse
        change = inverse * (grad - unit * jnp.mean(grad * unit, -1, keepdims=True))
        in_grad[i] = gh[rows] + change

    for_partner[...] = in_grad[1 - yl].astype(BF)
    ends = [
        moved(in_grad.at[yl], in_grad_out, put.at[0]),
        sent(for_partner, from_partner, send.at[1], recv.at[1], partner()),
    ]
    mlp_sum.narrow()
    attn_sum.spread()
    for copy in finals:
        copy.wait()
    result[1 - yl] = (kept[0] + others_half[1].astype(F32)).astype(BF)
    result[yl] = (kept[1] + others_half[0].astype(F32)).astype(BF)
    ends.append(moved(result, result_out, put.at[1]))
    mlp_sum.finish(mlp_ends)
    attn_sum.narrow()
    ends.extend(moved(mlp_ends[p], mlp_outs[p], put.at[2 + p]) for p in range(3))

    def along(start, gradient):
        weights = shard[:, :24, start : start + gradient.shape[2]]
        total = jnp.sum(weights * gradient, -1, keepdims=True)
        return total[0] + total[1]

    thin, half = attn_ends[0].shape[2], mlp_ends[0].shape[2]
    second = sum(
        along(3 * thin + 2 * half * p, one_sums[p]) + along(3 * thin + 2 * half * p + half, mlp_ends[p][...])
        for p in range(2)
    )
    attn_sum.finish(attn_ends)
    ends.extend(moved(attn_ends[p], attn_outs[p], put.at[5 + p]) for p in range(3))
    first = sum(along(thin * p, attn_ends[p][...]) for p in range(2))
    lane = lax.broadcasted_iota(jnp.int32, gain_part.shape, 1)
    gain_part[...] = jnp.where(lane == 0, first, second)
    swapped = sent(gain_part, gain_in, send.at[4], recv.at[4], partner())
    swapped.wait()
    gain_part[...] = gain_part[...] + gain_in[...]
    ends.append(moved(gain_part, gains_out, put.at[8]))
    for copy in ends:
        copy.wait()


def backward(x, grad_hidden, branch, n1t, q, kv, probs, mixed, wq, wkv, wo, tables, data, kept, away, shard, one_sums):
    rows, width = branch.shape
    third, wide = wq.shape[2], data[0].shape[-1]
    heads = (2, rows, third)
    weights = (2, width, third)
    half = (2, STEP, width)
    return call(
        backward_kernel,
        (x, grad_hidden, branch, n1t, q, kv, probs, mixed, wq, wkv, wo, tables, *data, kept, away, shard, *one_sums),
        [ANY] * 11 + [VMEM] + [ANY] * 8,
        [shaped((2, 24, wide), F32)] * 3
        + [shaped((2, 24, third), F32)] * 3
        + [shaped(half), shaped(half[1:], F32), shaped(half[1:]), shaped((24, 128), F32)],
        [ANY] * 10,
        [
            pltpu.VMEM(half, BF),
            pltpu.VMEM((SEQ, width), F32),
            pltpu.VMEM((rows, width), BF),
            pltpu.VMEM((width, rows), BF),
            pltpu.VMEM((width, rows), BF),
            pltpu.VMEM(heads, BF),
            pltpu.VMEM(heads, BF),
            pltpu.VMEM((4, 4, SEQ, SEQ), BF),
            pltpu.VMEM(heads, BF),
            pltpu.VMEM(weights, BF),
            pltpu.VMEM(weights, BF),
            pltpu.VMEM(weights, BF),
            pltpu.VMEM(heads, BF),
            pltpu.VMEM(heads, BF),
            pltpu.VMEM(heads, BF),
            pltpu.VMEM((SEQ, width), BF),
            pltpu.VMEM((SEQ, width), F32),
            pltpu.VMEM((SEQ, width), BF),
            pltpu.VMEM(half, F32),
            pltpu.VMEM(half[1:], BF),
            pltpu.VMEM(half, F32),
            pltpu.VMEM(half, BF),
            pltpu.VMEM(half, BF),
            *[pltpu.VMEM((4, 4, 4, 48, third), BF) for _ in range(3)],
            *Reduce.buffers(wide, PLANE_X),
            *Reduce.buffers(third, SPARE_Y),
            *Reduce.semaphores,
            *Reduce.semaphores,
            *[pltpu.VMEM((2, 24, wide), F32) for _ in range(3)],
            *[pltpu.VMEM((2, 24, third), F32) for _ in range(3)],
            pltpu.VMEM(shard.shape, F32),
            pltpu.VMEM((2, 2, 24, wide), F32),
            pltpu.VMEM((24, 128), F32),
            pltpu.VMEM((24, 128), F32),
            pltpu.SemaphoreType.DMA((15,)),
            pltpu.SemaphoreType.DMA((9,)),
            pltpu.SemaphoreType.DMA((5,)),
            pltpu.SemaphoreType.DMA((5,)),
        ],
        "attn_backward_reduce",
        3,
    )


def last_kernel(own, theirs, result_in, one, two, attn, gains_one, gains_two, gain_sums, outs):
    result, in_grad, dq, dk, dv, do, dg, du, dd, gain_one_grad, gain_two_grad = outs
    yl = lax.axis_index("yl")
    result[...] = result_in[...]
    in_grad[yl] = own[...]
    in_grad[1 - yl] = theirs[...].astype(F32)
    gain_one, gain_two = as_column(gains_one), as_column(gains_two)
    thin, half = attn[0].shape[2], two[0].shape[2]
    keys = [[], []]
    for c in range(2):
        dq[:, c * thin : (c + 1) * thin] = attn[0][c] * gain_one
        for k in range(2):
            keys[k].append(attn[1][c, :, k * (thin // 2) : (k + 1) * (thin // 2)] * gain_one)
        do[:, c * thin : (c + 1) * thin] = attn[2][c]
        for k, part in enumerate((one, two)):
            start = (2 * c + k) * half
            dg[:, start : start + half] = part[0][c] * gain_two
            du[:, start : start + half] = part[1][c] * gain_two
            dd[:, start : start + half] = part[2][c]
    dk[...] = jnp.concatenate(keys[0], -1)
    dv[...] = jnp.concatenate(keys[1], -1)
    lane = lax.broadcasted_iota(jnp.int32, gain_sums.shape, 1)
    grads = (gain_sums[...] / jnp.where(lane == 0, gain_one, gain_two)).T
    gain_one_grad[...] = grads[0:1, :24]
    gain_two_grad[...] = grads[1:2, :24]


def placed_outputs(own, theirs, result, one, two, attn, gains, gain_sums):
    width, thin, half = own.shape[1], attn[0].shape[2], two[0].shape[2]

    def kernel(*refs):
        last_kernel(*refs[:3], refs[3:6], refs[6:9], refs[9:12], *refs[12:15], refs[15:])

    return pl.pallas_call(
        kernel,
        out_shape=[
            shaped((2, STEP, width)),
            shaped((2, STEP, width), F32),
            shaped((24, 2 * thin), F32),
            shaped((24, thin), F32),
            shaped((24, thin), F32),
            shaped((24, 2 * thin), F32),
            shaped((24, 4 * half), F32),
            shaped((24, 4 * half), F32),
            shaped((24, 4 * half), F32),
            shaped((1, 24), F32),
            shaped((1, 24), F32),
        ],
        in_specs=[VMEM] * 15,
        out_specs=[VMEM] * 11,
        compiler_params=pltpu.CompilerParams(vmem_limit_bytes=VMEM_LIMIT),
        name="place_outputs",
    )(own, theirs, result, *one, *two, *attn, *gains, gain_sums)


def tables_for(count, heads, plain):
    half = HEAD // 2
    inverse = np.float32(ROPE_BASE) ** (-(np.arange(half, dtype=np.float32) * np.float32(2.0)) / np.float32(HEAD))
    angle = np.arange(count, dtype=np.float32)[:, None] * inverse.astype(np.float32)[None, :]
    cosine, sine = np.cos(angle), np.sin(angle)
    cosine = np.tile(np.concatenate([cosine, cosine], -1), (1, heads))
    sine = np.tile(np.concatenate([-sine, sine], -1), (1, heads))
    cosine = np.concatenate([cosine, np.ones((count, plain), np.float32)], -1)
    sine = np.concatenate([sine, np.zeros((count, plain), np.float32)], -1)
    return np.stack([cosine, sine]).astype(np.float32)


def body(
    inputs,
    out_grad,
    lengths,
    query_weight,
    key_matrix,
    value_matrix,
    output_weight,
    gate_weight,
    up_weight,
    down_weight,
    attn_gain,
    mlp_gain,
):
    width = inputs.shape[2]
    own_weights = (
        query_weight,
        key_matrix,
        value_matrix,
        output_weight.T,
        gate_weight,
        up_weight,
        down_weight.T,
    )
    gains = (attn_gain.reshape(1, -1), mlp_gain.reshape(1, -1))
    third, wide = query_weight.shape[1] // 2, gate_weight.shape[1] // 2
    tables = jnp.asarray(np.concatenate([tables_for(SEQ, 4, 0), tables_for(SEQ, 2, 2 * HEAD)]))

    results = forward(
        own_weights, gains, lengths.reshape(1, -1), inputs, out_grad, tables, third, wide
    )
    two, one = results[:3], results[3:6]
    x, n1t, q, kv, probs, mixed, hidden, n2, n2t, cot, cott = results[6:17]
    (wq, wkv, wo), grads, acts, shard = results[17:20], results[20:23], results[23:26], results[26]

    def joined(w):
        return w.reshape(2, width, -1)

    def blocked(w):
        return w.reshape(2, 4, 4, 48, -1)

    *one_sums, dg, du, dd, kept, away, branch, grad_hidden = middle(
        n2, cot, hidden, n2t, cott, one, two, acts, [blocked(w) for w in grads]
    )
    *sums, result, in_grad, in_grad_theirs, gain_sums = backward(
        x,
        grad_hidden,
        branch,
        n1t,
        q,
        kv,
        probs,
        mixed,
        joined(wq),
        joined(wkv),
        joined(wo),
        tables,
        [blocked(w) for w in (dg, du, dd)],
        kept,
        away,
        shard,
        one_sums[:2],
    )
    result, in_grad, dq, dk, dv, do, dg, du, dd, gain_one_grad, gain_two_grad = placed_outputs(
        in_grad, in_grad_theirs, result, one_sums, sums[:3], sums[3:], gains, gain_sums
    )
    return result, in_grad, dq, dk, dv, do.T, dg, du, dd.T, gain_one_grad.reshape(24), gain_two_grad.reshape(24)


def solution(mesh):
    fine = Mesh(mesh.devices.reshape(2, 4, 4, 2, 2), AXES)
    rows = P(None, AXES, None)
    into, out = P(DP, "yl"), P("yl", DP)
    return jax.shard_map(
        body,
        mesh=fine,
        in_specs=(rows, rows, P(None, DP), into, into, into, out, into, into, out, P(DP), P(DP)),
        out_specs=(rows, rows, into, into, into, out, into, into, out, P(DP), P(DP)),
        check_vma=False,
    )
```

```python
import math

import jax
import jax.numpy as jnp
import numpy as np
from jax import lax
from jax.experimental import pallas as pl
from jax.experimental.pallas import tpu as pltpu
from jax.sharding import Mesh
from jax.sharding import PartitionSpec as P

HEAD = 96
EPS = 1e-05
ROPE_BASE = 100000.0
AXES = ("yh", "x", "z", "core", "yl")
DP = ("yh", "x", "z", "core")
MESH = pl.DeviceIdType.MESH
BF = jnp.bfloat16
F32 = jnp.float32
EVEN = (("x", "y", "z"), ("y", "z", "x"), ("z", "x", "y"))
SPARE_Y = (("x", "z", "y"), ("y", "x", "z"), ("y", "z", "x"))
PLANE_Z = (("w", "x", "z"), ("w", "z", "x"), ("w", "x", "z"))
PLANE_X = (("w", "z", "x"), ("w", "x", "z"), ("w", "z", "x"))
PLANE = (("w", "x", "z"), ("w", "z", "x"), ("w", "x", "z"), ("w", "z", "x"))
SEQ = 256
ROWS = 512
STEP = 128
CHUNK = 256
VMEM_LIMIT = 62 * 1024 * 1024


def coordinates():
    x, z, yh, yl = (lax.axis_index(a) for a in ("x", "z", "yh", "yl"))
    return {"x": x, "z": z, "y": yh * 2 + yl, "w": yh}


def extent(axis):
    return 2 if axis == "w" else 4


def around(at, axis, by):
    return lax.rem(at[axis] + (by + 4), extent(axis))


def others(axis):
    return (1,) if axis == "w" else (1, -1, 2)


def peer(at, axis, by):
    value = around(at, axis, by)
    if axis == "y":
        return {"yh": value // 2, "yl": lax.rem(value, 2)}
    return {"yh" if axis == "w" else axis: value}


def sibling():
    return {"core": 1 - lax.axis_index("core")}


def partner():
    return {"yl": 1 - lax.axis_index("yl")}


def slot(at, axis, by=0):
    value = around(at, axis, by)
    return lax.rem(value, 2) * 2 + value // 2 if axis == "y" else value


def dimensions(order):
    return ("w" if "w" in order else "y", "x", "z")


def place(at, order, count, half=None, shifted=None):
    out = []
    for axis in dimensions(order):
        if axis in order[:count]:
            size = extent(axis)
            if half is not None and half[0] == axis:
                out.append(pl.ds(size // 2 * half[1], size // 2))
            else:
                out.append(pl.ds(0, size))
        else:
            out.append(slot(at, axis, shifted[1] if shifted is not None and shifted[0] == axis else 0))
    return tuple(out)


def greet(at):
    barrier = pltpu.get_barrier_semaphore()
    for axis in ("x", "y", "z"):
        for by in (1, -1, 2):
            pl.semaphore_signal(barrier, inc=1, device_id=peer(at, axis, by), device_id_type=MESH)
    pl.semaphore_signal(barrier, inc=1, device_id=sibling(), device_id_type=MESH)
    pl.semaphore_wait(barrier, 10)


def sent(src, dst, send, recv, device):
    copy = pltpu.make_async_remote_copy(
        src_ref=src, dst_ref=dst, send_sem=send, recv_sem=recv, device_id=device, device_id_type=MESH
    )
    copy.start()
    return copy


def moved(src, dst, sem):
    copy = pltpu.make_async_copy(src, dst, sem)
    copy.start()
    return copy


class Gather:
    @staticmethod
    def semaphores(orders):
        count = len(orders)
        shapes = (count,), (count, 2, 3), (count, 2, 3), (count, 2, 2, 3), (count, 2, 2, 3)
        return [pltpu.SemaphoreType.DMA(shape) for shape in shapes]

    def __init__(self, at, srcs, outs, semaphores, orders):
        self.at, self.srcs, self.outs, self.orders = at, srcs, outs, orders
        self.local, self.send, self.recv, self.ring_send, self.ring_recv = semaphores
        self.own, self.direct, self.ring = [], {}, {}

    def arrive(self, p, stage):
        for copy in self.direct.get((p, stage), ()):
            copy.wait_recv()
        if (p, stage, 0, 0) in self.ring:
            for d in range(2):
                self.ring[p, stage, d, 1 - d].wait_recv()
                self.ring[p, stage, d, 2].wait_recv()

    def to_all(self, stage):
        at = self.at
        for p, order in enumerate(self.orders):
            if stage:
                self.own[p].wait()
                self.arrive(p, 0)
            else:
                self.own.append(moved(self.srcs[p], self.outs[p].at[place(at, order, 0)], self.local.at[p]))
            group = self.outs[p].at[place(at, order, stage)]
            self.direct[p, stage] = [
                sent(
                    group if stage else self.srcs[p],
                    group,
                    self.send.at[p, stage, d],
                    self.recv.at[p, stage, d],
                    peer(at, order[stage], by),
                )
                for d, by in enumerate(others(order[stage]))
            ]

    def pass_on(self, p, stage, d, k, block):
        self.ring[p, stage, d, k] = sent(
            block,
            block,
            self.ring_send.at[p, stage - 1, d, k],
            self.ring_recv.at[p, stage - 1, d, k],
            peer(self.at, self.orders[p][stage], 1 - 2 * d),
        )

    def spread(self, stage, *pieces):
        for p in pieces or range(len(self.orders)):
            order = self.orders[p]
            if stage == 1:
                self.own[p].wait()
            self.arrive(p, stage - 1)
            for t in range(2):
                for d in range(2):
                    h = t if d == 0 else 1 - t
                    self.pass_on(p, stage, d, h, self.outs[p].at[place(self.at, order, stage, (order[0], h))])

    def forward(self, stage):
        for p, order in enumerate(self.orders):
            for d, by in enumerate((1, -1)):
                self.ring[p, stage, d, d].wait_recv()
                where = place(self.at, order, stage, (order[0], d), (order[stage], -by))
                self.pass_on(p, stage, d, 2, self.outs[p].at[where])

    def finish(self):
        for copies in self.direct.values():
            for copy in copies:
                copy.wait_send()
        for copy in self.ring.values():
            copy.wait_send()


class Reduce:
    @staticmethod
    def semaphores(orders):
        count = len(orders)
        shapes = (count, 3), *[(count, 2, 3)] * 4, (count, 2), (count, 2)
        return [pltpu.SemaphoreType.DMA(shape) for shape in shapes]

    @staticmethod
    def buffers(columns, orders):
        def per_piece(*shape):
            return [pltpu.VMEM(shape + (48, width), BF) for width in columns]

        size = extent(dimensions(orders[0])[0])
        return [
            *per_piece(2, size // 2, 4),
            *per_piece(size, 4),
            *per_piece(2, size // 2, 4),
            *per_piece(2, size, 4),
            *per_piece(3, size),
            *per_piece(3),
            *[pltpu.VMEM((48, width), F32) for width in columns],
        ]

    def __init__(self, at, data, buffers, semaphores, orders):
        self.at, self.data, self.orders = at, data, orders
        self.side, self.kept, self.far, self.near, self.second, self.third, self.sums = (
            buffers[len(orders) * k : len(orders) * (k + 1)] for k in range(7)
        )
        self.load, self.first_send, self.first_recv, self.send, self.recv, self.end_send, self.end_recv = semaphores
        self.loads, self.copies = {}, {}

    def left(self, p):
        order = self.orders[p]
        return [axis for axis in dimensions(order) if axis != order[2]]

    def inside(self, p, first, second=None):
        whole = slice(None) if second is None else second
        return (first, whole) if self.left(p)[0] == self.orders[p][1] else (whole, first)

    def start(self, *pieces):
        at, s, r = self.at, self.first_send, self.first_recv
        for p in pieces or range(len(self.orders)):
            order = self.orders[p]
            axis, cut = order[2], self.left(p)[0]
            size = extent(cut) // 2
            for d, by in enumerate((1, -1)):
                block = self.data[p].at[place(at, order, 2, (cut, d), (axis, 2))]
                self.copies[p, d, 0] = sent(block, self.far[p].at[d], s.at[p, d, 0], r.at[p, d, 0], peer(at, axis, by))
            for d, by in enumerate((1, -1)):
                h = 1 - d
                block = self.data[p].at[place(at, order, 2, (cut, h), (axis, by))]
                self.copies[p, d, 1] = sent(
                    block, self.near[p].at[d, pl.ds(size * h, size)], s.at[p, d, 1], r.at[p, d, 1], peer(at, axis, by)
                )
                block = self.data[p].at[place(at, order, 2, (cut, d), (axis, by))]
                self.loads[p, d] = moved(block, self.side[p].at[d], self.load.at[p, d])
            self.loads[p, 2] = moved(self.data[p].at[place(at, order, 2)], self.kept[p], self.load.at[p, 2])

    def relay(self):
        for p, order in enumerate(self.orders):
            size = extent(self.left(p)[0]) // 2
            for d, by in enumerate((1, -1)):
                self.loads[p, d].wait()
                self.copies[p, d, 0].wait_recv()
                side, far = self.side[p], self.far[p]

                @pl.loop(0, 4 * size)
                def _(i, d=d, side=side, far=far):
                    a, b = i // 4, lax.rem(i, 4)
                    side[d, a, b] = (side[d, a, b].astype(F32) + far[d, a, b].astype(F32)).astype(BF)

                self.copies[p, d, 2] = sent(
                    side.at[d],
                    self.near[p].at[d, pl.ds(size * d, size)],
                    self.first_send.at[p, d, 2],
                    self.first_recv.at[p, d, 2],
                    peer(self.at, order[2], by),
                )

    def spread(self):
        at = self.at
        for p, order in enumerate(self.orders):
            self.loads[p, 2].wait()
            for d in range(2):
                self.copies[p, d, 1].wait_recv()
                self.copies[p, d, 2].wait_recv()
            kept, near = self.kept[p], self.near[p]
            for d, by in enumerate((*others(order[1]), 0)):
                group = slot(at, order[1], by)

                @pl.loop(0, extent(order[0]))
                def _(i, p=p, kept=kept, near=near, group=group):
                    where = self.inside(p, group, i)
                    total = kept[where].astype(F32) + near[(0, *where)].astype(F32) + near[(1, *where)].astype(F32)
                    kept[where] = total.astype(BF)

                if by:
                    self.copies[p, "b", d] = sent(
                        kept.at[self.inside(p, group)],
                        self.second[p].at[d],
                        self.send.at[p, 0, d],
                        self.recv.at[p, 0, d],
                        peer(at, order[1], by),
                    )

    def narrow(self):
        at = self.at
        for p, order in enumerate(self.orders):
            for d in range(len(others(order[1]))):
                self.copies[p, "b", d].wait_recv()
            kept, second, mine = self.kept[p], self.second[p], slot(at, order[1])
            for d, by in enumerate((*others(order[0]), 0)):
                index = slot(at, order[0], by)
                where = self.inside(p, mine, index)
                total = kept[where].astype(F32)
                for k in range(3):
                    total = total + second[k, index].astype(F32)
                kept[where] = total.astype(BF)
                if by:
                    self.copies[p, "c", d] = sent(
                        kept.at[where],
                        self.third[p].at[d],
                        self.send.at[p, 1, d],
                        self.recv.at[p, 1, d],
                        peer(at, order[0], by),
                    )

    def finish(self, outs):
        at, core, ends = self.at, lax.axis_index("core"), []
        for p, order in enumerate(self.orders):
            total = self.kept[p][self.inside(p, slot(at, order[1]), slot(at, order[0]))].astype(F32)
            for d in range(len(others(order[0]))):
                self.copies[p, "c", d].wait_recv()
                total = total + self.third[p][d].astype(F32)
            self.sums[p][...] = total
            theirs = self.sums[p].at[pl.ds(pl.multiple_of(24 * (1 - core), 8), 24)]
            mine = self.sums[p].at[pl.ds(pl.multiple_of(24 * core, 8), 24)]
            ends.append(sent(theirs, outs[p].at[core], self.end_send.at[p, 0], self.end_recv.at[p, 0], sibling()))
            ends.append(moved(mine, outs[p].at[core], self.end_send.at[p, 1]))
        for copy in self.copies.values():
            copy.wait_send()
        for copy in ends:
            copy.wait()


def in_four(refs):
    half = refs[2].shape[-1] // 2
    lead = (slice(None),) * (len(refs[2].shape) - 1)
    return [refs[0], refs[1], *(refs[2].at[(*lead, pl.ds(k * half, half))] for k in range(2))]


def nn(left, right):
    return lax.dot_general(left, right, (((1,), (0,)), ((), ())), preferred_element_type=F32)


def nt(left, right):
    return lax.dot_general(left, right, (((1,), (1,)), ((), ())), preferred_element_type=F32)


def tn(left, right):
    return lax.dot_general(left, right, (((0,), (0,)), ((), ())), preferred_element_type=F32)


def inverse_rms(values):
    return lax.rsqrt(jnp.mean(values * values, -1, keepdims=True) + EPS)


def swap(values, first):
    width = values.shape[-1]
    return jnp.where(first, pltpu.roll(values, width - HEAD // 2, 1), pltpu.roll(values, HEAD // 2, 1))


def first_half(shape):
    return lax.rem(lax.broadcasted_iota(jnp.int32, shape, 1), HEAD) < HEAD // 2


def as_column(row):
    size = row.shape[1]
    square = jnp.broadcast_to(row[...].astype(F32), (size, size))
    diagonal = lax.broadcasted_iota(jnp.int32, (size, size), 0) == lax.broadcasted_iota(jnp.int32, (size, size), 1)
    return jnp.sum(jnp.where(diagonal, square, 0.0), -1, keepdims=True)


def rows_at(start, size):
    return pl.ds(pl.multiple_of(start, size), size)


ANY = pl.BlockSpec(memory_space=pl.ANY)
VMEM = pl.BlockSpec(memory_space=pltpu.VMEM)


def shaped(shape, kind=BF):
    return jax.ShapeDtypeStruct(shape, kind)


def call(kernel, operands, in_specs, results, out_specs, scratch, name, collective_id, **more):
    return pl.pallas_call(
        kernel,
        out_shape=results,
        in_specs=in_specs,
        out_specs=out_specs,
        scratch_shapes=scratch,
        compiler_params=pltpu.CompilerParams(
            collective_id=collective_id, has_side_effects=True, vmem_limit_bytes=VMEM_LIMIT
        ),
        name=name,
        **more,
    )(*operands)


def hidden_units(m, c, count, sub, n2, cot, weights, acts):
    rows = pl.ds(pl.multiple_of(m * ROWS + c * SEQ, SEQ), count * SEQ)
    columns = pl.ds(sub * CHUNK, CHUNK)
    gate_w, up_w, down_w = (w[..., columns].reshape(-1, CHUNK) for w in weights)
    gate = nn(n2[rows], gate_w)
    up = nn(n2[rows], up_w)
    sigma = 0.5 + 0.5 * jnp.tanh(0.5 * gate)
    silu = gate * sigma
    grad_active = nn(cot[m, pl.ds(c, count)].reshape(count * SEQ, -1), down_w)
    acts[0][rows, columns] = (silu * up).astype(BF)
    acts[1][rows, columns] = (grad_active * up * (sigma + silu * (1.0 - sigma))).astype(BF)
    acts[2][rows, columns] = (grad_active * silu).astype(BF)


def unit_gradients(n2t, cott, acts, staging, outs, sems, rows=None, added=False, written=True):
    whole, copies = slice(None) if rows is None else rows, []
    for k, (left, right, target) in enumerate(((n2t, acts[1], 0), (n2t, acts[2], 1), (cott, acts[0], 2))):
        for sub in range(2):
            columns = pl.ds(sub * CHUNK, CHUNK)
            value = nn(left[:, whole], right[whole, columns])
            if added:
                value = value + staging[2 * k + sub].astype(F32)
            staging[2 * k + sub] = value.astype(BF)
            if written:
                copies.append(moved(staging.at[2 * k + sub], outs[target].at[:, columns], sems.at[2 * k + sub]))
    return copies


def forward_kernel(third, wide, *refs):
    own_weights, gains_one, gains_two, lengths, xin, gin, tables = refs[:7], *refs[7:13]
    refs = refs[1:]
    full_two, full_one = refs[12:15], refs[15:18]
    (
        x_out, n1t_out, q_out, kv_out, probs_out, mixed_out, hidden_out, n2_out, n2t_out, cot_out, cott_out,
    ) = refs[18:29]
    attn_out, grads_out, acts_out, shard_out = refs[29:32], refs[32:35], refs[35:38], refs[38]
    refs = refs[1:]
    (
        shard, got_shard, packed, xs, gs, normed, q, kv, probs, mixed, hidden, n2, n2t, cott, part, arrived, n1t,
        valid, staging,
    ) = refs[38:57]
    full_attn, weights, acts = refs[57:60], refs[60:63], refs[63:66]
    attn_sems, one_sems, two_sems = refs[66:71], refs[71:76], refs[76:81]
    pair_send, pair_recv, row_send, row_recv, far_send, far_recv, own_sem, out_sem, put_sem = refs[81:]
    at = coordinates()
    core, yl = lax.axis_index("core"), lax.axis_index("yl")
    own_x = moved(xin.at[yl], xs.at[core, yl], own_sem.at[0])
    own_g = moved(gin, gs.at[:, core, yl], own_sem.at[1])

    query, key, value, output, *mlp_weights = (ref[...].astype(F32) for ref in own_weights)
    gain_one, gain_two = as_column(gains_one), as_column(gains_two)
    small = key.shape[1] // 2
    for c in range(2):
        thin = slice(c * small, (c + 1) * small)
        parts = [
            query[:, c * third : (c + 1) * third] * gain_one,
            jnp.concatenate([key[:, thin] * gain_one, value[:, thin] * gain_one], -1),
            output[:, c * third : (c + 1) * third],
            *(
                w[:, c * wide : (c + 1) * wide] * g
                for w, g in zip(mlp_weights, (gain_two, gain_two, jnp.ones_like(gain_two)))
            ),
        ]
        column = 0
        for part_value in parts:
            shard[c, :24, column : column + part_value.shape[1]] = part_value
            column += part_value.shape[1]
        lane = lax.broadcasted_iota(jnp.int32, (8, 2 * SEQ), 1)
        ends = jnp.where(lane < SEQ, lengths[:, 0:1], lengths[:, 1:2] + SEQ)
        shard[c, 24:, : 2 * SEQ] = jnp.where(lane < ends, 1.0, 0.0)
    greet(at)
    swap_shard = sent(shard.at[1 - core], got_shard, pair_send.at[0], pair_recv.at[0], sibling())

    rows = {}

    def exchange(k):
        ours, theirs, dst = (
            (xin.at[yl], xin.at[1 - yl], xs.at[core, yl]),
            (gin, gin, gs.at[:, core, yl]),
        )[k]
        rows[k, 0] = sent(theirs, dst, row_send.at[k, 0], row_recv.at[k, 0], partner())
        rows[k, 1] = sent(ours, dst, row_send.at[k, 1], row_recv.at[k, 1], sibling())

    def share(k):
        block = (xs.at[core, 1 - yl], gs.at[:, core, 1 - yl])[k]
        rows[k, 0].wait_recv()
        rows[k, 2] = sent(block, block, row_send.at[k, 2], row_recv.at[k, 2], sibling())

    def settle(k):
        (own_x, own_g)[k].wait()
        rows[k, 0].wait_send()
        rows[k, 1].wait()
        rows[k, 2].wait()

    swap_shard.wait()
    low, high = shard[core], got_shard[...]
    first, last = jnp.where(core == 0, low, high), jnp.where(core == 0, high, low)
    packed[...] = jnp.concatenate([first[:24], last[:24]], 0).astype(BF)
    for c, rows_of in enumerate((first, last)):
        for m in range(2):
            valid[m, c] = rows_of[24:32, m * SEQ : (m + 1) * SEQ]

    def pieces(start, size, step):
        return [packed.at[:, pl.ds(start + k * step, size)] for k in range(3)]

    half = wide // 2
    attn = Gather(at, pieces(0, third, third), full_attn, attn_sems, EVEN)
    one = Gather(at, pieces(3 * third, half, wide), weights, one_sems, PLANE_Z)
    two = Gather(at, pieces(3 * third + half, half, wide), full_two, two_sems, PLANE_X)
    attn.to_all(0)
    one.to_all(0)
    attn.to_all(1)
    one.spread(1)
    attn.spread(2, 0, 1)
    exchange(0)
    attn.spread(2, 2)
    two.to_all(0)
    one.forward(1)
    attn.forward(2)
    one.spread(2)
    share(0)
    settle(0)
    exchange(1)
    outs = [moved(xs, x_out, out_sem.at[0]), moved(shard, shard_out, out_sem.at[24])]

    @pl.loop(0, ROWS // STEP)
    def _(i):
        block = rows_at(i * STEP, STEP)
        values = xs[i // 2, lax.rem(i, 2)].astype(F32)
        normed[block] = (values * inverse_rms(values)).astype(BF)

    for p in range(2):
        attn.arrive(p, 2)
    two.spread(1)
    wq, wkv, wo = full_attn

    def weight(ref, y):
        return ref[pl.ds(2 * y, 2)].reshape(-1, third)

    @pl.loop(0, 2)
    def _(y):
        @pl.loop(0, ROWS // SEQ)
        def _(n):
            block = rows_at(n * SEQ, SEQ)
            left = normed[block]
            is_first = first_half((SEQ, third))
            for k, (w, result) in enumerate(((wq, q), (wkv, kv))):
                lin = nn(left, weight(w, y))
                result[y, block] = (lin * tables[2 * k] + swap(lin, is_first) * tables[2 * k + 1]).astype(BF)

    outs.append(moved(q, q_out, out_sem.at[5]))
    outs.append(moved(kv, kv_out, out_sem.at[6]))
    two.forward(1)
    one.forward(2)
    scale = 1.0 / math.sqrt(HEAD)

    @pl.loop(0, 4)
    def _(i):
        y, n = i // 2, lax.rem(i, 2)
        block = rows_at(n * SEQ, SEQ)
        t = lax.broadcasted_iota(jnp.int32, (SEQ, SEQ), 0)
        s = lax.broadcasted_iota(jnp.int32, (SEQ, SEQ), 1)
        keep = (s <= t) & (valid[yl, n, 0:1, :] > 0.5)
        queries, keys = q[y, block], kv[y, block]
        results = []
        for h in range(4):
            g = h // 2
            scores = nt(queries[:, h * HEAD : (h + 1) * HEAD], keys[:, g * HEAD : (g + 1) * HEAD]) * scale
            scores = jnp.where(keep, scores, -1e30)
            terms = jnp.exp(scores - jnp.max(scores, -1, keepdims=True))
            low_probs = (terms * (1.0 / jnp.sum(terms, -1, keepdims=True))).astype(BF)
            probs[i, h] = low_probs
            results.append(nn(low_probs, keys[:, (2 + g) * HEAD : (3 + g) * HEAD]))
        mixed[y, block] = jnp.concatenate(results, -1).astype(BF)

    outs.append(moved(probs, probs_out, out_sem.at[7]))
    outs.append(moved(mixed, mixed_out, out_sem.at[8]))
    two.spread(2)

    attn.arrive(2, 2)
    copies = []
    for i in range(ROWS // STEP):
        block = rows_at(lax.rem(2 * (1 - core) + i, 4) * STEP, STEP)
        part[block] = (nt(mixed[0, block], weight(wo, 0)) + nt(mixed[1, block], weight(wo, 1))).astype(BF)
        copies.append(sent(part.at[block], arrived.at[block], pair_send.at[1 + i], pair_recv.at[1 + i], sibling()))
    second_rows = {}
    mine, theirs = yl * ROWS, (1 - yl) * ROWS
    for i in range(ROWS // STEP):
        copies[(i + 2) % 4 if i < 2 else i - 2].wait_send()
        copies[i].wait_recv()
        number = lax.rem(2 * core + i, 4)
        block = rows_at(number * STEP, STEP)
        values = xs[number // 2, lax.rem(number, 2)].astype(F32) + (
            part[block].astype(F32) + arrived[block].astype(F32)
        )
        hidden[block] = values
        target = rows_at(mine + number * STEP, STEP)
        n2[target] = (values * inverse_rms(values)).astype(BF)
        if i < 2:
            second_rows[0, i] = sent(n2.at[target], n2.at[target], far_send.at[0, i], far_recv.at[0, i], partner())
    outs.append(moved(hidden.at[rows_at(core * SEQ, SEQ)], hidden_out, out_sem.at[9]))
    two.forward(2)
    attn.finish()
    outs.extend(moved(full_attn[p], attn_out[p], out_sem.at[2 + p]) for p in range(3))
    share(1)
    settle(1)

    for m in range(2):
        for c in range(2):
            for h in range(2):
                mask = valid[m, c][:, h * STEP : (h + 1) * STEP].T[:, 0:1]
                gs[m, c, h] = (gs[m, c, h].astype(F32) * mask).astype(BF)
    outs.append(moved(gs, cot_out, out_sem.at[10]))

    for p in range(3):
        one.arrive(p, 2)
    one.finish()
    outs.extend(moved(weights[p], full_one[p], out_sem.at[11 + p]) for p in range(3))
    mine_rows, their_rows = rows_at(mine, ROWS), rows_at(theirs, ROWS)
    for sub in range(2):
        hidden_units(yl, 0, 2, sub, n2, gs, weights, acts)
    outs.extend(moved(acts[p].at[mine_rows], acts_out[p].at[mine_rows], out_sem.at[15 + p]) for p in range(3))
    outs.append(moved(n2.at[mine_rows], n2_out.at[mine_rows], out_sem.at[18]))
    for m in range(2):
        for c in range(2):
            for h in range(2):
                cott[:, pl.ds(m * ROWS + (2 * c + h) * STEP, STEP)] = gs[m, c, h].T
    outs.append(moved(cott, cott_out, out_sem.at[14]))
    for i in range(ROWS // STEP):
        block = rows_at(mine + i * STEP, STEP)
        n2t[:, block] = n2[block].T
    unit_gradients(n2t, cott, acts, staging, grads_out, put_sem, mine_rows, written=False)
    n1t[...] = normed[...].T
    outs.append(moved(n1t, n1t_out, out_sem.at[1]))

    for i in range(2):
        second_rows[0, i].wait_recv()
        block = rows_at(theirs + (2 * core + i) * STEP, STEP)
        second_rows[1, i] = sent(n2.at[block], n2.at[block], far_send.at[1, i], far_recv.at[1, i], sibling())
    for sub in range(2):
        hidden_units(1 - yl, core, 1, sub, n2, gs, weights, acts)
    for i in range(2):
        second_rows[0, i].wait_send()
        second_rows[1, i].wait()
    for sub in range(2):
        hidden_units(1 - yl, 1 - core, 1, sub, n2, gs, weights, acts)
    outs.extend(moved(acts[p].at[their_rows], acts_out[p].at[their_rows], out_sem.at[20 + p]) for p in range(3))
    outs.append(moved(n2.at[their_rows], n2_out.at[their_rows], out_sem.at[23]))
    for i in range(ROWS // STEP):
        block = rows_at(theirs + i * STEP, STEP)
        n2t[:, block] = n2[block].T
    outs.append(moved(n2t, n2t_out, out_sem.at[19]))
    outs.extend(unit_gradients(n2t, cott, acts, staging, grads_out, put_sem, their_rows, added=True))
    for p in range(3):
        two.arrive(p, 2)
    two.finish()
    for copy in outs:
        copy.wait()


def forward(own_weights, gains, lengths, xin, gin, tables, third, wide):
    width = xin.shape[2]
    rows = (ROWS, width)
    both = (2 * ROWS, width)
    heads = (2, ROWS, third)
    square = (4, 4, SEQ, SEQ)
    half = wide // 2
    piece = (2, 4, 4, 48, half)
    return call(
        lambda *refs: forward_kernel(third, wide, *refs),
        (*own_weights, *gains, lengths, xin, gin, tables),
        [VMEM] * 10 + [ANY, ANY, VMEM],
        [shaped(piece)] * 6
        + [
            shaped((2, 2, 128, width)),
            shaped(rows[::-1]),
            shaped(heads),
            shaped(heads),
            shaped(square),
            shaped(heads),
            shaped((SEQ, width), F32),
            shaped(both),
            shaped(both[::-1]),
            shaped((2, 2, 2, 128, width)),
            shaped(both[::-1]),
        ]
        + [shaped((4, 4, 4, 48, third))] * 3
        + [shaped((width, half))] * 3
        + [shaped((2 * ROWS, half))] * 3
        + [shaped((2, 32, 3 * third + 3 * wide), F32)],
        [ANY] * 27,
        [
            pltpu.VMEM((2, 32, 3 * third + 3 * wide), F32),
            pltpu.VMEM((32, 3 * third + 3 * wide), F32),
            pltpu.VMEM((48, 3 * third + 3 * wide), BF),
            pltpu.VMEM((2, 2, 128, width), BF),
            pltpu.VMEM((2, 2, 2, 128, width), BF),
            pltpu.VMEM(rows, BF),
            pltpu.VMEM(heads, BF),
            pltpu.VMEM(heads, BF),
            pltpu.VMEM(square, BF),
            pltpu.VMEM(heads, BF),
            pltpu.VMEM(rows, F32),
            pltpu.VMEM(both, BF),
            pltpu.VMEM(both[::-1], BF),
            pltpu.VMEM(both[::-1], BF),
            pltpu.VMEM(rows, BF),
            pltpu.VMEM(rows, BF),
            pltpu.VMEM(rows[::-1], BF),
            pltpu.VMEM((2, 2, 8, SEQ), F32),
            pltpu.VMEM((6, width, CHUNK), BF),
            *[pltpu.VMEM((4, 4, 4, 48, third), BF) for _ in range(3)],
            *[pltpu.VMEM(piece, BF) for _ in range(3)],
            *[pltpu.VMEM((2 * ROWS, half), BF) for _ in range(3)],
            *Gather.semaphores(EVEN),
            *Gather.semaphores(PLANE_Z),
            *Gather.semaphores(PLANE_X),
            pltpu.SemaphoreType.DMA((5,)),
            pltpu.SemaphoreType.DMA((5,)),
            pltpu.SemaphoreType.DMA((2, 3)),
            pltpu.SemaphoreType.DMA((2, 3)),
            pltpu.SemaphoreType.DMA((2, 2)),
            pltpu.SemaphoreType.DMA((2, 2)),
            pltpu.SemaphoreType.DMA((2,)),
            pltpu.SemaphoreType.DMA((25,)),
            pltpu.SemaphoreType.DMA((6,)),
        ],
        "gather_attn_forward_mlp",
        1,
    )


def middle_kernel(*refs):
    n2_in, cot_in, hidden_in, n2t_in, cott_in = refs[:5]
    one_in, two_in, acts_in, data = refs[5:8], refs[8:11], refs[11:14], refs[14:17]
    sums_out, grads_out = refs[17:20], refs[20:23]
    kept_out, away_out, branch_out, grad_hidden_out = refs[23:27]
    (
        n2, cot, hidden, n2t, cott, staging, to_pair, from_pair, whole, from_far, keep, halves, to_far, branch, gh,
    ) = refs[27:42]
    one, two, acts_one, acts_two = refs[42:45], refs[45:48], refs[48:51], refs[51:54]
    buffers, reduce_sems = refs[54:82], refs[82:89]
    load, put, put_sem, pair_send, pair_recv, part_send, part_recv, far_send, far_recv = refs[89:]
    core, yl = lax.axis_index("core"), lax.axis_index("yl")
    at = coordinates()
    order = (
        (n2_in, n2),
        (two_in[0], two[0]),
        (two_in[1], two[1]),
        (cot_in, cot),
        (two_in[2], two[2]),
        *zip(acts_in[1:], acts_one[1:]),
        *zip(one_in[:2], one[:2]),
        (acts_in[0], acts_one[0]),
        (one_in[2], one[2]),
        (n2t_in, n2t),
        (cott_in, cott),
        (hidden_in, hidden),
    )
    loads = [moved(src, dst, load.at[k]) for k, (src, dst) in enumerate(order)]
    greet(at)
    total = Reduce(at, in_four(data), buffers, reduce_sems, PLANE)
    total.start()
    for k in range(5):
        loads[k].wait()
    for sub in range(2):
        hidden_units(1 - yl, 0, 2, sub, n2, cot, two, acts_two)
    for k in range(5, 11):
        loads[k].wait()

    def weight(ref):
        return ref[...].reshape(n2.shape[1], -1)

    def grad_rows(m, c):
        rows = rows_at(m * ROWS + c * SEQ, SEQ)
        return (nt(acts_one[1][rows], weight(one[0])) + nt(acts_one[2][rows], weight(one[1]))) + (
            nt(acts_two[1][rows], weight(two[0])) + nt(acts_two[2][rows], weight(two[1]))
        )

    def out_rows(m, c):
        rows = rows_at(m * ROWS + c * SEQ, SEQ)
        return nt(acts_one[0][rows], weight(one[2])) + nt(acts_two[0][rows], weight(two[2]))

    pair, far, shared = {}, {}, []

    def to_sibling(k, value):
        to_pair[k] = value.astype(BF)
        pair[k] = sent(to_pair.at[k], from_pair.at[k], pair_send.at[k], pair_recv.at[k], sibling())

    blocks = [pl.ds(i * STEP, STEP) for i in range(2)]
    to_pair[0] = grad_rows(1 - yl, 1 - core).astype(BF)
    for i, rows in enumerate(blocks):
        pair["far", i] = sent(
            to_pair.at[0, rows], from_pair.at[0, rows], part_send.at[0, i], part_recv.at[0, i], sibling()
        )
    keep[...] = grad_rows(1 - yl, core)
    for i, rows in enumerate(blocks):
        pair["far", i].wait_recv()
        whole[rows] = (keep[rows] + from_pair[0, rows].astype(F32)).astype(BF)
        far[i] = sent(whole.at[rows], from_far.at[rows], far_send.at[i], far_recv.at[i], partner())
    total.relay()
    for sub in range(2):
        hidden_units(yl, 0, 2, sub, n2, cot, two, acts_two)
    to_sibling(1, grad_rows(yl, 1 - core))
    keep[...] = grad_rows(yl, core)
    to_sibling(2, out_rows(1 - yl, 1 - core))
    to_sibling(3, out_rows(yl, 1 - core))
    for k in range(11, 14):
        loads[k].wait()
    total.spread()
    outs = unit_gradients(n2t, cott, acts_two, staging, grads_out, put_sem)
    total.narrow()

    for k, m in ((2, 1 - yl), (3, yl)):
        pair[k].wait_recv()
        value = out_rows(m, core) + from_pair[k].astype(F32)
        if k == 3:
            value = value + hidden[...]
        halves[k - 2] = value.reshape(2, STEP, -1)
        to_far[k - 2] = halves[k - 2, 1 - yl].astype(BF)
        outs.append(moved(halves.at[k - 2, yl], kept_out.at[k - 2], put.at[k]))
        outs.append(moved(to_far.at[k - 2], away_out.at[k - 2], put.at[k + 2]))
    pair[1].wait_recv()

    for i, rows in enumerate(blocks):
        far[i].wait_recv()
        grad = keep[rows] + (from_pair[1, rows].astype(F32) + from_far[rows].astype(F32))
        values = hidden[rows]
        inverse = inverse_rms(values)
        unit = values * inverse
        back = inverse * (grad - unit * jnp.mean(grad * unit, -1, keepdims=True))
        gh[rows] = cot[yl, core, i].astype(F32) + back
        branch[rows] = gh[rows].astype(BF)
        target = rows_at(core * SEQ + i * STEP, STEP)
        shared.append(
            sent(branch.at[rows], branch_out.at[target], part_send.at[1, i], part_recv.at[1, i], sibling())
        )
        outs.append(moved(branch.at[rows], branch_out.at[target], put.at[6 + i]))
    outs.append(moved(gh, grad_hidden_out, put.at[0]))
    total.finish(in_four(sums_out))
    for copy in shared:
        copy.wait()
    for copy in (*pair.values(), *far.values()):
        copy.wait_send()
    for copy in outs:
        copy.wait()


def middle(n2, cot, hidden, n2t, cott, one, two, acts, data):
    rows, width = n2.shape
    half = one[0].shape[-1]
    block = (SEQ, width)
    return call(
        middle_kernel,
        (n2, cot, hidden, n2t, cott, *one, *two, *acts, *data),
        [ANY] * 17,
        [shaped((2, 24, half), F32)] * 3
        + [shaped((width, half))] * 3
        + [
            shaped((2, STEP, width), F32),
            shaped((2, STEP, width)),
            shaped((ROWS, width)),
            shaped(block, F32),
        ],
        [ANY] * 10,
        [
            pltpu.VMEM((rows, width), BF),
            pltpu.VMEM(cot.shape, BF),
            pltpu.VMEM(block, F32),
            pltpu.VMEM((width, rows), BF),
            pltpu.VMEM((width, rows), BF),
            pltpu.VMEM((6, width, CHUNK), BF),
            pltpu.VMEM((4,) + block, BF),
            pltpu.VMEM((4,) + block, BF),
            pltpu.VMEM(block, BF),
            pltpu.VMEM(block, BF),
            pltpu.VMEM(block, F32),
            pltpu.VMEM((2, 2, STEP, width), F32),
            pltpu.VMEM((2, STEP, width), BF),
            pltpu.VMEM(block, BF),
            pltpu.VMEM(block, F32),
            *[pltpu.VMEM(one[0].shape, BF) for _ in range(6)],
            *[pltpu.VMEM((rows, half), BF) for _ in range(6)],
            *Reduce.buffers((half, half, half // 2, half // 2), PLANE),
            *Reduce.semaphores(PLANE),
            pltpu.SemaphoreType.DMA((14,)),
            pltpu.SemaphoreType.DMA((8,)),
            pltpu.SemaphoreType.DMA((6,)),
            pltpu.SemaphoreType.DMA((4,)),
            pltpu.SemaphoreType.DMA((4,)),
            pltpu.SemaphoreType.DMA((2, 2)),
            pltpu.SemaphoreType.DMA((2, 2)),
            pltpu.SemaphoreType.DMA((2,)),
            pltpu.SemaphoreType.DMA((2,)),
        ],
        "mlp_reduce",
        2,
    )


def backward_kernel(*refs):
    xall, grad_hidden_in, branch_in, n1t_in, q_in, kv_in, probs_in, mixed_in, wq_in, wkv_in, wo_in, tables = refs[:12]
    data, kept_in, away, shard_in, one_in = refs[12:15], *refs[15:18], refs[18:20]
    refs = refs[3:]
    mlp_outs, attn_outs, result_out, in_grad_out, from_partner = refs[17:20], refs[20:23], *refs[23:26]
    gains_out = refs[26]
    refs = refs[1:]
    (
        xs, gh, branch, branch_t, normed_t, q, kv, probs, mixed, wq, wkv, wo,
        grad_mixed, dq, dkv, part, keep_part, arrived, in_grad, for_partner, kept, others_half, result,
    ) = refs[26:49]
    attn_grads = refs[49:52]
    mlp_buffers, attn_buffers = refs[52:80], refs[80:101]
    mlp_sems, attn_sems = refs[101:108], refs[108:115]
    mlp_ends, attn_ends, shard, one_sums, gain_part, gain_in = refs[115:118], refs[118:121], *refs[121:125]
    load, put, send, recv = refs[125:]
    at = coordinates()
    core, yl = lax.axis_index("core"), lax.axis_index("yl")
    loads = [
        moved(src, dst, load.at[k])
        for k, (src, dst) in enumerate(
            (
                (branch_in, branch),
                (wo_in, wo),
                (mixed_in, mixed),
                (q_in, q),
                (kv_in, kv),
                (probs_in, probs),
                (n1t_in, normed_t),
                (wq_in, wq),
                (wkv_in, wkv),
                (grad_hidden_in, gh),
                (xall.at[core], xs),
                (kept_in, kept),
                (shard_in, shard),
                (one_in[0], one_sums.at[0]),
                (one_in[1], one_sums.at[1]),
            )
        )
    ]
    greet(at)
    mlp_sum = Reduce(at, in_four(data), mlp_buffers, mlp_sems, PLANE)
    attn_sum = Reduce(at, attn_grads, attn_buffers, attn_sems, SPARE_Y)
    mlp_sum.start()
    finals = [sent(away.at[k], others_half.at[k], send.at[2 + k], recv.at[2 + k], partner()) for k in range(2)]
    for k in range(2):
        loads[k].wait()
    for y in range(2):
        grad_mixed[y] = nn(branch[...], wo[y]).astype(BF)
    for k in range(2, 6):
        loads[k].wait()
    scale = 1.0 / math.sqrt(HEAD)

    def attention(i):
        y, n = i // 2, lax.rem(i, 2)
        rows = rows_at(n * SEQ, SEQ)
        queries, keys, grads = q[y, rows], kv[y, rows], grad_mixed[y, rows]
        grad_q, grad_k, grad_v = [], [None, None], [None, None]
        for h in range(4):
            g = h // 2
            key = keys[:, g * HEAD : (g + 1) * HEAD]
            value = keys[:, (2 + g) * HEAD : (3 + g) * HEAD]
            query = queries[:, h * HEAD : (h + 1) * HEAD]
            grad = grads[:, h * HEAD : (h + 1) * HEAD]
            low = probs[i, h]
            prob = low.astype(F32)
            grad_probs = nt(grad, value)
            grad_scores = (prob * (grad_probs - jnp.sum(grad_probs * prob, -1, keepdims=True))).astype(BF)
            grad_q.append(nn(grad_scores, key) * scale)
            back_k = tn(grad_scores, query) * scale
            back_v = tn(low, grad)
            grad_k[g] = back_k if grad_k[g] is None else grad_k[g] + back_k
            grad_v[g] = back_v if grad_v[g] is None else grad_v[g] + back_v
        first = first_half((SEQ, 4 * HEAD))
        for k, (pieces, target) in enumerate(((grad_q, dq), (grad_k + grad_v, dkv))):
            values = jnp.concatenate(pieces, -1)
            target[y, rows] = (values * tables[2 * k] - swap(values, first) * tables[2 * k + 1]).astype(BF)

    pl.loop(0, 2)(attention)
    mlp_sum.relay()
    pl.loop(2, 4)(attention)
    loads[6].wait()

    def weight_grad(p, left, right):
        for y in range(2):
            target = attn_grads[p].at[pl.ds(2 * y, 2)]
            target[...] = nn(left[...], right[y]).astype(BF).reshape(target.shape)
        attn_sum.start(p)

    weight_grad(0, normed_t, dq)
    weight_grad(1, normed_t, dkv)
    mlp_sum.spread()
    branch_t[...] = branch[...].T
    weight_grad(2, branch_t, mixed)
    for k in range(7, 15):
        loads[k].wait()

    def back(start):
        rows = rows_at(start, SEQ)
        return (nt(dq[0, rows], wq[0]) + nt(dq[1, rows], wq[1])) + (nt(dkv[0, rows], wkv[0]) + nt(dkv[1, rows], wkv[1]))

    part[...] = back((1 - core) * SEQ).astype(BF)
    pair = sent(part, arrived, send.at[0], recv.at[0], sibling())
    attn_sum.relay()
    keep_part[...] = back(core * SEQ)
    mlp_sum.narrow()
    pair.wait()

    @pl.loop(0, SEQ // STEP)
    def _(i):
        rows = rows_at(i * STEP, STEP)
        grad = keep_part[rows] + arrived[rows].astype(F32)
        values = xs[i].astype(F32)
        inverse = inverse_rms(values)
        unit = values * inverse
        change = inverse * (grad - unit * jnp.mean(grad * unit, -1, keepdims=True))
        in_grad[i] = gh[rows] + change

    for_partner[...] = in_grad[1 - yl].astype(BF)
    ends = [
        moved(in_grad.at[yl], in_grad_out, put.at[0]),
        sent(for_partner, from_partner, send.at[1], recv.at[1], partner()),
    ]
    attn_sum.spread()
    for copy in finals:
        copy.wait()
    result[1 - yl] = (kept[0] + others_half[1].astype(F32)).astype(BF)
    result[yl] = (kept[1] + others_half[0].astype(F32)).astype(BF)
    ends.append(moved(result, result_out, put.at[1]))
    mlp_sum.finish(in_four(mlp_ends))
    attn_sum.narrow()
    ends.extend(moved(mlp_ends[p], mlp_outs[p], put.at[2 + p]) for p in range(3))

    def along(start, gradient):
        weights = shard[:, :24, start : start + gradient.shape[2]]
        total = jnp.sum(weights * gradient, -1, keepdims=True)
        return total[0] + total[1]

    thin, half = attn_ends[0].shape[2], mlp_ends[0].shape[2]
    second = sum(
        along(3 * thin + 2 * half * p, one_sums[p]) + along(3 * thin + 2 * half * p + half, mlp_ends[p][...])
        for p in range(2)
    )
    attn_sum.finish(attn_ends)
    ends.extend(moved(attn_ends[p], attn_outs[p], put.at[5 + p]) for p in range(3))
    first = sum(along(thin * p, attn_ends[p][...]) for p in range(2))
    lane = lax.broadcasted_iota(jnp.int32, gain_part.shape, 1)
    gain_part[...] = jnp.where(lane == 0, first, second)
    swapped = sent(gain_part, gain_in, send.at[4], recv.at[4], partner())
    swapped.wait()
    gain_part[...] = gain_part[...] + gain_in[...]
    ends.append(moved(gain_part, gains_out, put.at[8]))
    for copy in ends:
        copy.wait()


def backward(x, grad_hidden, branch, n1t, q, kv, probs, mixed, wq, wkv, wo, tables, data, kept, away, shard, one_sums):
    rows, width = branch.shape
    third, wide = wq.shape[2], data[0].shape[-1]
    heads = (2, rows, third)
    weights = (2, width, third)
    half = (2, STEP, width)
    return call(
        backward_kernel,
        (x, grad_hidden, branch, n1t, q, kv, probs, mixed, wq, wkv, wo, tables, *data, kept, away, shard, *one_sums),
        [ANY] * 11 + [VMEM] + [ANY] * 8,
        [shaped((2, 24, wide), F32)] * 3
        + [shaped((2, 24, third), F32)] * 3
        + [shaped(half), shaped(half[1:], F32), shaped(half[1:]), shaped((24, 128), F32)],
        [ANY] * 10,
        [
            pltpu.VMEM(half, BF),
            pltpu.VMEM((SEQ, width), F32),
            pltpu.VMEM((rows, width), BF),
            pltpu.VMEM((width, rows), BF),
            pltpu.VMEM((width, rows), BF),
            pltpu.VMEM(heads, BF),
            pltpu.VMEM(heads, BF),
            pltpu.VMEM((4, 4, SEQ, SEQ), BF),
            pltpu.VMEM(heads, BF),
            pltpu.VMEM(weights, BF),
            pltpu.VMEM(weights, BF),
            pltpu.VMEM(weights, BF),
            pltpu.VMEM(heads, BF),
            pltpu.VMEM(heads, BF),
            pltpu.VMEM(heads, BF),
            pltpu.VMEM((SEQ, width), BF),
            pltpu.VMEM((SEQ, width), F32),
            pltpu.VMEM((SEQ, width), BF),
            pltpu.VMEM(half, F32),
            pltpu.VMEM(half[1:], BF),
            pltpu.VMEM(half, F32),
            pltpu.VMEM(half, BF),
            pltpu.VMEM(half, BF),
            *[pltpu.VMEM((4, 4, 4, 48, third), BF) for _ in range(3)],
            *Reduce.buffers((wide, wide, wide // 2, wide // 2), PLANE),
            *Reduce.buffers((third,) * 3, SPARE_Y),
            *Reduce.semaphores(PLANE),
            *Reduce.semaphores(SPARE_Y),
            *[pltpu.VMEM((2, 24, wide), F32) for _ in range(3)],
            *[pltpu.VMEM((2, 24, third), F32) for _ in range(3)],
            pltpu.VMEM(shard.shape, F32),
            pltpu.VMEM((2, 2, 24, wide), F32),
            pltpu.VMEM((24, 128), F32),
            pltpu.VMEM((24, 128), F32),
            pltpu.SemaphoreType.DMA((15,)),
            pltpu.SemaphoreType.DMA((9,)),
            pltpu.SemaphoreType.DMA((5,)),
            pltpu.SemaphoreType.DMA((5,)),
        ],
        "attn_backward_reduce",
        3,
    )


def last_kernel(own, theirs, result_in, one, two, attn, gains_one, gains_two, gain_sums, outs):
    result, in_grad, dq, dk, dv, do, dg, du, dd, gain_one_grad, gain_two_grad = outs
    yl = lax.axis_index("yl")
    result[...] = result_in[...]
    in_grad[yl] = own[...]
    in_grad[1 - yl] = theirs[...].astype(F32)
    gain_one, gain_two = as_column(gains_one), as_column(gains_two)
    thin, half = attn[0].shape[2], two[0].shape[2]
    keys = [[], []]
    for c in range(2):
        dq[:, c * thin : (c + 1) * thin] = attn[0][c] * gain_one
        for k in range(2):
            keys[k].append(attn[1][c, :, k * (thin // 2) : (k + 1) * (thin // 2)] * gain_one)
        do[:, c * thin : (c + 1) * thin] = attn[2][c]
        for k, part in enumerate((one, two)):
            start = (2 * c + k) * half
            dg[:, start : start + half] = part[0][c] * gain_two
            du[:, start : start + half] = part[1][c] * gain_two
            dd[:, start : start + half] = part[2][c]
    dk[...] = jnp.concatenate(keys[0], -1)
    dv[...] = jnp.concatenate(keys[1], -1)
    lane = lax.broadcasted_iota(jnp.int32, gain_sums.shape, 1)
    grads = (gain_sums[...] / jnp.where(lane == 0, gain_one, gain_two)).T
    gain_one_grad[...] = grads[0:1, :24]
    gain_two_grad[...] = grads[1:2, :24]


def placed_outputs(own, theirs, result, one, two, attn, gains, gain_sums):
    width, thin, half = own.shape[1], attn[0].shape[2], two[0].shape[2]

    def kernel(*refs):
        last_kernel(*refs[:3], refs[3:6], refs[6:9], refs[9:12], *refs[12:15], refs[15:])

    return pl.pallas_call(
        kernel,
        out_shape=[
            shaped((2, STEP, width)),
            shaped((2, STEP, width), F32),
            shaped((24, 2 * thin), F32),
            shaped((24, thin), F32),
            shaped((24, thin), F32),
            shaped((24, 2 * thin), F32),
            shaped((24, 4 * half), F32),
            shaped((24, 4 * half), F32),
            shaped((24, 4 * half), F32),
            shaped((1, 24), F32),
            shaped((1, 24), F32),
        ],
        in_specs=[VMEM] * 15,
        out_specs=[VMEM] * 11,
        compiler_params=pltpu.CompilerParams(vmem_limit_bytes=VMEM_LIMIT),
        name="place_outputs",
    )(own, theirs, result, *one, *two, *attn, *gains, gain_sums)


def tables_for(count, heads, plain):
    half = HEAD // 2
    inverse = np.float32(ROPE_BASE) ** (-(np.arange(half, dtype=np.float32) * np.float32(2.0)) / np.float32(HEAD))
    angle = np.arange(count, dtype=np.float32)[:, None] * inverse.astype(np.float32)[None, :]
    cosine, sine = np.cos(angle), np.sin(angle)
    cosine = np.tile(np.concatenate([cosine, cosine], -1), (1, heads))
    sine = np.tile(np.concatenate([-sine, sine], -1), (1, heads))
    cosine = np.concatenate([cosine, np.ones((count, plain), np.float32)], -1)
    sine = np.concatenate([sine, np.zeros((count, plain), np.float32)], -1)
    return np.stack([cosine, sine]).astype(np.float32)


def body(
    inputs,
    out_grad,
    lengths,
    query_weight,
    key_matrix,
    value_matrix,
    output_weight,
    gate_weight,
    up_weight,
    down_weight,
    attn_gain,
    mlp_gain,
):
    width = inputs.shape[2]
    own_weights = (
        query_weight,
        key_matrix,
        value_matrix,
        output_weight.T,
        gate_weight,
        up_weight,
        down_weight.T,
    )
    gains = (attn_gain.reshape(1, -1), mlp_gain.reshape(1, -1))
    third, wide = query_weight.shape[1] // 2, gate_weight.shape[1] // 2
    tables = jnp.asarray(np.concatenate([tables_for(SEQ, 4, 0), tables_for(SEQ, 2, 2 * HEAD)]))

    results = forward(
        own_weights, gains, lengths.reshape(1, -1), inputs, out_grad, tables, third, wide
    )
    two, one = results[:3], results[3:6]
    x, n1t, q, kv, probs, mixed, hidden, n2, n2t, cot, cott = results[6:17]
    (wq, wkv, wo), grads, acts, shard = results[17:20], results[20:23], results[23:26], results[26]

    def joined(w):
        return w.reshape(2, width, -1)

    def blocked(w):
        return w.reshape(2, 4, 4, 48, -1)

    *one_sums, dg, du, dd, kept, away, branch, grad_hidden = middle(
        n2, cot, hidden, n2t, cott, one, two, acts, [blocked(w) for w in grads]
    )
    *sums, result, in_grad, in_grad_theirs, gain_sums = backward(
        x,
        grad_hidden,
        branch,
        n1t,
        q,
        kv,
        probs,
        mixed,
        joined(wq),
        joined(wkv),
        joined(wo),
        tables,
        [blocked(w) for w in (dg, du, dd)],
        kept,
        away,
        shard,
        one_sums[:2],
    )
    result, in_grad, dq, dk, dv, do, dg, du, dd, gain_one_grad, gain_two_grad = placed_outputs(
        in_grad, in_grad_theirs, result, one_sums, sums[:3], sums[3:], gains, gain_sums
    )
    return result, in_grad, dq, dk, dv, do.T, dg, du, dd.T, gain_one_grad.reshape(24), gain_two_grad.reshape(24)


def solution(mesh):
    fine = Mesh(mesh.devices.reshape(2, 4, 4, 2, 2), AXES)
    rows = P(None, AXES, None)
    into, out = P(DP, "yl"), P("yl", DP)
    return jax.shard_map(
        body,
        mesh=fine,
        in_specs=(rows, rows, P(None, DP), into, into, into, out, into, into, out, P(DP), P(DP)),
        out_specs=(rows, rows, into, into, into, out, into, into, out, P(DP), P(DP)),
        check_vma=False,
    )
```

```python
import math

import jax
import jax.numpy as jnp
import numpy as np
from jax import lax
from jax.experimental import pallas as pl
from jax.experimental.pallas import tpu as pltpu
from jax.sharding import Mesh
from jax.sharding import PartitionSpec as P

HEAD = 96
EPS = 1e-05
ROPE_BASE = 100000.0
AXES = ("yh", "x", "z", "core", "yl")
DP = ("yh", "x", "z", "core")
MESH = pl.DeviceIdType.MESH
BF = jnp.bfloat16
F32 = jnp.float32
EVEN = (("x", "y", "z"), ("y", "z", "x"), ("z", "x", "y"))
SPARE_Y = (("x", "z", "y"), ("y", "x", "z"), ("y", "z", "x"))
PLANE_Z = (("w", "x", "z"), ("w", "z", "x"), ("w", "x", "z"))
PLANE_X = (("w", "z", "x"), ("w", "x", "z"), ("w", "z", "x"))
PLANE = (("w", "x", "z"), ("w", "z", "x"), ("w", "x", "z"), ("w", "z", "x"))
SEQ = 256
ROWS = 512
STEP = 128
CHUNK = 256
VMEM_LIMIT = 62 * 1024 * 1024


def coordinates():
    x, z, yh, yl = (lax.axis_index(a) for a in ("x", "z", "yh", "yl"))
    return {"x": x, "z": z, "y": yh * 2 + yl, "w": yh}


def extent(axis):
    return 2 if axis == "w" else 4


def around(at, axis, by):
    return lax.rem(at[axis] + (by + 4), extent(axis))


def others(axis):
    return (1,) if axis == "w" else (1, -1, 2)


def peer(at, axis, by):
    value = around(at, axis, by)
    if axis == "y":
        return {"yh": value // 2, "yl": lax.rem(value, 2)}
    return {"yh" if axis == "w" else axis: value}


def sibling():
    return {"core": 1 - lax.axis_index("core")}


def partner():
    return {"yl": 1 - lax.axis_index("yl")}


def slot(at, axis, by=0):
    value = around(at, axis, by)
    return lax.rem(value, 2) * 2 + value // 2 if axis == "y" else value


def dimensions(order):
    return ("w" if "w" in order else "y", "x", "z")


def place(at, order, count, half=None, shifted=None):
    out = []
    for axis in dimensions(order):
        if axis in order[:count]:
            size = extent(axis)
            if half is not None and half[0] == axis:
                out.append(pl.ds(size // 2 * half[1], size // 2))
            else:
                out.append(pl.ds(0, size))
        else:
            out.append(slot(at, axis, shifted[1] if shifted is not None and shifted[0] == axis else 0))
    return tuple(out)


def greet(at):
    barrier = pltpu.get_barrier_semaphore()
    for axis in ("x", "y", "z"):
        for by in (1, -1, 2):
            pl.semaphore_signal(barrier, inc=1, device_id=peer(at, axis, by), device_id_type=MESH)
    pl.semaphore_signal(barrier, inc=1, device_id=sibling(), device_id_type=MESH)
    pl.semaphore_wait(barrier, 10)


def sent(src, dst, send, recv, device):
    copy = pltpu.make_async_remote_copy(
        src_ref=src, dst_ref=dst, send_sem=send, recv_sem=recv, device_id=device, device_id_type=MESH
    )
    copy.start()
    return copy


def moved(src, dst, sem):
    copy = pltpu.make_async_copy(src, dst, sem)
    copy.start()
    return copy


class Gather:
    @staticmethod
    def semaphores(orders):
        count = len(orders)
        shapes = (count,), (count, 2, 3), (count, 2, 3), (count, 2, 2, 3), (count, 2, 2, 3)
        return [pltpu.SemaphoreType.DMA(shape) for shape in shapes]

    def __init__(self, at, srcs, outs, semaphores, orders):
        self.at, self.srcs, self.outs, self.orders = at, srcs, outs, orders
        self.local, self.send, self.recv, self.ring_send, self.ring_recv = semaphores
        self.own, self.direct, self.ring = [], {}, {}

    def arrive(self, p, stage):
        for copy in self.direct.get((p, stage), ()):
            copy.wait_recv()
        if (p, stage, 0, 0) in self.ring:
            for d in range(2):
                self.ring[p, stage, d, 1 - d].wait_recv()
                self.ring[p, stage, d, 2].wait_recv()

    def to_all(self, stage):
        at = self.at
        for p, order in enumerate(self.orders):
            if stage:
                self.own[p].wait()
                self.arrive(p, 0)
            else:
                self.own.append(moved(self.srcs[p], self.outs[p].at[place(at, order, 0)], self.local.at[p]))
            group = self.outs[p].at[place(at, order, stage)]
            self.direct[p, stage] = [
                sent(
                    group if stage else self.srcs[p],
                    group,
                    self.send.at[p, stage, d],
                    self.recv.at[p, stage, d],
                    peer(at, order[stage], by),
                )
                for d, by in enumerate(others(order[stage]))
            ]

    def pass_on(self, p, stage, d, k, block):
        self.ring[p, stage, d, k] = sent(
            block,
            block,
            self.ring_send.at[p, stage - 1, d, k],
            self.ring_recv.at[p, stage - 1, d, k],
            peer(self.at, self.orders[p][stage], 1 - 2 * d),
        )

    def spread(self, stage, *pieces):
        for p in pieces or range(len(self.orders)):
            order = self.orders[p]
            if stage == 1:
                self.own[p].wait()
            self.arrive(p, stage - 1)
            for t in range(2):
                for d in range(2):
                    h = t if d == 0 else 1 - t
                    self.pass_on(p, stage, d, h, self.outs[p].at[place(self.at, order, stage, (order[0], h))])

    def forward(self, stage):
        for p, order in enumerate(self.orders):
            for d, by in enumerate((1, -1)):
                self.ring[p, stage, d, d].wait_recv()
                where = place(self.at, order, stage, (order[0], d), (order[stage], -by))
                self.pass_on(p, stage, d, 2, self.outs[p].at[where])

    def finish(self):
        for copies in self.direct.values():
            for copy in copies:
                copy.wait_send()
        for copy in self.ring.values():
            copy.wait_send()


class Reduce:
    @staticmethod
    def semaphores(orders):
        count = len(orders)
        shapes = (count, 3), *[(count, 2, 3)] * 4, (count, 2), (count, 2)
        return [pltpu.SemaphoreType.DMA(shape) for shape in shapes]

    @staticmethod
    def buffers(columns, orders):
        def per_piece(*shape):
            return [pltpu.VMEM(shape + (48, width), BF) for width in columns]

        size = extent(dimensions(orders[0])[0])
        return [
            *per_piece(2, size // 2, 4),
            *per_piece(size, 4),
            *per_piece(2, size // 2, 4),
            *per_piece(2, size, 4),
            *per_piece(3, size),
            *per_piece(3),
            *[pltpu.VMEM((48, width), F32) for width in columns],
        ]

    def __init__(self, at, data, buffers, semaphores, orders):
        self.at, self.data, self.orders = at, data, orders
        self.side, self.kept, self.far, self.near, self.second, self.third, self.sums = (
            buffers[len(orders) * k : len(orders) * (k + 1)] for k in range(7)
        )
        self.load, self.first_send, self.first_recv, self.send, self.recv, self.end_send, self.end_recv = semaphores
        self.loads, self.copies = {}, {}

    def left(self, p):
        order = self.orders[p]
        return [axis for axis in dimensions(order) if axis != order[2]]

    def inside(self, p, first, second=None):
        whole = slice(None) if second is None else second
        return (first, whole) if self.left(p)[0] == self.orders[p][1] else (whole, first)

    def start(self, *pieces):
        at, s, r = self.at, self.first_send, self.first_recv
        for p in pieces or range(len(self.orders)):
            order = self.orders[p]
            axis, cut = order[2], self.left(p)[0]
            size = extent(cut) // 2
            for d, by in enumerate((1, -1)):
                block = self.data[p].at[place(at, order, 2, (cut, d), (axis, 2))]
                self.copies[p, d, 0] = sent(block, self.far[p].at[d], s.at[p, d, 0], r.at[p, d, 0], peer(at, axis, by))
            for d, by in enumerate((1, -1)):
                h = 1 - d
                block = self.data[p].at[place(at, order, 2, (cut, h), (axis, by))]
                self.copies[p, d, 1] = sent(
                    block, self.near[p].at[d, pl.ds(size * h, size)], s.at[p, d, 1], r.at[p, d, 1], peer(at, axis, by)
                )
                block = self.data[p].at[place(at, order, 2, (cut, d), (axis, by))]
                self.loads[p, d] = moved(block, self.side[p].at[d], self.load.at[p, d])
            self.loads[p, 2] = moved(self.data[p].at[place(at, order, 2)], self.kept[p], self.load.at[p, 2])

    def relay(self):
        for p, order in enumerate(self.orders):
            size = extent(self.left(p)[0]) // 2
            for d, by in enumerate((1, -1)):
                self.loads[p, d].wait()
                self.copies[p, d, 0].wait_recv()
                side, far = self.side[p], self.far[p]

                @pl.loop(0, 4 * size)
                def _(i, d=d, side=side, far=far):
                    a, b = i // 4, lax.rem(i, 4)
                    side[d, a, b] = (side[d, a, b].astype(F32) + far[d, a, b].astype(F32)).astype(BF)

                self.copies[p, d, 2] = sent(
                    side.at[d],
                    self.near[p].at[d, pl.ds(size * d, size)],
                    self.first_send.at[p, d, 2],
                    self.first_recv.at[p, d, 2],
                    peer(self.at, order[2], by),
                )

    def spread(self):
        at = self.at
        for p, order in enumerate(self.orders):
            self.loads[p, 2].wait()
            for d in range(2):
                self.copies[p, d, 1].wait_recv()
                self.copies[p, d, 2].wait_recv()
            kept, near = self.kept[p], self.near[p]
            for d, by in enumerate((*others(order[1]), 0)):
                group = slot(at, order[1], by)

                @pl.loop(0, extent(order[0]))
                def _(i, p=p, kept=kept, near=near, group=group):
                    where = self.inside(p, group, i)
                    total = kept[where].astype(F32) + near[(0, *where)].astype(F32) + near[(1, *where)].astype(F32)
                    kept[where] = total.astype(BF)

                if by:
                    self.copies[p, "b", d] = sent(
                        kept.at[self.inside(p, group)],
                        self.second[p].at[d],
                        self.send.at[p, 0, d],
                        self.recv.at[p, 0, d],
                        peer(at, order[1], by),
                    )

    def narrow(self):
        at = self.at
        for p, order in enumerate(self.orders):
            for d in range(len(others(order[1]))):
                self.copies[p, "b", d].wait_recv()
            kept, second, mine = self.kept[p], self.second[p], slot(at, order[1])
            for d, by in enumerate((*others(order[0]), 0)):
                index = slot(at, order[0], by)
                where = self.inside(p, mine, index)
                total = kept[where].astype(F32)
                for k in range(3):
                    total = total + second[k, index].astype(F32)
                kept[where] = total.astype(BF)
                if by:
                    self.copies[p, "c", d] = sent(
                        kept.at[where],
                        self.third[p].at[d],
                        self.send.at[p, 1, d],
                        self.recv.at[p, 1, d],
                        peer(at, order[0], by),
                    )

    def finish(self, outs):
        at, core, ends = self.at, lax.axis_index("core"), []
        for p, order in enumerate(self.orders):
            total = self.kept[p][self.inside(p, slot(at, order[1]), slot(at, order[0]))].astype(F32)
            for d in range(len(others(order[0]))):
                self.copies[p, "c", d].wait_recv()
                total = total + self.third[p][d].astype(F32)
            self.sums[p][...] = total
            theirs = self.sums[p].at[pl.ds(pl.multiple_of(24 * (1 - core), 8), 24)]
            mine = self.sums[p].at[pl.ds(pl.multiple_of(24 * core, 8), 24)]
            ends.append(sent(theirs, outs[p].at[core], self.end_send.at[p, 0], self.end_recv.at[p, 0], sibling()))
            ends.append(moved(mine, outs[p].at[core], self.end_send.at[p, 1]))
        for copy in self.copies.values():
            copy.wait_send()
        for copy in ends:
            copy.wait()


def in_four(refs):
    half = refs[2].shape[-1] // 2
    lead = (slice(None),) * (len(refs[2].shape) - 1)
    return [refs[0], refs[1], *(refs[2].at[(*lead, pl.ds(k * half, half))] for k in range(2))]


def nn(left, right):
    return lax.dot_general(left, right, (((1,), (0,)), ((), ())), preferred_element_type=F32)


def nt(left, right):
    return lax.dot_general(left, right, (((1,), (1,)), ((), ())), preferred_element_type=F32)


def tn(left, right):
    return lax.dot_general(left, right, (((0,), (0,)), ((), ())), preferred_element_type=F32)


def inverse_rms(values):
    return lax.rsqrt(jnp.mean(values * values, -1, keepdims=True) + EPS)


def swap(values, first):
    width = values.shape[-1]
    return jnp.where(first, pltpu.roll(values, width - HEAD // 2, 1), pltpu.roll(values, HEAD // 2, 1))


def first_half(shape):
    return lax.rem(lax.broadcasted_iota(jnp.int32, shape, 1), HEAD) < HEAD // 2


def as_column(row):
    size = row.shape[1]
    square = jnp.broadcast_to(row[...].astype(F32), (size, size))
    diagonal = lax.broadcasted_iota(jnp.int32, (size, size), 0) == lax.broadcasted_iota(jnp.int32, (size, size), 1)
    return jnp.sum(jnp.where(diagonal, square, 0.0), -1, keepdims=True)


def rows_at(start, size):
    return pl.ds(pl.multiple_of(start, size), size)


ANY = pl.BlockSpec(memory_space=pl.ANY)
VMEM = pl.BlockSpec(memory_space=pltpu.VMEM)


def shaped(shape, kind=BF):
    return jax.ShapeDtypeStruct(shape, kind)


def call(kernel, operands, in_specs, results, out_specs, scratch, name, collective_id, **more):
    return pl.pallas_call(
        kernel,
        out_shape=results,
        in_specs=in_specs,
        out_specs=out_specs,
        scratch_shapes=scratch,
        compiler_params=pltpu.CompilerParams(
            collective_id=collective_id, has_side_effects=True, vmem_limit_bytes=VMEM_LIMIT
        ),
        name=name,
        **more,
    )(*operands)


def hidden_units(m, c, count, sub, n2, cot, weights, acts):
    rows = pl.ds(pl.multiple_of(m * ROWS + c * SEQ, SEQ), count * SEQ)
    columns = pl.ds(sub * CHUNK, CHUNK)
    gate_w, up_w, down_w = (w[..., columns].reshape(-1, CHUNK) for w in weights)
    gate = nn(n2[rows], gate_w)
    up = nn(n2[rows], up_w)
    sigma = 0.5 + 0.5 * jnp.tanh(0.5 * gate)
    silu = gate * sigma
    grad_active = nn(cot[m, pl.ds(c, count)].reshape(count * SEQ, -1), down_w)
    acts[0][rows, columns] = (silu * up).astype(BF)
    acts[1][rows, columns] = (grad_active * up * (sigma + silu * (1.0 - sigma))).astype(BF)
    acts[2][rows, columns] = (grad_active * silu).astype(BF)


def unit_gradients(n2t, cott, acts, staging, outs, sems, rows=None, added=False, written=True):
    whole, copies = slice(None) if rows is None else rows, []
    for k, (left, right, target) in enumerate(((n2t, acts[1], 0), (n2t, acts[2], 1), (cott, acts[0], 2))):
        for sub in range(2):
            columns = pl.ds(sub * CHUNK, CHUNK)
            value = nn(left[:, whole], right[whole, columns])
            if added:
                value = value + staging[2 * k + sub].astype(F32)
            staging[2 * k + sub] = value.astype(BF)
            if written:
                copies.append(moved(staging.at[2 * k + sub], outs[target].at[:, columns], sems.at[2 * k + sub]))
    return copies


def forward_kernel(third, wide, *refs):
    own_weights, gains_one, gains_two, lengths, xin, gin, tables_in = refs[:7], *refs[7:13]
    refs = refs[1:]
    full_two, full_one = refs[12:15], refs[15:18]
    (
        x_out, n1t_out, q_out, kv_out, probs_out, mixed_out, hidden_out, n2_out, n2t_out, cot_out, cott_out,
    ) = refs[18:29]
    attn_out, grads_out, acts_out, shard_out = refs[29:32], refs[32:35], refs[35:38], refs[38]
    refs = refs[1:]
    (
        shard, got_shard, packed, xs, gs, normed, q, kv, probs, mixed, hidden, n2, n2t, cott, part, arrived, n1t,
        valid, staging,
    ) = refs[38:57]
    full_attn, weights, acts = refs[57:60], refs[60:63], refs[63:66]
    attn_sems, one_sems, two_sems = refs[66:71], refs[71:76], refs[76:81]
    tables, pair_send, pair_recv, row_send, row_recv, far_send, far_recv, own_sem, out_sem, put_sem = refs[81:]
    at = coordinates()
    core, yl = lax.axis_index("core"), lax.axis_index("yl")
    own_x = moved(xin.at[yl], xs.at[core, yl], own_sem.at[0])
    own_g = moved(gin, gs.at[:, core, yl], own_sem.at[1])
    table_copy = moved(tables_in, tables, own_sem.at[2])

    query, key, value, output, *mlp_weights = (ref[...].astype(F32) for ref in own_weights)
    gain_one, gain_two = as_column(gains_one), as_column(gains_two)
    small = key.shape[1] // 2
    for c in range(2):
        thin = slice(c * small, (c + 1) * small)
        parts = [
            query[:, c * third : (c + 1) * third] * gain_one,
            jnp.concatenate([key[:, thin] * gain_one, value[:, thin] * gain_one], -1),
            output[:, c * third : (c + 1) * third],
            *(
                w[:, c * wide : (c + 1) * wide] * g
                for w, g in zip(mlp_weights, (gain_two, gain_two, jnp.ones_like(gain_two)))
            ),
        ]
        column = 0
        for part_value in parts:
            shard[c, :24, column : column + part_value.shape[1]] = part_value
            column += part_value.shape[1]
        lane = lax.broadcasted_iota(jnp.int32, (8, 2 * SEQ), 1)
        ends = jnp.where(lane < SEQ, lengths[:, 0:1], lengths[:, 1:2] + SEQ)
        shard[c, 24:, : 2 * SEQ] = jnp.where(lane < ends, 1.0, 0.0)
    greet(at)
    swap_shard = sent(shard.at[1 - core], got_shard, pair_send.at[0], pair_recv.at[0], sibling())

    rows = {}

    def exchange(k):
        ours, theirs, dst = (
            (xin.at[yl], xin.at[1 - yl], xs.at[core, yl]),
            (gin, gin, gs.at[:, core, yl]),
        )[k]
        rows[k, 0] = sent(theirs, dst, row_send.at[k, 0], row_recv.at[k, 0], partner())
        rows[k, 1] = sent(ours, dst, row_send.at[k, 1], row_recv.at[k, 1], sibling())

    def share(k):
        block = (xs.at[core, 1 - yl], gs.at[:, core, 1 - yl])[k]
        rows[k, 0].wait_recv()
        rows[k, 2] = sent(block, block, row_send.at[k, 2], row_recv.at[k, 2], sibling())

    def settle(k):
        (own_x, own_g)[k].wait()
        rows[k, 0].wait_send()
        rows[k, 1].wait()
        rows[k, 2].wait()

    swap_shard.wait()
    low, high = shard[core], got_shard[...]
    first, last = jnp.where(core == 0, low, high), jnp.where(core == 0, high, low)
    packed[...] = jnp.concatenate([first[:24], last[:24]], 0).astype(BF)
    for c, rows_of in enumerate((first, last)):
        for m in range(2):
            valid[m, c] = rows_of[24:32, m * SEQ : (m + 1) * SEQ]

    def pieces(start, size, step):
        return [packed.at[:, pl.ds(start + k * step, size)] for k in range(3)]

    half = wide // 2
    attn = Gather(at, pieces(0, third, third), full_attn, attn_sems, EVEN)
    one = Gather(at, pieces(3 * third, half, wide), weights, one_sems, PLANE_Z)
    two = Gather(at, pieces(3 * third + half, half, wide), full_two, two_sems, PLANE_X)
    attn.to_all(0)
    one.to_all(0)
    attn.to_all(1)
    one.spread(1)
    attn.spread(2, 0, 1)
    exchange(0)
    attn.spread(2, 2)
    two.to_all(0)
    one.forward(1)
    attn.forward(2)
    one.spread(2)
    share(0)
    settle(0)
    exchange(1)
    outs = [moved(xs, x_out, out_sem.at[0]), moved(shard, shard_out, out_sem.at[24])]

    @pl.loop(0, ROWS // STEP)
    def _(i):
        block = rows_at(i * STEP, STEP)
        values = xs[i // 2, lax.rem(i, 2)].astype(F32)
        normed[block] = (values * inverse_rms(values)).astype(BF)

    for p in range(2):
        attn.arrive(p, 2)
    two.spread(1)
    wq, wkv, wo = full_attn
    table_copy.wait()

    def weight(ref, y):
        return ref[pl.ds(2 * y, 2)].reshape(-1, third)

    @pl.loop(0, 2)
    def _(y):
        @pl.loop(0, ROWS // SEQ)
        def _(n):
            block = rows_at(n * SEQ, SEQ)
            left = normed[block]
            is_first = first_half((SEQ, third))
            for k, (w, result) in enumerate(((wq, q), (wkv, kv))):
                lin = nn(left, weight(w, y))
                result[y, block] = (lin * tables[2 * k] + swap(lin, is_first) * tables[2 * k + 1]).astype(BF)

    outs.append(moved(q, q_out, out_sem.at[5]))
    outs.append(moved(kv, kv_out, out_sem.at[6]))
    two.forward(1)
    one.forward(2)
    scale = 1.0 / math.sqrt(HEAD)

    @pl.loop(0, 4)
    def _(i):
        y, n = i // 2, lax.rem(i, 2)
        block = rows_at(n * SEQ, SEQ)
        t = lax.broadcasted_iota(jnp.int32, (SEQ, SEQ), 0)
        s = lax.broadcasted_iota(jnp.int32, (SEQ, SEQ), 1)
        keep = (s <= t) & (valid[yl, n, 0:1, :] > 0.5)
        queries, keys = q[y, block], kv[y, block]
        results = []
        for h in range(4):
            g = h // 2
            scores = nt(queries[:, h * HEAD : (h + 1) * HEAD], keys[:, g * HEAD : (g + 1) * HEAD]) * scale
            scores = jnp.where(keep, scores, -1e30)
            terms = jnp.exp(scores - jnp.max(scores, -1, keepdims=True))
            low_probs = (terms * (1.0 / jnp.sum(terms, -1, keepdims=True))).astype(BF)
            probs[i, h] = low_probs
            results.append(nn(low_probs, keys[:, (2 + g) * HEAD : (3 + g) * HEAD]))
        mixed[y, block] = jnp.concatenate(results, -1).astype(BF)

    outs.append(moved(probs, probs_out, out_sem.at[7]))
    outs.append(moved(mixed, mixed_out, out_sem.at[8]))
    two.spread(2)

    attn.arrive(2, 2)
    copies = []
    for i in range(ROWS // STEP):
        block = rows_at(lax.rem(2 * (1 - core) + i, 4) * STEP, STEP)
        part[block] = (nt(mixed[0, block], weight(wo, 0)) + nt(mixed[1, block], weight(wo, 1))).astype(BF)
        copies.append(sent(part.at[block], arrived.at[block], pair_send.at[1 + i], pair_recv.at[1 + i], sibling()))
    second_rows = {}
    mine, theirs = yl * ROWS, (1 - yl) * ROWS
    for i in range(ROWS // STEP):
        copies[(i + 2) % 4 if i < 2 else i - 2].wait_send()
        copies[i].wait_recv()
        number = lax.rem(2 * core + i, 4)
        block = rows_at(number * STEP, STEP)
        values = xs[number // 2, lax.rem(number, 2)].astype(F32) + (
            part[block].astype(F32) + arrived[block].astype(F32)
        )
        hidden[block] = values
        target = rows_at(mine + number * STEP, STEP)
        n2[target] = (values * inverse_rms(values)).astype(BF)
        if i < 2:
            second_rows[0, i] = sent(n2.at[target], n2.at[target], far_send.at[0, i], far_recv.at[0, i], partner())
    outs.append(moved(hidden.at[rows_at(core * SEQ, SEQ)], hidden_out, out_sem.at[9]))
    attn.finish()
    outs.extend(moved(full_attn[p], attn_out[p], out_sem.at[2 + p]) for p in range(3))
    share(1)
    settle(1)

    for m in range(2):
        for c in range(2):
            for h in range(2):
                mask = valid[m, c][:, h * STEP : (h + 1) * STEP].T[:, 0:1]
                gs[m, c, h] = (gs[m, c, h].astype(F32) * mask).astype(BF)
    outs.append(moved(gs, cot_out, out_sem.at[10]))

    for p in range(3):
        one.arrive(p, 2)
    one.finish()
    outs.extend(moved(weights[p], full_one[p], out_sem.at[11 + p]) for p in range(3))
    mine_rows, their_rows = rows_at(mine, ROWS), rows_at(theirs, ROWS)
    for sub in range(2):
        hidden_units(yl, 0, 2, sub, n2, gs, weights, acts)
    two.forward(2)
    outs.extend(moved(acts[p].at[mine_rows], acts_out[p].at[mine_rows], out_sem.at[15 + p]) for p in range(3))
    outs.append(moved(n2.at[mine_rows], n2_out.at[mine_rows], out_sem.at[18]))
    for m in range(2):
        for c in range(2):
            for h in range(2):
                cott[:, pl.ds(m * ROWS + (2 * c + h) * STEP, STEP)] = gs[m, c, h].T
    outs.append(moved(cott, cott_out, out_sem.at[14]))
    for i in range(ROWS // STEP):
        block = rows_at(mine + i * STEP, STEP)
        n2t[:, block] = n2[block].T
    unit_gradients(n2t, cott, acts, staging, grads_out, put_sem, mine_rows, written=False)
    n1t[...] = normed[...].T
    outs.append(moved(n1t, n1t_out, out_sem.at[1]))

    for i in range(2):
        second_rows[0, i].wait_recv()
        block = rows_at(theirs + (2 * core + i) * STEP, STEP)
        second_rows[1, i] = sent(n2.at[block], n2.at[block], far_send.at[1, i], far_recv.at[1, i], sibling())
    for sub in range(2):
        hidden_units(1 - yl, core, 1, sub, n2, gs, weights, acts)
    for i in range(2):
        second_rows[0, i].wait_send()
        second_rows[1, i].wait()
    for sub in range(2):
        hidden_units(1 - yl, 1 - core, 1, sub, n2, gs, weights, acts)
    outs.extend(moved(acts[p].at[their_rows], acts_out[p].at[their_rows], out_sem.at[20 + p]) for p in range(3))
    outs.append(moved(n2.at[their_rows], n2_out.at[their_rows], out_sem.at[23]))
    for i in range(ROWS // STEP):
        block = rows_at(theirs + i * STEP, STEP)
        n2t[:, block] = n2[block].T
    outs.append(moved(n2t, n2t_out, out_sem.at[19]))
    outs.extend(unit_gradients(n2t, cott, acts, staging, grads_out, put_sem, their_rows, added=True))
    for p in range(3):
        two.arrive(p, 2)
    two.finish()
    for copy in outs:
        copy.wait()


def forward(own_weights, gains, lengths, xin, gin, tables, third, wide):
    width = xin.shape[2]
    rows = (ROWS, width)
    both = (2 * ROWS, width)
    heads = (2, ROWS, third)
    square = (4, 4, SEQ, SEQ)
    half = wide // 2
    piece = (2, 4, 4, 48, half)
    return call(
        lambda *refs: forward_kernel(third, wide, *refs),
        (*own_weights, *gains, lengths, xin, gin, tables),
        [VMEM] * 10 + [ANY, ANY, ANY],
        [shaped(piece)] * 6
        + [
            shaped((2, 2, 128, width)),
            shaped(rows[::-1]),
            shaped(heads),
            shaped(heads),
            shaped(square),
            shaped(heads),
            shaped((SEQ, width), F32),
            shaped(both),
            shaped(both[::-1]),
            shaped((2, 2, 2, 128, width)),
            shaped(both[::-1]),
        ]
        + [shaped((4, 4, 4, 48, third))] * 3
        + [shaped((width, half))] * 3
        + [shaped((2 * ROWS, half))] * 3
        + [shaped((2, 32, 3 * third + 3 * wide), F32)],
        [ANY] * 27,
        [
            pltpu.VMEM((2, 32, 3 * third + 3 * wide), F32),
            pltpu.VMEM((32, 3 * third + 3 * wide), F32),
            pltpu.VMEM((48, 3 * third + 3 * wide), BF),
            pltpu.VMEM((2, 2, 128, width), BF),
            pltpu.VMEM((2, 2, 2, 128, width), BF),
            pltpu.VMEM(rows, BF),
            pltpu.VMEM(heads, BF),
            pltpu.VMEM(heads, BF),
            pltpu.VMEM(square, BF),
            pltpu.VMEM(heads, BF),
            pltpu.VMEM(rows, F32),
            pltpu.VMEM(both, BF),
            pltpu.VMEM(both[::-1], BF),
            pltpu.VMEM(both[::-1], BF),
            pltpu.VMEM(rows, BF),
            pltpu.VMEM(rows, BF),
            pltpu.VMEM(rows[::-1], BF),
            pltpu.VMEM((2, 2, 8, SEQ), F32),
            pltpu.VMEM((6, width, CHUNK), BF),
            *[pltpu.VMEM((4, 4, 4, 48, third), BF) for _ in range(3)],
            *[pltpu.VMEM(piece, BF) for _ in range(3)],
            *[pltpu.VMEM((2 * ROWS, half), BF) for _ in range(3)],
            *Gather.semaphores(EVEN),
            *Gather.semaphores(PLANE_Z),
            *Gather.semaphores(PLANE_X),
            pltpu.VMEM(tables.shape, F32),
            pltpu.SemaphoreType.DMA((5,)),
            pltpu.SemaphoreType.DMA((5,)),
            pltpu.SemaphoreType.DMA((2, 3)),
            pltpu.SemaphoreType.DMA((2, 3)),
            pltpu.SemaphoreType.DMA((2, 2)),
            pltpu.SemaphoreType.DMA((2, 2)),
            pltpu.SemaphoreType.DMA((3,)),
            pltpu.SemaphoreType.DMA((25,)),
            pltpu.SemaphoreType.DMA((6,)),
        ],
        "gather_attn_forward_mlp",
        1,
    )


def middle_kernel(*refs):
    n2_in, cot_in, hidden_in, n2t_in, cott_in = refs[:5]
    one_in, two_in, acts_in, data = refs[5:8], refs[8:11], refs[11:14], refs[14:17]
    sums_out, grads_out = refs[17:20], refs[20:23]
    kept_out, away_out, branch_out, grad_hidden_out = refs[23:27]
    (
        n2, cot, hidden, n2t, cott, staging, to_pair, from_pair, whole, from_far, keep, halves, to_far, branch, gh,
    ) = refs[27:42]
    one, two, acts_one, acts_two = refs[42:45], refs[45:48], refs[48:51], refs[51:54]
    buffers, reduce_sems = refs[54:82], refs[82:89]
    load, put, put_sem, pair_send, pair_recv, part_send, part_recv, far_send, far_recv = refs[89:]
    core, yl = lax.axis_index("core"), lax.axis_index("yl")
    at = coordinates()
    order = (
        (n2_in, n2),
        (two_in[0], two[0]),
        (two_in[1], two[1]),
        (cot_in, cot),
        (two_in[2], two[2]),
        *zip(acts_in[1:], acts_one[1:]),
        *zip(one_in[:2], one[:2]),
        (acts_in[0], acts_one[0]),
        (one_in[2], one[2]),
        (n2t_in, n2t),
        (cott_in, cott),
        (hidden_in, hidden),
    )
    loads = [moved(src, dst, load.at[k]) for k, (src, dst) in enumerate(order)]
    greet(at)
    total = Reduce(at, in_four(data), buffers, reduce_sems, PLANE)
    total.start()
    for k in range(5):
        loads[k].wait()
    for sub in range(2):
        hidden_units(1 - yl, 0, 2, sub, n2, cot, two, acts_two)
    for k in range(5, 11):
        loads[k].wait()

    def weight(ref):
        return ref[...].reshape(n2.shape[1], -1)

    def grad_rows(m, c):
        rows = rows_at(m * ROWS + c * SEQ, SEQ)
        return (nt(acts_one[1][rows], weight(one[0])) + nt(acts_one[2][rows], weight(one[1]))) + (
            nt(acts_two[1][rows], weight(two[0])) + nt(acts_two[2][rows], weight(two[1]))
        )

    def out_rows(m, c):
        rows = rows_at(m * ROWS + c * SEQ, SEQ)
        return nt(acts_one[0][rows], weight(one[2])) + nt(acts_two[0][rows], weight(two[2]))

    pair, far, shared = {}, {}, []

    def to_sibling(k, value):
        to_pair[k] = value.astype(BF)
        pair[k] = sent(to_pair.at[k], from_pair.at[k], pair_send.at[k], pair_recv.at[k], sibling())

    blocks = [pl.ds(i * STEP, STEP) for i in range(2)]
    to_pair[0] = grad_rows(1 - yl, 1 - core).astype(BF)
    for i, rows in enumerate(blocks):
        pair["far", i] = sent(
            to_pair.at[0, rows], from_pair.at[0, rows], part_send.at[0, i], part_recv.at[0, i], sibling()
        )
    keep[...] = grad_rows(1 - yl, core)
    for i, rows in enumerate(blocks):
        pair["far", i].wait_recv()
        whole[rows] = (keep[rows] + from_pair[0, rows].astype(F32)).astype(BF)
        far[i] = sent(whole.at[rows], from_far.at[rows], far_send.at[i], far_recv.at[i], partner())
    total.relay()
    for sub in range(2):
        hidden_units(yl, 0, 2, sub, n2, cot, two, acts_two)
    to_sibling(1, grad_rows(yl, 1 - core))
    keep[...] = grad_rows(yl, core)
    to_sibling(2, out_rows(1 - yl, 1 - core))
    to_sibling(3, out_rows(yl, 1 - core))
    for k in range(11, 14):
        loads[k].wait()
    total.spread()
    outs = unit_gradients(n2t, cott, acts_two, staging, grads_out, put_sem)
    total.narrow()

    for k, m in ((2, 1 - yl), (3, yl)):
        pair[k].wait_recv()
        value = out_rows(m, core) + from_pair[k].astype(F32)
        if k == 3:
            value = value + hidden[...]
        halves[k - 2] = value.reshape(2, STEP, -1)
        to_far[k - 2] = halves[k - 2, 1 - yl].astype(BF)
        outs.append(moved(halves.at[k - 2, yl], kept_out.at[k - 2], put.at[k]))
        outs.append(moved(to_far.at[k - 2], away_out.at[k - 2], put.at[k + 2]))
    pair[1].wait_recv()

    for i, rows in enumerate(blocks):
        far[i].wait_recv()
        grad = keep[rows] + (from_pair[1, rows].astype(F32) + from_far[rows].astype(F32))
        values = hidden[rows]
        inverse = inverse_rms(values)
        unit = values * inverse
        back = inverse * (grad - unit * jnp.mean(grad * unit, -1, keepdims=True))
        gh[rows] = cot[yl, core, i].astype(F32) + back
        branch[rows] = gh[rows].astype(BF)
        target = rows_at(core * SEQ + i * STEP, STEP)
        shared.append(
            sent(branch.at[rows], branch_out.at[target], part_send.at[1, i], part_recv.at[1, i], sibling())
        )
        outs.append(moved(branch.at[rows], branch_out.at[target], put.at[6 + i]))
    outs.append(moved(gh, grad_hidden_out, put.at[0]))
    total.finish(in_four(sums_out))
    for copy in shared:
        copy.wait()
    for copy in (*pair.values(), *far.values()):
        copy.wait_send()
    for copy in outs:
        copy.wait()


def middle(n2, cot, hidden, n2t, cott, one, two, acts, data):
    rows, width = n2.shape
    half = one[0].shape[-1]
    block = (SEQ, width)
    return call(
        middle_kernel,
        (n2, cot, hidden, n2t, cott, *one, *two, *acts, *data),
        [ANY] * 17,
        [shaped((2, 24, half), F32)] * 3
        + [shaped((width, half))] * 3
        + [
            shaped((2, STEP, width), F32),
            shaped((2, STEP, width)),
            shaped((ROWS, width)),
            shaped(block, F32),
        ],
        [ANY] * 10,
        [
            pltpu.VMEM((rows, width), BF),
            pltpu.VMEM(cot.shape, BF),
            pltpu.VMEM(block, F32),
            pltpu.VMEM((width, rows), BF),
            pltpu.VMEM((width, rows), BF),
            pltpu.VMEM((6, width, CHUNK), BF),
            pltpu.VMEM((4,) + block, BF),
            pltpu.VMEM((4,) + block, BF),
            pltpu.VMEM(block, BF),
            pltpu.VMEM(block, BF),
            pltpu.VMEM(block, F32),
            pltpu.VMEM((2, 2, STEP, width), F32),
            pltpu.VMEM((2, STEP, width), BF),
            pltpu.VMEM(block, BF),
            pltpu.VMEM(block, F32),
            *[pltpu.VMEM(one[0].shape, BF) for _ in range(6)],
            *[pltpu.VMEM((rows, half), BF) for _ in range(6)],
            *Reduce.buffers((half, half, half // 2, half // 2), PLANE),
            *Reduce.semaphores(PLANE),
            pltpu.SemaphoreType.DMA((14,)),
            pltpu.SemaphoreType.DMA((8,)),
            pltpu.SemaphoreType.DMA((6,)),
            pltpu.SemaphoreType.DMA((4,)),
            pltpu.SemaphoreType.DMA((4,)),
            pltpu.SemaphoreType.DMA((2, 2)),
            pltpu.SemaphoreType.DMA((2, 2)),
            pltpu.SemaphoreType.DMA((2,)),
            pltpu.SemaphoreType.DMA((2,)),
        ],
        "mlp_reduce",
        2,
    )


def backward_kernel(*refs):
    xall, grad_hidden_in, branch_in, n1t_in, q_in, kv_in, probs_in, mixed_in, wq_in, wkv_in, wo_in, tables_in = refs[:12]
    data, kept_in, away, shard_in, one_in = refs[12:15], *refs[15:18], refs[18:20]
    refs = refs[3:]
    mlp_outs, attn_outs, result_out, in_grad_out, from_partner = refs[17:20], refs[20:23], *refs[23:26]
    gains_out, gain_in = refs[26:28]
    refs = refs[2:]
    (
        xs, gh, branch, branch_t, normed_t, q, kv, probs, mixed, wq, wkv, wo,
        grad_mixed, dq, dkv, part, keep_part, arrived, in_grad, for_partner, kept, others_half, result,
    ) = refs[26:49]
    attn_grads = refs[49:52]
    mlp_buffers, attn_buffers = refs[52:80], refs[80:101]
    mlp_sems, attn_sems = refs[101:108], refs[108:115]
    mlp_ends, attn_ends, shard, one_sums, gain_part, tables = refs[115:118], refs[118:121], *refs[121:125]
    load, put, send, recv = refs[125:]
    at = coordinates()
    core, yl = lax.axis_index("core"), lax.axis_index("yl")
    loads = [
        moved(src, dst, load.at[k])
        for k, (src, dst) in enumerate(
            (
                (branch_in, branch),
                (wo_in, wo),
                (mixed_in, mixed),
                (q_in, q),
                (kv_in, kv),
                (probs_in, probs),
                (n1t_in, normed_t),
                (wq_in, wq),
                (wkv_in, wkv),
                (grad_hidden_in, gh),
                (xall.at[core], xs),
                (kept_in, kept),
                (shard_in, shard),
                (one_in[0], one_sums.at[0]),
                (one_in[1], one_sums.at[1]),
                (tables_in, tables),
            )
        )
    ]
    greet(at)
    mlp_sum = Reduce(at, in_four(data), mlp_buffers, mlp_sems, PLANE)
    attn_sum = Reduce(at, attn_grads, attn_buffers, attn_sems, SPARE_Y)
    mlp_sum.start()
    finals = [sent(away.at[k], others_half.at[k], send.at[2 + k], recv.at[2 + k], partner()) for k in range(2)]
    for k in range(2):
        loads[k].wait()
    for y in range(2):
        grad_mixed[y] = nn(branch[...], wo[y]).astype(BF)
    for k in (2, 3, 4, 5, 15):
        loads[k].wait()
    scale = 1.0 / math.sqrt(HEAD)

    def attention(i):
        y, n = i // 2, lax.rem(i, 2)
        rows = rows_at(n * SEQ, SEQ)
        queries, keys, grads = q[y, rows], kv[y, rows], grad_mixed[y, rows]
        grad_q, grad_k, grad_v = [], [None, None], [None, None]
        for h in range(4):
            g = h // 2
            key = keys[:, g * HEAD : (g + 1) * HEAD]
            value = keys[:, (2 + g) * HEAD : (3 + g) * HEAD]
            query = queries[:, h * HEAD : (h + 1) * HEAD]
            grad = grads[:, h * HEAD : (h + 1) * HEAD]
            low = probs[i, h]
            prob = low.astype(F32)
            grad_probs = nt(grad, value)
            grad_scores = (prob * (grad_probs - jnp.sum(grad_probs * prob, -1, keepdims=True))).astype(BF)
            grad_q.append(nn(grad_scores, key) * scale)
            back_k = tn(grad_scores, query) * scale
            back_v = tn(low, grad)
            grad_k[g] = back_k if grad_k[g] is None else grad_k[g] + back_k
            grad_v[g] = back_v if grad_v[g] is None else grad_v[g] + back_v
        first = first_half((SEQ, 4 * HEAD))
        for k, (pieces, target) in enumerate(((grad_q, dq), (grad_k + grad_v, dkv))):
            values = jnp.concatenate(pieces, -1)
            target[y, rows] = (values * tables[2 * k] - swap(values, first) * tables[2 * k + 1]).astype(BF)

    pl.loop(0, 2)(attention)
    mlp_sum.relay()
    pl.loop(2, 4)(attention)
    loads[6].wait()

    def weight_grad(p, left, right):
        for y in range(2):
            target = attn_grads[p].at[pl.ds(2 * y, 2)]
            target[...] = nn(left[...], right[y]).astype(BF).reshape(target.shape)
        attn_sum.start(p)

    weight_grad(0, normed_t, dq)
    weight_grad(1, normed_t, dkv)
    mlp_sum.spread()
    branch_t[...] = branch[...].T
    weight_grad(2, branch_t, mixed)
    for k in range(7, 15):
        loads[k].wait()

    def back(start):
        rows = rows_at(start, SEQ)
        return (nt(dq[0, rows], wq[0]) + nt(dq[1, rows], wq[1])) + (nt(dkv[0, rows], wkv[0]) + nt(dkv[1, rows], wkv[1]))

    part[...] = back((1 - core) * SEQ).astype(BF)
    pair = sent(part, arrived, send.at[0], recv.at[0], sibling())
    attn_sum.relay()
    keep_part[...] = back(core * SEQ)
    mlp_sum.narrow()
    pair.wait()

    @pl.loop(0, SEQ // STEP)
    def _(i):
        rows = rows_at(i * STEP, STEP)
        grad = keep_part[rows] + arrived[rows].astype(F32)
        values = xs[i].astype(F32)
        inverse = inverse_rms(values)
        unit = values * inverse
        change = inverse * (grad - unit * jnp.mean(grad * unit, -1, keepdims=True))
        in_grad[i] = gh[rows] + change

    for_partner[...] = in_grad[1 - yl].astype(BF)
    ends = [
        moved(in_grad.at[yl], in_grad_out, put.at[0]),
        sent(for_partner, from_partner, send.at[1], recv.at[1], partner()),
    ]
    attn_sum.spread()
    for copy in finals:
        copy.wait()
    result[1 - yl] = (kept[0] + others_half[1].astype(F32)).astype(BF)
    result[yl] = (kept[1] + others_half[0].astype(F32)).astype(BF)
    ends.append(moved(result, result_out, put.at[1]))
    mlp_sum.finish(in_four(mlp_ends))
    attn_sum.narrow()
    ends.extend(moved(mlp_ends[p], mlp_outs[p], put.at[2 + p]) for p in range(3))

    def along(start, gradient):
        weights = shard[:, :24, start : start + gradient.shape[2]]
        total = jnp.sum(weights * gradient, -1, keepdims=True)
        return total[0] + total[1]

    thin, half = attn_ends[0].shape[2], mlp_ends[0].shape[2]
    second = sum(
        along(3 * thin + 2 * half * p, one_sums[p]) + along(3 * thin + 2 * half * p + half, mlp_ends[p][...])
        for p in range(2)
    )
    attn_sum.finish(attn_ends)
    ends.extend(moved(attn_ends[p], attn_outs[p], put.at[5 + p]) for p in range(3))
    first = sum(along(thin * p, attn_ends[p][...]) for p in range(2))
    lane = lax.broadcasted_iota(jnp.int32, gain_part.shape, 1)
    gain_part[...] = jnp.where(lane == 0, first, second)
    ends.append(sent(gain_part, gain_in, send.at[4], recv.at[4], partner()))
    ends.append(moved(gain_part, gains_out, put.at[8]))
    for copy in ends:
        copy.wait()


def backward(x, grad_hidden, branch, n1t, q, kv, probs, mixed, wq, wkv, wo, tables, data, kept, away, shard, one_sums):
    rows, width = branch.shape
    third, wide = wq.shape[2], data[0].shape[-1]
    heads = (2, rows, third)
    weights = (2, width, third)
    half = (2, STEP, width)
    return call(
        backward_kernel,
        (x, grad_hidden, branch, n1t, q, kv, probs, mixed, wq, wkv, wo, tables, *data, kept, away, shard, *one_sums),
        [ANY] * 20,
        [shaped((2, 24, wide), F32)] * 3
        + [shaped((2, 24, third), F32)] * 3
        + [shaped(half), shaped(half[1:], F32), shaped(half[1:])]
        + [shaped((24, 128), F32)] * 2,
        [ANY] * 11,
        [
            pltpu.VMEM(half, BF),
            pltpu.VMEM((SEQ, width), F32),
            pltpu.VMEM((rows, width), BF),
            pltpu.VMEM((width, rows), BF),
            pltpu.VMEM((width, rows), BF),
            pltpu.VMEM(heads, BF),
            pltpu.VMEM(heads, BF),
            pltpu.VMEM((4, 4, SEQ, SEQ), BF),
            pltpu.VMEM(heads, BF),
            pltpu.VMEM(weights, BF),
            pltpu.VMEM(weights, BF),
            pltpu.VMEM(weights, BF),
            pltpu.VMEM(heads, BF),
            pltpu.VMEM(heads, BF),
            pltpu.VMEM(heads, BF),
            pltpu.VMEM((SEQ, width), BF),
            pltpu.VMEM((SEQ, width), F32),
            pltpu.VMEM((SEQ, width), BF),
            pltpu.VMEM(half, F32),
            pltpu.VMEM(half[1:], BF),
            pltpu.VMEM(half, F32),
            pltpu.VMEM(half, BF),
            pltpu.VMEM(half, BF),
            *[pltpu.VMEM((4, 4, 4, 48, third), BF) for _ in range(3)],
            *Reduce.buffers((wide, wide, wide // 2, wide // 2), PLANE),
            *Reduce.buffers((third,) * 3, SPARE_Y),
            *Reduce.semaphores(PLANE),
            *Reduce.semaphores(SPARE_Y),
            *[pltpu.VMEM((2, 24, wide), F32) for _ in range(3)],
            *[pltpu.VMEM((2, 24, third), F32) for _ in range(3)],
            pltpu.VMEM(shard.shape, F32),
            pltpu.VMEM((2, 2, 24, wide), F32),
            pltpu.VMEM((24, 128), F32),
            pltpu.VMEM(tables.shape, F32),
            pltpu.SemaphoreType.DMA((16,)),
            pltpu.SemaphoreType.DMA((9,)),
            pltpu.SemaphoreType.DMA((5,)),
            pltpu.SemaphoreType.DMA((5,)),
        ],
        "attn_backward_reduce",
        3,
    )


def last_kernel(own, theirs, result_in, one, two, attn, gains_one, gains_two, gain_sums, more, outs):
    result, in_grad, dq, dk, dv, do, dg, du, dd, gain_one_grad, gain_two_grad = outs
    yl = lax.axis_index("yl")
    result[...] = result_in[...]
    in_grad[yl] = own[...]
    in_grad[1 - yl] = theirs[...].astype(F32)
    gain_one, gain_two = as_column(gains_one), as_column(gains_two)
    thin, half = attn[0].shape[2], two[0].shape[2]
    keys = [[], []]
    for c in range(2):
        dq[:, c * thin : (c + 1) * thin] = attn[0][c] * gain_one
        for k in range(2):
            keys[k].append(attn[1][c, :, k * (thin // 2) : (k + 1) * (thin // 2)] * gain_one)
        do[:, c * thin : (c + 1) * thin] = attn[2][c]
        for k, part in enumerate((one, two)):
            start = (2 * c + k) * half
            dg[:, start : start + half] = part[0][c] * gain_two
            du[:, start : start + half] = part[1][c] * gain_two
            dd[:, start : start + half] = part[2][c]
    dk[...] = jnp.concatenate(keys[0], -1)
    dv[...] = jnp.concatenate(keys[1], -1)
    lane = lax.broadcasted_iota(jnp.int32, gain_sums.shape, 1)
    grads = ((gain_sums[...] + more[...]) / jnp.where(lane == 0, gain_one, gain_two)).T
    gain_one_grad[...] = grads[0:1, :24]
    gain_two_grad[...] = grads[1:2, :24]


def placed_outputs(own, theirs, result, one, two, attn, gains, gain_sums, more_gain_sums):
    width, thin, half = own.shape[1], attn[0].shape[2], two[0].shape[2]

    def kernel(*refs):
        last_kernel(*refs[:3], refs[3:6], refs[6:9], refs[9:12], *refs[12:16], refs[16:])

    return pl.pallas_call(
        kernel,
        out_shape=[
            shaped((2, STEP, width)),
            shaped((2, STEP, width), F32),
            shaped((24, 2 * thin), F32),
            shaped((24, thin), F32),
            shaped((24, thin), F32),
            shaped((24, 2 * thin), F32),
            shaped((24, 4 * half), F32),
            shaped((24, 4 * half), F32),
            shaped((24, 4 * half), F32),
            shaped((1, 24), F32),
            shaped((1, 24), F32),
        ],
        in_specs=[VMEM] * 16,
        out_specs=[VMEM] * 11,
        compiler_params=pltpu.CompilerParams(vmem_limit_bytes=VMEM_LIMIT),
        name="place_outputs",
    )(own, theirs, result, *one, *two, *attn, *gains, gain_sums, more_gain_sums)


def tables_for(count, heads, plain):
    half = HEAD // 2
    inverse = np.float32(ROPE_BASE) ** (-(np.arange(half, dtype=np.float32) * np.float32(2.0)) / np.float32(HEAD))
    angle = np.arange(count, dtype=np.float32)[:, None] * inverse.astype(np.float32)[None, :]
    cosine, sine = np.cos(angle), np.sin(angle)
    cosine = np.tile(np.concatenate([cosine, cosine], -1), (1, heads))
    sine = np.tile(np.concatenate([-sine, sine], -1), (1, heads))
    cosine = np.concatenate([cosine, np.ones((count, plain), np.float32)], -1)
    sine = np.concatenate([sine, np.zeros((count, plain), np.float32)], -1)
    return np.stack([cosine, sine]).astype(np.float32)


def body(
    inputs,
    out_grad,
    lengths,
    query_weight,
    key_matrix,
    value_matrix,
    output_weight,
    gate_weight,
    up_weight,
    down_weight,
    attn_gain,
    mlp_gain,
):
    width = inputs.shape[2]
    own_weights = (
        query_weight,
        key_matrix,
        value_matrix,
        output_weight.T,
        gate_weight,
        up_weight,
        down_weight.T,
    )
    gains = (attn_gain.reshape(1, -1), mlp_gain.reshape(1, -1))
    third, wide = query_weight.shape[1] // 2, gate_weight.shape[1] // 2
    tables = jnp.asarray(np.concatenate([tables_for(SEQ, 4, 0), tables_for(SEQ, 2, 2 * HEAD)]))

    results = forward(
        own_weights, gains, lengths.reshape(1, -1), inputs, out_grad, tables, third, wide
    )
    two, one = results[:3], results[3:6]
    x, n1t, q, kv, probs, mixed, hidden, n2, n2t, cot, cott = results[6:17]
    (wq, wkv, wo), grads, acts, shard = results[17:20], results[20:23], results[23:26], results[26]

    def joined(w):
        return w.reshape(2, width, -1)

    def blocked(w):
        return w.reshape(2, 4, 4, 48, -1)

    *one_sums, dg, du, dd, kept, away, branch, grad_hidden = middle(
        n2, cot, hidden, n2t, cott, one, two, acts, [blocked(w) for w in grads]
    )
    *sums, result, in_grad, in_grad_theirs, gain_sums, more_gain_sums = backward(
        x,
        grad_hidden,
        branch,
        n1t,
        q,
        kv,
        probs,
        mixed,
        joined(wq),
        joined(wkv),
        joined(wo),
        tables,
        [blocked(w) for w in (dg, du, dd)],
        kept,
        away,
        shard,
        one_sums[:2],
    )
    result, in_grad, dq, dk, dv, do, dg, du, dd, gain_one_grad, gain_two_grad = placed_outputs(
        in_grad, in_grad_theirs, result, one_sums, sums[:3], sums[3:], gains, gain_sums, more_gain_sums
    )
    return result, in_grad, dq, dk, dv, do.T, dg, du, dd.T, gain_one_grad.reshape(24), gain_two_grad.reshape(24)


def solution(mesh):
    fine = Mesh(mesh.devices.reshape(2, 4, 4, 2, 2), AXES)
    rows = P(None, AXES, None)
    into, out = P(DP, "yl"), P("yl", DP)
    return jax.shard_map(
        body,
        mesh=fine,
        in_specs=(rows, rows, P(None, DP), into, into, into, out, into, into, out, P(DP), P(DP)),
        out_specs=(rows, rows, into, into, into, out, into, into, out, P(DP), P(DP)),
        check_vma=False,
    )
```

```python
import math

import jax
import jax.numpy as jnp
import numpy as np
from jax import lax
from jax.experimental import pallas as pl
from jax.experimental.pallas import tpu as pltpu
from jax.sharding import Mesh
from jax.sharding import PartitionSpec as P

HEAD = 96
EPS = 1e-05
ROPE_BASE = 100000.0
AXES = ("yh", "x", "z", "core", "yl")
DP = ("yh", "x", "z", "core")
MESH = pl.DeviceIdType.MESH
BF = jnp.bfloat16
F32 = jnp.float32
EVEN = (("x", "y", "z"), ("y", "z", "x"), ("z", "x", "y"))
SPARE_Y = (("x", "z", "y"), ("y", "x", "z"), ("y", "z", "x"))
PLANE_Z = (("w", "x", "z"), ("w", "z", "x"), ("w", "x", "z"))
PLANE_X = (("w", "z", "x"), ("w", "x", "z"), ("w", "z", "x"))
PLANE = (("w", "x", "z"), ("w", "z", "x"), ("w", "x", "z"), ("w", "z", "x"))
SEQ = 256
ROWS = 512
STEP = 128
CHUNK = 256
VMEM_LIMIT = 62 * 1024 * 1024


def coordinates():
    x, z, yh, yl = (lax.axis_index(a) for a in ("x", "z", "yh", "yl"))
    return {"x": x, "z": z, "y": yh * 2 + yl, "w": yh}


def extent(axis):
    return 2 if axis == "w" else 4


def around(at, axis, by):
    return lax.rem(at[axis] + (by + 4), extent(axis))


def others(axis):
    return (1,) if axis == "w" else (1, -1, 2)


def peer(at, axis, by):
    value = around(at, axis, by)
    if axis == "y":
        return {"yh": value // 2, "yl": lax.rem(value, 2)}
    return {"yh" if axis == "w" else axis: value}


def sibling():
    return {"core": 1 - lax.axis_index("core")}


def partner():
    return {"yl": 1 - lax.axis_index("yl")}


def slot(at, axis, by=0):
    value = around(at, axis, by)
    return lax.rem(value, 2) * 2 + value // 2 if axis == "y" else value


def dimensions(order):
    return ("w" if "w" in order else "y", "x", "z")


def place(at, order, count, half=None, shifted=None):
    out = []
    for axis in dimensions(order):
        if axis in order[:count]:
            size = extent(axis)
            if half is not None and half[0] == axis:
                out.append(pl.ds(size // 2 * half[1], size // 2))
            else:
                out.append(pl.ds(0, size))
        else:
            out.append(slot(at, axis, shifted[1] if shifted is not None and shifted[0] == axis else 0))
    return tuple(out)


def greet(at):
    barrier = pltpu.get_barrier_semaphore()
    for axis in ("x", "y", "z"):
        for by in (1, -1, 2):
            pl.semaphore_signal(barrier, inc=1, device_id=peer(at, axis, by), device_id_type=MESH)
    pl.semaphore_signal(barrier, inc=1, device_id=sibling(), device_id_type=MESH)
    pl.semaphore_wait(barrier, 10)


def sent(src, dst, send, recv, device):
    copy = pltpu.make_async_remote_copy(
        src_ref=src, dst_ref=dst, send_sem=send, recv_sem=recv, device_id=device, device_id_type=MESH
    )
    copy.start()
    return copy


def moved(src, dst, sem):
    copy = pltpu.make_async_copy(src, dst, sem)
    copy.start()
    return copy


class Gather:
    @staticmethod
    def semaphores(orders):
        count = len(orders)
        shapes = (count,), (count, 2, 3), (count, 2, 3), (count, 2, 2, 3), (count, 2, 2, 3)
        return [pltpu.SemaphoreType.DMA(shape) for shape in shapes]

    def __init__(self, at, srcs, outs, semaphores, orders):
        self.at, self.srcs, self.outs, self.orders = at, srcs, outs, orders
        self.local, self.send, self.recv, self.ring_send, self.ring_recv = semaphores
        self.own, self.direct, self.ring = [], {}, {}

    def arrive(self, p, stage):
        for copy in self.direct.get((p, stage), ()):
            copy.wait_recv()
        if (p, stage, 0, 0) in self.ring:
            for d in range(2):
                self.ring[p, stage, d, 1 - d].wait_recv()
                self.ring[p, stage, d, 2].wait_recv()

    def to_all(self, stage):
        at = self.at
        for p, order in enumerate(self.orders):
            if stage:
                self.own[p].wait()
                self.arrive(p, 0)
            else:
                self.own.append(moved(self.srcs[p], self.outs[p].at[place(at, order, 0)], self.local.at[p]))
            group = self.outs[p].at[place(at, order, stage)]
            self.direct[p, stage] = [
                sent(
                    group if stage else self.srcs[p],
                    group,
                    self.send.at[p, stage, d],
                    self.recv.at[p, stage, d],
                    peer(at, order[stage], by),
                )
                for d, by in enumerate(others(order[stage]))
            ]

    def pass_on(self, p, stage, d, k, block):
        self.ring[p, stage, d, k] = sent(
            block,
            block,
            self.ring_send.at[p, stage - 1, d, k],
            self.ring_recv.at[p, stage - 1, d, k],
            peer(self.at, self.orders[p][stage], 1 - 2 * d),
        )

    def spread(self, stage, *pieces):
        for p in pieces or range(len(self.orders)):
            order = self.orders[p]
            if stage == 1:
                self.own[p].wait()
            self.arrive(p, stage - 1)
            for t in range(2):
                for d in range(2):
                    h = t if d == 0 else 1 - t
                    self.pass_on(p, stage, d, h, self.outs[p].at[place(self.at, order, stage, (order[0], h))])

    def forward(self, stage):
        for p, order in enumerate(self.orders):
            for d, by in enumerate((1, -1)):
                self.ring[p, stage, d, d].wait_recv()
                where = place(self.at, order, stage, (order[0], d), (order[stage], -by))
                self.pass_on(p, stage, d, 2, self.outs[p].at[where])

    def finish(self):
        for copies in self.direct.values():
            for copy in copies:
                copy.wait_send()
        for copy in self.ring.values():
            copy.wait_send()


class Reduce:
    @staticmethod
    def semaphores(orders):
        count = len(orders)
        shapes = (count, 3), *[(count, 2, 3)] * 4, (count, 2), (count, 2)
        return [pltpu.SemaphoreType.DMA(shape) for shape in shapes]

    @staticmethod
    def buffers(columns, orders):
        def per_piece(*shape):
            return [pltpu.VMEM(shape + (48, width), BF) for width in columns]

        size = extent(dimensions(orders[0])[0])
        return [
            *per_piece(2, size // 2, 4),
            *per_piece(size, 4),
            *per_piece(2, size // 2, 4),
            *per_piece(2, size, 4),
            *per_piece(3, size),
            *per_piece(3),
            *[pltpu.VMEM((48, width), F32) for width in columns],
        ]

    def __init__(self, at, data, buffers, semaphores, orders):
        self.at, self.data, self.orders = at, data, orders
        self.side, self.kept, self.far, self.near, self.second, self.third, self.sums = (
            buffers[len(orders) * k : len(orders) * (k + 1)] for k in range(7)
        )
        self.load, self.first_send, self.first_recv, self.send, self.recv, self.end_send, self.end_recv = semaphores
        self.loads, self.copies = {}, {}

    def left(self, p):
        order = self.orders[p]
        return [axis for axis in dimensions(order) if axis != order[2]]

    def inside(self, p, first, second=None):
        whole = slice(None) if second is None else second
        return (first, whole) if self.left(p)[0] == self.orders[p][1] else (whole, first)

    def start(self, *pieces):
        at, s, r = self.at, self.first_send, self.first_recv
        for p in pieces or range(len(self.orders)):
            order = self.orders[p]
            axis, cut = order[2], self.left(p)[0]
            size = extent(cut) // 2
            for d, by in enumerate((1, -1)):
                block = self.data[p].at[place(at, order, 2, (cut, d), (axis, 2))]
                self.copies[p, d, 0] = sent(block, self.far[p].at[d], s.at[p, d, 0], r.at[p, d, 0], peer(at, axis, by))
            for d, by in enumerate((1, -1)):
                h = 1 - d
                block = self.data[p].at[place(at, order, 2, (cut, h), (axis, by))]
                self.copies[p, d, 1] = sent(
                    block, self.near[p].at[d, pl.ds(size * h, size)], s.at[p, d, 1], r.at[p, d, 1], peer(at, axis, by)
                )
                block = self.data[p].at[place(at, order, 2, (cut, d), (axis, by))]
                self.loads[p, d] = moved(block, self.side[p].at[d], self.load.at[p, d])
            self.loads[p, 2] = moved(self.data[p].at[place(at, order, 2)], self.kept[p], self.load.at[p, 2])

    def relay(self):
        for p, order in enumerate(self.orders):
            size = extent(self.left(p)[0]) // 2
            for d, by in enumerate((1, -1)):
                self.loads[p, d].wait()
                self.copies[p, d, 0].wait_recv()
                side, far = self.side[p], self.far[p]

                @pl.loop(0, 4 * size)
                def _(i, d=d, side=side, far=far):
                    a, b = i // 4, lax.rem(i, 4)
                    side[d, a, b] = side[d, a, b] + far[d, a, b]

                self.copies[p, d, 2] = sent(
                    side.at[d],
                    self.near[p].at[d, pl.ds(size * d, size)],
                    self.first_send.at[p, d, 2],
                    self.first_recv.at[p, d, 2],
                    peer(self.at, order[2], by),
                )

    def spread(self):
        at = self.at
        for p, order in enumerate(self.orders):
            self.loads[p, 2].wait()
            for d in range(2):
                self.copies[p, d, 1].wait_recv()
                self.copies[p, d, 2].wait_recv()
            kept, near = self.kept[p], self.near[p]
            for d, by in enumerate((*others(order[1]), 0)):
                group = slot(at, order[1], by)

                @pl.loop(0, extent(order[0]))
                def _(i, p=p, kept=kept, near=near, group=group):
                    where = self.inside(p, group, i)
                    total = kept[where].astype(F32) + near[(0, *where)].astype(F32) + near[(1, *where)].astype(F32)
                    kept[where] = total.astype(BF)

                if by:
                    self.copies[p, "b", d] = sent(
                        kept.at[self.inside(p, group)],
                        self.second[p].at[d],
                        self.send.at[p, 0, d],
                        self.recv.at[p, 0, d],
                        peer(at, order[1], by),
                    )

    def narrow(self):
        at = self.at
        for p, order in enumerate(self.orders):
            for d in range(len(others(order[1]))):
                self.copies[p, "b", d].wait_recv()
            kept, second, mine = self.kept[p], self.second[p], slot(at, order[1])
            for d, by in enumerate((*others(order[0]), 0)):
                index = slot(at, order[0], by)
                where = self.inside(p, mine, index)
                total = kept[where].astype(F32)
                for k in range(3):
                    total = total + second[k, index].astype(F32)
                kept[where] = total.astype(BF)
                if by:
                    self.copies[p, "c", d] = sent(
                        kept.at[where],
                        self.third[p].at[d],
                        self.send.at[p, 1, d],
                        self.recv.at[p, 1, d],
                        peer(at, order[0], by),
                    )

    def finish(self, outs):
        at, core, ends = self.at, lax.axis_index("core"), []
        for p, order in enumerate(self.orders):
            total = self.kept[p][self.inside(p, slot(at, order[1]), slot(at, order[0]))].astype(F32)
            for d in range(len(others(order[0]))):
                self.copies[p, "c", d].wait_recv()
                total = total + self.third[p][d].astype(F32)
            self.sums[p][...] = total
            theirs = self.sums[p].at[pl.ds(pl.multiple_of(24 * (1 - core), 8), 24)]
            mine = self.sums[p].at[pl.ds(pl.multiple_of(24 * core, 8), 24)]
            ends.append(sent(theirs, outs[p].at[core], self.end_send.at[p, 0], self.end_recv.at[p, 0], sibling()))
            ends.append(moved(mine, outs[p].at[core], self.end_send.at[p, 1]))
        for copy in self.copies.values():
            copy.wait_send()
        for copy in ends:
            copy.wait()


def in_four(refs):
    half = refs[2].shape[-1] // 2
    lead = (slice(None),) * (len(refs[2].shape) - 1)
    return [refs[0], refs[1], *(refs[2].at[(*lead, pl.ds(k * half, half))] for k in range(2))]


def nn(left, right):
    return lax.dot_general(left, right, (((1,), (0,)), ((), ())), preferred_element_type=F32)


def nt(left, right):
    return lax.dot_general(left, right, (((1,), (1,)), ((), ())), preferred_element_type=F32)


def tn(left, right):
    return lax.dot_general(left, right, (((0,), (0,)), ((), ())), preferred_element_type=F32)


def inverse_rms(values):
    return lax.rsqrt(jnp.mean(values * values, -1, keepdims=True) + EPS)


def swap(values, first):
    width = values.shape[-1]
    return jnp.where(first, pltpu.roll(values, width - HEAD // 2, 1), pltpu.roll(values, HEAD // 2, 1))


def first_half(shape):
    return lax.rem(lax.broadcasted_iota(jnp.int32, shape, 1), HEAD) < HEAD // 2


def as_column(row):
    size = row.shape[1]
    square = jnp.broadcast_to(row[...].astype(F32), (size, size))
    diagonal = lax.broadcasted_iota(jnp.int32, (size, size), 0) == lax.broadcasted_iota(jnp.int32, (size, size), 1)
    return jnp.sum(jnp.where(diagonal, square, 0.0), -1, keepdims=True)


def rows_at(start, size):
    return pl.ds(pl.multiple_of(start, size), size)


ANY = pl.BlockSpec(memory_space=pl.ANY)
VMEM = pl.BlockSpec(memory_space=pltpu.VMEM)


def shaped(shape, kind=BF):
    return jax.ShapeDtypeStruct(shape, kind)


def call(kernel, operands, in_specs, results, out_specs, scratch, name, collective_id, **more):
    return pl.pallas_call(
        kernel,
        out_shape=results,
        in_specs=in_specs,
        out_specs=out_specs,
        scratch_shapes=scratch,
        compiler_params=pltpu.CompilerParams(
            collective_id=collective_id, has_side_effects=True, vmem_limit_bytes=VMEM_LIMIT
        ),
        name=name,
        **more,
    )(*operands)


def hidden_units(m, c, count, sub, n2, cot, weights, acts):
    rows = pl.ds(pl.multiple_of(m * ROWS + c * SEQ, SEQ), count * SEQ)
    columns = pl.ds(sub * CHUNK, CHUNK)
    gate_w, up_w, down_w = (w[..., columns].reshape(-1, CHUNK) for w in weights)
    gate = nn(n2[rows], gate_w)
    up = nn(n2[rows], up_w)
    sigma = jax.nn.sigmoid(gate)
    silu = gate * sigma
    grad_active = nn(cot[m, pl.ds(c, count)].reshape(count * SEQ, -1), down_w)
    acts[0][rows, columns] = (silu * up).astype(BF)
    acts[1][rows, columns] = (grad_active * up * (sigma + silu * (1.0 - sigma))).astype(BF)
    acts[2][rows, columns] = (grad_active * silu).astype(BF)


def unit_gradients(n2t, cott, acts, staging, outs, sems, rows=None, added=False, written=True):
    whole, copies = slice(None) if rows is None else rows, []
    for k, (left, right, target) in enumerate(((n2t, acts[1], 0), (n2t, acts[2], 1), (cott, acts[0], 2))):
        for sub in range(2):
            columns = pl.ds(sub * CHUNK, CHUNK)
            value = nn(left[:, whole], right[whole, columns])
            if added:
                value = value + staging[2 * k + sub].astype(F32)
            staging[2 * k + sub] = value.astype(BF)
            if written:
                copies.append(moved(staging.at[2 * k + sub], outs[target].at[:, columns], sems.at[2 * k + sub]))
    return copies


def forward_kernel(third, wide, *refs):
    own_weights, gains_one, gains_two, lengths, xin, gin, tables_in = refs[:7], *refs[7:13]
    refs = refs[1:]
    full_two, full_one = refs[12:15], refs[15:18]
    (
        x_out, n1t_out, q_out, kv_out, probs_out, mixed_out, hidden_out, n2_out, n2t_out, cot_out, cott_out,
    ) = refs[18:29]
    attn_out, grads_out, acts_out, shard_out = refs[29:32], refs[32:35], refs[35:38], refs[38]
    refs = refs[1:]
    (
        shard, got_shard, packed, xs, gs, normed, q, kv, probs, mixed, hidden, n2, n2t, cott, part, arrived, n1t,
        valid, staging,
    ) = refs[38:57]
    full_attn, weights, acts = refs[57:60], refs[60:63], refs[63:66]
    attn_sems, one_sems, two_sems = refs[66:71], refs[71:76], refs[76:81]
    tables, pair_send, pair_recv, row_send, row_recv, far_send, far_recv, own_sem, out_sem, put_sem = refs[81:]
    at = coordinates()
    core, yl = lax.axis_index("core"), lax.axis_index("yl")
    own_x = moved(xin.at[yl], xs.at[core, yl], own_sem.at[0])
    own_g = moved(gin, gs.at[:, core, yl], own_sem.at[1])
    table_copy = moved(tables_in, tables, own_sem.at[2])

    query, key, value, output, *mlp_weights = (ref[...].astype(F32) for ref in own_weights)
    gain_one, gain_two = as_column(gains_one), as_column(gains_two)
    small = key.shape[1] // 2
    for c in range(2):
        thin = slice(c * small, (c + 1) * small)
        parts = [
            query[:, c * third : (c + 1) * third] * gain_one,
            jnp.concatenate([key[:, thin] * gain_one, value[:, thin] * gain_one], -1),
            output[:, c * third : (c + 1) * third],
            *(
                w[:, c * wide : (c + 1) * wide] * g
                for w, g in zip(mlp_weights, (gain_two, gain_two, jnp.ones_like(gain_two)))
            ),
        ]
        column = 0
        for part_value in parts:
            shard[c, :24, column : column + part_value.shape[1]] = part_value
            column += part_value.shape[1]
        lane = lax.broadcasted_iota(jnp.int32, (8, 2 * SEQ), 1)
        ends = jnp.where(lane < SEQ, lengths[:, 0:1], lengths[:, 1:2] + SEQ)
        shard[c, 24:, : 2 * SEQ] = jnp.where(lane < ends, 1.0, 0.0)
    greet(at)
    swap_shard = sent(shard.at[1 - core], got_shard, pair_send.at[0], pair_recv.at[0], sibling())

    rows = {}

    def exchange(k):
        ours, theirs, dst = (
            (xin.at[yl], xin.at[1 - yl], xs.at[core, yl]),
            (gin, gin, gs.at[:, core, yl]),
        )[k]
        rows[k, 0] = sent(theirs, dst, row_send.at[k, 0], row_recv.at[k, 0], partner())
        rows[k, 1] = sent(ours, dst, row_send.at[k, 1], row_recv.at[k, 1], sibling())

    def share(k):
        block = (xs.at[core, 1 - yl], gs.at[:, core, 1 - yl])[k]
        rows[k, 0].wait_recv()
        rows[k, 2] = sent(block, block, row_send.at[k, 2], row_recv.at[k, 2], sibling())

    def settle(k):
        (own_x, own_g)[k].wait()
        rows[k, 0].wait_send()
        rows[k, 1].wait()
        rows[k, 2].wait()

    swap_shard.wait()
    low, high = shard[core], got_shard[...]
    first, last = jnp.where(core == 0, low, high), jnp.where(core == 0, high, low)
    packed[...] = jnp.concatenate([first[:24], last[:24]], 0).astype(BF)
    for c, rows_of in enumerate((first, last)):
        for m in range(2):
            valid[m, c] = rows_of[24:32, m * SEQ : (m + 1) * SEQ]

    def pieces(start, size, step):
        return [packed.at[:, pl.ds(start + k * step, size)] for k in range(3)]

    half = wide // 2
    attn = Gather(at, pieces(0, third, third), full_attn, attn_sems, EVEN)
    one = Gather(at, pieces(3 * third, half, wide), weights, one_sems, PLANE_Z)
    two = Gather(at, pieces(3 * third + half, half, wide), full_two, two_sems, PLANE_X)
    attn.to_all(0)
    one.to_all(0)
    attn.to_all(1)
    one.spread(1)
    attn.spread(2, 0, 1)
    exchange(0)
    attn.spread(2, 2)
    two.to_all(0)
    one.forward(1)
    attn.forward(2)
    one.spread(2)
    share(0)
    settle(0)
    exchange(1)
    outs = [moved(xs, x_out, out_sem.at[0]), moved(shard, shard_out, out_sem.at[24])]

    @pl.loop(0, ROWS // STEP)
    def _(i):
        block = rows_at(i * STEP, STEP)
        values = xs[i // 2, lax.rem(i, 2)].astype(F32)
        normed[block] = (values * inverse_rms(values)).astype(BF)

    for p in range(2):
        attn.arrive(p, 2)
    two.spread(1)
    wq, wkv, wo = full_attn
    table_copy.wait()

    def weight(ref, y):
        return ref[pl.ds(2 * y, 2)].reshape(-1, third)

    @pl.loop(0, 2)
    def _(y):
        @pl.loop(0, ROWS // SEQ)
        def _(n):
            block = rows_at(n * SEQ, SEQ)
            left = normed[block]
            is_first = first_half((SEQ, third))
            for k, (w, result) in enumerate(((wq, q), (wkv, kv))):
                lin = nn(left, weight(w, y))
                result[y, block] = (lin * tables[2 * k] + swap(lin, is_first) * tables[2 * k + 1]).astype(BF)

    outs.append(moved(q, q_out, out_sem.at[5]))
    outs.append(moved(kv, kv_out, out_sem.at[6]))
    two.forward(1)
    one.forward(2)
    scale = 1.0 / math.sqrt(HEAD)

    @pl.loop(0, 4)
    def _(i):
        y, n = i // 2, lax.rem(i, 2)
        block = rows_at(n * SEQ, SEQ)
        t = lax.broadcasted_iota(jnp.int32, (SEQ, SEQ), 0)
        s = lax.broadcasted_iota(jnp.int32, (SEQ, SEQ), 1)
        keep = (s <= t) & (valid[yl, n, 0:1, :] > 0.5)
        queries, keys = q[y, block], kv[y, block]
        results = []
        for h in range(4):
            g = h // 2
            scores = nt(queries[:, h * HEAD : (h + 1) * HEAD], keys[:, g * HEAD : (g + 1) * HEAD]) * scale
            scores = jnp.where(keep, scores, -1e30)
            terms = jnp.exp(scores - jnp.max(scores, -1, keepdims=True))
            low_probs = (terms * (1.0 / jnp.sum(terms, -1, keepdims=True))).astype(BF)
            probs[i, h] = low_probs
            results.append(nn(low_probs, keys[:, (2 + g) * HEAD : (3 + g) * HEAD]))
        mixed[y, block] = jnp.concatenate(results, -1).astype(BF)

    outs.append(moved(probs, probs_out, out_sem.at[7]))
    outs.append(moved(mixed, mixed_out, out_sem.at[8]))
    two.spread(2)

    attn.arrive(2, 2)
    copies = []
    for i in range(ROWS // STEP):
        block = rows_at(lax.rem(2 * (1 - core) + i, 4) * STEP, STEP)
        part[block] = (nt(mixed[0, block], weight(wo, 0)) + nt(mixed[1, block], weight(wo, 1))).astype(BF)
        copies.append(sent(part.at[block], arrived.at[block], pair_send.at[1 + i], pair_recv.at[1 + i], sibling()))
    second_rows = {}
    mine, theirs = yl * ROWS, (1 - yl) * ROWS
    for i in range(ROWS // STEP):
        copies[(i + 2) % 4 if i < 2 else i - 2].wait_send()
        copies[i].wait_recv()
        number = lax.rem(2 * core + i, 4)
        block = rows_at(number * STEP, STEP)
        values = xs[number // 2, lax.rem(number, 2)].astype(F32) + (
            part[block].astype(F32) + arrived[block].astype(F32)
        )
        hidden[block] = values
        target = rows_at(mine + number * STEP, STEP)
        n2[target] = (values * inverse_rms(values)).astype(BF)
        if i < 2:
            second_rows[0, i] = sent(n2.at[target], n2.at[target], far_send.at[0, i], far_recv.at[0, i], partner())
    outs.append(moved(hidden.at[rows_at(core * SEQ, SEQ)], hidden_out, out_sem.at[9]))
    attn.finish()
    outs.extend(moved(full_attn[p], attn_out[p], out_sem.at[2 + p]) for p in range(3))
    share(1)
    settle(1)

    for m in range(2):
        for c in range(2):
            for h in range(2):
                mask = valid[m, c][:, h * STEP : (h + 1) * STEP].T[:, 0:1]
                gs[m, c, h] = (gs[m, c, h].astype(F32) * mask).astype(BF)
    outs.append(moved(gs, cot_out, out_sem.at[10]))

    for p in range(3):
        one.arrive(p, 2)
    one.finish()
    outs.extend(moved(weights[p], full_one[p], out_sem.at[11 + p]) for p in range(3))
    mine_rows, their_rows = rows_at(mine, ROWS), rows_at(theirs, ROWS)
    for sub in range(2):
        hidden_units(yl, 0, 2, sub, n2, gs, weights, acts)
    two.forward(2)
    outs.extend(moved(acts[p].at[mine_rows], acts_out[p].at[mine_rows], out_sem.at[15 + p]) for p in range(3))
    outs.append(moved(n2.at[mine_rows], n2_out.at[mine_rows], out_sem.at[18]))
    for m in range(2):
        for c in range(2):
            for h in range(2):
                cott[:, pl.ds(m * ROWS + (2 * c + h) * STEP, STEP)] = gs[m, c, h].T
    outs.append(moved(cott, cott_out, out_sem.at[14]))
    for i in range(ROWS // STEP):
        block = rows_at(mine + i * STEP, STEP)
        n2t[:, block] = n2[block].T
    unit_gradients(n2t, cott, acts, staging, grads_out, put_sem, mine_rows, written=False)
    n1t[...] = normed[...].T
    outs.append(moved(n1t, n1t_out, out_sem.at[1]))

    for i in range(2):
        second_rows[0, i].wait_recv()
        block = rows_at(theirs + (2 * core + i) * STEP, STEP)
        second_rows[1, i] = sent(n2.at[block], n2.at[block], far_send.at[1, i], far_recv.at[1, i], sibling())
    for sub in range(2):
        hidden_units(1 - yl, core, 1, sub, n2, gs, weights, acts)
    for i in range(2):
        block = rows_at(theirs + (2 * core + i) * STEP, STEP)
        n2t[:, block] = n2[block].T
    for i in range(2):
        second_rows[0, i].wait_send()
        second_rows[1, i].wait()
    for sub in range(2):
        hidden_units(1 - yl, 1 - core, 1, sub, n2, gs, weights, acts)
    outs.extend(moved(acts[p].at[their_rows], acts_out[p].at[their_rows], out_sem.at[20 + p]) for p in range(3))
    outs.append(moved(n2.at[their_rows], n2_out.at[their_rows], out_sem.at[23]))
    for i in range(2):
        block = rows_at(theirs + (2 * (1 - core) + i) * STEP, STEP)
        n2t[:, block] = n2[block].T
    outs.append(moved(n2t, n2t_out, out_sem.at[19]))
    outs.extend(unit_gradients(n2t, cott, acts, staging, grads_out, put_sem, their_rows, added=True))
    for p in range(3):
        two.arrive(p, 2)
    two.finish()
    for copy in outs:
        copy.wait()


def forward(own_weights, gains, lengths, xin, gin, tables, third, wide):
    width = xin.shape[2]
    rows = (ROWS, width)
    both = (2 * ROWS, width)
    heads = (2, ROWS, third)
    square = (4, 4, SEQ, SEQ)
    half = wide // 2
    piece = (2, 4, 4, 48, half)
    return call(
        lambda *refs: forward_kernel(third, wide, *refs),
        (*own_weights, *gains, lengths, xin, gin, tables),
        [VMEM] * 10 + [ANY, ANY, ANY],
        [shaped(piece)] * 6
        + [
            shaped((2, 2, 128, width)),
            shaped(rows[::-1]),
            shaped(heads),
            shaped(heads),
            shaped(square),
            shaped(heads),
            shaped((SEQ, width), F32),
            shaped(both),
            shaped(both[::-1]),
            shaped((2, 2, 2, 128, width)),
            shaped(both[::-1]),
        ]
        + [shaped((4, 4, 4, 48, third))] * 3
        + [shaped((width, half))] * 3
        + [shaped((2 * ROWS, half))] * 3
        + [shaped((2, 32, 3 * third + 3 * wide), F32)],
        [ANY] * 27,
        [
            pltpu.VMEM((2, 32, 3 * third + 3 * wide), F32),
            pltpu.VMEM((32, 3 * third + 3 * wide), F32),
            pltpu.VMEM((48, 3 * third + 3 * wide), BF),
            pltpu.VMEM((2, 2, 128, width), BF),
            pltpu.VMEM((2, 2, 2, 128, width), BF),
            pltpu.VMEM(rows, BF),
            pltpu.VMEM(heads, BF),
            pltpu.VMEM(heads, BF),
            pltpu.VMEM(square, BF),
            pltpu.VMEM(heads, BF),
            pltpu.VMEM(rows, F32),
            pltpu.VMEM(both, BF),
            pltpu.VMEM(both[::-1], BF),
            pltpu.VMEM(both[::-1], BF),
            pltpu.VMEM(rows, BF),
            pltpu.VMEM(rows, BF),
            pltpu.VMEM(rows[::-1], BF),
            pltpu.VMEM((2, 2, 8, SEQ), F32),
            pltpu.VMEM((6, width, CHUNK), BF),
            *[pltpu.VMEM((4, 4, 4, 48, third), BF) for _ in range(3)],
            *[pltpu.VMEM(piece, BF) for _ in range(3)],
            *[pltpu.VMEM((2 * ROWS, half), BF) for _ in range(3)],
            *Gather.semaphores(EVEN),
            *Gather.semaphores(PLANE_Z),
            *Gather.semaphores(PLANE_X),
            pltpu.VMEM(tables.shape, F32),
            pltpu.SemaphoreType.DMA((5,)),
            pltpu.SemaphoreType.DMA((5,)),
            pltpu.SemaphoreType.DMA((2, 3)),
            pltpu.SemaphoreType.DMA((2, 3)),
            pltpu.SemaphoreType.DMA((2, 2)),
            pltpu.SemaphoreType.DMA((2, 2)),
            pltpu.SemaphoreType.DMA((3,)),
            pltpu.SemaphoreType.DMA((25,)),
            pltpu.SemaphoreType.DMA((6,)),
        ],
        "gather_attn_forward_mlp",
        1,
    )


def middle_kernel(*refs):
    n2_in, cot_in, hidden_in, n2t_in, cott_in = refs[:5]
    one_in, two_in, acts_in, data = refs[5:8], refs[8:11], refs[11:14], refs[14:17]
    sums_out, grads_out = refs[17:20], refs[20:23]
    kept_out, away_out, branch_out, grad_hidden_out = refs[23:27]
    (
        n2, cot, hidden, n2t, cott, staging, to_pair, from_pair, whole, from_far, keep, halves, to_far, branch, gh,
    ) = refs[27:42]
    one, two, acts_one, acts_two = refs[42:45], refs[45:48], refs[48:51], refs[51:54]
    buffers, reduce_sems = refs[54:82], refs[82:89]
    load, put, put_sem, pair_send, pair_recv, part_send, part_recv, far_send, far_recv = refs[89:]
    core, yl = lax.axis_index("core"), lax.axis_index("yl")
    at = coordinates()
    order = (
        (n2_in, n2),
        (two_in[0], two[0]),
        (two_in[1], two[1]),
        (cot_in, cot),
        (two_in[2], two[2]),
        *zip(acts_in[1:], acts_one[1:]),
        *zip(one_in[:2], one[:2]),
        (acts_in[0], acts_one[0]),
        (one_in[2], one[2]),
        (n2t_in, n2t),
        (cott_in, cott),
        (hidden_in, hidden),
    )
    loads = [moved(src, dst, load.at[k]) for k, (src, dst) in enumerate(order)]
    greet(at)
    total = Reduce(at, in_four(data), buffers, reduce_sems, PLANE)
    total.start()
    for k in range(5):
        loads[k].wait()
    for sub in range(2):
        hidden_units(1 - yl, 0, 2, sub, n2, cot, two, acts_two)
    for k in range(5, 11):
        loads[k].wait()

    def weight(ref):
        return ref[...].reshape(n2.shape[1], -1)

    def grad_rows(m, c):
        rows = rows_at(m * ROWS + c * SEQ, SEQ)
        return (nt(acts_one[1][rows], weight(one[0])) + nt(acts_one[2][rows], weight(one[1]))) + (
            nt(acts_two[1][rows], weight(two[0])) + nt(acts_two[2][rows], weight(two[1]))
        )

    def out_rows(m, c):
        rows = rows_at(m * ROWS + c * SEQ, SEQ)
        return nt(acts_one[0][rows], weight(one[2])) + nt(acts_two[0][rows], weight(two[2]))

    pair, far, shared = {}, {}, []

    def to_sibling(k, value):
        to_pair[k] = value.astype(BF)
        pair[k] = sent(to_pair.at[k], from_pair.at[k], pair_send.at[k], pair_recv.at[k], sibling())

    blocks = [pl.ds(i * STEP, STEP) for i in range(2)]
    to_pair[0] = grad_rows(1 - yl, 1 - core).astype(BF)
    for i, rows in enumerate(blocks):
        pair["far", i] = sent(
            to_pair.at[0, rows], from_pair.at[0, rows], part_send.at[0, i], part_recv.at[0, i], sibling()
        )
    keep[...] = grad_rows(1 - yl, core)
    for i, rows in enumerate(blocks):
        pair["far", i].wait_recv()
        whole[rows] = (keep[rows] + from_pair[0, rows].astype(F32)).astype(BF)
        far[i] = sent(whole.at[rows], from_far.at[rows], far_send.at[i], far_recv.at[i], partner())
    total.relay()
    for sub in range(2):
        hidden_units(yl, 0, 2, sub, n2, cot, two, acts_two)
    to_sibling(1, grad_rows(yl, 1 - core))
    keep[...] = grad_rows(yl, core)
    to_sibling(2, out_rows(1 - yl, 1 - core))
    to_sibling(3, out_rows(yl, 1 - core))
    for k in range(11, 14):
        loads[k].wait()
    total.spread()
    outs = unit_gradients(n2t, cott, acts_two, staging, grads_out, put_sem)
    total.narrow()

    for k, m in ((2, 1 - yl), (3, yl)):
        pair[k].wait_recv()
        value = out_rows(m, core) + from_pair[k].astype(F32)
        if k == 3:
            value = value + hidden[...]
        halves[k - 2] = value.reshape(2, STEP, -1)
        to_far[k - 2] = halves[k - 2, 1 - yl].astype(BF)
        outs.append(moved(halves.at[k - 2, yl], kept_out.at[k - 2], put.at[k]))
        outs.append(moved(to_far.at[k - 2], away_out.at[k - 2], put.at[k + 2]))
    pair[1].wait_recv()

    for i, rows in enumerate(blocks):
        far[i].wait_recv()
        grad = keep[rows] + (from_pair[1, rows].astype(F32) + from_far[rows].astype(F32))
        values = hidden[rows]
        inverse = inverse_rms(values)
        unit = values * inverse
        back = inverse * (grad - unit * jnp.mean(grad * unit, -1, keepdims=True))
        gh[rows] = cot[yl, core, i].astype(F32) + back
        branch[rows] = gh[rows].astype(BF)
        target = rows_at(core * SEQ + i * STEP, STEP)
        shared.append(
            sent(branch.at[rows], branch_out.at[target], part_send.at[1, i], part_recv.at[1, i], sibling())
        )
        outs.append(moved(branch.at[rows], branch_out.at[target], put.at[6 + i]))
    outs.append(moved(gh, grad_hidden_out, put.at[0]))
    total.finish(in_four(sums_out))
    for copy in shared:
        copy.wait()
    for copy in (*pair.values(), *far.values()):
        copy.wait_send()
    for copy in outs:
        copy.wait()


def middle(n2, cot, hidden, n2t, cott, one, two, acts, data):
    rows, width = n2.shape
    half = one[0].shape[-1]
    block = (SEQ, width)
    return call(
        middle_kernel,
        (n2, cot, hidden, n2t, cott, *one, *two, *acts, *data),
        [ANY] * 17,
        [shaped((2, 24, half), F32)] * 3
        + [shaped((width, half))] * 3
        + [
            shaped((2, STEP, width), F32),
            shaped((2, STEP, width)),
            shaped((ROWS, width)),
            shaped(block, F32),
        ],
        [ANY] * 10,
        [
            pltpu.VMEM((rows, width), BF),
            pltpu.VMEM(cot.shape, BF),
            pltpu.VMEM(block, F32),
            pltpu.VMEM((width, rows), BF),
            pltpu.VMEM((width, rows), BF),
            pltpu.VMEM((6, width, CHUNK), BF),
            pltpu.VMEM((4,) + block, BF),
            pltpu.VMEM((4,) + block, BF),
            pltpu.VMEM(block, BF),
            pltpu.VMEM(block, BF),
            pltpu.VMEM(block, F32),
            pltpu.VMEM((2, 2, STEP, width), F32),
            pltpu.VMEM((2, STEP, width), BF),
            pltpu.VMEM(block, BF),
            pltpu.VMEM(block, F32),
            *[pltpu.VMEM(one[0].shape, BF) for _ in range(6)],
            *[pltpu.VMEM((rows, half), BF) for _ in range(6)],
            *Reduce.buffers((half, half, half // 2, half // 2), PLANE),
            *Reduce.semaphores(PLANE),
            pltpu.SemaphoreType.DMA((14,)),
            pltpu.SemaphoreType.DMA((8,)),
            pltpu.SemaphoreType.DMA((6,)),
            pltpu.SemaphoreType.DMA((4,)),
            pltpu.SemaphoreType.DMA((4,)),
            pltpu.SemaphoreType.DMA((2, 2)),
            pltpu.SemaphoreType.DMA((2, 2)),
            pltpu.SemaphoreType.DMA((2,)),
            pltpu.SemaphoreType.DMA((2,)),
        ],
        "mlp_reduce",
        2,
    )


def backward_kernel(*refs):
    xall, grad_hidden_in, branch_in, n1t_in, q_in, kv_in, probs_in, mixed_in, wq_in, wkv_in, wo_in, tables_in = refs[:12]
    data, kept_in, away, shard_in, one_in = refs[12:15], *refs[15:18], refs[18:20]
    refs = refs[3:]
    mlp_outs, attn_outs, result_out, in_grad_out, from_partner = refs[17:20], refs[20:23], *refs[23:26]
    gains_out, gain_in = refs[26:28]
    refs = refs[2:]
    (
        xs, gh, branch, branch_t, normed_t, q, kv, probs, mixed, wq, wkv, wo,
        grad_mixed, dq, dkv, part, keep_part, arrived, in_grad, for_partner, kept, others_half, result,
    ) = refs[26:49]
    attn_grads = refs[49:52]
    mlp_buffers, attn_buffers = refs[52:80], refs[80:101]
    mlp_sems, attn_sems = refs[101:108], refs[108:115]
    mlp_ends, attn_ends, shard, one_sums, gain_part, tables = refs[115:118], refs[118:121], *refs[121:125]
    load, put, send, recv = refs[125:]
    at = coordinates()
    core, yl = lax.axis_index("core"), lax.axis_index("yl")
    loads = [
        moved(src, dst, load.at[k])
        for k, (src, dst) in enumerate(
            (
                (branch_in, branch),
                (wo_in, wo),
                (mixed_in, mixed),
                (q_in, q),
                (kv_in, kv),
                (probs_in, probs),
                (n1t_in, normed_t),
                (wq_in, wq),
                (wkv_in, wkv),
                (grad_hidden_in, gh),
                (xall.at[core], xs),
                (kept_in, kept),
                (shard_in, shard),
                (one_in[0], one_sums.at[0]),
                (one_in[1], one_sums.at[1]),
                (tables_in, tables),
            )
        )
    ]
    greet(at)
    mlp_sum = Reduce(at, in_four(data), mlp_buffers, mlp_sems, PLANE)
    attn_sum = Reduce(at, attn_grads, attn_buffers, attn_sems, SPARE_Y)
    mlp_sum.start()
    finals = [sent(away.at[k], others_half.at[k], send.at[2 + k], recv.at[2 + k], partner()) for k in range(2)]
    for k in range(2):
        loads[k].wait()
    for y in range(2):
        grad_mixed[y] = nn(branch[...], wo[y]).astype(BF)
    for k in (2, 3, 4, 5, 15):
        loads[k].wait()
    scale = 1.0 / math.sqrt(HEAD)

    def attention(i):
        y, n = i // 2, lax.rem(i, 2)
        rows = rows_at(n * SEQ, SEQ)
        queries, keys, grads = q[y, rows], kv[y, rows], grad_mixed[y, rows]
        grad_q, grad_k, grad_v = [], [None, None], [None, None]
        for h in range(4):
            g = h // 2
            key = keys[:, g * HEAD : (g + 1) * HEAD]
            value = keys[:, (2 + g) * HEAD : (3 + g) * HEAD]
            query = queries[:, h * HEAD : (h + 1) * HEAD]
            grad = grads[:, h * HEAD : (h + 1) * HEAD]
            low = probs[i, h]
            prob = low.astype(F32)
            grad_probs = nt(grad, value)
            grad_scores = (prob * (grad_probs - jnp.sum(grad_probs * prob, -1, keepdims=True))).astype(BF)
            grad_q.append(nn(grad_scores, key) * scale)
            back_k = tn(grad_scores, query) * scale
            back_v = tn(low, grad)
            grad_k[g] = back_k if grad_k[g] is None else grad_k[g] + back_k
            grad_v[g] = back_v if grad_v[g] is None else grad_v[g] + back_v
        first = first_half((SEQ, 4 * HEAD))
        for k, (pieces, target) in enumerate(((grad_q, dq), (grad_k + grad_v, dkv))):
            values = jnp.concatenate(pieces, -1)
            target[y, rows] = (values * tables[2 * k] - swap(values, first) * tables[2 * k + 1]).astype(BF)

    pl.loop(0, 2)(attention)
    mlp_sum.relay()
    pl.loop(2, 4)(attention)
    loads[6].wait()

    def weight_grad(p, left, right):
        for y in range(2):
            target = attn_grads[p].at[pl.ds(2 * y, 2)]
            target[...] = nn(left[...], right[y]).astype(BF).reshape(target.shape)
        attn_sum.start(p)

    weight_grad(0, normed_t, dq)
    weight_grad(1, normed_t, dkv)
    mlp_sum.spread()
    branch_t[...] = branch[...].T
    weight_grad(2, branch_t, mixed)
    for k in range(7, 15):
        loads[k].wait()

    def back(start):
        rows = rows_at(start, SEQ)
        return (nt(dq[0, rows], wq[0]) + nt(dq[1, rows], wq[1])) + (nt(dkv[0, rows], wkv[0]) + nt(dkv[1, rows], wkv[1]))

    part[...] = back((1 - core) * SEQ).astype(BF)
    pair = sent(part, arrived, send.at[0], recv.at[0], sibling())
    attn_sum.relay()
    keep_part[...] = back(core * SEQ)
    mlp_sum.narrow()
    pair.wait()

    @pl.loop(0, SEQ // STEP)
    def _(i):
        rows = rows_at(i * STEP, STEP)
        grad = keep_part[rows] + arrived[rows].astype(F32)
        values = xs[i].astype(F32)
        inverse = inverse_rms(values)
        unit = values * inverse
        change = inverse * (grad - unit * jnp.mean(grad * unit, -1, keepdims=True))
        in_grad[i] = gh[rows] + change

    for_partner[...] = in_grad[1 - yl].astype(BF)
    ends = [
        moved(in_grad.at[yl], in_grad_out, put.at[0]),
        sent(for_partner, from_partner, send.at[1], recv.at[1], partner()),
    ]
    attn_sum.spread()
    for copy in finals:
        copy.wait()
    result[1 - yl] = (kept[0] + others_half[1].astype(F32)).astype(BF)
    result[yl] = (kept[1] + others_half[0].astype(F32)).astype(BF)
    ends.append(moved(result, result_out, put.at[1]))
    mlp_sum.finish(in_four(mlp_ends))
    attn_sum.narrow()
    ends.extend(moved(mlp_ends[p], mlp_outs[p], put.at[2 + p]) for p in range(3))

    def along(start, gradient):
        weights = shard[:, :24, start : start + gradient.shape[2]]
        total = jnp.sum(weights * gradient, -1, keepdims=True)
        return total[0] + total[1]

    thin, half = attn_ends[0].shape[2], mlp_ends[0].shape[2]
    second = sum(
        along(3 * thin + 2 * half * p, one_sums[p]) + along(3 * thin + 2 * half * p + half, mlp_ends[p][...])
        for p in range(2)
    )
    attn_sum.finish(attn_ends)
    ends.extend(moved(attn_ends[p], attn_outs[p], put.at[5 + p]) for p in range(3))
    first = sum(along(thin * p, attn_ends[p][...]) for p in range(2))
    lane = lax.broadcasted_iota(jnp.int32, gain_part.shape, 1)
    gain_part[...] = jnp.where(lane == 0, first, second)
    ends.append(sent(gain_part, gain_in, send.at[4], recv.at[4], partner()))
    ends.append(moved(gain_part, gains_out, put.at[8]))
    for copy in ends:
        copy.wait()


def backward(x, grad_hidden, branch, n1t, q, kv, probs, mixed, wq, wkv, wo, tables, data, kept, away, shard, one_sums):
    rows, width = branch.shape
    third, wide = wq.shape[2], data[0].shape[-1]
    heads = (2, rows, third)
    weights = (2, width, third)
    half = (2, STEP, width)
    return call(
        backward_kernel,
        (x, grad_hidden, branch, n1t, q, kv, probs, mixed, wq, wkv, wo, tables, *data, kept, away, shard, *one_sums),
        [ANY] * 20,
        [shaped((2, 24, wide), F32)] * 3
        + [shaped((2, 24, third), F32)] * 3
        + [shaped(half), shaped(half[1:], F32), shaped(half[1:])]
        + [shaped((24, 128), F32)] * 2,
        [ANY] * 11,
        [
            pltpu.VMEM(half, BF),
            pltpu.VMEM((SEQ, width), F32),
            pltpu.VMEM((rows, width), BF),
            pltpu.VMEM((width, rows), BF),
            pltpu.VMEM((width, rows), BF),
            pltpu.VMEM(heads, BF),
            pltpu.VMEM(heads, BF),
            pltpu.VMEM((4, 4, SEQ, SEQ), BF),
            pltpu.VMEM(heads, BF),
            pltpu.VMEM(weights, BF),
            pltpu.VMEM(weights, BF),
            pltpu.VMEM(weights, BF),
            pltpu.VMEM(heads, BF),
            pltpu.VMEM(heads, BF),
            pltpu.VMEM(heads, BF),
            pltpu.VMEM((SEQ, width), BF),
            pltpu.VMEM((SEQ, width), F32),
            pltpu.VMEM((SEQ, width), BF),
            pltpu.VMEM(half, F32),
            pltpu.VMEM(half[1:], BF),
            pltpu.VMEM(half, F32),
            pltpu.VMEM(half, BF),
            pltpu.VMEM(half, BF),
            *[pltpu.VMEM((4, 4, 4, 48, third), BF) for _ in range(3)],
            *Reduce.buffers((wide, wide, wide // 2, wide // 2), PLANE),
            *Reduce.buffers((third,) * 3, SPARE_Y),
            *Reduce.semaphores(PLANE),
            *Reduce.semaphores(SPARE_Y),
            *[pltpu.VMEM((2, 24, wide), F32) for _ in range(3)],
            *[pltpu.VMEM((2, 24, third), F32) for _ in range(3)],
            pltpu.VMEM(shard.shape, F32),
            pltpu.VMEM((2, 2, 24, wide), F32),
            pltpu.VMEM((24, 128), F32),
            pltpu.VMEM(tables.shape, F32),
            pltpu.SemaphoreType.DMA((16,)),
            pltpu.SemaphoreType.DMA((9,)),
            pltpu.SemaphoreType.DMA((5,)),
            pltpu.SemaphoreType.DMA((5,)),
        ],
        "attn_backward_reduce",
        3,
    )


def last_kernel(own, theirs, result_in, one, two, attn, gains_one, gains_two, gain_sums, more, outs):
    result, in_grad, dq, dk, dv, do, dg, du, dd, gain_one_grad, gain_two_grad = outs
    yl = lax.axis_index("yl")
    result[...] = result_in[...]
    in_grad[yl] = own[...]
    in_grad[1 - yl] = theirs[...].astype(F32)
    gain_one, gain_two = as_column(gains_one), as_column(gains_two)
    thin, half = attn[0].shape[2], two[0].shape[2]
    keys = [[], []]
    for c in range(2):
        dq[:, c * thin : (c + 1) * thin] = attn[0][c] * gain_one
        for k in range(2):
            keys[k].append(attn[1][c, :, k * (thin // 2) : (k + 1) * (thin // 2)] * gain_one)
        do[:, c * thin : (c + 1) * thin] = attn[2][c]
        for k, part in enumerate((one, two)):
            start = (2 * c + k) * half
            dg[:, start : start + half] = part[0][c] * gain_two
            du[:, start : start + half] = part[1][c] * gain_two
            dd[:, start : start + half] = part[2][c]
    dk[...] = jnp.concatenate(keys[0], -1)
    dv[...] = jnp.concatenate(keys[1], -1)
    lane = lax.broadcasted_iota(jnp.int32, gain_sums.shape, 1)
    grads = ((gain_sums[...] + more[...]) / jnp.where(lane == 0, gain_one, gain_two)).T
    gain_one_grad[...] = grads[0:1, :24]
    gain_two_grad[...] = grads[1:2, :24]


def placed_outputs(own, theirs, result, one, two, attn, gains, gain_sums, more_gain_sums):
    width, thin, half = own.shape[1], attn[0].shape[2], two[0].shape[2]

    def kernel(*refs):
        last_kernel(*refs[:3], refs[3:6], refs[6:9], refs[9:12], *refs[12:16], refs[16:])

    return pl.pallas_call(
        kernel,
        out_shape=[
            shaped((2, STEP, width)),
            shaped((2, STEP, width), F32),
            shaped((24, 2 * thin), F32),
            shaped((24, thin), F32),
            shaped((24, thin), F32),
            shaped((24, 2 * thin), F32),
            shaped((24, 4 * half), F32),
            shaped((24, 4 * half), F32),
            shaped((24, 4 * half), F32),
            shaped((1, 24), F32),
            shaped((1, 24), F32),
        ],
        in_specs=[VMEM] * 16,
        out_specs=[VMEM] * 11,
        compiler_params=pltpu.CompilerParams(vmem_limit_bytes=VMEM_LIMIT),
        name="place_outputs",
    )(own, theirs, result, *one, *two, *attn, *gains, gain_sums, more_gain_sums)


def tables_for(count, heads, plain):
    half = HEAD // 2
    inverse = np.float32(ROPE_BASE) ** (-(np.arange(half, dtype=np.float32) * np.float32(2.0)) / np.float32(HEAD))
    angle = np.arange(count, dtype=np.float32)[:, None] * inverse.astype(np.float32)[None, :]
    cosine, sine = np.cos(angle), np.sin(angle)
    cosine = np.tile(np.concatenate([cosine, cosine], -1), (1, heads))
    sine = np.tile(np.concatenate([-sine, sine], -1), (1, heads))
    cosine = np.concatenate([cosine, np.ones((count, plain), np.float32)], -1)
    sine = np.concatenate([sine, np.zeros((count, plain), np.float32)], -1)
    return np.stack([cosine, sine]).astype(np.float32)


def body(
    inputs,
    out_grad,
    lengths,
    query_weight,
    key_matrix,
    value_matrix,
    output_weight,
    gate_weight,
    up_weight,
    down_weight,
    attn_gain,
    mlp_gain,
):
    width = inputs.shape[2]
    own_weights = (
        query_weight,
        key_matrix,
        value_matrix,
        output_weight.T,
        gate_weight,
        up_weight,
        down_weight.T,
    )
    gains = (attn_gain.reshape(1, -1), mlp_gain.reshape(1, -1))
    third, wide = query_weight.shape[1] // 2, gate_weight.shape[1] // 2
    tables = jnp.asarray(np.concatenate([tables_for(SEQ, 4, 0), tables_for(SEQ, 2, 2 * HEAD)]))

    results = forward(
        own_weights, gains, lengths.reshape(1, -1), inputs, out_grad, tables, third, wide
    )
    two, one = results[:3], results[3:6]
    x, n1t, q, kv, probs, mixed, hidden, n2, n2t, cot, cott = results[6:17]
    (wq, wkv, wo), grads, acts, shard = results[17:20], results[20:23], results[23:26], results[26]

    def joined(w):
        return w.reshape(2, width, -1)

    def blocked(w):
        return w.reshape(2, 4, 4, 48, -1)

    *one_sums, dg, du, dd, kept, away, branch, grad_hidden = middle(
        n2, cot, hidden, n2t, cott, one, two, acts, [blocked(w) for w in grads]
    )
    *sums, result, in_grad, in_grad_theirs, gain_sums, more_gain_sums = backward(
        x,
        grad_hidden,
        branch,
        n1t,
        q,
        kv,
        probs,
        mixed,
        joined(wq),
        joined(wkv),
        joined(wo),
        tables,
        [blocked(w) for w in (dg, du, dd)],
        kept,
        away,
        shard,
        one_sums[:2],
    )
    result, in_grad, dq, dk, dv, do, dg, du, dd, gain_one_grad, gain_two_grad = placed_outputs(
        in_grad, in_grad_theirs, result, one_sums, sums[:3], sums[3:], gains, gain_sums, more_gain_sums
    )
    return result, in_grad, dq, dk, dv, do.T, dg, du, dd.T, gain_one_grad.reshape(24), gain_two_grad.reshape(24)


def solution(mesh):
    fine = Mesh(mesh.devices.reshape(2, 4, 4, 2, 2), AXES)
    rows = P(None, AXES, None)
    into, out = P(DP, "yl"), P("yl", DP)
    return jax.shard_map(
        body,
        mesh=fine,
        in_specs=(rows, rows, P(None, DP), into, into, into, out, into, into, out, P(DP), P(DP)),
        out_specs=(rows, rows, into, into, into, out, into, into, out, P(DP), P(DP)),
        check_vma=False,
    )
```

```python
import math

import jax
import jax.numpy as jnp
import numpy as np
from jax import lax
from jax.experimental import pallas as pl
from jax.experimental.pallas import tpu as pltpu
from jax.sharding import Mesh
from jax.sharding import PartitionSpec as P

HEAD = 96
EPS = 1e-05
ROPE_BASE = 100000.0
AXES = ("yh", "x", "z", "core", "yl")
DP = ("yh", "x", "z", "core")
MESH = pl.DeviceIdType.MESH
BF = jnp.bfloat16
F32 = jnp.float32
EVEN = (("x", "y", "z"), ("y", "z", "x"), ("z", "x", "y"))
SPARE_Y = (("x", "z", "y"), ("y", "x", "z"), ("y", "z", "x"))
PLANE_Z = (("w", "x", "z"), ("w", "z", "x"), ("w", "x", "z"))
PLANE_X = (("w", "z", "x"), ("w", "x", "z"), ("w", "z", "x"))
PLANE = (("w", "x", "z"), ("w", "z", "x"), ("w", "x", "z"), ("w", "z", "x"))
SEQ = 256
ROWS = 512
STEP = 128
CHUNK = 256
VMEM_LIMIT = 62 * 1024 * 1024


def coordinates():
    x, z, yh, yl = (lax.axis_index(a) for a in ("x", "z", "yh", "yl"))
    return {"x": x, "z": z, "y": yh * 2 + yl, "w": yh}


def extent(axis):
    return 2 if axis == "w" else 4


def around(at, axis, by):
    return lax.rem(at[axis] + (by + 4), extent(axis))


def others(axis):
    return (1,) if axis == "w" else (1, -1, 2)


def peer(at, axis, by):
    value = around(at, axis, by)
    if axis == "y":
        return {"yh": value // 2, "yl": lax.rem(value, 2)}
    return {"yh" if axis == "w" else axis: value}


def sibling():
    return {"core": 1 - lax.axis_index("core")}


def partner():
    return {"yl": 1 - lax.axis_index("yl")}


def slot(at, axis, by=0):
    value = around(at, axis, by)
    return lax.rem(value, 2) * 2 + value // 2 if axis == "y" else value


def dimensions(order):
    return ("w" if "w" in order else "y", "x", "z")


def place(at, order, count, half=None, shifted=None):
    out = []
    for axis in dimensions(order):
        if axis in order[:count]:
            size = extent(axis)
            if half is not None and half[0] == axis:
                out.append(pl.ds(size // 2 * half[1], size // 2))
            else:
                out.append(pl.ds(0, size))
        else:
            out.append(slot(at, axis, shifted[1] if shifted is not None and shifted[0] == axis else 0))
    return tuple(out)


def greet(at):
    barrier = pltpu.get_barrier_semaphore()
    for axis in ("x", "y", "z"):
        for by in (1, -1, 2):
            pl.semaphore_signal(barrier, inc=1, device_id=peer(at, axis, by), device_id_type=MESH)
    pl.semaphore_signal(barrier, inc=1, device_id=sibling(), device_id_type=MESH)
    pl.semaphore_wait(barrier, 10)


def sent(src, dst, send, recv, device):
    copy = pltpu.make_async_remote_copy(
        src_ref=src, dst_ref=dst, send_sem=send, recv_sem=recv, device_id=device, device_id_type=MESH
    )
    copy.start()
    return copy


def moved(src, dst, sem):
    copy = pltpu.make_async_copy(src, dst, sem)
    copy.start()
    return copy


class Gather:
    @staticmethod
    def semaphores(orders):
        count = len(orders)
        shapes = (count,), (count, 2, 3), (count, 2, 3), (count, 2, 2, 3), (count, 2, 2, 3)
        return [pltpu.SemaphoreType.DMA(shape) for shape in shapes]

    def __init__(self, at, srcs, outs, semaphores, orders):
        self.at, self.srcs, self.outs, self.orders = at, srcs, outs, orders
        self.local, self.send, self.recv, self.ring_send, self.ring_recv = semaphores
        self.own, self.direct, self.ring = [], {}, {}

    def arrive(self, p, stage):
        for copy in self.direct.get((p, stage), ()):
            copy.wait_recv()
        if (p, stage, 0, 0) in self.ring:
            for d in range(2):
                self.ring[p, stage, d, 1 - d].wait_recv()
                self.ring[p, stage, d, 2].wait_recv()

    def to_all(self, stage):
        at = self.at
        for p, order in enumerate(self.orders):
            if stage:
                self.own[p].wait()
                self.arrive(p, 0)
            else:
                self.own.append(moved(self.srcs[p], self.outs[p].at[place(at, order, 0)], self.local.at[p]))
            group = self.outs[p].at[place(at, order, stage)]
            self.direct[p, stage] = [
                sent(
                    group if stage else self.srcs[p],
                    group,
                    self.send.at[p, stage, d],
                    self.recv.at[p, stage, d],
                    peer(at, order[stage], by),
                )
                for d, by in enumerate(others(order[stage]))
            ]

    def pass_on(self, p, stage, d, k, block):
        self.ring[p, stage, d, k] = sent(
            block,
            block,
            self.ring_send.at[p, stage - 1, d, k],
            self.ring_recv.at[p, stage - 1, d, k],
            peer(self.at, self.orders[p][stage], 1 - 2 * d),
        )

    def spread(self, stage, *pieces):
        for p in pieces or range(len(self.orders)):
            order = self.orders[p]
            if stage == 1:
                self.own[p].wait()
            self.arrive(p, stage - 1)
            for t in range(2):
                for d in range(2):
                    h = t if d == 0 else 1 - t
                    self.pass_on(p, stage, d, h, self.outs[p].at[place(self.at, order, stage, (order[0], h))])

    def forward(self, stage):
        for p, order in enumerate(self.orders):
            for d, by in enumerate((1, -1)):
                self.ring[p, stage, d, d].wait_recv()
                where = place(self.at, order, stage, (order[0], d), (order[stage], -by))
                self.pass_on(p, stage, d, 2, self.outs[p].at[where])

    def finish(self):
        for copies in self.direct.values():
            for copy in copies:
                copy.wait_send()
        for copy in self.ring.values():
            copy.wait_send()


class Reduce:
    @staticmethod
    def semaphores(orders):
        count = len(orders)
        shapes = (count, 3), *[(count, 2, 3)] * 4, (count, 2), (count, 2)
        return [pltpu.SemaphoreType.DMA(shape) for shape in shapes]

    @staticmethod
    def buffers(columns, orders):
        def per_piece(*shape):
            return [pltpu.VMEM(shape + (48, width), BF) for width in columns]

        size = extent(dimensions(orders[0])[0])
        return [
            *per_piece(2, size // 2, 4),
            *per_piece(size, 4),
            *per_piece(2, size // 2, 4),
            *per_piece(2, size, 4),
            *per_piece(3, size),
            *per_piece(3),
            *[pltpu.VMEM((48, width), F32) for width in columns],
        ]

    def __init__(self, at, data, buffers, semaphores, orders):
        self.at, self.data, self.orders = at, data, orders
        self.side, self.kept, self.far, self.near, self.second, self.third, self.sums = (
            buffers[len(orders) * k : len(orders) * (k + 1)] for k in range(7)
        )
        self.load, self.first_send, self.first_recv, self.send, self.recv, self.end_send, self.end_recv = semaphores
        self.loads, self.copies = {}, {}

    def left(self, p):
        order = self.orders[p]
        return [axis for axis in dimensions(order) if axis != order[2]]

    def inside(self, p, first, second=None):
        whole = slice(None) if second is None else second
        return (first, whole) if self.left(p)[0] == self.orders[p][1] else (whole, first)

    def start(self, *pieces):
        at, s, r = self.at, self.first_send, self.first_recv
        for p in pieces or range(len(self.orders)):
            order = self.orders[p]
            axis, cut = order[2], self.left(p)[0]
            size = extent(cut) // 2
            for d, by in enumerate((1, -1)):
                block = self.data[p].at[place(at, order, 2, (cut, d), (axis, 2))]
                self.copies[p, d, 0] = sent(block, self.far[p].at[d], s.at[p, d, 0], r.at[p, d, 0], peer(at, axis, by))
            for d, by in enumerate((1, -1)):
                h = 1 - d
                block = self.data[p].at[place(at, order, 2, (cut, h), (axis, by))]
                self.copies[p, d, 1] = sent(
                    block, self.near[p].at[d, pl.ds(size * h, size)], s.at[p, d, 1], r.at[p, d, 1], peer(at, axis, by)
                )
                block = self.data[p].at[place(at, order, 2, (cut, d), (axis, by))]
                self.loads[p, d] = moved(block, self.side[p].at[d], self.load.at[p, d])
            self.loads[p, 2] = moved(self.data[p].at[place(at, order, 2)], self.kept[p], self.load.at[p, 2])

    def relay(self):
        for p, order in enumerate(self.orders):
            size = extent(self.left(p)[0]) // 2
            for d, by in enumerate((1, -1)):
                self.loads[p, d].wait()
                self.copies[p, d, 0].wait_recv()
                side, far = self.side[p], self.far[p]

                @pl.loop(0, 4 * size)
                def _(i, d=d, side=side, far=far):
                    a, b = i // 4, lax.rem(i, 4)
                    side[d, a, b] = side[d, a, b] + far[d, a, b]

                self.copies[p, d, 2] = sent(
                    side.at[d],
                    self.near[p].at[d, pl.ds(size * d, size)],
                    self.first_send.at[p, d, 2],
                    self.first_recv.at[p, d, 2],
                    peer(self.at, order[2], by),
                )

    def spread(self):
        at = self.at
        for p, order in enumerate(self.orders):
            self.loads[p, 2].wait()
            for d in range(2):
                self.copies[p, d, 1].wait_recv()
                self.copies[p, d, 2].wait_recv()
            kept, near = self.kept[p], self.near[p]
            for d, by in enumerate((*others(order[1]), 0)):
                group = slot(at, order[1], by)

                @pl.loop(0, extent(order[0]))
                def _(i, p=p, kept=kept, near=near, group=group):
                    where = self.inside(p, group, i)
                    total = kept[where].astype(F32) + near[(0, *where)].astype(F32) + near[(1, *where)].astype(F32)
                    kept[where] = total.astype(BF)

                if by:
                    self.copies[p, "b", d] = sent(
                        kept.at[self.inside(p, group)],
                        self.second[p].at[d],
                        self.send.at[p, 0, d],
                        self.recv.at[p, 0, d],
                        peer(at, order[1], by),
                    )

    def narrow(self):
        at = self.at
        for p, order in enumerate(self.orders):
            for d in range(len(others(order[1]))):
                self.copies[p, "b", d].wait_recv()
            kept, second, mine = self.kept[p], self.second[p], slot(at, order[1])
            for d, by in enumerate((*others(order[0]), 0)):
                index = slot(at, order[0], by)
                where = self.inside(p, mine, index)
                total = kept[where].astype(F32)
                for k in range(3):
                    total = total + second[k, index].astype(F32)
                kept[where] = total.astype(BF)
                if by:
                    self.copies[p, "c", d] = sent(
                        kept.at[where],
                        self.third[p].at[d],
                        self.send.at[p, 1, d],
                        self.recv.at[p, 1, d],
                        peer(at, order[0], by),
                    )

    def finish(self, outs):
        at, core, ends = self.at, lax.axis_index("core"), []
        for p, order in enumerate(self.orders):
            total = self.kept[p][self.inside(p, slot(at, order[1]), slot(at, order[0]))].astype(F32)
            for d in range(len(others(order[0]))):
                self.copies[p, "c", d].wait_recv()
                total = total + self.third[p][d].astype(F32)
            self.sums[p][...] = total
            theirs = self.sums[p].at[pl.ds(pl.multiple_of(24 * (1 - core), 8), 24)]
            mine = self.sums[p].at[pl.ds(pl.multiple_of(24 * core, 8), 24)]
            ends.append(sent(theirs, outs[p].at[core], self.end_send.at[p, 0], self.end_recv.at[p, 0], sibling()))
            ends.append(moved(mine, outs[p].at[core], self.end_send.at[p, 1]))
        for copy in self.copies.values():
            copy.wait_send()
        for copy in ends:
            copy.wait()


def in_four(refs):
    half = refs[2].shape[-1] // 2
    lead = (slice(None),) * (len(refs[2].shape) - 1)
    return [refs[0], refs[1], *(refs[2].at[(*lead, pl.ds(k * half, half))] for k in range(2))]


def nn(left, right):
    return lax.dot_general(left, right, (((1,), (0,)), ((), ())), preferred_element_type=F32)


def nt(left, right):
    return lax.dot_general(left, right, (((1,), (1,)), ((), ())), preferred_element_type=F32)


def tn(left, right):
    return lax.dot_general(left, right, (((0,), (0,)), ((), ())), preferred_element_type=F32)


def inverse_rms(values):
    return lax.rsqrt(jnp.mean(values * values, -1, keepdims=True) + EPS)


def swap(values, first):
    width = values.shape[-1]
    return jnp.where(first, pltpu.roll(values, width - HEAD // 2, 1), pltpu.roll(values, HEAD // 2, 1))


def first_half(shape):
    return lax.rem(lax.broadcasted_iota(jnp.int32, shape, 1), HEAD) < HEAD // 2


def as_column(row):
    size = row.shape[1]
    square = jnp.broadcast_to(row[...].astype(F32), (size, size))
    diagonal = lax.broadcasted_iota(jnp.int32, (size, size), 0) == lax.broadcasted_iota(jnp.int32, (size, size), 1)
    return jnp.sum(jnp.where(diagonal, square, 0.0), -1, keepdims=True)


def rows_at(start, size):
    return pl.ds(pl.multiple_of(start, size), size)


ANY = pl.BlockSpec(memory_space=pl.ANY)
VMEM = pl.BlockSpec(memory_space=pltpu.VMEM)


def shaped(shape, kind=BF):
    return jax.ShapeDtypeStruct(shape, kind)


def call(kernel, operands, in_specs, results, out_specs, scratch, name, collective_id, **more):
    return pl.pallas_call(
        kernel,
        out_shape=results,
        in_specs=in_specs,
        out_specs=out_specs,
        scratch_shapes=scratch,
        compiler_params=pltpu.CompilerParams(
            collective_id=collective_id, has_side_effects=True, vmem_limit_bytes=VMEM_LIMIT
        ),
        name=name,
        **more,
    )(*operands)


def hidden_units(m, c, count, sub, n2, cot, weights, acts):
    rows = pl.ds(pl.multiple_of(m * ROWS + c * SEQ, SEQ), count * SEQ)
    columns = pl.ds(sub * CHUNK, CHUNK)
    gate_w, up_w, down_w = (w[..., columns].reshape(-1, CHUNK) for w in weights)
    gate = nn(n2[rows], gate_w)
    up = nn(n2[rows], up_w)
    sigma = jax.nn.sigmoid(gate)
    silu = gate * sigma
    grad_active = nn(cot[m, pl.ds(c, count)].reshape(count * SEQ, -1), down_w)
    acts[0][rows, columns] = (silu * up).astype(BF)
    acts[1][rows, columns] = (grad_active * up * (sigma + silu * (1.0 - sigma))).astype(BF)
    acts[2][rows, columns] = (grad_active * silu).astype(BF)


def unit_gradients(n2t, cott, acts, staging, outs, sems, rows=None, added=False, written=True):
    whole, copies = slice(None) if rows is None else rows, []
    for k, (left, right, target) in enumerate(((n2t, acts[1], 0), (n2t, acts[2], 1), (cott, acts[0], 2))):
        for sub in range(2):
            columns = pl.ds(sub * CHUNK, CHUNK)
            value = nn(left[:, whole], right[whole, columns])
            if added:
                value = value + staging[2 * k + sub].astype(F32)
            staging[2 * k + sub] = value.astype(BF)
            if written:
                copies.append(moved(staging.at[2 * k + sub], outs[target].at[:, columns], sems.at[2 * k + sub]))
    return copies


def forward_kernel(third, wide, *refs):
    own_weights, gains_one, gains_two, lengths, xin, gin, tables_in = refs[:7], *refs[7:13]
    refs = refs[1:]
    full_two, full_one = refs[12:15], refs[15:18]
    (
        x_out, n1t_out, q_out, kv_out, probs_out, mixed_out, hidden_out, n2_out, n2t_out, cot_out, cott_out,
    ) = refs[18:29]
    attn_out, grads_out, acts_out, shard_out = refs[29:32], refs[32:35], refs[35:38], refs[38]
    refs = refs[1:]
    (
        shard, got_shard, packed, xs, gs, normed, q, kv, probs, mixed, hidden, n2, n2t, cott, part, arrived, n1t,
        valid, staging,
    ) = refs[38:57]
    full_attn, weights, acts = refs[57:60], refs[60:63], refs[63:66]
    attn_sems, one_sems, two_sems = refs[66:71], refs[71:76], refs[76:81]
    tables, pair_send, pair_recv, row_send, row_recv, far_send, far_recv, own_sem, out_sem, put_sem = refs[81:]
    at = coordinates()
    core, yl = lax.axis_index("core"), lax.axis_index("yl")
    own_x = moved(xin.at[yl], xs.at[core, yl], own_sem.at[0])
    own_g = moved(gin, gs.at[:, core, yl], own_sem.at[1])
    table_copy = moved(tables_in, tables, own_sem.at[2])

    query, key, value, output, *mlp_weights = (ref[...].astype(F32) for ref in own_weights)
    gain_one, gain_two = as_column(gains_one), as_column(gains_two)
    small = key.shape[1] // 2
    for c in range(2):
        thin = slice(c * small, (c + 1) * small)
        parts = [
            query[:, c * third : (c + 1) * third] * gain_one,
            jnp.concatenate([key[:, thin] * gain_one, value[:, thin] * gain_one], -1),
            output[:, c * third : (c + 1) * third],
            *(
                w[:, c * wide : (c + 1) * wide] * g
                for w, g in zip(mlp_weights, (gain_two, gain_two, jnp.ones_like(gain_two)))
            ),
        ]
        column = 0
        for part_value in parts:
            shard[c, :24, column : column + part_value.shape[1]] = part_value
            column += part_value.shape[1]
        lane = lax.broadcasted_iota(jnp.int32, (8, 2 * SEQ), 1)
        ends = jnp.where(lane < SEQ, lengths[:, 0:1], lengths[:, 1:2] + SEQ)
        shard[c, 24:, : 2 * SEQ] = jnp.where(lane < ends, 1.0, 0.0)
    greet(at)
    swap_shard = sent(shard.at[1 - core], got_shard, pair_send.at[0], pair_recv.at[0], sibling())

    rows = {}

    def exchange(k):
        ours, theirs, dst = (
            (xin.at[yl], xin.at[1 - yl], xs.at[core, yl]),
            (gin, gin, gs.at[:, core, yl]),
        )[k]
        rows[k, 0] = sent(theirs, dst, row_send.at[k, 0], row_recv.at[k, 0], partner())
        rows[k, 1] = sent(ours, dst, row_send.at[k, 1], row_recv.at[k, 1], sibling())

    def share(k):
        block = (xs.at[core, 1 - yl], gs.at[:, core, 1 - yl])[k]
        rows[k, 0].wait_recv()
        rows[k, 2] = sent(block, block, row_send.at[k, 2], row_recv.at[k, 2], sibling())

    def settle(k):
        (own_x, own_g)[k].wait()
        rows[k, 0].wait_send()
        rows[k, 1].wait()
        rows[k, 2].wait()

    swap_shard.wait()
    low, high = shard[core], got_shard[...]
    first, last = jnp.where(core == 0, low, high), jnp.where(core == 0, high, low)
    packed[...] = jnp.concatenate([first[:24], last[:24]], 0).astype(BF)
    for c, rows_of in enumerate((first, last)):
        for m in range(2):
            valid[m, c] = rows_of[24:32, m * SEQ : (m + 1) * SEQ]

    def pieces(start, size, step):
        return [packed.at[:, pl.ds(start + k * step, size)] for k in range(3)]

    half = wide // 2
    attn = Gather(at, pieces(0, third, third), full_attn, attn_sems, EVEN)
    one = Gather(at, pieces(3 * third, half, wide), weights, one_sems, PLANE_Z)
    two = Gather(at, pieces(3 * third + half, half, wide), full_two, two_sems, PLANE_X)
    attn.to_all(0)
    one.to_all(0)
    attn.to_all(1)
    one.spread(1)
    attn.spread(2, 0, 1)
    exchange(0)
    attn.spread(2, 2)
    two.to_all(0)
    one.forward(1)
    attn.forward(2)
    one.spread(2)
    share(0)
    settle(0)
    exchange(1)
    outs = [moved(xs, x_out, out_sem.at[0]), moved(shard, shard_out, out_sem.at[24])]

    @pl.loop(0, ROWS // STEP)
    def _(i):
        block = rows_at(i * STEP, STEP)
        values = xs[i // 2, lax.rem(i, 2)].astype(F32)
        normed[block] = (values * inverse_rms(values)).astype(BF)

    for p in range(2):
        attn.arrive(p, 2)
    two.spread(1)
    wq, wkv, wo = full_attn
    table_copy.wait()

    def weight(ref, y):
        return ref[pl.ds(2 * y, 2)].reshape(-1, third)

    @pl.loop(0, 2)
    def _(y):
        @pl.loop(0, ROWS // SEQ)
        def _(n):
            block = rows_at(n * SEQ, SEQ)
            left = normed[block]
            is_first = first_half((SEQ, third))
            for k, (w, result) in enumerate(((wq, q), (wkv, kv))):
                lin = nn(left, weight(w, y))
                result[y, block] = (lin * tables[2 * k] + swap(lin, is_first) * tables[2 * k + 1]).astype(BF)

    outs.append(moved(q, q_out, out_sem.at[5]))
    outs.append(moved(kv, kv_out, out_sem.at[6]))
    two.forward(1)
    one.forward(2)
    scale = 1.0 / math.sqrt(HEAD)

    @pl.loop(0, 4)
    def _(i):
        y, n = i // 2, lax.rem(i, 2)
        block = rows_at(n * SEQ, SEQ)
        t = lax.broadcasted_iota(jnp.int32, (SEQ, SEQ), 0)
        s = lax.broadcasted_iota(jnp.int32, (SEQ, SEQ), 1)
        keep = (s <= t) & (valid[yl, n, 0:1, :] > 0.5)
        queries, keys = q[y, block], kv[y, block]
        results = []
        for h in range(4):
            g = h // 2
            scores = nt(queries[:, h * HEAD : (h + 1) * HEAD], keys[:, g * HEAD : (g + 1) * HEAD]) * scale
            scores = jnp.where(keep, scores, -1e30)
            terms = jnp.exp(scores - jnp.max(scores, -1, keepdims=True))
            low_probs = (terms * (1.0 / jnp.sum(terms, -1, keepdims=True))).astype(BF)
            probs[i, h] = low_probs
            results.append(nn(low_probs, keys[:, (2 + g) * HEAD : (3 + g) * HEAD]))
        mixed[y, block] = jnp.concatenate(results, -1).astype(BF)

    outs.append(moved(probs, probs_out, out_sem.at[7]))
    outs.append(moved(mixed, mixed_out, out_sem.at[8]))
    two.spread(2)

    attn.arrive(2, 2)
    copies = []
    for i in range(ROWS // STEP):
        block = rows_at(lax.rem(2 * (1 - core) + i, 4) * STEP, STEP)
        part[block] = (nt(mixed[0, block], weight(wo, 0)) + nt(mixed[1, block], weight(wo, 1))).astype(BF)
        copies.append(sent(part.at[block], arrived.at[block], pair_send.at[1 + i], pair_recv.at[1 + i], sibling()))
    second_rows = {}
    mine, theirs = yl * ROWS, (1 - yl) * ROWS
    for i in range(ROWS // STEP):
        copies[(i + 2) % 4 if i < 2 else i - 2].wait_send()
        copies[i].wait_recv()
        number = lax.rem(2 * core + i, 4)
        block = rows_at(number * STEP, STEP)
        values = xs[number // 2, lax.rem(number, 2)].astype(F32) + (
            part[block].astype(F32) + arrived[block].astype(F32)
        )
        hidden[block] = values
        target = rows_at(mine + number * STEP, STEP)
        n2[target] = (values * inverse_rms(values)).astype(BF)
        if i < 2:
            second_rows[0, i] = sent(n2.at[target], n2.at[target], far_send.at[0, i], far_recv.at[0, i], partner())
    outs.append(moved(hidden.at[rows_at(core * SEQ, SEQ)], hidden_out, out_sem.at[9]))
    attn.finish()
    outs.extend(moved(full_attn[p], attn_out[p], out_sem.at[2 + p]) for p in range(3))
    share(1)
    settle(1)

    for m in range(2):
        for c in range(2):
            for h in range(2):
                mask = valid[m, c][:, h * STEP : (h + 1) * STEP].T[:, 0:1]
                gs[m, c, h] = (gs[m, c, h].astype(F32) * mask).astype(BF)
    outs.append(moved(gs, cot_out, out_sem.at[10]))

    for p in range(3):
        one.arrive(p, 2)
    one.finish()
    outs.extend(moved(weights[p], full_one[p], out_sem.at[11 + p]) for p in range(3))
    mine_rows, their_rows = rows_at(mine, ROWS), rows_at(theirs, ROWS)
    for sub in range(2):
        hidden_units(yl, 0, 2, sub, n2, gs, weights, acts)
    two.forward(2)
    outs.extend(moved(acts[p].at[mine_rows], acts_out[p].at[mine_rows], out_sem.at[15 + p]) for p in range(3))
    outs.append(moved(n2.at[mine_rows], n2_out.at[mine_rows], out_sem.at[18]))
    for m in range(2):
        for c in range(2):
            for h in range(2):
                cott[:, pl.ds(m * ROWS + (2 * c + h) * STEP, STEP)] = gs[m, c, h].T
    outs.append(moved(cott, cott_out, out_sem.at[14]))
    for i in range(ROWS // STEP):
        block = rows_at(mine + i * STEP, STEP)
        n2t[:, block] = n2[block].T
    unit_gradients(n2t, cott, acts, staging, grads_out, put_sem, mine_rows, written=False)
    n1t[...] = normed[...].T
    outs.append(moved(n1t, n1t_out, out_sem.at[1]))

    for i in range(2):
        second_rows[0, i].wait_recv()
        block = rows_at(theirs + (2 * core + i) * STEP, STEP)
        second_rows[1, i] = sent(n2.at[block], n2.at[block], far_send.at[1, i], far_recv.at[1, i], sibling())
    for sub in range(2):
        hidden_units(1 - yl, core, 1, sub, n2, gs, weights, acts)
    for i in range(2):
        block = rows_at(theirs + (2 * core + i) * STEP, STEP)
        n2t[:, block] = n2[block].T
    for i in range(2):
        second_rows[0, i].wait_send()
        second_rows[1, i].wait()
    for sub in range(2):
        hidden_units(1 - yl, 1 - core, 1, sub, n2, gs, weights, acts)
    outs.extend(moved(acts[p].at[their_rows], acts_out[p].at[their_rows], out_sem.at[20 + p]) for p in range(3))
    outs.append(moved(n2.at[their_rows], n2_out.at[their_rows], out_sem.at[23]))
    for i in range(2):
        block = rows_at(theirs + (2 * (1 - core) + i) * STEP, STEP)
        n2t[:, block] = n2[block].T
    outs.append(moved(n2t, n2t_out, out_sem.at[19]))
    outs.extend(unit_gradients(n2t, cott, acts, staging, grads_out, put_sem, their_rows, added=True))
    for p in range(3):
        two.arrive(p, 2)
    two.finish()
    for copy in outs:
        copy.wait()


def forward(own_weights, gains, lengths, xin, gin, tables, third, wide):
    width = xin.shape[2]
    rows = (ROWS, width)
    both = (2 * ROWS, width)
    heads = (2, ROWS, third)
    square = (4, 4, SEQ, SEQ)
    half = wide // 2
    piece = (2, 4, 4, 48, half)
    return call(
        lambda *refs: forward_kernel(third, wide, *refs),
        (*own_weights, *gains, lengths, xin, gin, tables),
        [VMEM] * 10 + [ANY, ANY, ANY],
        [shaped(piece)] * 6
        + [
            shaped((2, 2, 128, width)),
            shaped(rows[::-1]),
            shaped(heads),
            shaped(heads),
            shaped(square),
            shaped(heads),
            shaped((SEQ, width), F32),
            shaped(both),
            shaped(both[::-1]),
            shaped((2, 2, 2, 128, width)),
            shaped(both[::-1]),
        ]
        + [shaped((4, 4, 4, 48, third))] * 3
        + [shaped((width, half))] * 3
        + [shaped((2 * ROWS, half))] * 3
        + [shaped((2, 32, 3 * third + 3 * wide), F32)],
        [ANY] * 27,
        [
            pltpu.VMEM((2, 32, 3 * third + 3 * wide), F32),
            pltpu.VMEM((32, 3 * third + 3 * wide), F32),
            pltpu.VMEM((48, 3 * third + 3 * wide), BF),
            pltpu.VMEM((2, 2, 128, width), BF),
            pltpu.VMEM((2, 2, 2, 128, width), BF),
            pltpu.VMEM(rows, BF),
            pltpu.VMEM(heads, BF),
            pltpu.VMEM(heads, BF),
            pltpu.VMEM(square, BF),
            pltpu.VMEM(heads, BF),
            pltpu.VMEM(rows, F32),
            pltpu.VMEM(both, BF),
            pltpu.VMEM(both[::-1], BF),
            pltpu.VMEM(both[::-1], BF),
            pltpu.VMEM(rows, BF),
            pltpu.VMEM(rows, BF),
            pltpu.VMEM(rows[::-1], BF),
            pltpu.VMEM((2, 2, 8, SEQ), F32),
            pltpu.VMEM((6, width, CHUNK), BF),
            *[pltpu.VMEM((4, 4, 4, 48, third), BF) for _ in range(3)],
            *[pltpu.VMEM(piece, BF) for _ in range(3)],
            *[pltpu.VMEM((2 * ROWS, half), BF) for _ in range(3)],
            *Gather.semaphores(EVEN),
            *Gather.semaphores(PLANE_Z),
            *Gather.semaphores(PLANE_X),
            pltpu.VMEM(tables.shape, F32),
            pltpu.SemaphoreType.DMA((5,)),
            pltpu.SemaphoreType.DMA((5,)),
            pltpu.SemaphoreType.DMA((2, 3)),
            pltpu.SemaphoreType.DMA((2, 3)),
            pltpu.SemaphoreType.DMA((2, 2)),
            pltpu.SemaphoreType.DMA((2, 2)),
            pltpu.SemaphoreType.DMA((3,)),
            pltpu.SemaphoreType.DMA((25,)),
            pltpu.SemaphoreType.DMA((6,)),
        ],
        "gather_attn_forward_mlp",
        1,
    )


def middle_kernel(*refs):
    n2_in, cot_in, hidden_in, n2t_in, cott_in = refs[:5]
    one_in, two_in, acts_in, data = refs[5:8], refs[8:11], refs[11:14], refs[14:17]
    sums_out, grads_out = refs[17:20], refs[20:23]
    kept_out, away_out, branch_out, grad_hidden_out = refs[23:27]
    (
        n2, cot, hidden, n2t, cott, staging, to_pair, from_pair, whole, from_far, keep, halves, to_far, branch, gh,
    ) = refs[27:42]
    one, two, acts_one, acts_two = refs[42:45], refs[45:48], refs[48:51], refs[51:54]
    buffers, reduce_sems = refs[54:82], refs[82:89]
    load, put, put_sem, pair_send, pair_recv, part_send, part_recv, far_send, far_recv = refs[89:]
    core, yl = lax.axis_index("core"), lax.axis_index("yl")
    at = coordinates()
    order = (
        (n2_in, n2),
        (two_in[0], two[0]),
        (two_in[1], two[1]),
        (cot_in, cot),
        (two_in[2], two[2]),
        *zip(acts_in[1:], acts_one[1:]),
        *zip(one_in[:2], one[:2]),
        (acts_in[0], acts_one[0]),
        (one_in[2], one[2]),
        (n2t_in, n2t),
        (cott_in, cott),
        (hidden_in, hidden),
    )
    loads = [moved(src, dst, load.at[k]) for k, (src, dst) in enumerate(order)]
    greet(at)
    total = Reduce(at, in_four(data), buffers, reduce_sems, PLANE)
    total.start()
    for k in range(5):
        loads[k].wait()
    for sub in range(2):
        hidden_units(1 - yl, 0, 2, sub, n2, cot, two, acts_two)
    for k in range(5, 11):
        loads[k].wait()

    def weight(ref):
        return ref[...].reshape(n2.shape[1], -1)

    def grad_rows(m, c):
        rows = rows_at(m * ROWS + c * SEQ, SEQ)
        return (nt(acts_one[1][rows], weight(one[0])) + nt(acts_one[2][rows], weight(one[1]))) + (
            nt(acts_two[1][rows], weight(two[0])) + nt(acts_two[2][rows], weight(two[1]))
        )

    def out_rows(m, c):
        rows = rows_at(m * ROWS + c * SEQ, SEQ)
        return nt(acts_one[0][rows], weight(one[2])) + nt(acts_two[0][rows], weight(two[2]))

    pair, far, shared = {}, {}, []

    def to_sibling(k, value):
        to_pair[k] = value.astype(BF)
        pair[k] = sent(to_pair.at[k], from_pair.at[k], pair_send.at[k], pair_recv.at[k], sibling())

    blocks = [pl.ds(i * STEP, STEP) for i in range(2)]
    to_pair[0] = grad_rows(1 - yl, 1 - core).astype(BF)
    for i, rows in enumerate(blocks):
        pair["far", i] = sent(
            to_pair.at[0, rows], from_pair.at[0, rows], part_send.at[0, i], part_recv.at[0, i], sibling()
        )
    keep[...] = grad_rows(1 - yl, core)
    for i, rows in enumerate(blocks):
        pair["far", i].wait_recv()
        whole[rows] = (keep[rows] + from_pair[0, rows].astype(F32)).astype(BF)
        far[i] = sent(whole.at[rows], from_far.at[rows], far_send.at[i], far_recv.at[i], partner())
    total.relay()
    for sub in range(2):
        hidden_units(yl, 0, 2, sub, n2, cot, two, acts_two)
    to_sibling(1, grad_rows(yl, 1 - core))
    keep[...] = grad_rows(yl, core)
    to_sibling(2, out_rows(1 - yl, 1 - core))
    to_sibling(3, out_rows(yl, 1 - core))
    for k in range(11, 14):
        loads[k].wait()
    total.spread()
    outs = unit_gradients(n2t, cott, acts_two, staging, grads_out, put_sem)
    total.narrow()

    for k, m in ((2, 1 - yl), (3, yl)):
        pair[k].wait_recv()
        value = out_rows(m, core) + from_pair[k].astype(F32)
        if k == 3:
            value = value + hidden[...]
        halves[k - 2] = value.reshape(2, STEP, -1)
        to_far[k - 2] = halves[k - 2, 1 - yl].astype(BF)
        outs.append(moved(halves.at[k - 2, yl], kept_out.at[k - 2], put.at[k]))
        outs.append(moved(to_far.at[k - 2], away_out.at[k - 2], put.at[k + 2]))
    pair[1].wait_recv()

    for i, rows in enumerate(blocks):
        far[i].wait_recv()
        grad = keep[rows] + (from_pair[1, rows].astype(F32) + from_far[rows].astype(F32))
        values = hidden[rows]
        inverse = inverse_rms(values)
        unit = values * inverse
        back = inverse * (grad - unit * jnp.mean(grad * unit, -1, keepdims=True))
        gh[rows] = cot[yl, core, i].astype(F32) + back
        branch[rows] = gh[rows].astype(BF)
        target = rows_at(core * SEQ + i * STEP, STEP)
        shared.append(
            sent(branch.at[rows], branch_out.at[target], part_send.at[1, i], part_recv.at[1, i], sibling())
        )
        outs.append(moved(branch.at[rows], branch_out.at[target], put.at[6 + i]))
    outs.append(moved(gh, grad_hidden_out, put.at[0]))
    total.finish(in_four(sums_out))
    for copy in shared:
        copy.wait()
    for copy in (*pair.values(), *far.values()):
        copy.wait_send()
    for copy in outs:
        copy.wait()


def middle(n2, cot, hidden, n2t, cott, one, two, acts, data):
    rows, width = n2.shape
    half = one[0].shape[-1]
    block = (SEQ, width)
    return call(
        middle_kernel,
        (n2, cot, hidden, n2t, cott, *one, *two, *acts, *data),
        [ANY] * 17,
        [shaped((2, 24, half), F32)] * 3
        + [shaped((width, half))] * 3
        + [
            shaped((2, STEP, width), F32),
            shaped((2, STEP, width)),
            shaped((ROWS, width)),
            shaped(block, F32),
        ],
        [ANY] * 10,
        [
            pltpu.VMEM((rows, width), BF),
            pltpu.VMEM(cot.shape, BF),
            pltpu.VMEM(block, F32),
            pltpu.VMEM((width, rows), BF),
            pltpu.VMEM((width, rows), BF),
            pltpu.VMEM((6, width, CHUNK), BF),
            pltpu.VMEM((4,) + block, BF),
            pltpu.VMEM((4,) + block, BF),
            pltpu.VMEM(block, BF),
            pltpu.VMEM(block, BF),
            pltpu.VMEM(block, F32),
            pltpu.VMEM((2, 2, STEP, width), F32),
            pltpu.VMEM((2, STEP, width), BF),
            pltpu.VMEM(block, BF),
            pltpu.VMEM(block, F32),
            *[pltpu.VMEM(one[0].shape, BF) for _ in range(6)],
            *[pltpu.VMEM((rows, half), BF) for _ in range(6)],
            *Reduce.buffers((half, half, half // 2, half // 2), PLANE),
            *Reduce.semaphores(PLANE),
            pltpu.SemaphoreType.DMA((14,)),
            pltpu.SemaphoreType.DMA((8,)),
            pltpu.SemaphoreType.DMA((6,)),
            pltpu.SemaphoreType.DMA((4,)),
            pltpu.SemaphoreType.DMA((4,)),
            pltpu.SemaphoreType.DMA((2, 2)),
            pltpu.SemaphoreType.DMA((2, 2)),
            pltpu.SemaphoreType.DMA((2,)),
            pltpu.SemaphoreType.DMA((2,)),
        ],
        "mlp_reduce",
        2,
    )


def backward_kernel(*refs):
    xall, grad_hidden_in, branch_in, n1t_in, q_in, kv_in, probs_in, mixed_in, wq_in, wkv_in, wo_in, tables_in = refs[:12]
    data, kept_in, away, shard_in, one_in = refs[12:15], *refs[15:18], refs[18:20]
    refs = refs[3:]
    mlp_outs, attn_outs, result_out, in_grad_out, from_partner = refs[17:20], refs[20:23], *refs[23:26]
    gains_out, gain_in = refs[26:28]
    refs = refs[2:]
    (
        xs, gh, branch, branch_t, normed_t, q, kv, probs, mixed, wq, wkv, wo,
        grad_mixed, dq, dkv, part, keep_part, arrived, in_grad, for_partner, kept, others_half, result,
    ) = refs[26:49]
    attn_grads = refs[49:52]
    mlp_buffers, attn_buffers = refs[52:80], refs[80:101]
    mlp_sems, attn_sems = refs[101:108], refs[108:115]
    mlp_ends, attn_ends, shard, one_sums, gain_part, tables = refs[115:118], refs[118:121], *refs[121:125]
    load, put, send, recv = refs[125:]
    at = coordinates()
    core, yl = lax.axis_index("core"), lax.axis_index("yl")
    loads = [
        moved(src, dst, load.at[k])
        for k, (src, dst) in enumerate(
            (
                (branch_in, branch),
                (wo_in, wo),
                (mixed_in, mixed),
                (q_in, q),
                (kv_in, kv),
                (probs_in, probs),
                (n1t_in, normed_t),
                (wq_in, wq),
                (wkv_in, wkv),
                (grad_hidden_in, gh),
                (xall.at[core], xs),
                (kept_in, kept),
                (shard_in, shard),
                (one_in[0], one_sums.at[0]),
                (one_in[1], one_sums.at[1]),
                (tables_in, tables),
            )
        )
    ]
    greet(at)
    mlp_sum = Reduce(at, in_four(data), mlp_buffers, mlp_sems, PLANE)
    attn_sum = Reduce(at, attn_grads, attn_buffers, attn_sems, SPARE_Y)
    mlp_sum.start()
    finals = [sent(away.at[k], others_half.at[k], send.at[2 + k], recv.at[2 + k], partner()) for k in range(2)]
    for k in range(2):
        loads[k].wait()
    for y in range(2):
        grad_mixed[y] = nn(branch[...], wo[y]).astype(BF)
    for k in (2, 3, 4, 5, 15):
        loads[k].wait()
    scale = 1.0 / math.sqrt(HEAD)

    def attention(i):
        y, n = i // 2, lax.rem(i, 2)
        rows = rows_at(n * SEQ, SEQ)
        queries, keys, grads = q[y, rows], kv[y, rows], grad_mixed[y, rows]
        grad_q, grad_k, grad_v = [], [None, None], [None, None]
        for h in range(4):
            g = h // 2
            key = keys[:, g * HEAD : (g + 1) * HEAD]
            value = keys[:, (2 + g) * HEAD : (3 + g) * HEAD]
            query = queries[:, h * HEAD : (h + 1) * HEAD]
            grad = grads[:, h * HEAD : (h + 1) * HEAD]
            low = probs[i, h]
            prob = low.astype(F32)
            grad_probs = nt(grad, value)
            grad_scores = (prob * (grad_probs - jnp.sum(grad_probs * prob, -1, keepdims=True))).astype(BF)
            grad_q.append(nn(grad_scores, key) * scale)
            back_k = tn(grad_scores, query) * scale
            back_v = tn(low, grad)
            grad_k[g] = back_k if grad_k[g] is None else grad_k[g] + back_k
            grad_v[g] = back_v if grad_v[g] is None else grad_v[g] + back_v
        first = first_half((SEQ, 4 * HEAD))
        for k, (pieces, target) in enumerate(((grad_q, dq), (grad_k + grad_v, dkv))):
            values = jnp.concatenate(pieces, -1)
            target[y, rows] = (values * tables[2 * k] - swap(values, first) * tables[2 * k + 1]).astype(BF)

    pl.loop(0, 2)(attention)
    mlp_sum.relay()
    pl.loop(2, 4)(attention)
    loads[6].wait()

    def weight_grad(p, left, right):
        for y in range(2):
            target = attn_grads[p].at[pl.ds(2 * y, 2)]
            target[...] = nn(left[...], right[y]).astype(BF).reshape(target.shape)
        attn_sum.start(p)

    weight_grad(0, normed_t, dq)
    weight_grad(1, normed_t, dkv)
    mlp_sum.spread()
    branch_t[...] = branch[...].T
    weight_grad(2, branch_t, mixed)
    for k in range(7, 15):
        loads[k].wait()

    def back(start):
        rows = rows_at(start, SEQ)
        return (nt(dq[0, rows], wq[0]) + nt(dq[1, rows], wq[1])) + (nt(dkv[0, rows], wkv[0]) + nt(dkv[1, rows], wkv[1]))

    part[...] = back((1 - core) * SEQ).astype(BF)
    pair = sent(part, arrived, send.at[0], recv.at[0], sibling())
    attn_sum.relay()
    keep_part[...] = back(core * SEQ)
    mlp_sum.narrow()
    pair.wait()

    @pl.loop(0, SEQ // STEP)
    def _(i):
        rows = rows_at(i * STEP, STEP)
        grad = keep_part[rows] + arrived[rows].astype(F32)
        values = xs[i].astype(F32)
        inverse = inverse_rms(values)
        unit = values * inverse
        change = inverse * (grad - unit * jnp.mean(grad * unit, -1, keepdims=True))
        in_grad[i] = gh[rows] + change

    for_partner[...] = in_grad[1 - yl].astype(BF)
    ends = [
        moved(in_grad.at[yl], in_grad_out, put.at[0]),
        sent(for_partner, from_partner, send.at[1], recv.at[1], partner()),
    ]
    attn_sum.spread()
    for copy in finals:
        copy.wait()
    result[1 - yl] = (kept[0] + others_half[1].astype(F32)).astype(BF)
    result[yl] = (kept[1] + others_half[0].astype(F32)).astype(BF)
    ends.append(moved(result, result_out, put.at[1]))
    mlp_sum.finish(in_four(mlp_ends))
    attn_sum.narrow()
    ends.extend(moved(mlp_ends[p], mlp_outs[p], put.at[2 + p]) for p in range(3))

    def along(start, gradient):
        weights = shard[:, :24, start : start + gradient.shape[2]]
        total = jnp.sum(weights * gradient, -1, keepdims=True)
        return total[0] + total[1]

    thin, half = attn_ends[0].shape[2], mlp_ends[0].shape[2]
    second = sum(
        along(3 * thin + 2 * half * p, one_sums[p]) + along(3 * thin + 2 * half * p + half, mlp_ends[p][...])
        for p in range(2)
    )
    attn_sum.finish(attn_ends)
    ends.extend(moved(attn_ends[p], attn_outs[p], put.at[5 + p]) for p in range(3))
    first = sum(along(thin * p, attn_ends[p][...]) for p in range(2))
    lane = lax.broadcasted_iota(jnp.int32, gain_part.shape, 1)
    gain_part[...] = jnp.where(lane == 0, first, second)
    ends.append(sent(gain_part, gain_in, send.at[4], recv.at[4], partner()))
    ends.append(moved(gain_part, gains_out, put.at[8]))
    for copy in ends:
        copy.wait()


def backward(x, grad_hidden, branch, n1t, q, kv, probs, mixed, wq, wkv, wo, tables, data, kept, away, shard, one_sums):
    rows, width = branch.shape
    third, wide = wq.shape[2], data[0].shape[-1]
    heads = (2, rows, third)
    weights = (2, width, third)
    half = (2, STEP, width)
    return call(
        backward_kernel,
        (x, grad_hidden, branch, n1t, q, kv, probs, mixed, wq, wkv, wo, tables, *data, kept, away, shard, *one_sums),
        [ANY] * 20,
        [shaped((2, 24, wide), F32)] * 3
        + [shaped((2, 24, third), F32)] * 3
        + [shaped(half), shaped(half[1:], F32), shaped(half[1:])]
        + [shaped((24, 128), F32)] * 2,
        [ANY] * 11,
        [
            pltpu.VMEM(half, BF),
            pltpu.VMEM((SEQ, width), F32),
            pltpu.VMEM((rows, width), BF),
            pltpu.VMEM((width, rows), BF),
            pltpu.VMEM((width, rows), BF),
            pltpu.VMEM(heads, BF),
            pltpu.VMEM(heads, BF),
            pltpu.VMEM((4, 4, SEQ, SEQ), BF),
            pltpu.VMEM(heads, BF),
            pltpu.VMEM(weights, BF),
            pltpu.VMEM(weights, BF),
            pltpu.VMEM(weights, BF),
            pltpu.VMEM(heads, BF),
            pltpu.VMEM(heads, BF),
            pltpu.VMEM(heads, BF),
            pltpu.VMEM((SEQ, width), BF),
            pltpu.VMEM((SEQ, width), F32),
            pltpu.VMEM((SEQ, width), BF),
            pltpu.VMEM(half, F32),
            pltpu.VMEM(half[1:], BF),
            pltpu.VMEM(half, F32),
            pltpu.VMEM(half, BF),
            pltpu.VMEM(half, BF),
            *[pltpu.VMEM((4, 4, 4, 48, third), BF) for _ in range(3)],
            *Reduce.buffers((wide, wide, wide // 2, wide // 2), PLANE),
            *Reduce.buffers((third,) * 3, SPARE_Y),
            *Reduce.semaphores(PLANE),
            *Reduce.semaphores(SPARE_Y),
            *[pltpu.VMEM((2, 24, wide), F32) for _ in range(3)],
            *[pltpu.VMEM((2, 24, third), F32) for _ in range(3)],
            pltpu.VMEM(shard.shape, F32),
            pltpu.VMEM((2, 2, 24, wide), F32),
            pltpu.VMEM((24, 128), F32),
            pltpu.VMEM(tables.shape, F32),
            pltpu.SemaphoreType.DMA((16,)),
            pltpu.SemaphoreType.DMA((9,)),
            pltpu.SemaphoreType.DMA((5,)),
            pltpu.SemaphoreType.DMA((5,)),
        ],
        "attn_backward_reduce",
        3,
    )


def last_kernel(own, theirs, result_in, one, two, attn, gains_one, gains_two, gain_sums, more, outs, wide, sems):
    result, in_grad, dq, dk, dv, do, dg, du, dd, gain_one_grad, gain_two_grad = outs
    yl = lax.axis_index("yl")
    copies = [moved(own, in_grad.at[yl], sems.at[0]), moved(result_in, result, sems.at[1])]
    wide[...] = theirs[...].astype(F32)
    copies.append(moved(wide, in_grad.at[1 - yl], sems.at[2]))
    gain_one, gain_two = as_column(gains_one), as_column(gains_two)
    thin, half = attn[0].shape[2], two[0].shape[2]
    keys = [[], []]
    for c in range(2):
        dq[:, c * thin : (c + 1) * thin] = attn[0][c] * gain_one
        for k in range(2):
            keys[k].append(attn[1][c, :, k * (thin // 2) : (k + 1) * (thin // 2)] * gain_one)
        do[:, c * thin : (c + 1) * thin] = attn[2][c]
        for k, part in enumerate((one, two)):
            start = (2 * c + k) * half
            dg[:, start : start + half] = part[0][c] * gain_two
            du[:, start : start + half] = part[1][c] * gain_two
            dd[:, start : start + half] = part[2][c]
    dk[...] = jnp.concatenate(keys[0], -1)
    dv[...] = jnp.concatenate(keys[1], -1)
    lane = lax.broadcasted_iota(jnp.int32, gain_sums.shape, 1)
    grads = ((gain_sums[...] + more[...]) / jnp.where(lane == 0, gain_one, gain_two)).T
    gain_one_grad[...] = grads[0:1, :24]
    gain_two_grad[...] = grads[1:2, :24]
    for copy in copies:
        copy.wait()


def placed_outputs(own, theirs, result, one, two, attn, gains, gain_sums, more_gain_sums):
    width, thin, half = own.shape[1], attn[0].shape[2], two[0].shape[2]

    def kernel(*refs):
        last_kernel(*refs[:3], refs[3:6], refs[6:9], refs[9:12], *refs[12:16], refs[16:27], *refs[27:])

    return pl.pallas_call(
        kernel,
        out_shape=[
            shaped((2, STEP, width)),
            shaped((2, STEP, width), F32),
            shaped((24, 2 * thin), F32),
            shaped((24, thin), F32),
            shaped((24, thin), F32),
            shaped((24, 2 * thin), F32),
            shaped((24, 4 * half), F32),
            shaped((24, 4 * half), F32),
            shaped((24, 4 * half), F32),
            shaped((1, 24), F32),
            shaped((1, 24), F32),
        ],
        in_specs=[ANY, VMEM, ANY] + [VMEM] * 13,
        out_specs=[ANY] * 2 + [VMEM] * 9,
        scratch_shapes=[pltpu.VMEM((STEP, width), F32), pltpu.SemaphoreType.DMA((3,))],
        compiler_params=pltpu.CompilerParams(vmem_limit_bytes=VMEM_LIMIT),
        name="place_outputs",
    )(own, theirs, result, *one, *two, *attn, *gains, gain_sums, more_gain_sums)


def tables_for(count, heads, plain):
    half = HEAD // 2
    inverse = np.float32(ROPE_BASE) ** (-(np.arange(half, dtype=np.float32) * np.float32(2.0)) / np.float32(HEAD))
    angle = np.arange(count, dtype=np.float32)[:, None] * inverse.astype(np.float32)[None, :]
    cosine, sine = np.cos(angle), np.sin(angle)
    cosine = np.tile(np.concatenate([cosine, cosine], -1), (1, heads))
    sine = np.tile(np.concatenate([-sine, sine], -1), (1, heads))
    cosine = np.concatenate([cosine, np.ones((count, plain), np.float32)], -1)
    sine = np.concatenate([sine, np.zeros((count, plain), np.float32)], -1)
    return np.stack([cosine, sine]).astype(np.float32)


def body(
    inputs,
    out_grad,
    lengths,
    query_weight,
    key_matrix,
    value_matrix,
    output_weight,
    gate_weight,
    up_weight,
    down_weight,
    attn_gain,
    mlp_gain,
):
    width = inputs.shape[2]
    own_weights = (
        query_weight,
        key_matrix,
        value_matrix,
        output_weight.T,
        gate_weight,
        up_weight,
        down_weight.T,
    )
    gains = (attn_gain.reshape(1, -1), mlp_gain.reshape(1, -1))
    third, wide = query_weight.shape[1] // 2, gate_weight.shape[1] // 2
    tables = jnp.asarray(np.concatenate([tables_for(SEQ, 4, 0), tables_for(SEQ, 2, 2 * HEAD)]))

    results = forward(
        own_weights, gains, lengths.reshape(1, -1), inputs, out_grad, tables, third, wide
    )
    two, one = results[:3], results[3:6]
    x, n1t, q, kv, probs, mixed, hidden, n2, n2t, cot, cott = results[6:17]
    (wq, wkv, wo), grads, acts, shard = results[17:20], results[20:23], results[23:26], results[26]

    def joined(w):
        return w.reshape(2, width, -1)

    def blocked(w):
        return w.reshape(2, 4, 4, 48, -1)

    *one_sums, dg, du, dd, kept, away, branch, grad_hidden = middle(
        n2, cot, hidden, n2t, cott, one, two, acts, [blocked(w) for w in grads]
    )
    *sums, result, in_grad, in_grad_theirs, gain_sums, more_gain_sums = backward(
        x,
        grad_hidden,
        branch,
        n1t,
        q,
        kv,
        probs,
        mixed,
        joined(wq),
        joined(wkv),
        joined(wo),
        tables,
        [blocked(w) for w in (dg, du, dd)],
        kept,
        away,
        shard,
        one_sums[:2],
    )
    result, in_grad, dq, dk, dv, do, dg, du, dd, gain_one_grad, gain_two_grad = placed_outputs(
        in_grad, in_grad_theirs, result, one_sums, sums[:3], sums[3:], gains, gain_sums, more_gain_sums
    )
    return result, in_grad, dq, dk, dv, do.T, dg, du, dd.T, gain_one_grad.reshape(24), gain_two_grad.reshape(24)


def solution(mesh):
    fine = Mesh(mesh.devices.reshape(2, 4, 4, 2, 2), AXES)
    rows = P(None, AXES, None)
    into, out = P(DP, "yl"), P("yl", DP)
    return jax.shard_map(
        body,
        mesh=fine,
        in_specs=(rows, rows, P(None, DP), into, into, into, out, into, into, out, P(DP), P(DP)),
        out_specs=(rows, rows, into, into, into, out, into, into, out, P(DP), P(DP)),
        check_vma=False,
    )
```
